32 devices in a mesh: row: 4 (over y, x), proto: 8 (over z, core).
Axes of the slice: x: 2, y: 2, z: 4, core: 2. Of those that a mesh axis runs over, the one named last changes fastest.
Arguments:
- embeddings: bfloat16 [8192, 1024], P('row'), may hold values from -24 to 24, as said below
- prototypes: bfloat16 [8192, 1024], P('proto', 'row'), may hold values from -6 to 6
- block_mask: int32 [64, 64], P('row', 'proto'), may hold values from 0 to 1, as said below
Outputs:
- targets: bfloat16 [8192, 1024], P('row', 'proto')
- row_potential: float32 [8192], P('row')
- column_potential: float32 [8192], P('proto')
The draws below stay inside these ranges and needn't reach their ends.
Inputs may be any that keep to these rules, and one draw needn't show every extreme that they name: `block_mask`: every row tile and every prototype tile has at least one candidate tile. `embeddings`: some rows copy a scaled prototype.
All inputs are finite; a program needn't handle non-finite values.
Results may differ from the reference program's by a relative error of at most 0.02.
Values may be sent and summed in bfloat16 or wider, within the bound.
No kernel may reach another device: no remote copies, remote signals or barrier semaphores. Data moves between devices by JAX's collectives and lax.ppermute only.
A program may use at most 64 MiB of HBM per device.

```python
import math
import jax
import jax.numpy as jnp
from jax import lax

D = 1024
TILE = 128
ITERS = 3
R_DEV = 2048
K_DEV = 1024
ROWS = 8192
PROTOS = 8192
ROW_BLOCKS = 64
PROTO_BLOCKS = 64
N_PROTO = 8


def layout(key):
    row_perm = jax.random.permutation(jax.random.fold_in(key, 11), ROW_BLOCKS)
    proto_perm = jax.random.permutation(jax.random.fold_in(key, 12), PROTO_BLOCKS)
    return (row_perm, proto_perm)


def drawn(key):
    row_perm, proto_perm = layout(key)
    modulus = min(ROW_BLOCKS, PROTO_BLOCKS)
    chosen = jnp.arange(0, ROW_BLOCKS, 8, dtype=jnp.int32)
    inverse = jnp.argsort(proto_perm)
    proto_block = inverse[row_perm[chosen] % modulus].astype(jnp.int32)
    rows_at = chosen * TILE + 3
    protos_at = proto_block * TILE + 5
    strength = 3.5 + 1.75 * (proto_block % 3).astype(jnp.float32)
    return (rows_at, protos_at, strength)


def proto_base(key):
    inner = jax.random.fold_in(key, 21)
    rows_at, protos_at, strength = drawn(key)
    base = jnp.clip(jax.random.normal(inner, (PROTOS, D), jnp.float32), -6.0, 6.0)
    shrink = 1.0 / (16.0 * strength)
    noise = 0.02 * jax.random.normal(jax.random.fold_in(key, 22), (protos_at.shape[0], D), jnp.float32)
    base = base.at[protos_at + 1].set((1.0 - shrink)[:, None] * base[protos_at] + noise)
    return jnp.clip(base, -6.0, 6.0)


def draw_prototypes(key, part):
    return proto_base(key).astype(jnp.bfloat16)


def draw_embeddings(key, part):
    values = jnp.clip(jax.random.normal(jax.random.fold_in(key, 31), (ROWS, D), jnp.float32), -6.0, 6.0)
    base = proto_base(key).astype(jnp.bfloat16).astype(jnp.float32)
    rows_at, protos_at, strength = drawn(key)
    factor = strength * (8.0 / math.sqrt(D))
    values = values.at[rows_at].set(factor[:, None] * base[protos_at])
    return jnp.clip(values, -24.0, 24.0).astype(jnp.bfloat16)


def draw_block_mask(key, part):
    row_perm, proto_perm = layout(key)
    modulus = min(ROW_BLOCKS, PROTO_BLOCKS)
    sure = row_perm[:, None] % modulus == proto_perm[None, :] % modulus
    level = 100 + 200 * jnp.arange(ROW_BLOCKS, dtype=jnp.int32) // ROW_BLOCKS
    rolled = jax.random.randint(jax.random.fold_in(key, 13), (ROW_BLOCKS, PROTO_BLOCKS), 0, 1000)
    return jnp.where(sure | (rolled < level[:, None]), 1, 0).astype(jnp.int32)


def setup_inputs(seed: int = 0) -> dict:
    keys = jax.random.split(jax.random.key(seed), 4)
    return {
        "embeddings": draw_embeddings(jax.random.fold_in(keys[3], 71), 0),
        "prototypes": draw_prototypes(jax.random.fold_in(keys[3], 71), 0),
        "block_mask": draw_block_mask(jax.random.fold_in(keys[3], 71), 0),
    }


NEGATIVE = -1e+30

def expand_mask(mask_rows):
    allowed = mask_rows == 1
    return jnp.repeat(jnp.repeat(allowed, TILE, axis=0), TILE, axis=1)

def reference(embeddings, prototypes, block_mask):
    scale = 4.0 / math.sqrt(D)
    protos_wide = prototypes.astype(jnp.float32)
    log_column = math.log(ROWS / PROTOS)
    blocks = jnp.arange(ROWS // R_DEV, dtype=jnp.int32)

    def similar_block(index):
        rows_part = lax.dynamic_slice_in_dim(embeddings, index * R_DEV, R_DEV, 0).astype(jnp.float32)
        mask_part = lax.dynamic_slice_in_dim(block_mask, index * (R_DEV // TILE), R_DEV // TILE, 0)
        similar = jnp.dot(rows_part, protos_wide.T, precision=lax.Precision.HIGHEST) * scale
        return (similar, expand_mask(mask_part))
    column_potential = jnp.zeros((PROTOS,), jnp.float32)
    row_potential = jnp.zeros((ROWS,), jnp.float32)
    for sweep in range(ITERS):

        def one_block(carry, index):
            column_peak, column_total = carry
            similar, allowed = similar_block(index)
            shifted = similar + column_potential[None, :]
            peak = lax.optimization_barrier(jnp.max(jnp.where(allowed, shifted, NEGATIVE), axis=1))
            total = lax.optimization_barrier(jnp.sum(jnp.where(allowed, jnp.exp(shifted - peak[:, None]), 0.0), axis=1))
            row_block = -(peak + jnp.log(total))
            lifted = similar + row_block[:, None]
            block_peak = lax.optimization_barrier(jnp.max(jnp.where(allowed, lifted, NEGATIVE), axis=0))
            new_peak = jnp.maximum(column_peak, block_peak)
            new_total = column_total * jnp.exp(column_peak - new_peak) + lax.optimization_barrier(jnp.sum(jnp.where(allowed, jnp.exp(lifted - new_peak[None, :]), 0.0), axis=0))
            return ((new_peak, new_total), row_block)
        start = (jnp.full((PROTOS,), NEGATIVE, jnp.float32), jnp.zeros((PROTOS,), jnp.float32))
        (column_peak, column_total), row_blocks = lax.scan(one_block, start, blocks)
        row_potential = row_blocks.reshape(ROWS)
        column_potential = log_column - (column_peak + jnp.log(column_total))

    def final_block(index):
        similar, allowed = similar_block(index)
        row_part = lax.dynamic_slice_in_dim(row_potential, index * R_DEV, R_DEV, 0)
        plan = jnp.where(allowed, jnp.exp(similar + row_part[:, None] + column_potential[None, :]), 0.0).astype(jnp.bfloat16)
        plan_wide = plan.reshape(R_DEV, N_PROTO, K_DEV).astype(jnp.float32)
        protos_split = protos_wide.reshape(N_PROTO, K_DEV, D)
        partial_value = jnp.einsum('rnk,nkd->nrd', plan_wide, protos_split, precision=lax.Precision.HIGHEST).astype(jnp.bfloat16)
        return lax.optimization_barrier(jnp.sum(partial_value.astype(jnp.float32), axis=0)).astype(jnp.bfloat16)
    targets = lax.map(final_block, blocks).reshape(ROWS, D)
    return (targets, row_potential, column_potential)
```

```python
import math

import jax
import jax.numpy as jnp
from jax import lax
from jax.sharding import PartitionSpec as P

ITERS = 3

NEGATIVE = -1e30


def expand_mask(block_mask, tile):
    allowed = block_mask == 1
    return jnp.repeat(jnp.repeat(allowed, tile, axis=0), tile, axis=1)


def swap(x, axis, offset):
    size = lax.axis_size(axis)
    return lax.ppermute(x, axis, [(i, i ^ offset) for i in range(size)])


def pair_sum(terms):
    while len(terms) > 1:
        terms = [terms[i] + terms[i + 1] for i in range(0, len(terms), 2)]
    return terms[0]


def exchange_lse(local, axis):
    every = [local] + [swap(local, axis, j) for j in range(1, lax.axis_size(axis))]
    peak = every[0]
    for part in every[1:]:
        peak = jnp.maximum(peak, part)
    return peak + jnp.log(pair_sum([jnp.exp(part - peak) for part in every]))


def local_lse(values, allowed, axis):
    values = jnp.where(allowed, values, NEGATIVE)
    peak = jnp.max(values, axis=axis, keepdims=True)
    total = jnp.sum(jnp.where(allowed, jnp.exp(values - peak), 0.0), axis=axis)
    return jnp.squeeze(peak, axis) + jnp.log(total)


def gather_features(shard):
    if lax.axis_size("row") != 4:
        return lax.all_gather(shard, "row", axis=1, tiled=True)
    half = shard.shape[0] // 2
    near = swap(shard, "row", 1)
    far = swap(shard, "row", 2)
    top = swap(far[:half], "row", 1)
    bottom = swap(near[half:], "row", 2)
    cross = jnp.concatenate([top, bottom], axis=0)
    me = lax.axis_index("row")
    width = shard.shape[1]
    out = jnp.zeros((shard.shape[0], 4 * width), shard.dtype)
    for offset, part in enumerate((shard, near, far, cross)):
        out = lax.dynamic_update_slice_in_dim(out, part, (me ^ offset) * width, 1)
    return out


def scatter_partials(partial_value):
    size = lax.axis_size("proto")
    line = size // 2
    me = lax.axis_index("proto")
    z, core = me // 2, me % 2
    rows, features = partial_value.shape
    width = features // size
    split = partial_value.reshape(rows, line, 2, width).transpose(2, 1, 0, 3)
    mine = lax.dynamic_index_in_dim(split, core, 0, keepdims=False)
    other = lax.dynamic_index_in_dim(split, 1 - core, 0, keepdims=False)
    got = lax.ppermute(other, "proto", [(i, i ^ 1) for i in range(size)])
    both = mine.astype(jnp.float32) + got.astype(jnp.float32)
    up = [(i, i + 2) for i in range(size - 2)]
    down = [(i + 2, i) for i in range(size - 2)]

    def chunk(index):
        return lax.dynamic_index_in_dim(both, jnp.clip(index, 0, line - 1), 0, keepdims=False)

    from_below = jnp.zeros((rows, width), jnp.float32)
    from_above = jnp.zeros((rows, width), jnp.float32)
    for step in range(1, line):
        send_up = chunk(line - step + z) + from_below
        send_down = chunk(z - (line - step)) + from_above
        from_below = lax.ppermute(send_up.astype(jnp.bfloat16), "proto", up).astype(jnp.float32)
        from_above = lax.ppermute(send_down.astype(jnp.bfloat16), "proto", down).astype(jnp.float32)
    return (chunk(z) + from_below + from_above).astype(jnp.bfloat16)


def shards(embeddings, prototypes, block_mask):
    features = gather_features(prototypes)
    scale = 4.0 / math.sqrt(features.shape[1])
    similar = (
        lax.dot_general(
            embeddings, features, (((1,), (1,)), ((), ())), preferred_element_type=jnp.float32
        )
        * scale
    )
    tile = similar.shape[0] // block_mask.shape[0]
    allowed = expand_mask(block_mask, tile)
    rows_all = similar.shape[0] * lax.axis_size("row")
    protos_all = similar.shape[1] * lax.axis_size("proto")
    log_column = math.log(rows_all / protos_all)
    column_potential = jnp.zeros((similar.shape[1],), jnp.float32)
    for sweep in range(ITERS):
        row_potential = -exchange_lse(
            local_lse(similar + column_potential[None, :], allowed, 1), "proto"
        )
        column_potential = log_column - exchange_lse(
            local_lse(similar + row_potential[:, None], allowed, 0), "row"
        )
    plan = jnp.where(
        allowed, jnp.exp(similar + row_potential[:, None] + column_potential[None, :]), 0.0
    ).astype(jnp.bfloat16)
    partial_value = jnp.dot(plan, features, preferred_element_type=jnp.float32)
    targets = scatter_partials(partial_value.astype(jnp.bfloat16))
    return (targets, row_potential, column_potential)


def solution(mesh):
    return jax.shard_map(
        shards,
        mesh=mesh,
        in_specs=(P("row", None), P("proto", "row"), P("row", "proto")),
        out_specs=(P("row", "proto"), P("row"), P("proto")),
        check_vma=False,
    )
```

```python
import math

import jax
import jax.numpy as jnp
from jax import lax
from jax.sharding import PartitionSpec as P

ITERS = 3

NEGATIVE = -1e30


def expand_mask(block_mask, tile):
    allowed = block_mask == 1
    return jnp.repeat(jnp.repeat(allowed, tile, axis=0), tile, axis=1)


def swap(x, axis, offset):
    size = lax.axis_size(axis)
    return lax.ppermute(x, axis, [(i, i ^ offset) for i in range(size)])


def exchange_lse(local, axis):
    size = lax.axis_size(axis)
    if axis == "proto":
        every = lax.all_gather(local, axis)
    else:
        copies = jnp.broadcast_to(local[None, :], (size, local.shape[0]))
        every = lax.all_to_all(copies, axis, 0, 0)
    peak = jnp.max(every, axis=0)
    return peak + jnp.log(jnp.sum(jnp.exp(every - peak[None, :]), axis=0))


def local_lse(values, allowed, axis):
    values = jnp.where(allowed, values, NEGATIVE)
    peak = jnp.max(values, axis=axis, keepdims=True)
    total = jnp.sum(jnp.where(allowed, jnp.exp(values - peak), 0.0), axis=axis)
    return jnp.squeeze(peak, axis) + jnp.log(total)


def gather_features(shard):
    if lax.axis_size("row") != 4:
        return lax.all_gather(shard, "row", axis=1, tiled=True)
    half = shard.shape[0] // 2
    near = swap(shard, "row", 1)
    far = swap(shard, "row", 2)
    top = swap(far[:half], "row", 1)
    bottom = swap(near[half:], "row", 2)
    cross = jnp.concatenate([top, bottom], axis=0)
    me = lax.axis_index("row")
    width = shard.shape[1]
    out = jnp.zeros((shard.shape[0], 4 * width), shard.dtype)
    for offset, part in enumerate((shard, near, far, cross)):
        out = lax.dynamic_update_slice_in_dim(out, part, (me ^ offset) * width, 1)
    return out


def scatter_partials(partial_value):
    size = lax.axis_size("proto")
    line = size // 2
    me = lax.axis_index("proto")
    z, core = me // 2, me % 2
    rows, features = partial_value.shape
    width = features // size
    split = partial_value.reshape(rows, line, 2, width).transpose(2, 1, 0, 3)
    mine = lax.dynamic_index_in_dim(split, core, 0, keepdims=False)
    other = lax.dynamic_index_in_dim(split, 1 - core, 0, keepdims=False)
    got = lax.ppermute(other, "proto", [(i, i ^ 1) for i in range(size)])
    both = mine.astype(jnp.float32) + got.astype(jnp.float32)
    up = [(i, i + 2) for i in range(size - 2)]
    down = [(i + 2, i) for i in range(size - 2)]

    def chunk(index):
        return lax.dynamic_index_in_dim(both, jnp.clip(index, 0, line - 1), 0, keepdims=False)

    from_below = jnp.zeros((rows, width), jnp.float32)
    from_above = jnp.zeros((rows, width), jnp.float32)
    for step in range(1, line):
        send_up = chunk(line - step + z) + from_below
        send_down = chunk(z - (line - step)) + from_above
        from_below = lax.ppermute(send_up.astype(jnp.bfloat16), "proto", up).astype(jnp.float32)
        from_above = lax.ppermute(send_down.astype(jnp.bfloat16), "proto", down).astype(jnp.float32)
    return (chunk(z) + from_below + from_above).astype(jnp.bfloat16)


def shards(embeddings, prototypes, block_mask):
    features = gather_features(prototypes)
    scale = 4.0 / math.sqrt(features.shape[1])
    similar = (
        lax.dot_general(
            embeddings, features, (((1,), (1,)), ((), ())), preferred_element_type=jnp.float32
        )
        * scale
    )
    tile = similar.shape[0] // block_mask.shape[0]
    allowed = expand_mask(block_mask, tile)
    rows_all = similar.shape[0] * lax.axis_size("row")
    protos_all = similar.shape[1] * lax.axis_size("proto")
    log_column = math.log(rows_all / protos_all)
    column_potential = jnp.zeros((similar.shape[1],), jnp.float32)
    for sweep in range(ITERS):
        row_potential = -exchange_lse(
            local_lse(similar + column_potential[None, :], allowed, 1), "proto"
        )
        column_potential = log_column - exchange_lse(
            local_lse(similar + row_potential[:, None], allowed, 0), "row"
        )
    plan = jnp.where(
        allowed, jnp.exp(similar + row_potential[:, None] + column_potential[None, :]), 0.0
    ).astype(jnp.bfloat16)
    partial_value = jnp.dot(plan, features, preferred_element_type=jnp.float32)
    targets = scatter_partials(partial_value.astype(jnp.bfloat16))
    return (targets, row_potential, column_potential)


def solution(mesh):
    return jax.shard_map(
        shards,
        mesh=mesh,
        in_specs=(P("row", None), P("proto", "row"), P("row", "proto")),
        out_specs=(P("row", "proto"), P("row"), P("proto")),
        check_vma=False,
    )
```

```python
import functools
import math

import jax
import jax.numpy as jnp
from jax import lax
from jax.experimental import pallas as pl
from jax.experimental.pallas import tpu as pltpu
from jax.sharding import PartitionSpec as P

ITERS = 3
TILE = 128
NEGATIVE = -1e30

VMEM = pl.BlockSpec(memory_space=pltpu.VMEM)
SMEM = pl.BlockSpec(memory_space=pltpu.SMEM)


def swap(x, axis, offset):
    size = lax.axis_size(axis)
    return lax.ppermute(x, axis, [(i, i ^ offset) for i in range(size)])


def pair_sum(terms):
    while len(terms) > 1:
        terms = [terms[i] + terms[i + 1] for i in range(0, len(terms), 2)]
    return terms[0]


def combine(parts):
    peak = functools.reduce(jnp.maximum, parts)
    return peak + jnp.log(pair_sum([jnp.exp(part - peak) for part in parts]))


def tile_lists(mask):
    count = mask.shape[1]
    at = jnp.arange(count, dtype=jnp.int32)
    before = jnp.sum(jnp.where(at[None, :] < at[:, None], mask[:, None, :], 0), axis=2)
    hit = (mask[:, None, :] == 1) & (before[:, None, :] == at[None, :, None])
    places = jnp.sum(jnp.where(hit, at[None, None, :], 0), axis=2)
    return jnp.sum(mask, axis=1), places


def row_pass(count_ref, list_ref, s_ref, c_ref, out_ref):
    row_tiles, columns = list_ref.shape
    lane = lax.broadcasted_iota(jnp.int32, (TILE, TILE), 1)

    def one_row_tile(t, found):
        count = count_ref[t]

        def score(k):
            u = list_ref[t, k]
            tile = s_ref[t * columns + u]
            return tile if c_ref is None else tile + c_ref[pl.ds(u, 1), :]

        peak = lax.fori_loop(
            0, count, lambda k, a: jnp.maximum(a, score(k)), jnp.full((TILE, TILE), NEGATIVE, jnp.float32)
        )
        peak = jnp.max(peak, axis=1, keepdims=True)
        total = lax.fori_loop(
            0, count, lambda k, a: a + jnp.exp(score(k) - peak), jnp.zeros((TILE, TILE), jnp.float32)
        )
        total = jnp.sum(total, axis=1, keepdims=True)
        return jnp.where(lane == t, peak + jnp.log(total), found)

    found = lax.fori_loop(0, row_tiles, one_row_tile, jnp.zeros((TILE, TILE), jnp.float32))
    out_ref[...] = found.T[:row_tiles]


def spread_rows(row, wide_ref):
    row_tiles = row.shape[0]
    standing = jnp.concatenate(
        [row, jnp.zeros((TILE - row_tiles, TILE), jnp.float32)], axis=0
    ).T
    for t in range(row_tiles):
        wide_ref[t] = jnp.broadcast_to(standing[:, t : t + 1], (TILE, TILE))


def panel_kernel(widths, blocks, count_ref, list_ref, ccount_ref, clist_ref, offset_ref, *refs):
    e_ref, (s_ref, out_ref) = refs[0], refs[-2:]
    pieces = refs[1:-2]
    columns, row_tiles = clist_ref.shape
    scale = 4.0 / math.sqrt(e_ref.shape[1])
    core = offset_ref[0]
    half = columns // 2
    at = 0
    groups = []
    for group in range(2):
        groups.append([])
        for number in blocks:
            groups[-1].append(pieces[at : at + number])
            at += number
    for group in range(2):
        first = (core if group == 0 else 1 - core) * half
        for u in range(half):
            column = first + u

            def one_tile(k, carry, group=group, u=u, column=column):
                t = clist_ref[column, k]
                total = None
                for j, width in enumerate(widths):
                    parts = groups[group][j]
                    each = half // len(parts)
                    block = parts[u // each][(u % each) * TILE : (u % each + 1) * TILE, :]
                    start = pl.multiple_of(offset_ref[1 + j], TILE)
                    rows = e_ref[pl.ds(pl.multiple_of(t * TILE, TILE), TILE), pl.ds(start, width)]
                    product = lax.dot_general(
                        rows, block, (((1,), (1,)), ((), ())), preferred_element_type=jnp.float32
                    )
                    total = product if total is None else total + product
                s_ref[t * columns + column] = total * scale
                return carry

            lax.fori_loop(0, ccount_ref[column], one_tile, 0)
    row_pass(count_ref, list_ref, s_ref, None, out_ref)


def row_kernel(log_column, count_ref, list_ref, s_ref, *refs):
    parts, (out_ref, c_ref) = refs[:-2], refs[-2:]
    c_ref[...] = log_column - combine([part[...] for part in parts])
    row_pass(count_ref, list_ref, s_ref, c_ref, out_ref)


def column_kernel(ccount_ref, clist_ref, s_ref, *refs):
    parts, (out_ref, r_ref, wide_ref) = refs[:-3], refs[-3:]
    columns = clist_ref.shape[0]
    row = -combine([part[...] for part in parts])
    r_ref[...] = row
    spread_rows(row, wide_ref)

    def one_column_tile(u, carry):
        count = ccount_ref[u]

        def score(k):
            t = clist_ref[u, k]
            return s_ref[t * columns + u] + wide_ref[t]

        peak = lax.fori_loop(
            0, count, lambda k, a: jnp.maximum(a, score(k)), jnp.full((TILE, TILE), NEGATIVE, jnp.float32)
        )
        peak = jnp.max(peak, axis=0, keepdims=True)
        total = lax.fori_loop(
            0, count, lambda k, a: a + jnp.exp(score(k) - peak), jnp.zeros((TILE, TILE), jnp.float32)
        )
        total = jnp.sum(total, axis=0, keepdims=True)
        out_ref[pl.ds(u, 1), :] = peak + jnp.log(total)
        return carry

    lax.fori_loop(0, columns, one_column_tile, 0)


def plan_kernel(log_column, lines, count_ref, list_ref, s_ref, r_ref, p_ref, *refs):
    parts, (out_ref, c_ref, wide_ref) = refs[:-3], refs[-3:]
    row_tiles, columns = list_ref.shape
    c_ref[...] = log_column - combine([part[...] for part in parts])
    spread_rows(r_ref[...], wide_ref)
    width = p_ref.shape[1] // lines

    def one_row_tile(t, carry):
        def one_tile(k, total):
            u = list_ref[t, k]
            plan = jnp.exp(s_ref[t * columns + u] + wide_ref[t] + c_ref[pl.ds(u, 1), :])
            block = p_ref[pl.ds(pl.multiple_of(u * TILE, TILE), TILE), :]
            return total + jnp.dot(
                plan.astype(jnp.bfloat16), block, preferred_element_type=jnp.float32
            )

        total = lax.fori_loop(
            0, count_ref[t], one_tile, jnp.zeros((TILE, p_ref.shape[1]), jnp.float32)
        ).astype(jnp.bfloat16)
        for z in range(lines):
            out_ref[z, pl.ds(pl.multiple_of(t * TILE, TILE), TILE), :] = total[
                :, z * width : (z + 1) * width
            ]
        return carry

    lax.fori_loop(0, row_tiles, one_row_tile, 0)


def params(mebibytes):
    return pltpu.CompilerParams(vmem_limit_bytes=mebibytes * 2**20)


def gather_features(shard):
    width = shard.shape[1]
    me = lax.axis_index("row")
    if lax.axis_size("row") != 4 or width % TILE:
        return [(lax.all_gather(shard, "row", axis=1, tiled=True),)], [jnp.int32(0)]
    half = shard.shape[0] // 2
    near = swap(shard, "row", 1)
    far = swap(shard, "row", 2)
    top = swap(far[:half], "row", 1)
    bottom = swap(near[half:], "row", 2)
    starts = [(me ^ offset) * width for offset in range(4)]
    return [(shard,), (near,), (far,), (top, bottom)], starts


def chip_features(groups, starts, core, width, lines):
    halves = []
    for pieces in groups:
        whole = jnp.zeros((pieces[0][0].shape[0], 2 * lines * width), jnp.bfloat16)
        for blocks, start in zip(pieces, starts):
            block = blocks[0] if len(blocks) == 1 else jnp.concatenate(blocks, axis=0)
            whole = lax.dynamic_update_slice_in_dim(whole, block, start, 1)
        whole = whole.reshape(whole.shape[0], lines, 2, width)
        halves.append(lax.dynamic_index_in_dim(whole, core, 2, keepdims=False))
    first = jnp.where(core == 0, halves[0], halves[1])
    second = jnp.where(core == 0, halves[1], halves[0])
    return jnp.concatenate([first, second], axis=0).reshape(-1, lines * width)


def scatter_partials(split):
    size = lax.axis_size("proto")
    line = size // 2
    z = lax.axis_index("proto") // 2
    up = [(i, i + 2) for i in range(size - 2)]
    down = [(i + 2, i) for i in range(size - 2)]

    def chunk(index):
        index = jnp.clip(index, 0, line - 1)
        return lax.dynamic_index_in_dim(split, index, 0, keepdims=False).astype(jnp.float32)

    from_below = from_above = None
    for step in range(1, line):
        send_up, send_down = chunk(line - step + z), chunk(z - (line - step))
        if step > 1:
            send_up, send_down = send_up + from_below, send_down + from_above
        send_up, send_down = lax.optimization_barrier(
            (send_up.astype(jnp.bfloat16), send_down.astype(jnp.bfloat16))
        )
        from_below = lax.ppermute(send_up, "proto", up)
        from_above = lax.ppermute(send_down, "proto", down)
        from_below, from_above = lax.optimization_barrier((from_below, from_above))
        from_below, from_above = from_below.astype(jnp.float32), from_above.astype(jnp.float32)
    return (chunk(z) + from_below + from_above).astype(jnp.bfloat16)


def shards(embeddings, prototypes, block_mask):
    n_row, n_proto = lax.axis_size("row"), lax.axis_size("proto")
    lines = n_proto // 2
    core = lax.axis_index("proto") % 2
    rows, features = embeddings.shape
    protos = 2 * prototypes.shape[0]
    width = features // n_proto
    log_column = math.log(rows * n_row / (protos * lines))

    other_mask = swap(block_mask, "proto", 1)
    own, starts = gather_features(prototypes)
    sibling = [tuple(swap(block, "proto", 1) for block in blocks) for blocks in own]

    mask = jnp.where(block_mask == 1, 1, 0)
    other_mask = jnp.where(other_mask == 1, 1, 0)
    mask = jnp.where(
        core == 0,
        jnp.concatenate([mask, other_mask], axis=1),
        jnp.concatenate([other_mask, mask], axis=1),
    )
    row_tiles, columns = mask.shape
    counts, lists = tile_lists(mask)
    ccounts, clists = tile_lists(mask.T)

    row_shape = jax.ShapeDtypeStruct((row_tiles, TILE), jnp.float32)
    column_shape = jax.ShapeDtypeStruct((columns, TILE), jnp.float32)
    panel = pltpu.VMEM((row_tiles * columns, TILE, TILE), jnp.float32)
    wide = pltpu.VMEM((row_tiles, TILE, TILE), jnp.float32)
    offsets = jnp.stack([core.astype(jnp.int32)] + [s.astype(jnp.int32) for s in starts])
    pieces = [block for group in (own, sibling) for blocks in group for block in blocks]
    similar, row_part = pl.pallas_call(
        functools.partial(
            panel_kernel, [b[0].shape[1] for b in own], [len(b) for b in own]
        ),
        out_shape=(panel, row_shape),
        in_specs=[SMEM] * 5 + [VMEM] * (1 + len(pieces)),
        out_specs=(VMEM, VMEM),
        compiler_params=params(16),
        name="panel",
    )(counts, lists, ccounts, clists, offsets, embeddings, *pieces)
    chosen = chip_features((own, sibling), starts, core, width, lines)

    for sweep in range(ITERS):
        parts = [row_part] + [swap(row_part, "proto", 2 * j) for j in range(1, lines)]
        column_part, row_potential = pl.pallas_call(
            column_kernel,
            out_shape=(column_shape, row_shape),
            in_specs=[SMEM] * 2 + [VMEM] * (1 + len(parts)),
            out_specs=(VMEM, VMEM),
            scratch_shapes=[wide],
            compiler_params=params(8),
            name="column_pass",
        )(ccounts, clists, similar, *parts)
        parts = [column_part] + [swap(column_part, "row", j) for j in range(1, n_row)]
        if sweep < ITERS - 1:
            row_part, _ = pl.pallas_call(
                functools.partial(row_kernel, log_column),
                out_shape=(row_shape, column_shape),
                in_specs=[SMEM] * 2 + [VMEM] * (1 + len(parts)),
                out_specs=(VMEM, VMEM),
                compiler_params=params(8),
                name="row_pass",
            )(counts, lists, similar, *parts)
    split, column_potential = pl.pallas_call(
        functools.partial(plan_kernel, log_column, lines),
        out_shape=(jax.ShapeDtypeStruct((lines, rows, width), jnp.bfloat16), column_shape),
        in_specs=[SMEM] * 2 + [VMEM] * (3 + len(parts)),
        out_specs=(VMEM, VMEM),
        scratch_shapes=[wide],
        compiler_params=params(16),
        name="plan",
    )(counts, lists, similar, row_potential, chosen, *parts)
    targets = scatter_partials(split)
    half = columns // 2
    column_potential = lax.dynamic_slice_in_dim(column_potential, core * half, half, 0)
    return (targets, row_potential.reshape(rows), column_potential.reshape(protos // 2))


def solution(mesh):
    return jax.shard_map(
        shards,
        mesh=mesh,
        in_specs=(P("row", None), P("proto", "row"), P("row", "proto")),
        out_specs=(P("row", "proto"), P("row"), P("proto")),
        check_vma=False,
    )
```

```python
import functools
import math

import jax
import jax.numpy as jnp
from jax import lax
from jax.experimental import pallas as pl
from jax.experimental.pallas import tpu as pltpu
from jax.sharding import PartitionSpec as P

ITERS = 3
TILE = 128
NEGATIVE = -1e30

VMEM = pl.BlockSpec(memory_space=pltpu.VMEM)
SMEM = pl.BlockSpec(memory_space=pltpu.SMEM)


def swap(x, axis, offset):
    size = lax.axis_size(axis)
    return lax.ppermute(x, axis, [(i, i ^ offset) for i in range(size)])


def pair_sum(terms):
    while len(terms) > 1:
        terms = [terms[i] + terms[i + 1] for i in range(0, len(terms), 2)]
    return terms[0]


def combine(parts):
    peak = functools.reduce(jnp.maximum, parts)
    return peak + jnp.log(pair_sum([jnp.exp(part - peak) for part in parts]))


def ordered(mask):
    size = mask.shape[1]
    at = jnp.arange(size, dtype=jnp.int32)
    before = jnp.sum(jnp.where(at[None, :] < at[:, None], mask[:, None, :], 0), axis=2)
    hit = (mask[:, None, :] == 1) & (before[:, None, :] == at[None, :, None])
    places = jnp.sum(jnp.where(hit, at[None, None, :] - size, 0), axis=2) + size
    return places, jnp.sum(mask, axis=1)


def score_loop(count, step, start):
    return lax.fori_loop(0, count, lambda k, a: step(2 * k + 1, step(2 * k, a)), start)


def row_pass(list_ref, half_ref, s_ref, c_ref, acc_ref, out_ref):
    row_tiles, columns = list_ref.shape
    lane = lax.broadcasted_iota(jnp.int32, (TILE, TILE), 1)
    dummy = row_tiles * columns

    def score(t, k):
        u = list_ref[t, k]
        tile = s_ref[jnp.where(u == columns, dummy, t * columns + u)]
        return tile if c_ref is None else tile + c_ref[pl.ds(u, 1), :]

    for t in range(row_tiles):
        acc_ref[t] = score_loop(
            half_ref[t],
            lambda k, a, t=t: jnp.maximum(a, score(t, k)),
            jnp.full((TILE, TILE), NEGATIVE, jnp.float32),
        )
    peaks = jnp.zeros((TILE, TILE), jnp.float32)
    for t in range(row_tiles):
        peak = jnp.max(acc_ref[t], axis=1, keepdims=True)
        peaks = jnp.where(lane == t, peak, peaks)
        acc_ref[t] = jnp.broadcast_to(peak, (TILE, TILE))
    for t in range(row_tiles):
        acc_ref[t] = score_loop(
            half_ref[t],
            lambda k, a, t=t: a + jnp.exp(score(t, k) - acc_ref[t]),
            jnp.zeros((TILE, TILE), jnp.float32),
        )
    totals = jnp.zeros((TILE, TILE), jnp.float32)
    for t in range(row_tiles):
        totals = jnp.where(lane == t, jnp.sum(acc_ref[t], axis=1, keepdims=True), totals)
    out_ref[...] = (peaks + jnp.log(totals)).T[:row_tiles]


def spread_rows(row, wide_ref):
    row_tiles = row.shape[0]
    standing = jnp.concatenate(
        [row, jnp.zeros((TILE - row_tiles, TILE), jnp.float32)], axis=0
    ).T
    for t in range(row_tiles):
        wide_ref[t] = jnp.broadcast_to(standing[:, t : t + 1], (TILE, TILE))


def panel_kernel(row_blocks, list_ref, half_ref, plist_ref, pquarter_ref, offset_ref, *refs):
    e_ref, (s_ref, p_ref, out_ref, acc_ref) = refs[0], refs[-4:]
    pieces = refs[1:-4]
    row_tiles, columns = list_ref.shape
    scale = 4.0 / math.sqrt(e_ref.shape[1])
    core = offset_ref[0]
    protos = p_ref.shape[0] // 2
    for n, piece in enumerate(pieces):
        group, within = n * 2 // len(pieces), n % (len(pieces) // 2)
        rows, width = piece.shape
        first = (core if group == 0 else 1 - core) * protos + row_blocks[within]
        start = pl.multiple_of(offset_ref[1 + within], TILE)
        p_ref[pl.ds(pl.multiple_of(first, TILE), rows), pl.ds(start, width)] = piece[...]
    s_ref[row_tiles * columns] = jnp.full((TILE, TILE), NEGATIVE, jnp.float32)

    def one_pair(pair, carry):
        def four_tiles(k, carry):
            at = [jnp.minimum(plist_ref[pair, 4 * k + i], row_tiles - 1) for i in range(4)]
            rows = jnp.concatenate(
                [e_ref[pl.ds(pl.multiple_of(t * TILE, TILE), TILE), :] for t in at], axis=0
            )
            block = p_ref[pl.ds(pl.multiple_of(pair * 2 * TILE, TILE), 2 * TILE), :]
            product = scale * lax.dot_general(
                rows, block, (((1,), (1,)), ((), ())), preferred_element_type=jnp.float32
            )
            for i, t in enumerate(at):
                for side in range(2):
                    s_ref[t * columns + 2 * pair + side] = product[
                        i * TILE : (i + 1) * TILE, side * TILE : (side + 1) * TILE
                    ]
            return carry

        return lax.fori_loop(0, pquarter_ref[pair], four_tiles, carry)

    lax.fori_loop(0, columns // 2, one_pair, 0)
    row_pass(list_ref, half_ref, s_ref, None, acc_ref, out_ref)


def row_kernel(log_column, list_ref, half_ref, s_ref, *refs):
    parts, (out_ref, c_ref, acc_ref) = refs[:-3], refs[-3:]
    columns = list_ref.shape[1]
    c_ref[:columns] = log_column - combine([part[...] for part in parts])
    c_ref[columns:] = jnp.zeros((c_ref.shape[0] - columns, TILE), jnp.float32)
    row_pass(list_ref, half_ref, s_ref, c_ref, acc_ref, out_ref)


def column_kernel(list_ref, half_ref, s_ref, *refs):
    parts, (out_ref, r_ref, wide_ref, acc_ref) = refs[:-4], refs[-4:]
    columns, row_tiles = list_ref.shape
    dummy = row_tiles * columns
    row = -combine([part[...] for part in parts])
    r_ref[...] = row
    spread_rows(row, wide_ref)

    def score(u, k):
        t = list_ref[u, k]
        inside = jnp.minimum(t, row_tiles - 1)
        return s_ref[jnp.where(t == row_tiles, dummy, t * columns + u)] + wide_ref[inside]

    for u in range(columns):
        acc_ref[u] = score_loop(
            half_ref[u],
            lambda k, a, u=u: jnp.maximum(a, score(u, k)),
            jnp.full((TILE, TILE), NEGATIVE, jnp.float32),
        )
    peaks = [jnp.max(acc_ref[u], axis=0, keepdims=True) for u in range(columns)]
    for u in range(columns):
        acc_ref[u] = score_loop(
            half_ref[u],
            lambda k, a, u=u: a + jnp.exp(score(u, k) - peaks[u]),
            jnp.zeros((TILE, TILE), jnp.float32),
        )
    totals = [jnp.sum(acc_ref[u], axis=0, keepdims=True) for u in range(columns)]
    out_ref[...] = jnp.concatenate(peaks, axis=0) + jnp.log(jnp.concatenate(totals, axis=0))


def plan_kernel(log_column, lines, plist_ref, pquarter_ref, mask_ref, offset_ref, s_ref, r_ref, p_ref, *refs):
    parts, (out_ref, c_ref, wide_ref, total_ref) = refs[:-4], refs[-4:]
    row_tiles, columns = mask_ref.shape
    dummy = row_tiles * columns
    c_ref[...] = log_column - combine([part[...] for part in parts])
    spread_rows(r_ref[...], wide_ref)
    width = out_ref.shape[2]
    core = offset_ref[0]
    total_ref[...] = jnp.zeros(total_ref.shape, jnp.float32)

    def one_pair(pair, carry):
        first = pl.multiple_of(pair * 2 * TILE, TILE)
        if width % TILE:
            wide = p_ref[pl.ds(first, 2 * TILE), :]
            blocks = [
                jnp.where(core == 0, wide[:, z * 2 * width :][:, :width], wide[:, (z * 2 + 1) * width :][:, :width])
                for z in range(lines)
            ]
        else:
            blocks = [
                p_ref[pl.ds(first, 2 * TILE), pl.ds(pl.multiple_of((2 * z + core) * width, TILE), width)]
                for z in range(lines)
            ]
        block = jnp.concatenate(blocks, axis=1)

        def four_tiles(k, carry):
            at = [plist_ref[pair, 4 * k + i] for i in range(4)]
            inside = [jnp.minimum(t, row_tiles - 1) for t in at]
            strips = []
            for t, real in zip(at, inside):
                sides = []
                for side in range(2):
                    u = 2 * pair + side
                    good = (t < row_tiles) & (mask_ref[real, u] == 1)
                    tile = s_ref[jnp.where(good, t * columns + u, dummy)]
                    sides.append(jnp.exp(tile + wide_ref[real] + c_ref[pl.ds(u, 1), :]).astype(jnp.bfloat16))
                strips.append(jnp.concatenate(sides, axis=1))
            product = jnp.dot(
                jnp.concatenate(strips, axis=0), block, preferred_element_type=jnp.float32
            )
            for i, t in enumerate(inside):
                total_ref[t] += product[i * TILE : (i + 1) * TILE]
            return carry

        return lax.fori_loop(0, pquarter_ref[pair], four_tiles, carry)

    lax.fori_loop(0, columns // 2, one_pair, 0)
    for t in range(row_tiles):
        total = total_ref[t].astype(jnp.bfloat16)
        for z in range(lines):
            out_ref[z, t * TILE : (t + 1) * TILE, :] = total[:, z * width : (z + 1) * width]


def params(mebibytes):
    return pltpu.CompilerParams(vmem_limit_bytes=mebibytes * 2**20)


def gather_features(shard):
    width = shard.shape[1]
    me = lax.axis_index("row")

    def sibling(block):
        return swap(block, "proto", 1)

    if lax.axis_size("row") != 4 or width % TILE:
        whole = lax.all_gather(shard, "row", axis=1, tiled=True)
        return [whole, sibling(whole)], [0], [jnp.int32(0)]
    half = shard.shape[0] // 2
    top, bottom = shard[:half], shard[half:]
    near_bottom = swap(bottom, "row", 1)
    far_top = swap(top, "row", 2)
    near_top = swap(top, "row", 1)
    far_bottom = swap(bottom, "row", 2)
    cross_top = swap(far_top, "row", 1)
    cross_bottom = swap(near_bottom, "row", 2)
    pieces = [shard, near_top, near_bottom, far_top, far_bottom, cross_top, cross_bottom]
    firsts = [0, 0, half, 0, half, 0, half]
    starts = [(me ^ offset) * width for offset in (0, 1, 1, 2, 2, 3, 3)]
    return pieces + [sibling(piece) for piece in pieces], firsts, starts


def scatter_partials(split):
    size = lax.axis_size("proto")
    line = size // 2
    z = lax.axis_index("proto") // 2
    up = [(i, i + 2) for i in range(size - 2)]
    down = [(i + 2, i) for i in range(size - 2)]
    halves = []
    half = split.shape[1] // 2
    for part in range(2):

        def chunk(index):
            index = jnp.clip(index, 0, line - 1)
            at = lax.dynamic_slice(split, (index, part * half, 0), (1, half, split.shape[2]))
            return at[0].astype(jnp.float32)

        from_below = from_above = None
        for step in range(1, line):
            send_up, send_down = chunk(line - step + z), chunk(z - (line - step))
            if step > 1:
                send_up, send_down = send_up + from_below, send_down + from_above
            from_below = lax.ppermute(send_up.astype(jnp.bfloat16), "proto", up)
            from_above = lax.ppermute(send_down.astype(jnp.bfloat16), "proto", down)
            from_below, from_above = lax.optimization_barrier((from_below, from_above))
            from_below, from_above = from_below.astype(jnp.float32), from_above.astype(jnp.float32)
        halves.append((chunk(z) + from_below + from_above).astype(jnp.bfloat16))
    return jnp.concatenate(halves, axis=0)


def shards(embeddings, prototypes, block_mask):
    n_row, n_proto = lax.axis_size("row"), lax.axis_size("proto")
    lines = n_proto // 2
    core = lax.axis_index("proto") % 2
    rows, features = embeddings.shape
    protos = 2 * prototypes.shape[0]
    width = features // n_proto
    log_column = math.log(rows * n_row / (protos * lines))

    other_mask = swap(block_mask, "proto", 1)
    pieces, firsts, starts = gather_features(prototypes)

    mask = jnp.where(block_mask == 1, 1, 0)
    other_mask = jnp.where(other_mask == 1, 1, 0)
    mask = jnp.where(
        core == 0,
        jnp.concatenate([mask, other_mask], axis=1),
        jnp.concatenate([other_mask, mask], axis=1),
    )
    row_tiles, columns = mask.shape
    across = mask.T
    row_list, row_count = ordered(mask)
    column_list, column_count = ordered(across)
    pair_list, pair_count = ordered(jnp.max(across.reshape(columns // 2, 2, row_tiles), axis=1))
    row_half, column_half = (row_count + 1) // 2, (column_count + 1) // 2
    pair_quarter = (pair_count + 3) // 4
    offsets = jnp.stack([core.astype(jnp.int32)] + [s.astype(jnp.int32) for s in starts])

    row_shape = jax.ShapeDtypeStruct((row_tiles, TILE), jnp.float32)
    column_shape = jax.ShapeDtypeStruct((columns, TILE), jnp.float32)
    panel = pltpu.VMEM((row_tiles * columns + 1, TILE, TILE), jnp.float32)
    wide = pltpu.VMEM((row_tiles, TILE, TILE), jnp.float32)
    tall = pltpu.VMEM((columns, TILE, TILE), jnp.float32)
    similar, whole, row_part = pl.pallas_call(
        functools.partial(panel_kernel, firsts),
        out_shape=(panel, pltpu.VMEM((protos, features), jnp.bfloat16), row_shape),
        in_specs=[SMEM] * 5 + [VMEM] * (1 + len(pieces)),
        out_specs=(VMEM, VMEM, VMEM),
        scratch_shapes=[wide],
        compiler_params=params(12),
        name="panel",
    )(row_list, row_half, pair_list, pair_quarter, offsets, embeddings, *pieces)

    for sweep in range(ITERS):
        parts = [row_part] + [swap(row_part, "proto", 2 * j) for j in range(1, lines)]
        column_part, row_potential = pl.pallas_call(
            column_kernel,
            out_shape=(column_shape, row_shape),
            in_specs=[SMEM] * 2 + [VMEM] * (1 + len(parts)),
            out_specs=(VMEM, VMEM),
            scratch_shapes=[wide, tall],
            compiler_params=params(8),
            name="column_pass",
        )(column_list, column_half, similar, *parts)
        parts = [column_part] + [swap(column_part, "row", j) for j in range(1, n_row)]
        if sweep < ITERS - 1:
            row_part = pl.pallas_call(
                functools.partial(row_kernel, log_column),
                out_shape=row_shape,
                in_specs=[SMEM] * 2 + [VMEM] * (1 + len(parts)),
                out_specs=VMEM,
                scratch_shapes=[pltpu.VMEM((columns + 8, TILE), jnp.float32), wide],
                compiler_params=params(8),
                name="row_pass",
            )(row_list, row_half, similar, *parts)
    split, column_potential = pl.pallas_call(
        functools.partial(plan_kernel, log_column, lines),
        out_shape=(jax.ShapeDtypeStruct((lines, rows, width), jnp.bfloat16), column_shape),
        in_specs=[SMEM] * 4 + [VMEM] * (3 + len(parts)),
        out_specs=(VMEM, VMEM),
        scratch_shapes=[wide, pltpu.VMEM((row_tiles, TILE, lines * width), jnp.float32)],
        compiler_params=params(16),
        name="plan",
    )(pair_list, pair_quarter, mask, offsets, similar, row_potential, whole, *parts)
    targets = scatter_partials(split)
    half = columns // 2
    column_potential = lax.dynamic_slice_in_dim(column_potential, core * half, half, 0)
    return (targets, row_potential.reshape(rows), column_potential.reshape(protos // 2))


def solution(mesh):
    return jax.shard_map(
        shards,
        mesh=mesh,
        in_specs=(P("row", None), P("proto", "row"), P("row", "proto")),
        out_specs=(P("row", "proto"), P("row"), P("proto")),
        check_vma=False,
    )
```

```python
import functools
import math

import jax
import jax.numpy as jnp
from jax import lax
from jax.experimental import pallas as pl
from jax.experimental.pallas import tpu as pltpu
from jax.sharding import PartitionSpec as P

ITERS = 3
TILE = 128
NEGATIVE = -1e30

VMEM = pl.BlockSpec(memory_space=pltpu.VMEM)
HBM = pl.BlockSpec(memory_space=pltpu.HBM)
SMEM = pl.BlockSpec(memory_space=pltpu.SMEM)


def swap(x, axis, offset):
    size = lax.axis_size(axis)
    return lax.ppermute(x, axis, [(i, i ^ offset) for i in range(size)])


def pair_sum(terms):
    while len(terms) > 1:
        terms = [terms[i] + terms[i + 1] for i in range(0, len(terms), 2)]
    return terms[0]


def combine(parts):
    peak = functools.reduce(jnp.maximum, parts)
    return peak + jnp.log(pair_sum([jnp.exp(part - peak) for part in parts]))


def ordered(mask):
    size = mask.shape[1]
    at = jnp.arange(size, dtype=jnp.int32)
    before = jnp.sum(jnp.where(at[None, :] < at[:, None], mask[:, None, :], 0), axis=2)
    hit = (mask[:, None, :] == 1) & (before[:, None, :] == at[None, :, None])
    places = jnp.sum(jnp.where(hit, at[None, None, :] - size, 0), axis=2) + size
    return places, jnp.sum(mask, axis=1)


def score_loop(count, step, start):
    return lax.fori_loop(0, count, lambda k, a: step(2 * k + 1, step(2 * k, a)), start)


def row_pass(list_ref, half_ref, s_ref, c_ref, acc_ref, out_ref):
    row_tiles, columns = list_ref.shape
    lane = lax.broadcasted_iota(jnp.int32, (TILE, TILE), 1)
    dummy = row_tiles * columns

    def score(t, k):
        u = list_ref[t, k]
        tile = s_ref[jnp.where(u == columns, dummy, t * columns + u)]
        return tile if c_ref is None else tile + c_ref[pl.ds(u, 1), :]

    for t in range(row_tiles):
        acc_ref[t] = score_loop(
            half_ref[t],
            lambda k, a, t=t: jnp.maximum(a, score(t, k)),
            jnp.full((TILE, TILE), NEGATIVE, jnp.float32),
        )
    peaks = jnp.zeros((TILE, TILE), jnp.float32)
    for t in range(row_tiles):
        peak = jnp.max(acc_ref[t], axis=1, keepdims=True)
        peaks = jnp.where(lane == t, peak, peaks)
        acc_ref[t] = jnp.broadcast_to(peak, (TILE, TILE))
    for t in range(row_tiles):
        acc_ref[t] = score_loop(
            half_ref[t],
            lambda k, a, t=t: a + jnp.exp(score(t, k) - acc_ref[t]),
            jnp.zeros((TILE, TILE), jnp.float32),
        )
    totals = jnp.zeros((TILE, TILE), jnp.float32)
    for t in range(row_tiles):
        totals = jnp.where(lane == t, jnp.sum(acc_ref[t], axis=1, keepdims=True), totals)
    out_ref[...] = (peaks + jnp.log(totals)).T[:row_tiles]


def spread_rows(row, wide_ref):
    row_tiles = row.shape[0]
    standing = jnp.concatenate(
        [row, jnp.zeros((TILE - row_tiles, TILE), jnp.float32)], axis=0
    ).T
    for t in range(row_tiles):
        wide_ref[t] = jnp.broadcast_to(standing[:, t : t + 1], (TILE, TILE))


def panel_kernel(row_blocks, list_ref, half_ref, plist_ref, pquarter_ref, place_ref, e_hbm_ref, *refs):
    pieces, (s_ref, p_ref, out_ref, acc_ref, e_ref, sem) = refs[:-6], refs[-6:]
    load = pltpu.make_async_copy(e_hbm_ref, e_ref, sem.at[0])
    load.start()
    row_tiles, columns = list_ref.shape
    scale = 4.0 / math.sqrt(e_ref.shape[1])
    core = place_ref[0]
    protos = p_ref.shape[0] // 2
    for n, piece in enumerate(pieces):
        group, within = n * 2 // len(pieces), n % (len(pieces) // 2)
        rows, width = piece.shape
        first = (core if group == 0 else 1 - core) * protos + row_blocks[within]
        start = pl.multiple_of(place_ref[2 + within], TILE)
        place = p_ref.at[pl.ds(pl.multiple_of(first, TILE), rows), pl.ds(start, width)]
        if n == 0:
            own = pltpu.make_async_copy(piece, place, sem.at[1])
            own.start()
        else:
            place[...] = piece[...]
    s_ref[row_tiles * columns] = jnp.full((TILE, TILE), NEGATIVE, jnp.float32)
    own.wait()
    load.wait()

    def one_pair(pair, carry):
        def four_tiles(k, carry):
            at = [jnp.minimum(plist_ref[pair, 4 * k + i], row_tiles - 1) for i in range(4)]
            rows = jnp.concatenate(
                [e_ref[pl.ds(pl.multiple_of(t * TILE, TILE), TILE), :] for t in at], axis=0
            )
            block = p_ref[pl.ds(pl.multiple_of(pair * 2 * TILE, TILE), 2 * TILE), :]
            product = scale * lax.dot_general(
                rows, block, (((1,), (1,)), ((), ())), preferred_element_type=jnp.float32
            )
            for i, t in enumerate(at):
                for side in range(2):
                    s_ref[t * columns + 2 * pair + side] = product[
                        i * TILE : (i + 1) * TILE, side * TILE : (side + 1) * TILE
                    ]
            return carry

        return lax.fori_loop(0, pquarter_ref[pair], four_tiles, carry)

    lax.fori_loop(0, columns // 2, one_pair, 0)
    row_pass(list_ref, half_ref, s_ref, None, acc_ref, out_ref)


def row_kernel(log_column, list_ref, half_ref, s_ref, *refs):
    parts, (out_ref, c_ref, acc_ref) = refs[:-3], refs[-3:]
    columns = list_ref.shape[1]
    c_ref[:columns] = log_column - combine([part[...] for part in parts])
    c_ref[columns:] = jnp.zeros((c_ref.shape[0] - columns, TILE), jnp.float32)
    row_pass(list_ref, half_ref, s_ref, c_ref, acc_ref, out_ref)


def column_kernel(list_ref, half_ref, s_ref, *refs):
    parts, (out_ref, r_ref, wide_ref, acc_ref) = refs[:-4], refs[-4:]
    columns, row_tiles = list_ref.shape
    dummy = row_tiles * columns
    row = -combine([part[...] for part in parts])
    r_ref[...] = row
    spread_rows(row, wide_ref)

    def score(u, k):
        t = list_ref[u, k]
        inside = jnp.minimum(t, row_tiles - 1)
        return s_ref[jnp.where(t == row_tiles, dummy, t * columns + u)] + wide_ref[inside]

    for u in range(columns):
        acc_ref[u] = score_loop(
            half_ref[u],
            lambda k, a, u=u: jnp.maximum(a, score(u, k)),
            jnp.full((TILE, TILE), NEGATIVE, jnp.float32),
        )
    peaks = [jnp.max(acc_ref[u], axis=0, keepdims=True) for u in range(columns)]
    for u in range(columns):
        acc_ref[u] = score_loop(
            half_ref[u],
            lambda k, a, u=u: a + jnp.exp(score(u, k) - peaks[u]),
            jnp.zeros((TILE, TILE), jnp.float32),
        )
    totals = [jnp.sum(acc_ref[u], axis=0, keepdims=True) for u in range(columns)]
    out_ref[...] = jnp.concatenate(peaks, axis=0) + jnp.log(jnp.concatenate(totals, axis=0))


def plan_kernel(log_column, lines, plist_ref, pquarter_ref, mask_ref, place_ref, s_ref, r_ref, p_ref, *refs):
    parts, outs = refs[: -4 - lines], refs[-4 - lines : -4]
    own_ref, c_ref, wide_ref, total_ref = refs[-4:]
    row_tiles, columns = mask_ref.shape
    dummy = row_tiles * columns
    core, z = place_ref[0], place_ref[1]
    c_ref[...] = log_column - combine([part[...] for part in parts])
    half = columns // 2
    own_ref[...] = c_ref[pl.ds(pl.multiple_of(core * half, half), half), :]
    spread_rows(r_ref[...], wide_ref)
    width = outs[0].shape[1]
    fits = width % TILE == 0
    total_ref[...] = jnp.zeros(total_ref.shape, jnp.float32)

    def one_pair(pair, carry):
        first = pl.multiple_of(pair * 2 * TILE, TILE)
        blocks = []
        for j in range(lines):
            if fits:
                start = (2 * jnp.bitwise_xor(z, j) + core) * width
                blocks.append(p_ref[pl.ds(first, 2 * TILE), pl.ds(pl.multiple_of(start, TILE), width)])
            else:
                both = p_ref[pl.ds(first, 2 * TILE), 2 * j * width : 2 * (j + 1) * width]
                blocks.append(jnp.where(core == 0, both[:, :width], both[:, width:]))
        block = jnp.concatenate(blocks, axis=1)

        def four_tiles(k, carry):
            at = [plist_ref[pair, 4 * k + i] for i in range(4)]
            inside = [jnp.minimum(t, row_tiles - 1) for t in at]
            strips = []
            for t, real in zip(at, inside):
                sides = []
                for side in range(2):
                    u = 2 * pair + side
                    good = (t < row_tiles) & (mask_ref[real, u] == 1)
                    tile = s_ref[jnp.where(good, t * columns + u, dummy)]
                    sides.append(jnp.exp(tile + wide_ref[real] + c_ref[pl.ds(u, 1), :]).astype(jnp.bfloat16))
                strips.append(jnp.concatenate(sides, axis=1))
            product = jnp.dot(
                jnp.concatenate(strips, axis=0), block, preferred_element_type=jnp.float32
            )
            for i, t in enumerate(inside):
                total_ref[t] += product[i * TILE : (i + 1) * TILE]
            return carry

        return lax.fori_loop(0, pquarter_ref[pair], four_tiles, carry)

    lax.fori_loop(0, columns // 2, one_pair, 0)
    for t in range(row_tiles):
        total = total_ref[t].astype(jnp.bfloat16)
        for j in range(lines):
            block = total[:, j * width : (j + 1) * width]
            if fits:
                outs[j][t * TILE : (t + 1) * TILE, :] = block
            else:
                for k in range(lines):

                    @pl.when(jnp.bitwise_xor(z, k) == j)
                    def _():
                        outs[k][t * TILE : (t + 1) * TILE, :] = block


def params(mebibytes):
    return pltpu.CompilerParams(vmem_limit_bytes=mebibytes * 2**20)


def gather_features(shard):
    width = shard.shape[1]
    me = lax.axis_index("row")

    def sibling(block):
        return swap(block, "proto", 1)

    if lax.axis_size("row") != 4 or width % TILE:
        whole = lax.all_gather(shard, "row", axis=1, tiled=True)
        return [whole, sibling(whole)], [0], [jnp.int32(0)]
    half = shard.shape[0] // 2
    top, bottom = shard[:half], shard[half:]
    near_bottom = swap(bottom, "row", 1)
    far_top = swap(top, "row", 2)
    near_bottom, far_top, top, bottom = lax.optimization_barrier((near_bottom, far_top, top, bottom))
    cross_top = swap(far_top, "row", 1)
    cross_bottom = swap(near_bottom, "row", 2)
    near_top = swap(top, "row", 1)
    far_bottom = swap(bottom, "row", 2)
    pieces = [shard, near_top, near_bottom, far_top, far_bottom, cross_top, cross_bottom]
    firsts = [0, 0, half, 0, half, 0, half]
    starts = [(me ^ offset) * width for offset in (0, 1, 1, 2, 2, 3, 3)]
    return pieces + [sibling(piece) for piece in pieces], firsts, starts


def scatter_partials(blocks):
    blocks = list(blocks)
    distance = 1
    while distance < len(blocks):
        for j in range(len(blocks) - distance, 0, -2 * distance):
            got = swap(blocks[j].astype(jnp.bfloat16), "proto", 2 * distance).astype(jnp.float32)
            blocks[j ^ distance] = blocks[j ^ distance].astype(jnp.float32) + got
        distance *= 2
    return blocks[0].astype(jnp.bfloat16)


def shards(embeddings, prototypes, block_mask):
    n_row, n_proto = lax.axis_size("row"), lax.axis_size("proto")
    lines = n_proto // 2
    core = lax.axis_index("proto") % 2
    rows, features = embeddings.shape
    protos = 2 * prototypes.shape[0]
    width = features // n_proto
    log_column = math.log(rows * n_row / (protos * lines))

    other_mask = swap(block_mask, "proto", 1)
    pieces, firsts, starts = gather_features(prototypes)

    mask = jnp.where(block_mask == 1, 1, 0)
    other_mask = jnp.where(other_mask == 1, 1, 0)
    mask = jnp.where(
        core == 0,
        jnp.concatenate([mask, other_mask], axis=1),
        jnp.concatenate([other_mask, mask], axis=1),
    )
    row_tiles, columns = mask.shape
    across = mask.T
    row_list, row_count = ordered(mask)
    column_list, column_count = ordered(across)
    pair_list, pair_count = ordered(jnp.max(across.reshape(columns // 2, 2, row_tiles), axis=1))
    row_half, column_half = (row_count + 1) // 2, (column_count + 1) // 2
    pair_quarter = (pair_count + 3) // 4
    z = lax.axis_index("proto") // 2
    places = jnp.stack([place.astype(jnp.int32) for place in [core, z] + starts])

    row_shape = jax.ShapeDtypeStruct((row_tiles, TILE), jnp.float32)
    column_shape = jax.ShapeDtypeStruct((columns, TILE), jnp.float32)
    panel = pltpu.VMEM((row_tiles * columns + 1, TILE, TILE), jnp.float32)
    wide = pltpu.VMEM((row_tiles, TILE, TILE), jnp.float32)
    tall = pltpu.VMEM((columns, TILE, TILE), jnp.float32)
    similar, whole, row_part = pl.pallas_call(
        functools.partial(panel_kernel, firsts),
        out_shape=(panel, pltpu.VMEM((protos, features), jnp.bfloat16), row_shape),
        in_specs=[SMEM] * 5 + [HBM] * 2 + [VMEM] * (len(pieces) - 1),
        out_specs=(VMEM, VMEM, VMEM),
        scratch_shapes=[wide, pltpu.VMEM(embeddings.shape, jnp.bfloat16), pltpu.SemaphoreType.DMA((2,))],
        compiler_params=params(16),
        name="panel",
    )(row_list, row_half, pair_list, pair_quarter, places, embeddings, *pieces)

    for sweep in range(ITERS):
        parts = [row_part] + [swap(row_part, "proto", 2 * j) for j in range(1, lines)]
        column_part, row_potential = pl.pallas_call(
            column_kernel,
            out_shape=(column_shape, row_shape),
            in_specs=[SMEM] * 2 + [VMEM] * (1 + len(parts)),
            out_specs=(VMEM, VMEM),
            scratch_shapes=[wide, tall],
            compiler_params=params(8),
            name="column_pass",
        )(column_list, column_half, similar, *parts)
        parts = [column_part] + [swap(column_part, "row", j) for j in range(1, n_row)]
        if sweep < ITERS - 1:
            row_part = pl.pallas_call(
                functools.partial(row_kernel, log_column),
                out_shape=row_shape,
                in_specs=[SMEM] * 2 + [VMEM] * (1 + len(parts)),
                out_specs=VMEM,
                scratch_shapes=[pltpu.VMEM((columns + 8, TILE), jnp.float32), wide],
                compiler_params=params(8),
                name="row_pass",
            )(row_list, row_half, similar, *parts)
    half = columns // 2
    *blocks, column_potential = pl.pallas_call(
        functools.partial(plan_kernel, log_column, lines),
        out_shape=[jax.ShapeDtypeStruct((rows, width), jnp.bfloat16)] * lines
        + [jax.ShapeDtypeStruct((half, TILE), jnp.float32)],
        in_specs=[SMEM] * 4 + [VMEM] * (3 + len(parts)),
        out_specs=[VMEM] * (lines + 1),
        scratch_shapes=[
            pltpu.VMEM((columns, TILE), jnp.float32),
            wide,
            pltpu.VMEM((row_tiles, TILE, lines * width), jnp.float32),
        ],
        compiler_params=params(16),
        name="plan",
    )(pair_list, pair_quarter, mask, places, similar, row_potential, whole, *parts)
    targets = scatter_partials(blocks)
    return (targets, row_potential.reshape(rows), column_potential.reshape(protos // 2))


def solution(mesh):
    return jax.shard_map(
        shards,
        mesh=mesh,
        in_specs=(P("row", None), P("proto", "row"), P("row", "proto")),
        out_specs=(P("row", "proto"), P("row"), P("proto")),
        check_vma=False,
    )
```

```python
import functools
import math

import jax
import jax.numpy as jnp
from jax import lax
from jax.experimental import pallas as pl
from jax.experimental.pallas import tpu as pltpu
from jax.sharding import PartitionSpec as P

ITERS = 3
TILE = 128
NEGATIVE = -1e30

VMEM = pl.BlockSpec(memory_space=pltpu.VMEM)
HBM = pl.BlockSpec(memory_space=pltpu.HBM)
SMEM = pl.BlockSpec(memory_space=pltpu.SMEM)


def swap(x, axis, offset):
    size = lax.axis_size(axis)
    return lax.ppermute(x, axis, [(i, i ^ offset) for i in range(size)])


def pair_sum(terms):
    while len(terms) > 1:
        terms = [terms[i] + terms[i + 1] for i in range(0, len(terms), 2)]
    return terms[0]


def combine(parts):
    peak = functools.reduce(jnp.maximum, parts)
    return peak + jnp.log(pair_sum([jnp.exp(part - peak) for part in parts]))


def ordered(mask):
    size = mask.shape[1]
    at = jnp.arange(size, dtype=jnp.int32)
    before = jnp.sum(jnp.where(at[None, :] < at[:, None], mask[:, None, :], 0), axis=2)
    hit = (mask[:, None, :] == 1) & (before[:, None, :] == at[None, :, None])
    places = jnp.sum(jnp.where(hit, at[None, None, :] - size, 0), axis=2) + size
    return places, jnp.sum(mask, axis=1)


def score_loop(count, step, start):
    return lax.fori_loop(0, count, lambda k, a: step(2 * k + 1, step(2 * k, a)), start)


def row_pass(list_ref, half_ref, s_ref, c_ref, acc_ref, out_ref):
    row_tiles, columns = list_ref.shape
    lane = lax.broadcasted_iota(jnp.int32, (TILE, TILE), 1)
    dummy = row_tiles * columns

    def score(t, k):
        u = list_ref[t, k]
        tile = s_ref[jnp.where(u == columns, dummy, t * columns + u)]
        return tile if c_ref is None else tile + c_ref[pl.ds(u, 1), :]

    for t in range(row_tiles):
        acc_ref[t] = score_loop(
            half_ref[t],
            lambda k, a, t=t: jnp.maximum(a, score(t, k)),
            jnp.full((TILE, TILE), NEGATIVE, jnp.float32),
        )
    peaks = jnp.zeros((TILE, TILE), jnp.float32)
    for t in range(row_tiles):
        peak = jnp.max(acc_ref[t], axis=1, keepdims=True)
        peaks = jnp.where(lane == t, peak, peaks)
        acc_ref[t] = jnp.broadcast_to(peak, (TILE, TILE))
    for t in range(row_tiles):
        acc_ref[t] = score_loop(
            half_ref[t],
            lambda k, a, t=t: a + jnp.exp(score(t, k) - acc_ref[t]),
            jnp.zeros((TILE, TILE), jnp.float32),
        )
    totals = jnp.zeros((TILE, TILE), jnp.float32)
    for t in range(row_tiles):
        totals = jnp.where(lane == t, jnp.sum(acc_ref[t], axis=1, keepdims=True), totals)
    out_ref[...] = (peaks + jnp.log(totals)).T[:row_tiles]


def spread_rows(row, wide_ref):
    row_tiles = row.shape[0]
    standing = jnp.concatenate(
        [row, jnp.zeros((TILE - row_tiles, TILE), jnp.float32)], axis=0
    ).T
    for t in range(row_tiles):
        wide_ref[t] = jnp.broadcast_to(standing[:, t : t + 1], (TILE, TILE))


def panel_kernel(row_blocks, list_ref, half_ref, plist_ref, pquarter_ref, place_ref, e_hbm_ref, *refs):
    pieces, (s_ref, p_ref, out_ref, acc_ref, e_ref, sem) = refs[:-6], refs[-6:]
    load = pltpu.make_async_copy(e_hbm_ref, e_ref, sem.at[0])
    load.start()
    row_tiles, columns = list_ref.shape
    scale = 4.0 / math.sqrt(e_ref.shape[1])
    core = place_ref[0]
    protos = p_ref.shape[0] // 2
    for n, piece in enumerate(pieces):
        group, within = n * 2 // len(pieces), n % (len(pieces) // 2)
        rows, width = piece.shape
        first = (core if group == 0 else 1 - core) * protos + row_blocks[within]
        start = pl.multiple_of(place_ref[2 + within], TILE)
        place = p_ref.at[pl.ds(pl.multiple_of(first, TILE), rows), pl.ds(start, width)]
        if n == 0:
            own = pltpu.make_async_copy(piece, place, sem.at[1])
            own.start()
        else:
            place[...] = piece[...]
    s_ref[row_tiles * columns] = jnp.full((TILE, TILE), NEGATIVE, jnp.float32)
    own.wait()
    load.wait()

    def one_pair(pair, carry):
        def four_tiles(k, carry):
            at = [jnp.minimum(plist_ref[pair, 4 * k + i], row_tiles - 1) for i in range(4)]
            rows = jnp.concatenate(
                [e_ref[pl.ds(pl.multiple_of(t * TILE, TILE), TILE), :] for t in at], axis=0
            )
            block = p_ref[pl.ds(pl.multiple_of(pair * 2 * TILE, TILE), 2 * TILE), :]
            product = scale * lax.dot_general(
                rows, block, (((1,), (1,)), ((), ())), preferred_element_type=jnp.float32
            )
            for i, t in enumerate(at):
                for side in range(2):
                    s_ref[t * columns + 2 * pair + side] = product[
                        i * TILE : (i + 1) * TILE, side * TILE : (side + 1) * TILE
                    ]
            return carry

        return lax.fori_loop(0, pquarter_ref[pair], four_tiles, carry)

    lax.fori_loop(0, columns // 2, one_pair, 0)
    row_pass(list_ref, half_ref, s_ref, None, acc_ref, out_ref)


def four_loop(count, step, start):
    return lax.fori_loop(
        0, count, lambda k, a: functools.reduce(lambda b, i: step(4 * k + i, b), range(4), a), start
    )


def row_kernel(log_column, list_ref, half_ref, quarter_ref, s_ref, w_ref, m_ref, r_ref, *refs):
    parts, (out_ref, c_ref, v_ref, acc_ref) = refs[:-4], refs[-4:]
    row_tiles, columns = list_ref.shape
    dummy = row_tiles * columns
    column = log_column - combine([part[...] for part in parts])
    c_ref[:columns] = column
    v_ref[:columns] = jnp.exp(column + m_ref[...])
    rest = jnp.zeros((c_ref.shape[0] - columns, TILE), jnp.float32)
    c_ref[columns:] = rest
    v_ref[columns:] = rest
    lane = lax.broadcasted_iota(jnp.int32, (TILE, TILE), 1)

    def place(t, u):
        return jnp.where(u == columns, dummy, t * columns + u)

    for t in range(row_tiles):

        def one_tile(k, a, t=t):
            u = list_ref[t, k]
            return a + w_ref[place(t, u)].astype(jnp.float32) * v_ref[pl.ds(u, 1), :]

        acc_ref[t] = four_loop(quarter_ref[t], one_tile, jnp.zeros((TILE, TILE), jnp.float32))
    totals = jnp.zeros((TILE, TILE), jnp.float32)
    for t in range(row_tiles):
        totals = jnp.where(lane == t, jnp.sum(acc_ref[t], axis=1, keepdims=True), totals)
    totals = totals.T[:row_tiles]
    out_ref[...] = jnp.log(totals) - r_ref[...]
    small = jnp.min(totals, axis=1, keepdims=True)
    least = [jnp.min(small[t : t + 1, :]) for t in range(row_tiles)]
    for t in range(row_tiles):

        @pl.when(jnp.logical_not(least[t] > 1e-15))
        def _():
            def score(k):
                u = list_ref[t, k]
                return s_ref[place(t, u)] + c_ref[pl.ds(u, 1), :]

            peak = score_loop(
                half_ref[t],
                lambda k, a: jnp.maximum(a, score(k)),
                jnp.full((TILE, TILE), NEGATIVE, jnp.float32),
            )
            peak = jnp.max(peak, axis=1, keepdims=True)
            total = score_loop(
                half_ref[t],
                lambda k, a: a + jnp.exp(score(k) - peak),
                jnp.zeros((TILE, TILE), jnp.float32),
            )
            found = peak + jnp.log(jnp.sum(total, axis=1, keepdims=True))
            out_ref[t : t + 1, :] = jnp.broadcast_to(found, (TILE, TILE)).T[:1]


def first_column_kernel(list_ref, half_ref, s_ref, *refs):
    parts, (out_ref, r_ref, w_ref, m_ref, wide_ref, acc_ref) = refs[:-6], refs[-6:]
    columns, row_tiles = list_ref.shape
    dummy = row_tiles * columns
    row = -combine([part[...] for part in parts])
    r_ref[...] = row
    spread_rows(row, wide_ref)
    w_ref[dummy] = jnp.zeros((TILE, TILE), jnp.bfloat16)

    def score(u, k):
        t = list_ref[u, k]
        at = jnp.where(t == row_tiles, dummy, t * columns + u)
        return at, s_ref[at] + wide_ref[jnp.minimum(t, row_tiles - 1)]

    for u in range(columns):
        acc_ref[u] = score_loop(
            half_ref[u],
            lambda k, a, u=u: jnp.maximum(a, score(u, k)[1]),
            jnp.full((TILE, TILE), NEGATIVE, jnp.float32),
        )
    peaks = [jnp.max(acc_ref[u], axis=0, keepdims=True) for u in range(columns)]
    for u in range(columns):

        def one_tile(k, a, u=u):
            at, value = score(u, k)
            value = jnp.exp(value - peaks[u])
            w_ref[at] = value.astype(jnp.bfloat16)
            return a + value

        acc_ref[u] = score_loop(half_ref[u], one_tile, jnp.zeros((TILE, TILE), jnp.float32))
    totals = [jnp.sum(acc_ref[u], axis=0, keepdims=True) for u in range(columns)]
    peaks = jnp.concatenate(peaks, axis=0)
    m_ref[...] = peaks
    out_ref[...] = peaks + jnp.log(jnp.concatenate(totals, axis=0))


def column_kernel(list_ref, half_ref, quarter_ref, s_ref, w_ref, m_ref, first_ref, *refs):
    parts, (out_ref, r_ref, wide_ref, acc_ref) = refs[:-4], refs[-4:]
    columns, row_tiles = list_ref.shape
    dummy = row_tiles * columns
    row = -combine([part[...] for part in parts])
    r_ref[...] = row
    factor = jnp.exp(row - first_ref[...])
    spread_rows(factor, wide_ref)

    def place(t, u):
        return jnp.where(t == row_tiles, dummy, t * columns + u)

    for u in range(columns):

        def one_tile(k, a, u=u):
            t = list_ref[u, k]
            return a + w_ref[place(t, u)].astype(jnp.float32) * wide_ref[jnp.minimum(t, row_tiles - 1)]

        acc_ref[u] = four_loop(quarter_ref[u], one_tile, jnp.zeros((TILE, TILE), jnp.float32))
    totals = jnp.concatenate(
        [jnp.sum(acc_ref[u], axis=0, keepdims=True) for u in range(columns)], axis=0
    )
    out_ref[...] = m_ref[...] + jnp.log(totals)
    fine = (totals > 1e-15) & (totals < 1e30)
    fine = jnp.min(jnp.where(fine, 1.0, 0.0), axis=1, keepdims=True)
    fine = jnp.where(jnp.max(factor) < 1e15, fine, 0.0)
    least = [jnp.min(fine[u : u + 1, :]) for u in range(columns)]

    @pl.when(jnp.logical_not(jnp.min(fine) > 0.5))
    def _():
        spread_rows(row, wide_ref)
        for u in range(columns):

            @pl.when(jnp.logical_not(least[u] > 0.5))
            def _():
                def score(k):
                    t = list_ref[u, k]
                    return s_ref[place(t, u)] + wide_ref[jnp.minimum(t, row_tiles - 1)]

                peak = score_loop(
                    half_ref[u],
                    lambda k, a: jnp.maximum(a, score(k)),
                    jnp.full((TILE, TILE), NEGATIVE, jnp.float32),
                )
                peak = jnp.max(peak, axis=0, keepdims=True)
                total = score_loop(
                    half_ref[u],
                    lambda k, a: a + jnp.exp(score(k) - peak),
                    jnp.zeros((TILE, TILE), jnp.float32),
                )
                out_ref[u : u + 1, :] = peak + jnp.log(jnp.sum(total, axis=0, keepdims=True))


def plan_kernel(log_column, lines, plist_ref, pquarter_ref, mask_ref, place_ref, s_ref, r_ref, p_ref, *refs):
    parts, outs = refs[: -4 - lines], refs[-4 - lines : -4]
    own_ref, c_ref, wide_ref, total_ref = refs[-4:]
    row_tiles, columns = mask_ref.shape
    dummy = row_tiles * columns
    core, z = place_ref[0], place_ref[1]
    c_ref[...] = log_column - combine([part[...] for part in parts])
    half = columns // 2
    own_ref[...] = c_ref[pl.ds(pl.multiple_of(core * half, half), half), :]
    spread_rows(r_ref[...], wide_ref)
    width = outs[0].shape[1]
    fits = width % TILE == 0
    total_ref[...] = jnp.zeros(total_ref.shape, jnp.float32)

    def one_pair(pair, carry):
        first = pl.multiple_of(pair * 2 * TILE, TILE)
        blocks = []
        for j in range(lines):
            if fits:
                start = (2 * jnp.bitwise_xor(z, j) + core) * width
                blocks.append(p_ref[pl.ds(first, 2 * TILE), pl.ds(pl.multiple_of(start, TILE), width)])
            else:
                both = p_ref[pl.ds(first, 2 * TILE), 2 * j * width : 2 * (j + 1) * width]
                blocks.append(jnp.where(core == 0, both[:, :width], both[:, width:]))
        block = jnp.concatenate(blocks, axis=1)

        def four_tiles(k, carry):
            at = [plist_ref[pair, 4 * k + i] for i in range(4)]
            inside = [jnp.minimum(t, row_tiles - 1) for t in at]
            strips = []
            for t, real in zip(at, inside):
                sides = []
                for side in range(2):
                    u = 2 * pair + side
                    good = (t < row_tiles) & (mask_ref[real, u] == 1)
                    tile = s_ref[jnp.where(good, t * columns + u, dummy)]
                    sides.append(jnp.exp(tile + wide_ref[real] + c_ref[pl.ds(u, 1), :]).astype(jnp.bfloat16))
                strips.append(jnp.concatenate(sides, axis=1))
            product = jnp.dot(
                jnp.concatenate(strips, axis=0), block, preferred_element_type=jnp.float32
            )
            for i, t in enumerate(inside):
                total_ref[t] += product[i * TILE : (i + 1) * TILE]
            return carry

        return lax.fori_loop(0, pquarter_ref[pair], four_tiles, carry)

    lax.fori_loop(0, columns // 2, one_pair, 0)
    for t in range(row_tiles):
        total = total_ref[t].astype(jnp.bfloat16)
        for j in range(lines):
            block = total[:, j * width : (j + 1) * width]
            if fits:
                outs[j][t * TILE : (t + 1) * TILE, :] = block
            else:
                for k in range(lines):

                    @pl.when(jnp.bitwise_xor(z, k) == j)
                    def _():
                        outs[k][t * TILE : (t + 1) * TILE, :] = block


def params(mebibytes):
    return pltpu.CompilerParams(vmem_limit_bytes=mebibytes * 2**20)


def gather_features(shard):
    width = shard.shape[1]
    me = lax.axis_index("row")

    def sibling(block):
        return swap(block, "proto", 1)

    if lax.axis_size("row") != 4 or width % TILE:
        whole = lax.all_gather(shard, "row", axis=1, tiled=True)
        return [whole, sibling(whole)], [0], [jnp.int32(0)]
    half = shard.shape[0] // 2
    top, bottom = shard[:half], shard[half:]
    near_bottom = swap(bottom, "row", 1)
    far_top = swap(top, "row", 2)
    near_bottom, far_top, top, bottom = lax.optimization_barrier((near_bottom, far_top, top, bottom))
    cross_top = swap(far_top, "row", 1)
    cross_bottom = swap(near_bottom, "row", 2)
    near_top = swap(top, "row", 1)
    far_bottom = swap(bottom, "row", 2)
    pieces = [shard, near_top, near_bottom, far_top, far_bottom, cross_top, cross_bottom]
    firsts = [0, 0, half, 0, half, 0, half]
    starts = [(me ^ offset) * width for offset in (0, 1, 1, 2, 2, 3, 3)]
    return pieces + [sibling(piece) for piece in pieces], firsts, starts


def scatter_partials(blocks):
    blocks = list(blocks)
    distance = 1
    while distance < len(blocks):
        for j in range(len(blocks) - distance, 0, -2 * distance):
            got = swap(blocks[j].astype(jnp.bfloat16), "proto", 2 * distance).astype(jnp.float32)
            blocks[j ^ distance] = blocks[j ^ distance].astype(jnp.float32) + got
        distance *= 2
    return blocks[0].astype(jnp.bfloat16)


def shards(embeddings, prototypes, block_mask):
    n_row, n_proto = lax.axis_size("row"), lax.axis_size("proto")
    lines = n_proto // 2
    core = lax.axis_index("proto") % 2
    rows, features = embeddings.shape
    protos = 2 * prototypes.shape[0]
    width = features // n_proto
    log_column = math.log(rows * n_row / (protos * lines))

    other_mask = swap(block_mask, "proto", 1)
    pieces, firsts, starts = gather_features(prototypes)

    mask = jnp.where(block_mask == 1, 1, 0)
    other_mask = jnp.where(other_mask == 1, 1, 0)
    mask = jnp.where(
        core == 0,
        jnp.concatenate([mask, other_mask], axis=1),
        jnp.concatenate([other_mask, mask], axis=1),
    )
    row_tiles, columns = mask.shape
    across = mask.T
    row_list, row_count = ordered(mask)
    column_list, column_count = ordered(across)
    pair_list, pair_count = ordered(jnp.max(across.reshape(columns // 2, 2, row_tiles), axis=1))
    row_half, column_half = (row_count + 1) // 2, (column_count + 1) // 2
    row_quarter, column_quarter = (row_count + 3) // 4, (column_count + 3) // 4
    pair_quarter = (pair_count + 3) // 4
    z = lax.axis_index("proto") // 2
    places = jnp.stack([place.astype(jnp.int32) for place in [core, z] + starts])

    row_shape = jax.ShapeDtypeStruct((row_tiles, TILE), jnp.float32)
    column_shape = jax.ShapeDtypeStruct((columns, TILE), jnp.float32)
    panel = pltpu.VMEM((row_tiles * columns + 1, TILE, TILE), jnp.float32)
    wide = pltpu.VMEM((row_tiles, TILE, TILE), jnp.float32)
    tall = pltpu.VMEM((columns, TILE, TILE), jnp.float32)
    similar, whole, row_part = pl.pallas_call(
        functools.partial(panel_kernel, firsts),
        out_shape=(panel, pltpu.VMEM((protos, features), jnp.bfloat16), row_shape),
        in_specs=[SMEM] * 5 + [HBM] * 2 + [VMEM] * (len(pieces) - 1),
        out_specs=(VMEM, VMEM, VMEM),
        scratch_shapes=[wide, pltpu.VMEM(embeddings.shape, jnp.bfloat16), pltpu.SemaphoreType.DMA((2,))],
        compiler_params=params(12),
        name="panel",
    )(row_list, row_half, pair_list, pair_quarter, places, embeddings, *pieces)

    for sweep in range(ITERS):
        parts = [row_part] + [swap(row_part, "proto", 2 * j) for j in range(lines - 1, 0, -1)]
        parts = parts[:1] + parts[:0:-1]
        if sweep == 0:
            column_part, row_potential, kept, peaks = pl.pallas_call(
                first_column_kernel,
                out_shape=(column_shape, row_shape, pltpu.VMEM(panel.shape, jnp.bfloat16), column_shape),
                in_specs=[SMEM] * 2 + [VMEM] * (1 + len(parts)),
                out_specs=(VMEM,) * 4,
                scratch_shapes=[wide, tall],
                compiler_params=params(4),
                name="first_column_pass",
            )(column_list, column_half, similar, *parts)
            first_row = row_potential
        else:
            column_part, row_potential = pl.pallas_call(
                column_kernel,
                out_shape=(column_shape, row_shape),
                in_specs=[SMEM] * 3 + [VMEM] * (4 + len(parts)),
                out_specs=(VMEM, VMEM),
                scratch_shapes=[wide, tall],
                compiler_params=params(4),
                name="column_pass",
            )(column_list, column_half, column_quarter, similar, kept, peaks, first_row, *parts)
        parts = [column_part] + [swap(column_part, "row", j) for j in range(n_row - 1, 0, -1)]
        parts = parts[:1] + parts[:0:-1]
        if sweep < ITERS - 1:
            factors = pltpu.VMEM((columns + 8, TILE), jnp.float32)
            row_part = pl.pallas_call(
                functools.partial(row_kernel, log_column),
                out_shape=row_shape,
                in_specs=[SMEM] * 3 + [VMEM] * (4 + len(parts)),
                out_specs=VMEM,
                scratch_shapes=[factors, factors, wide],
                compiler_params=params(4),
                name="row_pass",
            )(row_list, row_half, row_quarter, similar, kept, peaks, first_row, *parts)
    half = columns // 2
    *blocks, column_potential = pl.pallas_call(
        functools.partial(plan_kernel, log_column, lines),
        out_shape=[jax.ShapeDtypeStruct((rows, width), jnp.bfloat16)] * lines
        + [jax.ShapeDtypeStruct((half, TILE), jnp.float32)],
        in_specs=[SMEM] * 4 + [VMEM] * (3 + len(parts)),
        out_specs=[VMEM] * (lines + 1),
        scratch_shapes=[
            pltpu.VMEM((columns, TILE), jnp.float32),
            wide,
            pltpu.VMEM((row_tiles, TILE, lines * width), jnp.float32),
        ],
        compiler_params=params(12),
        name="plan",
    )(pair_list, pair_quarter, mask, places, similar, row_potential, whole, *parts)
    targets = scatter_partials(blocks)
    return (targets, row_potential.reshape(rows), column_potential.reshape(protos // 2))


def solution(mesh):
    return jax.shard_map(
        shards,
        mesh=mesh,
        in_specs=(P("row", None), P("proto", "row"), P("row", "proto")),
        out_specs=(P("row", "proto"), P("row"), P("proto")),
        check_vma=False,
    )
```

```python
import functools
import math

import jax
import jax.numpy as jnp
from jax import lax
from jax.experimental import pallas as pl
from jax.experimental.pallas import tpu as pltpu
from jax.sharding import PartitionSpec as P

ITERS = 3
TILE = 128
NEGATIVE = -1e30

VMEM = pl.BlockSpec(memory_space=pltpu.VMEM)
HBM = pl.BlockSpec(memory_space=pltpu.HBM)
SMEM = pl.BlockSpec(memory_space=pltpu.SMEM)


def swap(x, axis, offset):
    size = lax.axis_size(axis)
    return lax.ppermute(x, axis, [(i, i ^ offset) for i in range(size)])


def pair_sum(terms):
    while len(terms) > 1:
        terms = [terms[i] + terms[i + 1] for i in range(0, len(terms), 2)]
    return terms[0]


def combine(parts):
    peak = functools.reduce(jnp.maximum, parts)
    return peak + jnp.log(pair_sum([jnp.exp(part - peak) for part in parts]))


class Table:
    def __init__(self, row_tiles, columns):
        self.row_tiles, self.columns = row_tiles, columns
        self.end = max(row_tiles, columns) + 4
        self.column_base = row_tiles
        self.pair_base = row_tiles + columns
        self.mask_base = self.pair_base + columns // 2
        self.shape = (self.mask_base + row_tiles, self.end + 1)
        self.dummy = row_tiles * columns

    def loop(self, ref, line, unroll, step, start):
        count = (ref[line, self.end] + unroll - 1) // unroll

        def several(k, a):
            for i in range(unroll):
                a = step(ref[line, unroll * k + i], a)
            return a

        return lax.fori_loop(0, count, several, start)

    def place(self, t, u):
        padding = (t == self.row_tiles) | (u == self.columns)
        return jnp.where(padding, self.dummy, t * self.columns + u)


def setup_kernel(table, own_ref, other_ref, out_ref):
    core = lax.rem(lax.axis_index("proto"), 2)
    half = table.columns // 2

    def mask_row(t, carry):
        for u in range(half):
            out_ref[table.mask_base + t, core * half + u] = jnp.where(own_ref[t, u] == 1, 1, 0)
            out_ref[table.mask_base + t, (1 - core) * half + u] = jnp.where(other_ref[t, u] == 1, 1, 0)
        return carry

    lax.fori_loop(0, table.row_tiles, mask_row, 0)

    def fill(line, size, allowed):
        count = jnp.int32(0)
        for i in range(size):
            out_ref[line, count] = i
            count = count + allowed(i)
        for i in range(4):
            out_ref[line, count + i] = size
        out_ref[line, table.end] = count

    def row_list(t, carry):
        fill(t, table.columns, lambda u: out_ref[table.mask_base + t, u])
        return carry

    def column_list(u, carry):
        fill(table.column_base + u, table.row_tiles, lambda t: out_ref[table.mask_base + t, u])
        return carry

    def pair_list(p, carry):
        fill(
            table.pair_base + p,
            table.row_tiles,
            lambda t: jnp.maximum(out_ref[table.mask_base + t, 2 * p], out_ref[table.mask_base + t, 2 * p + 1]),
        )
        return carry

    lax.fori_loop(0, table.row_tiles, row_list, 0)
    lax.fori_loop(0, table.columns, column_list, 0)
    lax.fori_loop(0, table.columns // 2, pair_list, 0)


def blank():
    return jnp.zeros((TILE, TILE), jnp.float32)


def lowest():
    return jnp.full((TILE, TILE), NEGATIVE, jnp.float32)


def bad_bits(good):
    bad = jnp.max(jnp.where(good, 0.0, 1.0), axis=1, keepdims=True)
    bit = jnp.left_shift(1, lax.broadcasted_iota(jnp.int32, bad.shape, 0))
    return jnp.sum(bad * bit.astype(jnp.float32)).astype(jnp.int32)


def has_bit(bits, i):
    return jnp.bitwise_and(bits, 1 << i) != 0


def spread_rows(row, wide_ref):
    row_tiles = row.shape[0]
    standing = jnp.concatenate(
        [row, jnp.zeros((TILE - row_tiles, TILE), jnp.float32)], axis=0
    ).T
    for t in range(row_tiles):
        wide_ref[t] = jnp.broadcast_to(standing[:, t : t + 1], (TILE, TILE))


def lying(tiles):
    lane = lax.broadcasted_iota(jnp.int32, (TILE, TILE), 1)
    found = blank()
    for t, tile in enumerate(tiles):
        found = jnp.where(lane == t, jnp.sum(tile, axis=1, keepdims=True), found)
    return found.T[: len(tiles)]


def panel_kernel(table, row_blocks, first_features, table_ref, e_hbm_ref, *refs):
    pieces, (s_ref, p_ref, out_ref, acc_ref, e_ref, sem) = refs[:-6], refs[-6:]
    load = pltpu.make_async_copy(e_hbm_ref, e_ref, sem.at[0])
    load.start()
    row_tiles, columns = table.row_tiles, table.columns
    scale = 4.0 / math.sqrt(e_ref.shape[1])
    core = lax.rem(lax.axis_index("proto"), 2)
    me = lax.axis_index("row")
    protos = p_ref.shape[0] // 2
    for n, piece in enumerate(pieces):
        group, within = n * 2 // len(pieces), n % (len(pieces) // 2)
        rows, width = piece.shape
        first = (core if group == 0 else 1 - core) * protos + row_blocks[within]
        start = 0
        if first_features[within] is not None:
            start = pl.multiple_of(jnp.bitwise_xor(me, first_features[within]) * width, TILE)
        place = p_ref.at[pl.ds(pl.multiple_of(first, TILE), rows), pl.ds(start, width)]
        if n == 0:
            own = pltpu.make_async_copy(piece, place, sem.at[1])
            own.start()
        else:
            place[...] = piece[...]
    s_ref[table.dummy] = lowest()
    for t in range(row_tiles):
        acc_ref[t] = lowest()
    own.wait()
    load.wait()

    def one_pair(pair, carry):
        line = table.pair_base + pair

        def four_tiles(k, carry):
            at = [jnp.minimum(table_ref[line, 4 * k + i], row_tiles - 1) for i in range(4)]
            rows = jnp.concatenate(
                [e_ref[pl.ds(pl.multiple_of(t * TILE, TILE), TILE), :] for t in at], axis=0
            )
            block = p_ref[pl.ds(pl.multiple_of(pair * 2 * TILE, TILE), 2 * TILE), :]
            product = scale * lax.dot_general(
                rows, block, (((1,), (1,)), ((), ())), preferred_element_type=jnp.float32
            )
            for i, t in enumerate(at):
                peak = acc_ref[t]
                for side in range(2):
                    u = 2 * pair + side
                    tile = product[i * TILE : (i + 1) * TILE, side * TILE : (side + 1) * TILE]
                    s_ref[t * columns + u] = tile
                    off = jnp.where(table_ref[table.mask_base + t, u] == 1, 0.0, NEGATIVE)
                    peak = jnp.maximum(peak, tile + off)
                acc_ref[t] = peak
            return carry

        return lax.fori_loop(0, (table_ref[line, table.end] + 3) // 4, four_tiles, carry)

    lax.fori_loop(0, columns // 2, one_pair, 0)

    lane = lax.broadcasted_iota(jnp.int32, (TILE, TILE), 1)
    peaks = blank()
    for t in range(row_tiles):
        peak = jnp.max(acc_ref[t], axis=1, keepdims=True)
        peaks = jnp.where(lane == t, peak, peaks)
        acc_ref[t] = jnp.broadcast_to(peak, (TILE, TILE))
    for t in range(row_tiles):
        acc_ref[t] = table.loop(
            table_ref,
            t,
            4,
            lambda u, a, t=t: a + jnp.exp(s_ref[table.place(t, u)] - acc_ref[t]),
            blank(),
        )
    out_ref[...] = peaks.T[:row_tiles] + jnp.log(lying([acc_ref[t] for t in range(row_tiles)]))


def row_kernel(table, log_column, table_ref, s_ref, w_ref, m_ref, r_ref, *refs):
    parts, (out_ref, c_ref, v_ref, acc_ref) = refs[:-4], refs[-4:]
    row_tiles, columns = table.row_tiles, table.columns
    column = log_column - combine([part[...] for part in parts])
    c_ref[:columns] = column
    v_ref[:columns] = jnp.exp(column + m_ref[...])
    rest = jnp.zeros((c_ref.shape[0] - columns, TILE), jnp.float32)
    c_ref[columns:] = rest
    v_ref[columns:] = rest

    for t in range(row_tiles):

        def one_tile(u, a, t=t):
            return a + w_ref[table.place(t, u)].astype(jnp.float32) * v_ref[pl.ds(u, 1), :]

        acc_ref[t] = table.loop(table_ref, t, 4, one_tile, blank())
    totals = lying([acc_ref[t] for t in range(row_tiles)])
    out_ref[...] = jnp.log(totals) - r_ref[...]
    bits = bad_bits(totals > 1e-15)

    @pl.when(bits != 0)
    def _():
        for t in range(row_tiles):

            @pl.when(has_bit(bits, t))
            def _():
                def score(u):
                    return s_ref[table.place(t, u)] + c_ref[pl.ds(u, 1), :]

                peak = table.loop(table_ref, t, 2, lambda u, a: jnp.maximum(a, score(u)), lowest())
                peak = jnp.max(peak, axis=1, keepdims=True)
                total = table.loop(table_ref, t, 2, lambda u, a: a + jnp.exp(score(u) - peak), blank())
                found = peak + jnp.log(jnp.sum(total, axis=1, keepdims=True))
                out_ref[t : t + 1, :] = jnp.broadcast_to(found, (TILE, TILE)).T[:1]


def slow_column(table, table_ref, u, s_ref, wide_ref, keep):
    line = table.column_base + u

    def score(t):
        at = table.place(t, u)
        return at, s_ref[at] + wide_ref[jnp.minimum(t, table.row_tiles - 1)]

    peak = table.loop(table_ref, line, 2, lambda t, a: jnp.maximum(a, score(t)[1]), lowest())
    peak = jnp.max(peak, axis=0, keepdims=True)

    def one_tile(t, a):
        at, value = score(t)
        value = jnp.exp(value - peak)
        keep(at, value)
        return a + value

    total = table.loop(table_ref, line, 2, one_tile, blank())
    return peak, jnp.sum(total, axis=0, keepdims=True)


def first_column_kernel(table, table_ref, s_ref, *refs):
    parts, (out_ref, r_ref, w_ref, m_ref, wide_ref, acc_ref) = refs[:-6], refs[-6:]
    row = -combine([part[...] for part in parts])
    r_ref[...] = row
    spread_rows(row, wide_ref)
    w_ref[table.dummy] = blank().astype(jnp.bfloat16)

    def keep(at, value):
        w_ref[at] = value.astype(jnp.bfloat16)

    for u in range(table.columns):

        def one_tile(t, a, u=u):
            at = table.place(t, u)
            value = jnp.exp(s_ref[at] + wide_ref[jnp.minimum(t, table.row_tiles - 1)])
            keep(at, value)
            return a + value

        acc_ref[u] = table.loop(table_ref, table.column_base + u, 4, one_tile, blank())
    totals = jnp.concatenate(
        [jnp.sum(acc_ref[u], axis=0, keepdims=True) for u in range(table.columns)], axis=0
    )
    m_ref[...] = jnp.zeros(m_ref.shape, jnp.float32)
    out_ref[...] = jnp.log(totals)
    bits = bad_bits(totals > 1e-15)

    @pl.when(bits != 0)
    def _():
        for u in range(table.columns):

            @pl.when(has_bit(bits, u))
            def _():
                peak, total = slow_column(table, table_ref, u, s_ref, wide_ref, keep)
                m_ref[u : u + 1, :] = peak
                out_ref[u : u + 1, :] = peak + jnp.log(total)


def column_kernel(table, table_ref, s_ref, w_ref, m_ref, first_ref, *refs):
    parts, (out_ref, r_ref, r_out_ref, wide_ref, acc_ref) = refs[:-5], refs[-5:]
    row = -combine([part[...] for part in parts])
    r_ref[...] = row
    r_out_ref[...] = row
    factor = jnp.exp(row - first_ref[...])
    spread_rows(factor, wide_ref)

    for u in range(table.columns):

        def one_tile(t, a, u=u):
            kept = w_ref[table.place(t, u)].astype(jnp.float32)
            return a + kept * wide_ref[jnp.minimum(t, table.row_tiles - 1)]

        acc_ref[u] = table.loop(table_ref, table.column_base + u, 4, one_tile, blank())
    totals = jnp.concatenate(
        [jnp.sum(acc_ref[u], axis=0, keepdims=True) for u in range(table.columns)], axis=0
    )
    out_ref[...] = m_ref[...] + jnp.log(totals)
    largest = jnp.max(jnp.max(factor, axis=1, keepdims=True), axis=0, keepdims=True)
    bits = bad_bits((totals > 1e-15) & (totals < 1e30) & (largest < 1e15))

    @pl.when(bits != 0)
    def _():
        spread_rows(row, wide_ref)
        for u in range(table.columns):

            @pl.when(has_bit(bits, u))
            def _():
                peak, total = slow_column(table, table_ref, u, s_ref, wide_ref, lambda at, value: None)
                out_ref[u : u + 1, :] = peak + jnp.log(total)


def plan_kernel(table, log_column, lines, table_ref, s_ref, r_ref, p_ref, *refs):
    parts, outs = refs[: -4 - lines], refs[-4 - lines : -4]
    own_ref, c_ref, wide_ref, total_ref = refs[-4:]
    row_tiles, columns = table.row_tiles, table.columns
    index = lax.axis_index("proto")
    core, z = lax.rem(index, 2), lax.div(index, 2)
    c_ref[...] = log_column - combine([part[...] for part in parts])
    half = columns // 2
    own_ref[...] = c_ref[pl.ds(pl.multiple_of(core * half, half), half), :]
    spread_rows(r_ref[...], wide_ref)
    width = outs[0].shape[1]
    fits = width % TILE == 0
    total_ref[...] = jnp.zeros(total_ref.shape, jnp.float32)

    def one_pair(pair, carry):
        first = pl.multiple_of(pair * 2 * TILE, TILE)
        line = table.pair_base + pair
        blocks = []
        for j in range(lines):
            if fits:
                start = (2 * jnp.bitwise_xor(z, j) + core) * width
                blocks.append(p_ref[pl.ds(first, 2 * TILE), pl.ds(pl.multiple_of(start, TILE), width)])
            else:
                both = p_ref[pl.ds(first, 2 * TILE), 2 * j * width : 2 * (j + 1) * width]
                blocks.append(jnp.where(core == 0, both[:, :width], both[:, width:]))
        block = jnp.concatenate(blocks, axis=1)

        def four_tiles(k, carry):
            at = [table_ref[line, 4 * k + i] for i in range(4)]
            inside = [jnp.minimum(t, row_tiles - 1) for t in at]
            strips = []
            for t, real in zip(at, inside):
                sides = []
                for side in range(2):
                    u = 2 * pair + side
                    good = (t < row_tiles) & (table_ref[table.mask_base + real, u] == 1)
                    tile = s_ref[jnp.where(good, t * columns + u, table.dummy)]
                    sides.append(jnp.exp(tile + wide_ref[real] + c_ref[pl.ds(u, 1), :]).astype(jnp.bfloat16))
                strips.append(jnp.concatenate(sides, axis=1))
            product = jnp.dot(
                jnp.concatenate(strips, axis=0), block, preferred_element_type=jnp.float32
            )
            for i, t in enumerate(inside):
                total_ref[t] += product[i * TILE : (i + 1) * TILE]
            return carry

        return lax.fori_loop(0, (table_ref[line, table.end] + 3) // 4, four_tiles, carry)

    lax.fori_loop(0, columns // 2, one_pair, 0)
    for t in range(row_tiles):
        total = total_ref[t].astype(jnp.bfloat16)
        for j in range(lines):
            block = total[:, j * width : (j + 1) * width]
            if fits:
                outs[j][t * TILE : (t + 1) * TILE, :] = block
            else:
                for k in range(lines):

                    @pl.when(jnp.bitwise_xor(z, k) == j)
                    def _():
                        outs[k][t * TILE : (t + 1) * TILE, :] = block


def params(mebibytes):
    return pltpu.CompilerParams(vmem_limit_bytes=mebibytes * 2**20)


def gather_features(shard):
    width = shard.shape[1]

    def sibling(block):
        return swap(block, "proto", 1)

    if lax.axis_size("row") != 4 or width % TILE:
        whole = lax.all_gather(shard, "row", axis=1, tiled=True)
        return [whole, sibling(whole)], [0], [None]
    half = shard.shape[0] // 2
    top, bottom = shard[:half], shard[half:]
    near_bottom = swap(bottom, "row", 1)
    far_top = swap(top, "row", 2)
    near_bottom, far_top, top, bottom = lax.optimization_barrier((near_bottom, far_top, top, bottom))
    cross_top = swap(far_top, "row", 1)
    cross_bottom = swap(near_bottom, "row", 2)
    near_top = swap(top, "row", 1)
    far_bottom = swap(bottom, "row", 2)
    pieces = [shard, near_top, near_bottom, far_top, far_bottom, cross_top, cross_bottom]
    firsts = [0, 0, half, 0, half, 0, half]
    return pieces + [sibling(piece) for piece in pieces], firsts, [0, 1, 1, 2, 2, 3, 3]


def scatter_partials(blocks):
    blocks = list(blocks)
    distance = 1
    while distance < len(blocks):
        for j in range(len(blocks) - distance, 0, -2 * distance):
            got = swap(blocks[j].astype(jnp.bfloat16), "proto", 2 * distance).astype(jnp.float32)
            blocks[j ^ distance] = blocks[j ^ distance].astype(jnp.float32) + got
        distance *= 2
    return blocks[0].astype(jnp.bfloat16)


def shards(embeddings, prototypes, block_mask):
    n_row, n_proto = lax.axis_size("row"), lax.axis_size("proto")
    lines = n_proto // 2
    rows, features = embeddings.shape
    protos = 2 * prototypes.shape[0]
    width = features // n_proto
    row_tiles, columns = block_mask.shape[0], 2 * block_mask.shape[1]
    log_column = math.log(rows * n_row / (protos * lines))
    table = Table(row_tiles, columns)

    other_mask = swap(block_mask, "proto", 1)
    pieces, firsts, owners = gather_features(prototypes)
    lists = pl.pallas_call(
        functools.partial(setup_kernel, table),
        out_shape=jax.ShapeDtypeStruct(table.shape, jnp.int32),
        in_specs=[SMEM] * 2,
        out_specs=SMEM,
        name="setup",
    )(block_mask, other_mask)

    row_shape = jax.ShapeDtypeStruct((row_tiles, TILE), jnp.float32)
    column_shape = jax.ShapeDtypeStruct((columns, TILE), jnp.float32)
    half = columns // 2
    panel = (table.dummy + 1, TILE, TILE)
    wide = pltpu.VMEM((row_tiles, TILE, TILE), jnp.float32)
    tall = pltpu.VMEM((columns, TILE, TILE), jnp.float32)
    factors = pltpu.VMEM((columns + 8, TILE), jnp.float32)
    similar, whole, row_part = pl.pallas_call(
        functools.partial(panel_kernel, table, firsts, owners),
        out_shape=(pltpu.VMEM(panel, jnp.float32), pltpu.VMEM((protos, features), jnp.bfloat16), row_shape),
        in_specs=[SMEM] + [pl.BlockSpec(memory_space=pl.ANY)] * 2 + [VMEM] * (len(pieces) - 1),
        out_specs=(VMEM, VMEM, VMEM),
        scratch_shapes=[wide, pltpu.VMEM(embeddings.shape, jnp.bfloat16), pltpu.SemaphoreType.DMA((2,))],
        compiler_params=params(12),
        name="panel",
    )(lists, embeddings, *pieces)

    def row_exchange(part):
        others = [swap(part, "proto", 2 * j) for j in range(lines - 1, 0, -1)]
        return [part] + others[::-1]

    def column_exchange(part):
        others = [swap(part, "row", j) for j in range(n_row - 1, 0, -1)]
        return [part] + others[::-1]

    parts = row_exchange(row_part)
    column_part, first_row, kept, peaks = pl.pallas_call(
        functools.partial(first_column_kernel, table),
        out_shape=(column_shape, row_shape, pltpu.VMEM(panel, jnp.bfloat16), column_shape),
        in_specs=[SMEM] + [VMEM] * (1 + len(parts)),
        out_specs=(VMEM,) * 4,
        scratch_shapes=[wide, tall],
        compiler_params=params(4),
        name="first_column_pass",
    )(lists, similar, *parts)
    for sweep in range(1, ITERS):
        parts = column_exchange(column_part)
        row_part = pl.pallas_call(
            functools.partial(row_kernel, table, log_column),
            out_shape=row_shape,
            in_specs=[SMEM] + [VMEM] * (4 + len(parts)),
            out_specs=VMEM,
            scratch_shapes=[factors, factors, wide],
            compiler_params=params(4),
            name="row_pass",
        )(lists, similar, kept, peaks, first_row, *parts)
        parts = row_exchange(row_part)
        column_part, row_potential, row_out = pl.pallas_call(
            functools.partial(column_kernel, table),
            out_shape=(column_shape, row_shape, row_shape),
            in_specs=[SMEM] + [VMEM] * (4 + len(parts)),
            out_specs=(VMEM,) * 3,
            scratch_shapes=[wide, tall],
            compiler_params=params(4),
            name="column_pass",
        )(lists, similar, kept, peaks, first_row, *parts)
    parts = column_exchange(column_part)
    *blocks, column_potential = pl.pallas_call(
        functools.partial(plan_kernel, table, log_column, lines),
        out_shape=[jax.ShapeDtypeStruct((rows, width), jnp.bfloat16)] * lines
        + [jax.ShapeDtypeStruct((half, TILE), jnp.float32)],
        in_specs=[SMEM] + [VMEM] * (3 + len(parts)),
        out_specs=[VMEM] * (lines + 1),
        scratch_shapes=[
            pltpu.VMEM((columns, TILE), jnp.float32),
            wide,
            pltpu.VMEM((row_tiles, TILE, lines * width), jnp.float32),
        ],
        compiler_params=params(12),
        name="plan",
    )(lists, similar, row_potential, whole, *parts)
    targets = scatter_partials(blocks)
    return (targets, row_out.reshape(rows), column_potential.reshape(protos // 2))


def solution(mesh):
    return jax.shard_map(
        shards,
        mesh=mesh,
        in_specs=(P("row", None), P("proto", "row"), P("row", "proto")),
        out_specs=(P("row", "proto"), P("row"), P("proto")),
        check_vma=False,
    )
```

```python
import functools
import math

import jax
import jax.numpy as jnp
from jax import lax
from jax.experimental import pallas as pl
from jax.experimental.pallas import tpu as pltpu
from jax.sharding import PartitionSpec as P

ITERS = 3
TILE = 128
NEGATIVE = -1e30

VMEM = pl.BlockSpec(memory_space=pltpu.VMEM)
HBM = pl.BlockSpec(memory_space=pltpu.HBM)
SMEM = pl.BlockSpec(memory_space=pltpu.SMEM)


def swap(x, axis, offset):
    size = lax.axis_size(axis)
    return lax.ppermute(x, axis, [(i, i ^ offset) for i in range(size)])


def pair_sum(terms):
    while len(terms) > 1:
        terms = [terms[i] + terms[i + 1] for i in range(0, len(terms), 2)]
    return terms[0]


def combine(parts):
    peak = functools.reduce(jnp.maximum, parts)
    return peak + jnp.log(pair_sum([jnp.exp(part - peak) for part in parts]))


class Table:
    def __init__(self, row_tiles, columns):
        self.row_tiles, self.columns = row_tiles, columns
        self.line = max(row_tiles, columns) + 8
        self.column_base = row_tiles
        self.pair_base = row_tiles + columns
        self.mask_at = (self.pair_base + columns // 2) * self.line
        self.dummy = row_tiles * columns

    def build(self, mask):
        across = mask.T
        pairs = jnp.max(across.reshape(self.columns // 2, 2, self.row_tiles), axis=1)
        lines = [self.lines(mask), self.lines(across), self.lines(pairs)]
        return jnp.concatenate([part.reshape(-1) for part in lines] + [mask.reshape(-1)])

    def lines(self, mask):
        size = mask.shape[1]
        at = jnp.arange(size, dtype=jnp.int32)
        slot = jnp.arange(self.line, dtype=jnp.int32)
        before = jnp.sum(jnp.where(at[None, :] < at[:, None], mask[:, None, :], 0), axis=2)
        hit = (mask[:, None, :] == 1) & (before[:, None, :] == slot[None, :, None])
        places = jnp.sum(jnp.where(hit, at[None, None, :] - size, 0), axis=2) + size
        count = jnp.sum(mask, axis=1, keepdims=True)
        places = jnp.where(slot[None, :] == self.line - 2, (count + 1) // 2, places)
        return jnp.where(slot[None, :] == self.line - 1, (count + 3) // 4, places)

    def steps(self, ref, line, unroll):
        return ref[line * self.line + self.line - (2 if unroll == 2 else 1)]

    def entry(self, ref, line, k):
        return ref[line * self.line + k]

    def allowed(self, ref, t, u):
        return ref[self.mask_at + t * self.columns + u]

    def loop(self, ref, line, unroll, step, start):
        def several(k, a):
            for i in range(unroll):
                a = step(self.entry(ref, line, unroll * k + i), a)
            return a

        return lax.fori_loop(0, self.steps(ref, line, unroll), several, start)

    def place(self, t, u):
        padding = (t == self.row_tiles) | (u == self.columns)
        return jnp.where(padding, self.dummy, t * self.columns + u)


def blank():
    return jnp.zeros((TILE, TILE), jnp.float32)


def lowest():
    return jnp.full((TILE, TILE), NEGATIVE, jnp.float32)


def bad_bits(good):
    bad = jnp.max(jnp.where(good, 0.0, 1.0), axis=1, keepdims=True)
    bit = jnp.left_shift(1, lax.broadcasted_iota(jnp.int32, bad.shape, 0))
    return jnp.sum(bad * bit.astype(jnp.float32)).astype(jnp.int32)


def has_bit(bits, i):
    return jnp.bitwise_and(bits, 1 << i) != 0


def spread_rows(row, wide_ref):
    row_tiles = row.shape[0]
    standing = jnp.concatenate(
        [row, jnp.zeros((TILE - row_tiles, TILE), jnp.float32)], axis=0
    ).T
    for t in range(row_tiles):
        wide_ref[t] = jnp.broadcast_to(standing[:, t : t + 1], (TILE, TILE))


def lying(tiles):
    lane = lax.broadcasted_iota(jnp.int32, (TILE, TILE), 1)
    found = blank()
    for t, tile in enumerate(tiles):
        found = jnp.where(lane == t, jnp.sum(tile, axis=1, keepdims=True), found)
    return found.T[: len(tiles)]


class Piece:
    def __init__(self, own, first, owner):
        self.own, self.first, self.owner = own, first, owner

    def copy_to(self, p_ref, piece):
        core, me = lax.rem(lax.axis_index("proto"), 2), lax.axis_index("row")
        rows, width = piece.shape
        first = (core if self.own else 1 - core) * (p_ref.shape[0] // 2) + self.first
        start = 0
        if self.owner is not None:
            start = pl.multiple_of(jnp.bitwise_xor(me, self.owner) * width, TILE)
        p_ref[pl.ds(pl.multiple_of(first, TILE), rows), pl.ds(start, width)] = piece[...]


def score_pairs(table, table_ref, e_ref, p_ref, s_ref, features, add, done):
    row_tiles, columns = table.row_tiles, table.columns
    scale = 4.0 / math.sqrt(e_ref.shape[1])

    def one_pair(pair, carry):
        line = table.pair_base + pair
        spans = features(pair)

        def four_tiles(k, carry):
            at = [jnp.minimum(table.entry(table_ref, line, 4 * k + i), row_tiles - 1) for i in range(4)]
            product = None
            for span in spans:
                rows = jnp.concatenate(
                    [e_ref[pl.ds(pl.multiple_of(t * TILE, TILE), TILE), span] for t in at], axis=0
                )
                block = p_ref[pl.ds(pl.multiple_of(pair * 2 * TILE, TILE), 2 * TILE), span]
                part = lax.dot_general(
                    rows, block, (((1,), (1,)), ((), ())), preferred_element_type=jnp.float32
                )
                product = part if product is None else product + part
            product = scale * product
            tiles = {}
            for i, t in enumerate(at):
                for side in range(2):
                    where = t * columns + 2 * pair + side
                    tile = product[i * TILE : (i + 1) * TILE, side * TILE : (side + 1) * TILE]
                    tiles[i, side] = (where, s_ref[where] + tile if add else tile)
            for where, tile in tiles.values():
                s_ref[where] = tile
            if done is not None:
                for i, t in enumerate(at):
                    done(t, 2 * pair, tiles[i, 0][1], tiles[i, 1][1])
            return carry

        return lax.fori_loop(0, table.steps(table_ref, line, 4), four_tiles, carry)

    lax.fori_loop(0, columns // 2, one_pair, 0)


def quarters(owners, p_ref, columns):
    me = lax.axis_index("row")
    width = p_ref.shape[1] // 4
    pairs = columns // 4

    def features(pair):
        top = lax.rem(pair, pairs) < pairs // 2
        spans = []
        for first, second in owners:
            owner = jnp.bitwise_xor(me, jnp.where(top, first, second))
            spans.append(pl.ds(pl.multiple_of(owner * width, TILE), width))
        return spans

    return features


def early_panel_kernel(table, places, table_ref, e_hbm_ref, *refs):
    pieces, (s_ref, p_ref, e_ref, sem) = refs[:-4], refs[-4:]
    load = pltpu.make_async_copy(e_hbm_ref, e_ref, sem)
    load.start()
    for place, piece in zip(places, pieces):
        place.copy_to(p_ref, piece)
    s_ref[table.dummy] = lowest()
    load.wait()
    features = quarters([(0, 0), (2, 1)], p_ref, table.columns)
    score_pairs(table, table_ref, e_ref, p_ref, s_ref, features, False, None)


def panel_kernel(table, places, add, table_ref, e_ref, *refs):
    pieces, (s_ref, p_ref, out_ref, acc_ref) = refs[:-4], refs[-4:]
    if add:
        pieces = pieces[:-2]
    row_tiles = table.row_tiles
    for place, piece in zip(places, pieces):
        place.copy_to(p_ref, piece)
    for t in range(row_tiles):
        acc_ref[t] = lowest()

    def done(t, u, left, right):
        peak = acc_ref[t]
        for side, tile in enumerate((left, right)):
            off = jnp.where(table.allowed(table_ref, t, u + side) == 1, 0.0, NEGATIVE)
            peak = jnp.maximum(peak, tile + off)
        acc_ref[t] = peak

    if add:
        features = quarters([(1, 2), (3, 3)], p_ref, table.columns)
    else:
        s_ref[table.dummy] = lowest()
        features = lambda pair: [slice(None)]
    score_pairs(table, table_ref, e_ref, p_ref, s_ref, features, add, done)

    lane = lax.broadcasted_iota(jnp.int32, (TILE, TILE), 1)
    peaks = blank()
    for t in range(row_tiles):
        peak = jnp.max(acc_ref[t], axis=1, keepdims=True)
        peaks = jnp.where(lane == t, peak, peaks)
        acc_ref[t] = jnp.broadcast_to(peak, (TILE, TILE))
    for t in range(row_tiles):
        acc_ref[t] = table.loop(
            table_ref,
            t,
            4,
            lambda u, a, t=t: a + jnp.exp(s_ref[table.place(t, u)] - acc_ref[t]),
            blank(),
        )
    out_ref[...] = peaks.T[:row_tiles] + jnp.log(lying([acc_ref[t] for t in range(row_tiles)]))


def row_kernel(table, log_column, table_ref, s_ref, w_ref, m_ref, r_ref, *refs):
    parts, (out_ref, c_ref, v_ref, acc_ref) = refs[:-4], refs[-4:]
    row_tiles, columns = table.row_tiles, table.columns
    column = log_column - combine([part[...] for part in parts])
    c_ref[:columns] = column
    v_ref[:columns] = jnp.exp(column + m_ref[...])
    rest = jnp.zeros((c_ref.shape[0] - columns, TILE), jnp.float32)
    c_ref[columns:] = rest
    v_ref[columns:] = rest

    for t in range(row_tiles):

        def one_tile(u, a, t=t):
            return a + w_ref[table.place(t, u)].astype(jnp.float32) * v_ref[pl.ds(u, 1), :]

        acc_ref[t] = table.loop(table_ref, t, 4, one_tile, blank())
    totals = lying([acc_ref[t] for t in range(row_tiles)])
    out_ref[...] = jnp.log(totals) - r_ref[...]
    bits = bad_bits(totals > 1e-15)

    @pl.when(bits != 0)
    def _():
        for t in range(row_tiles):

            @pl.when(has_bit(bits, t))
            def _():
                def score(u):
                    return s_ref[table.place(t, u)] + c_ref[pl.ds(u, 1), :]

                peak = table.loop(table_ref, t, 2, lambda u, a: jnp.maximum(a, score(u)), lowest())
                peak = jnp.max(peak, axis=1, keepdims=True)
                total = table.loop(table_ref, t, 2, lambda u, a: a + jnp.exp(score(u) - peak), blank())
                found = peak + jnp.log(jnp.sum(total, axis=1, keepdims=True))
                out_ref[t : t + 1, :] = jnp.broadcast_to(found, (TILE, TILE)).T[:1]


def slow_column(table, table_ref, u, s_ref, wide_ref, keep):
    line = table.column_base + u

    def score(t):
        at = table.place(t, u)
        return at, s_ref[at] + wide_ref[jnp.minimum(t, table.row_tiles - 1)]

    peak = table.loop(table_ref, line, 2, lambda t, a: jnp.maximum(a, score(t)[1]), lowest())
    peak = jnp.max(peak, axis=0, keepdims=True)

    def one_tile(t, a):
        at, value = score(t)
        value = jnp.exp(value - peak)
        keep(at, value)
        return a + value

    total = table.loop(table_ref, line, 2, one_tile, blank())
    return peak, jnp.sum(total, axis=0, keepdims=True)


def first_column_kernel(table, table_ref, s_ref, *refs):
    parts, (out_ref, r_ref, w_ref, m_ref, wide_ref, acc_ref) = refs[:-6], refs[-6:]
    row = -combine([part[...] for part in parts])
    r_ref[...] = row
    spread_rows(row, wide_ref)
    w_ref[table.dummy] = blank().astype(jnp.bfloat16)

    def keep(at, value):
        w_ref[at] = value.astype(jnp.bfloat16)

    for u in range(table.columns):

        def one_tile(t, a, u=u):
            at = table.place(t, u)
            value = jnp.exp(s_ref[at] + wide_ref[jnp.minimum(t, table.row_tiles - 1)])
            keep(at, value)
            return a + value

        acc_ref[u] = table.loop(table_ref, table.column_base + u, 4, one_tile, blank())
    totals = jnp.concatenate(
        [jnp.sum(acc_ref[u], axis=0, keepdims=True) for u in range(table.columns)], axis=0
    )
    m_ref[...] = jnp.zeros(m_ref.shape, jnp.float32)
    out_ref[...] = jnp.log(totals)
    bits = bad_bits(totals > 1e-15)

    @pl.when(bits != 0)
    def _():
        for u in range(table.columns):

            @pl.when(has_bit(bits, u))
            def _():
                peak, total = slow_column(table, table_ref, u, s_ref, wide_ref, keep)
                m_ref[u : u + 1, :] = peak
                out_ref[u : u + 1, :] = peak + jnp.log(total)


def column_kernel(table, table_ref, s_ref, w_ref, m_ref, first_ref, *refs):
    parts, (out_ref, r_ref, r_out_ref, wide_ref, acc_ref) = refs[:-5], refs[-5:]
    row = -combine([part[...] for part in parts])
    r_ref[...] = row
    r_out_ref[...] = row
    factor = jnp.exp(row - first_ref[...])
    spread_rows(factor, wide_ref)

    for u in range(table.columns):

        def one_tile(t, a, u=u):
            kept = w_ref[table.place(t, u)].astype(jnp.float32)
            return a + kept * wide_ref[jnp.minimum(t, table.row_tiles - 1)]

        acc_ref[u] = table.loop(table_ref, table.column_base + u, 4, one_tile, blank())
    totals = jnp.concatenate(
        [jnp.sum(acc_ref[u], axis=0, keepdims=True) for u in range(table.columns)], axis=0
    )
    out_ref[...] = m_ref[...] + jnp.log(totals)
    largest = jnp.max(jnp.max(factor, axis=1, keepdims=True), axis=0, keepdims=True)
    bits = bad_bits((totals > 1e-15) & (totals < 1e30) & (largest < 1e15))

    @pl.when(bits != 0)
    def _():
        spread_rows(row, wide_ref)
        for u in range(table.columns):

            @pl.when(has_bit(bits, u))
            def _():
                peak, total = slow_column(table, table_ref, u, s_ref, wide_ref, lambda at, value: None)
                out_ref[u : u + 1, :] = peak + jnp.log(total)


def plan_kernel(table, log_column, lines, table_ref, s_ref, r_ref, p_ref, *refs):
    parts, outs = refs[: -4 - lines], refs[-4 - lines : -4]
    own_ref, c_ref, wide_ref, total_ref = refs[-4:]
    row_tiles, columns = table.row_tiles, table.columns
    index = lax.axis_index("proto")
    core, z = lax.rem(index, 2), lax.div(index, 2)
    c_ref[...] = log_column - combine([part[...] for part in parts])
    half = columns // 2
    own_ref[...] = c_ref[pl.ds(pl.multiple_of(core * half, half), half), :]
    spread_rows(r_ref[...], wide_ref)
    width = outs[0].shape[1]
    fits = width % TILE == 0
    total_ref[...] = jnp.zeros(total_ref.shape, jnp.float32)

    def one_pair(pair, carry):
        first = pl.multiple_of(pair * 2 * TILE, TILE)
        line = table.pair_base + pair
        blocks = []
        for j in range(lines):
            if fits:
                start = (2 * jnp.bitwise_xor(z, j) + core) * width
                blocks.append(p_ref[pl.ds(first, 2 * TILE), pl.ds(pl.multiple_of(start, TILE), width)])
            else:
                both = p_ref[pl.ds(first, 2 * TILE), 2 * j * width : 2 * (j + 1) * width]
                blocks.append(jnp.where(core == 0, both[:, :width], both[:, width:]))
        block = jnp.concatenate(blocks, axis=1)

        def four_tiles(k, carry):
            at = [table.entry(table_ref, line, 4 * k + i) for i in range(4)]
            inside = [jnp.minimum(t, row_tiles - 1) for t in at]
            strips = []
            for t, real in zip(at, inside):
                sides = []
                for side in range(2):
                    u = 2 * pair + side
                    good = (t < row_tiles) & (table.allowed(table_ref, real, u) == 1)
                    tile = s_ref[jnp.where(good, t * columns + u, table.dummy)]
                    sides.append(jnp.exp(tile + wide_ref[real] + c_ref[pl.ds(u, 1), :]).astype(jnp.bfloat16))
                strips.append(jnp.concatenate(sides, axis=1))
            product = jnp.dot(
                jnp.concatenate(strips, axis=0), block, preferred_element_type=jnp.float32
            )
            for i, t in enumerate(inside):
                total_ref[t] += product[i * TILE : (i + 1) * TILE]
            return carry

        return lax.fori_loop(0, table.steps(table_ref, line, 4), four_tiles, carry)

    lax.fori_loop(0, columns // 2, one_pair, 0)
    for t in range(row_tiles):
        total = total_ref[t].astype(jnp.bfloat16)
        for j in range(lines):
            block = total[:, j * width : (j + 1) * width]
            if fits:
                outs[j][t * TILE : (t + 1) * TILE, :] = block
            else:
                for k in range(lines):

                    @pl.when(jnp.bitwise_xor(z, k) == j)
                    def _():
                        outs[k][t * TILE : (t + 1) * TILE, :] = block


def params(mebibytes):
    return pltpu.CompilerParams(vmem_limit_bytes=mebibytes * 2**20)


def sibling(block):
    return swap(block, "proto", 1)


def tied(*arrays):
    return lax.optimization_barrier(arrays)


def make_panel(table, lists, embeddings, shard, rows, features):
    width = shard.shape[1]
    protos = 2 * shard.shape[0]
    panel = pltpu.VMEM((table.dummy + 1, TILE, TILE), jnp.float32)
    whole = pltpu.VMEM((protos, features), jnp.bfloat16)
    row_shape = jax.ShapeDtypeStruct((table.row_tiles, TILE), jnp.float32)
    peaks = pltpu.VMEM((table.row_tiles, TILE, TILE), jnp.float32)

    def late(places, add, e, pieces, before):
        at = 2 + len(pieces)
        return pl.pallas_call(
            functools.partial(panel_kernel, table, places, add),
            out_shape=(panel, whole, row_shape),
            in_specs=[SMEM] + [VMEM] * (1 + len(pieces) + len(before)),
            out_specs=(VMEM, VMEM, VMEM),
            scratch_shapes=[peaks],
            input_output_aliases={at: 0, at + 1: 1} if add else {},
            compiler_params=params(8),
            name="panel",
        )(lists, e, *pieces, *before)

    if lax.axis_size("row") != 4 or width % TILE:
        every = lax.all_gather(shard, "row", axis=1, tiled=True)
        places = [Piece(True, 0, None), Piece(False, 0, None)]
        return late(places, False, embeddings, [every, sibling(every)], [])
    half = shard.shape[0] // 2
    top, bottom = shard[:half], shard[half:]
    near_bottom = swap(bottom, "row", 1)
    far_top = swap(top, "row", 2)
    near_bottom, far_top, top, bottom = tied(near_bottom, far_top, top, bottom)
    cross_top = swap(far_top, "row", 1)
    cross_bottom = swap(near_bottom, "row", 2)
    near_top = swap(top, "row", 1)
    far_bottom = swap(bottom, "row", 2)
    pieces = [shard, near_bottom, far_top]
    pieces += [sibling(piece) for piece in pieces]
    places = [Piece(own, *at) for own in (True, False) for at in ((0, 0), (half, 1), (0, 2))]
    visits = table.dummy * TILE * TILE
    similar, known, e = pl.pallas_call(
        functools.partial(early_panel_kernel, table, places),
        out_shape=(panel, whole, pltpu.VMEM(embeddings.shape, jnp.bfloat16)),
        in_specs=[SMEM, pl.BlockSpec(memory_space=pl.ANY)] + [VMEM] * len(pieces),
        out_specs=(VMEM, VMEM, VMEM),
        scratch_shapes=[pltpu.SemaphoreType.DMA],
        compiler_params=params(6),
        cost_estimate=pl.CostEstimate(
            flops=visits * features, bytes_accessed=8 * visits, transcendentals=0
        ),
        name="early_panel",
    )(lists, embeddings, *pieces)
    cross_top, cross_bottom, near_top, far_bottom, similar, known, e = tied(
        cross_top, cross_bottom, near_top, far_bottom, similar, known, e
    )
    pieces = [near_top, far_bottom, cross_top, cross_bottom]
    pieces += [sibling(piece) for piece in pieces]
    places = [Piece(own, *at) for own in (True, False) for at in ((0, 1), (half, 2), (0, 3), (half, 3))]
    return late(places, True, e, pieces, [similar, known])


def scatter_partials(blocks):
    blocks = list(blocks)
    distance = 1
    while distance < len(blocks):
        for j in range(len(blocks) - distance, 0, -2 * distance):
            got = swap(blocks[j].astype(jnp.bfloat16), "proto", 2 * distance).astype(jnp.float32)
            blocks[j ^ distance] = blocks[j ^ distance].astype(jnp.float32) + got
        distance *= 2
    return blocks[0].astype(jnp.bfloat16)


def shards(embeddings, prototypes, block_mask):
    n_row, n_proto = lax.axis_size("row"), lax.axis_size("proto")
    lines = n_proto // 2
    rows, features = embeddings.shape
    protos = 2 * prototypes.shape[0]
    width = features // n_proto
    row_tiles, columns = block_mask.shape[0], 2 * block_mask.shape[1]
    log_column = math.log(rows * n_row / (protos * lines))
    table = Table(row_tiles, columns)

    other_mask = swap(block_mask, "proto", 1)
    mask, other_mask = jnp.where(block_mask == 1, 1, 0), jnp.where(other_mask == 1, 1, 0)
    lists = table.build(
        jnp.where(
            lax.axis_index("proto") % 2 == 0,
            jnp.concatenate([mask, other_mask], axis=1),
            jnp.concatenate([other_mask, mask], axis=1),
        )
    )

    row_shape = jax.ShapeDtypeStruct((row_tiles, TILE), jnp.float32)
    column_shape = jax.ShapeDtypeStruct((columns, TILE), jnp.float32)
    half = columns // 2
    panel = (table.dummy + 1, TILE, TILE)
    wide = pltpu.VMEM((row_tiles, TILE, TILE), jnp.float32)
    tall = pltpu.VMEM((columns, TILE, TILE), jnp.float32)
    factors = pltpu.VMEM((columns + 8, TILE), jnp.float32)
    similar, whole, row_part = make_panel(table, lists, embeddings, prototypes, rows, features)

    def row_exchange(part):
        others = [swap(part, "proto", 2 * j) for j in range(lines - 1, 0, -1)]
        return [part] + others[::-1]

    def column_exchange(part):
        others = [swap(part, "row", j) for j in range(n_row - 1, 0, -1)]
        return [part] + others[::-1]

    parts = row_exchange(row_part)
    column_part, first_row, kept, peaks = pl.pallas_call(
        functools.partial(first_column_kernel, table),
        out_shape=(column_shape, row_shape, pltpu.VMEM(panel, jnp.bfloat16), column_shape),
        in_specs=[SMEM] + [VMEM] * (1 + len(parts)),
        out_specs=(VMEM,) * 4,
        scratch_shapes=[wide, tall],
        compiler_params=params(4),
        name="first_column_pass",
    )(lists, similar, *parts)
    for sweep in range(1, ITERS):
        parts = column_exchange(column_part)
        row_part = pl.pallas_call(
            functools.partial(row_kernel, table, log_column),
            out_shape=row_shape,
            in_specs=[SMEM] + [VMEM] * (4 + len(parts)),
            out_specs=VMEM,
            scratch_shapes=[factors, factors, wide],
            compiler_params=params(4),
            name="row_pass",
        )(lists, similar, kept, peaks, first_row, *parts)
        parts = row_exchange(row_part)
        column_part, row_potential, row_out = pl.pallas_call(
            functools.partial(column_kernel, table),
            out_shape=(column_shape, row_shape, row_shape),
            in_specs=[SMEM] + [VMEM] * (4 + len(parts)),
            out_specs=(VMEM,) * 3,
            scratch_shapes=[wide, tall],
            compiler_params=params(4),
            name="column_pass",
        )(lists, similar, kept, peaks, first_row, *parts)
    parts = column_exchange(column_part)
    *blocks, column_potential = pl.pallas_call(
        functools.partial(plan_kernel, table, log_column, lines),
        out_shape=[jax.ShapeDtypeStruct((rows, width), jnp.bfloat16)] * lines
        + [jax.ShapeDtypeStruct((half, TILE), jnp.float32)],
        in_specs=[SMEM] + [VMEM] * (3 + len(parts)),
        out_specs=[VMEM] * (lines + 1),
        scratch_shapes=[
            pltpu.VMEM((columns, TILE), jnp.float32),
            wide,
            pltpu.VMEM((row_tiles, TILE, lines * width), jnp.float32),
        ],
        compiler_params=params(12),
        name="plan",
    )(lists, similar, row_potential, whole, *parts)
    targets = scatter_partials(blocks)
    return (targets, row_out.reshape(rows), column_potential.reshape(protos // 2))


def solution(mesh):
    return jax.shard_map(
        shards,
        mesh=mesh,
        in_specs=(P("row", None), P("proto", "row"), P("row", "proto")),
        out_specs=(P("row", "proto"), P("row"), P("proto")),
        check_vma=False,
    )
```

```python
import functools
import math

import jax
import jax.numpy as jnp
from jax import lax
from jax.experimental import pallas as pl
from jax.experimental.pallas import tpu as pltpu
from jax.sharding import PartitionSpec as P

ITERS = 3
TILE = 128
NEGATIVE = -1e30

VMEM = pl.BlockSpec(memory_space=pltpu.VMEM)
HBM = pl.BlockSpec(memory_space=pltpu.HBM)
SMEM = pl.BlockSpec(memory_space=pltpu.SMEM)


def swap(x, axis, offset):
    size = lax.axis_size(axis)
    return lax.ppermute(x, axis, [(i, i ^ offset) for i in range(size)])


def pair_sum(terms):
    while len(terms) > 1:
        terms = [terms[i] + terms[i + 1] for i in range(0, len(terms), 2)]
    return terms[0]


def combine(parts):
    peak = functools.reduce(jnp.maximum, parts)
    return peak + jnp.log(pair_sum([jnp.exp(part - peak) for part in parts]))


class Table:
    def __init__(self, row_tiles, columns):
        self.row_tiles, self.columns = row_tiles, columns
        self.line = max(row_tiles, columns) + 8
        self.column_base = row_tiles
        self.pair_base = row_tiles + columns
        self.mask_at = (self.pair_base + columns // 2) * self.line
        self.item_at = self.mask_at + row_tiles * columns
        self.items = (columns // 2) * -(-row_tiles // 4)
        self.total_at = self.item_at + 2 * (self.items + 1)
        self.dummy = row_tiles * columns

    def build(self, mask):
        across = mask.T
        pairs = jnp.max(across.reshape(self.columns // 2, 2, self.row_tiles), axis=1)
        lines = [self.lines(mask), self.lines(across), self.lines(pairs)]
        flat = [part.reshape(-1) for part in lines] + [mask.reshape(-1)]
        steps = (jnp.sum(pairs, axis=1) + 3) // 4
        at = jnp.arange(self.columns // 2, dtype=jnp.int32)
        first = jnp.sum(jnp.where(at[None, :] < at[:, None], steps[None, :], 0), axis=1)
        total = jnp.sum(steps)
        item = jnp.minimum(jnp.arange(self.items + 1, dtype=jnp.int32), total - 1)
        pair = jnp.sum(jnp.where(item[:, None] >= (first + steps)[None, :], 1, 0), axis=1)
        step = item - jnp.sum(jnp.where(pair[:, None] == at[None, :], first[None, :], 0), axis=1)
        flat += [(self.pair_base + pair) * self.line + 4 * step, pair]
        return jnp.concatenate(flat + [jnp.stack([total, (total + 1) // 2])])

    def each_item(self, ref, visit):
        def two(k, carry):
            for i in range(2):
                number = 2 * k + i
                at = ref[self.item_at + number]
                visit(
                    number,
                    number < ref[self.total_at],
                    ref[self.item_at + self.items + 1 + number],
                    [ref[at + n] for n in range(4)],
                )
            return carry

        lax.fori_loop(0, ref[self.total_at + 1], two, 0)

    def empty_bits(self, ref, base, count):
        bits = jnp.int32(0)
        for i in range(count):
            bits = bits + jnp.where(self.steps(ref, base + i, 4) == 0, 1 << i, 0)
        return bits

    def lines(self, mask):
        size = mask.shape[1]
        at = jnp.arange(size, dtype=jnp.int32)
        slot = jnp.arange(self.line, dtype=jnp.int32)
        before = jnp.sum(jnp.where(at[None, :] < at[:, None], mask[:, None, :], 0), axis=2)
        hit = (mask[:, None, :] == 1) & (before[:, None, :] == slot[None, :, None])
        places = jnp.sum(jnp.where(hit, at[None, None, :] - size, 0), axis=2) + size
        count = jnp.sum(mask, axis=1, keepdims=True)
        places = jnp.where(slot[None, :] == self.line - 2, (count + 1) // 2, places)
        return jnp.where(slot[None, :] == self.line - 1, (count + 3) // 4, places)

    def steps(self, ref, line, unroll):
        return ref[line * self.line + self.line - (2 if unroll == 2 else 1)]

    def entry(self, ref, line, k):
        return ref[line * self.line + k]

    def allowed(self, ref, t, u):
        return ref[self.mask_at + t * self.columns + u]

    def loop(self, ref, line, unroll, step, start):
        def several(k, a):
            for i in range(unroll):
                a = step(self.entry(ref, line, unroll * k + i), a)
            return a

        return lax.fori_loop(0, self.steps(ref, line, unroll), several, start)

    def place(self, t, u):
        padding = (t == self.row_tiles) | (u == self.columns)
        return jnp.where(padding, self.dummy, t * self.columns + u)


def blank():
    return jnp.zeros((TILE, TILE), jnp.float32)


def lowest():
    return jnp.full((TILE, TILE), NEGATIVE, jnp.float32)


def bad_bits(good):
    bad = jnp.max(jnp.where(good, 0.0, 1.0), axis=1, keepdims=True)
    bit = jnp.left_shift(1, lax.broadcasted_iota(jnp.int32, bad.shape, 0))
    return jnp.sum(bad * bit.astype(jnp.float32)).astype(jnp.int32)


def has_bit(bits, i):
    return jnp.bitwise_and(bits, 1 << i) != 0


def spread_rows(row, wide_ref):
    row_tiles = row.shape[0]
    standing = jnp.concatenate(
        [row, jnp.zeros((TILE - row_tiles, TILE), jnp.float32)], axis=0
    ).T
    for t in range(row_tiles):
        wide_ref[t] = jnp.broadcast_to(standing[:, t : t + 1], (TILE, TILE))


def lying(tiles):
    lane = lax.broadcasted_iota(jnp.int32, (TILE, TILE), 1)
    found = blank()
    for t, tile in enumerate(tiles):
        found = jnp.where(lane == t, jnp.sum(tile, axis=1, keepdims=True), found)
    return found.T[: len(tiles)]


class Piece:
    def __init__(self, own, first, owner):
        self.own, self.first, self.owner = own, first, owner

    def copy_to(self, p_ref, piece):
        core, me = lax.rem(lax.axis_index("proto"), 2), lax.axis_index("row")
        rows, width = piece.shape
        first = (core if self.own else 1 - core) * (p_ref.shape[0] // 2) + self.first
        start = 0
        if self.owner is not None:
            start = pl.multiple_of(jnp.bitwise_xor(me, self.owner) * width, TILE)
        p_ref[pl.ds(pl.multiple_of(first, TILE), rows), pl.ds(start, width)] = piece[...]


def score_pairs(table, table_ref, e_ref, p_ref, s_ref, features, add, done):
    row_tiles, columns = table.row_tiles, table.columns
    scale = 4.0 / math.sqrt(e_ref.shape[1])

    def visit(number, real, pair, tiles):
        at = [jnp.minimum(t, row_tiles - 1) for t in tiles]
        product = None
        for span in features(pair):
            rows = jnp.concatenate(
                [e_ref[pl.ds(pl.multiple_of(t * TILE, TILE), TILE), span] for t in at], axis=0
            )
            block = p_ref[pl.ds(pl.multiple_of(pair * 2 * TILE, TILE), 2 * TILE), span]
            part = lax.dot_general(
                rows, block, (((1,), (1,)), ((), ())), preferred_element_type=jnp.float32
            )
            product = part if product is None else product + part
        product = (jnp.where(real, scale, 0.0) if add else scale) * product
        found = {}
        for i, t in enumerate(at):
            for side in range(2):
                where = t * columns + 2 * pair + side
                tile = product[i * TILE : (i + 1) * TILE, side * TILE : (side + 1) * TILE]
                found[i, side] = (where, s_ref[where] + tile if add else tile)
        for where, tile in found.values():
            s_ref[where] = tile
        if done is not None:
            for i, t in enumerate(at):
                done(t, 2 * pair, found[i, 0][1], found[i, 1][1])

    table.each_item(table_ref, visit)


def quarters(owners, p_ref, columns):
    me = lax.axis_index("row")
    width = p_ref.shape[1] // 4
    pairs = columns // 4

    def features(pair):
        top = lax.rem(pair, pairs) < pairs // 2
        spans = []
        for first, second in owners:
            owner = jnp.bitwise_xor(me, jnp.where(top, first, second))
            spans.append(pl.ds(pl.multiple_of(owner * width, TILE), width))
        return spans

    return features


def early_panel_kernel(table, places, table_ref, e_hbm_ref, *refs):
    pieces, (s_ref, p_ref, e_ref, sem) = refs[:-4], refs[-4:]
    load = pltpu.make_async_copy(e_hbm_ref, e_ref, sem)
    load.start()
    for place, piece in zip(places, pieces):
        place.copy_to(p_ref, piece)
    s_ref[table.dummy] = lowest()
    load.wait()
    features = quarters([(0, 0), (2, 1)], p_ref, table.columns)
    score_pairs(table, table_ref, e_ref, p_ref, s_ref, features, False, None)


def panel_kernel(table, places, add, table_ref, e_ref, *refs):
    pieces, (s_ref, p_ref, out_ref, acc_ref) = refs[:-4], refs[-4:]
    if add:
        pieces = pieces[:-2]
    row_tiles = table.row_tiles
    for place, piece in zip(places, pieces):
        place.copy_to(p_ref, piece)
    for t in range(row_tiles):
        acc_ref[t] = lowest()

    def done(t, u, left, right):
        peak = acc_ref[t]
        for side, tile in enumerate((left, right)):
            off = jnp.where(table.allowed(table_ref, t, u + side) == 1, 0.0, NEGATIVE)
            peak = jnp.maximum(peak, tile + off)
        acc_ref[t] = peak

    if add:
        features = quarters([(1, 2), (3, 3)], p_ref, table.columns)
    else:
        s_ref[table.dummy] = lowest()
        features = lambda pair: [slice(None)]
    score_pairs(table, table_ref, e_ref, p_ref, s_ref, features, add, done)

    lane = lax.broadcasted_iota(jnp.int32, (TILE, TILE), 1)
    peaks = blank()
    for t in range(row_tiles):
        peak = jnp.max(acc_ref[t], axis=1, keepdims=True)
        peaks = jnp.where(lane == t, peak, peaks)
        acc_ref[t] = jnp.broadcast_to(peak, (TILE, TILE))
    for t in range(row_tiles):
        acc_ref[t] = table.loop(
            table_ref,
            t,
            4,
            lambda u, a, t=t: a + jnp.exp(s_ref[table.place(t, u)] - acc_ref[t]),
            blank(),
        )
    out_ref[...] = peaks.T[:row_tiles] + jnp.log(lying([acc_ref[t] for t in range(row_tiles)]))


def row_kernel(table, log_column, table_ref, s_ref, w_ref, m_ref, r_ref, *refs):
    parts, (out_ref, c_ref, v_ref, acc_ref) = refs[:-4], refs[-4:]
    row_tiles, columns = table.row_tiles, table.columns
    column = log_column - combine([part[...] for part in parts])
    c_ref[:columns] = column
    v_ref[:columns] = jnp.exp(column + m_ref[...])
    rest = jnp.zeros((c_ref.shape[0] - columns, TILE), jnp.float32)
    c_ref[columns:] = rest
    v_ref[columns:] = rest

    for t in range(row_tiles):

        def one_tile(u, a, t=t):
            return a + w_ref[table.place(t, u)].astype(jnp.float32) * v_ref[pl.ds(u, 1), :]

        acc_ref[t] = table.loop(table_ref, t, 4, one_tile, blank())
    totals = lying([acc_ref[t] for t in range(row_tiles)])
    out_ref[...] = jnp.log(totals) - r_ref[...]
    bits = bad_bits(totals > 1e-15) - table.empty_bits(table_ref, 0, row_tiles)

    @pl.when(bits != 0)
    def _():
        for t in range(row_tiles):

            @pl.when(has_bit(bits, t))
            def _():
                def score(u):
                    return s_ref[table.place(t, u)] + c_ref[pl.ds(u, 1), :]

                peak = table.loop(table_ref, t, 2, lambda u, a: jnp.maximum(a, score(u)), lowest())
                peak = jnp.max(peak, axis=1, keepdims=True)
                total = table.loop(table_ref, t, 2, lambda u, a: a + jnp.exp(score(u) - peak), blank())
                found = peak + jnp.log(jnp.sum(total, axis=1, keepdims=True))
                out_ref[t : t + 1, :] = jnp.broadcast_to(found, (TILE, TILE)).T[:1]


def slow_column(table, table_ref, u, s_ref, wide_ref, keep):
    line = table.column_base + u

    def score(t):
        at = table.place(t, u)
        return at, s_ref[at] + wide_ref[jnp.minimum(t, table.row_tiles - 1)]

    peak = table.loop(table_ref, line, 2, lambda t, a: jnp.maximum(a, score(t)[1]), lowest())
    peak = jnp.max(peak, axis=0, keepdims=True)

    def one_tile(t, a):
        at, value = score(t)
        value = jnp.exp(value - peak)
        keep(at, value)
        return a + value

    total = table.loop(table_ref, line, 2, one_tile, blank())
    return peak, jnp.sum(total, axis=0, keepdims=True)


def first_column_kernel(table, table_ref, s_ref, *refs):
    parts, (out_ref, r_ref, w_ref, m_ref, wide_ref, acc_ref) = refs[:-6], refs[-6:]
    row = -combine([part[...] for part in parts])
    r_ref[...] = row
    spread_rows(row, wide_ref)
    w_ref[table.dummy] = blank().astype(jnp.bfloat16)

    def keep(at, value):
        w_ref[at] = value.astype(jnp.bfloat16)

    for u in range(table.columns):

        def one_tile(t, a, u=u):
            at = table.place(t, u)
            value = jnp.exp(s_ref[at] + wide_ref[jnp.minimum(t, table.row_tiles - 1)])
            keep(at, value)
            return a + value

        acc_ref[u] = table.loop(table_ref, table.column_base + u, 4, one_tile, blank())
    totals = jnp.concatenate(
        [jnp.sum(acc_ref[u], axis=0, keepdims=True) for u in range(table.columns)], axis=0
    )
    m_ref[...] = jnp.zeros(m_ref.shape, jnp.float32)
    out_ref[...] = jnp.log(totals)
    bits = bad_bits(totals > 1e-15) - table.empty_bits(table_ref, table.column_base, table.columns)

    @pl.when(bits != 0)
    def _():
        for u in range(table.columns):

            @pl.when(has_bit(bits, u))
            def _():
                peak, total = slow_column(table, table_ref, u, s_ref, wide_ref, keep)
                m_ref[u : u + 1, :] = peak
                out_ref[u : u + 1, :] = peak + jnp.log(total)


def column_kernel(table, table_ref, s_ref, w_ref, m_ref, first_ref, *refs):
    parts, (out_ref, r_ref, r_out_ref, wide_ref, acc_ref) = refs[:-5], refs[-5:]
    row = -combine([part[...] for part in parts])
    r_ref[...] = row
    r_out_ref[...] = row
    factor = jnp.exp(row - first_ref[...])
    spread_rows(factor, wide_ref)

    for u in range(table.columns):

        def one_tile(t, a, u=u):
            kept = w_ref[table.place(t, u)].astype(jnp.float32)
            return a + kept * wide_ref[jnp.minimum(t, table.row_tiles - 1)]

        acc_ref[u] = table.loop(table_ref, table.column_base + u, 4, one_tile, blank())
    totals = jnp.concatenate(
        [jnp.sum(acc_ref[u], axis=0, keepdims=True) for u in range(table.columns)], axis=0
    )
    out_ref[...] = m_ref[...] + jnp.log(totals)
    largest = jnp.max(jnp.max(factor, axis=1, keepdims=True), axis=0, keepdims=True)
    bits = bad_bits((totals > 1e-15) & (totals < 1e30) & (largest < 1e15))
    bits = bits - table.empty_bits(table_ref, table.column_base, table.columns)

    @pl.when(bits != 0)
    def _():
        spread_rows(row, wide_ref)
        for u in range(table.columns):

            @pl.when(has_bit(bits, u))
            def _():
                peak, total = slow_column(table, table_ref, u, s_ref, wide_ref, lambda at, value: None)
                out_ref[u : u + 1, :] = peak + jnp.log(total)


def plan_blocks(table, table_ref, p_ref, lines, wanted, width, strip, outs, total_ref):
    row_tiles = table.row_tiles
    index = lax.axis_index("proto")
    core, z = lax.rem(index, 2), lax.div(index, 2)
    fits = width % TILE == 0
    total_ref[...] = jnp.zeros(total_ref.shape, jnp.float32)

    def visit(number, real, pair, tiles):
        first = pl.multiple_of(pair * 2 * TILE, TILE)
        blocks = []
        for j in wanted if fits else range(lines):
            if fits:
                start = (2 * jnp.bitwise_xor(z, j) + core) * width
                blocks.append(p_ref[pl.ds(first, 2 * TILE), pl.ds(pl.multiple_of(start, TILE), width)])
            else:
                both = p_ref[pl.ds(first, 2 * TILE), 2 * j * width : 2 * (j + 1) * width]
                blocks.append(jnp.where(core == 0, both[:, :width], both[:, width:]))
        product = jnp.dot(
            strip(number, real, pair, tiles),
            jnp.concatenate(blocks, axis=1),
            preferred_element_type=jnp.float32,
        )
        for i, t in enumerate(tiles):
            total_ref[jnp.minimum(t, row_tiles - 1)] += product[i * TILE : (i + 1) * TILE]

    table.each_item(table_ref, visit)
    for t in range(row_tiles):
        total = total_ref[t].astype(jnp.bfloat16)
        rows = slice(t * TILE, (t + 1) * TILE)
        for n, j in enumerate(wanted):
            if fits:
                outs[n][rows, :] = total[:, n * width : (n + 1) * width]
                continue
            for k in range(lines):

                @pl.when(jnp.bitwise_xor(z, j) == k)
                def _():
                    outs[n][rows, :] = total[:, k * width : (k + 1) * width]


def plan_kernel(table, log_column, lines, table_ref, s_ref, r_ref, p_ref, *refs):
    parts, (out_ref, kept_ref, own_ref, c_ref, wide_ref, total_ref) = refs[:-6], refs[-6:]
    row_tiles, columns = table.row_tiles, table.columns
    core = lax.rem(lax.axis_index("proto"), 2)
    c_ref[...] = log_column - combine([part[...] for part in parts])
    half = columns // 2
    own_ref[...] = c_ref[pl.ds(pl.multiple_of(core * half, half), half), :]
    spread_rows(r_ref[...], wide_ref)

    def strip(number, real, pair, tiles):
        strips = []
        for t in tiles:
            inside = jnp.minimum(t, row_tiles - 1)
            sides = []
            for side in range(2):
                u = 2 * pair + side
                good = real & (t < row_tiles) & (table.allowed(table_ref, inside, u) == 1)
                tile = s_ref[jnp.where(good, t * columns + u, table.dummy)]
                sides.append(jnp.exp(tile + wide_ref[inside] + c_ref[pl.ds(u, 1), :]).astype(jnp.bfloat16))
            strips.append(jnp.concatenate(sides, axis=1))
        strips = jnp.concatenate(strips, axis=0)
        kept_ref[number] = strips
        return strips

    width = out_ref.shape[1]
    plan_blocks(table, table_ref, p_ref, lines, [lines - 1], width, strip, [out_ref], total_ref)


def rest_kernel(table, lines, table_ref, kept_ref, p_ref, *refs):
    outs, total_ref = refs[:-1], refs[-1]
    width = outs[0].shape[1]
    strip = lambda number, real, pair, tiles: kept_ref[number]
    plan_blocks(table, table_ref, p_ref, lines, list(range(lines - 1)), width, strip, outs, total_ref)


def params(mebibytes):
    return pltpu.CompilerParams(vmem_limit_bytes=mebibytes * 2**20)


def sibling(block):
    return swap(block, "proto", 1)


def tied(*arrays):
    return lax.optimization_barrier(arrays)


def make_panel(table, lists, embeddings, shard, rows, features):
    width = shard.shape[1]
    protos = 2 * shard.shape[0]
    panel = pltpu.VMEM((table.dummy + 1, TILE, TILE), jnp.float32)
    whole = pltpu.VMEM((protos, features), jnp.bfloat16)
    row_shape = jax.ShapeDtypeStruct((table.row_tiles, TILE), jnp.float32)
    peaks = pltpu.VMEM((table.row_tiles, TILE, TILE), jnp.float32)

    def late(places, add, e, pieces, before):
        at = 2 + len(pieces)
        return pl.pallas_call(
            functools.partial(panel_kernel, table, places, add),
            out_shape=(panel, whole, row_shape),
            in_specs=[SMEM] + [VMEM] * (1 + len(pieces) + len(before)),
            out_specs=(VMEM, VMEM, VMEM),
            scratch_shapes=[peaks],
            input_output_aliases={at: 0, at + 1: 1} if add else {},
            compiler_params=params(8),
            name="panel",
        )(lists, e, *pieces, *before)

    if lax.axis_size("row") != 4 or width % TILE:
        every = lax.all_gather(shard, "row", axis=1, tiled=True)
        places = [Piece(True, 0, None), Piece(False, 0, None)]
        return late(places, False, embeddings, [every, sibling(every)], [])
    half = shard.shape[0] // 2
    top, bottom = shard[:half], shard[half:]
    near_bottom = swap(bottom, "row", 1)
    far_top = swap(top, "row", 2)
    near_bottom, far_top, top, bottom = tied(near_bottom, far_top, top, bottom)
    cross_top = swap(far_top, "row", 1)
    cross_bottom = swap(near_bottom, "row", 2)
    near_top = swap(top, "row", 1)
    far_bottom = swap(bottom, "row", 2)
    pieces = [shard, near_bottom, far_top]
    pieces += [sibling(piece) for piece in pieces]
    places = [Piece(own, *at) for own in (True, False) for at in ((0, 0), (half, 1), (0, 2))]
    visits = table.dummy * TILE * TILE
    similar, known, e = pl.pallas_call(
        functools.partial(early_panel_kernel, table, places),
        out_shape=(panel, whole, pltpu.VMEM(embeddings.shape, jnp.bfloat16)),
        in_specs=[SMEM, pl.BlockSpec(memory_space=pl.ANY)] + [VMEM] * len(pieces),
        out_specs=(VMEM, VMEM, VMEM),
        scratch_shapes=[pltpu.SemaphoreType.DMA],
        compiler_params=params(6),
        cost_estimate=pl.CostEstimate(
            flops=visits * features, bytes_accessed=8 * visits, transcendentals=0
        ),
        name="early_panel",
    )(lists, embeddings, *pieces)
    cross_top, cross_bottom, near_top, far_bottom, similar, known, e = tied(
        cross_top, cross_bottom, near_top, far_bottom, similar, known, e
    )
    pieces = [near_top, far_bottom, cross_top, cross_bottom]
    pieces += [sibling(piece) for piece in pieces]
    places = [Piece(own, *at) for own in (True, False) for at in ((0, 1), (half, 2), (0, 3), (half, 3))]
    return late(places, True, e, pieces, [similar, known])


def scatter_partials(blocks):
    blocks = list(blocks)
    distance = 1
    while distance < len(blocks):
        for j in range(len(blocks) - distance, 0, -2 * distance):
            got = swap(blocks[j].astype(jnp.bfloat16), "proto", 2 * distance).astype(jnp.float32)
            blocks[j ^ distance] = blocks[j ^ distance].astype(jnp.float32) + got
        distance *= 2
    return blocks[0].astype(jnp.bfloat16)


def shards(embeddings, prototypes, block_mask):
    n_row, n_proto = lax.axis_size("row"), lax.axis_size("proto")
    lines = n_proto // 2
    rows, features = embeddings.shape
    protos = 2 * prototypes.shape[0]
    width = features // n_proto
    row_tiles, columns = block_mask.shape[0], 2 * block_mask.shape[1]
    log_column = math.log(rows * n_row / (protos * lines))
    table = Table(row_tiles, columns)

    other_mask = swap(block_mask, "proto", 1)
    mask, other_mask = jnp.where(block_mask == 1, 1, 0), jnp.where(other_mask == 1, 1, 0)
    lists = table.build(
        jnp.where(
            lax.axis_index("proto") % 2 == 0,
            jnp.concatenate([mask, other_mask], axis=1),
            jnp.concatenate([other_mask, mask], axis=1),
        )
    )

    row_shape = jax.ShapeDtypeStruct((row_tiles, TILE), jnp.float32)
    column_shape = jax.ShapeDtypeStruct((columns, TILE), jnp.float32)
    half = columns // 2
    panel = (table.dummy + 1, TILE, TILE)
    wide = pltpu.VMEM((row_tiles, TILE, TILE), jnp.float32)
    tall = pltpu.VMEM((columns, TILE, TILE), jnp.float32)
    factors = pltpu.VMEM((columns + 8, TILE), jnp.float32)
    similar, whole, row_part = make_panel(table, lists, embeddings, prototypes, rows, features)

    def row_exchange(part):
        others = [swap(part, "proto", 2 * j) for j in range(lines - 1, 0, -1)]
        return [part] + others[::-1]

    def column_exchange(part):
        others = [swap(part, "row", j) for j in range(n_row - 1, 0, -1)]
        return [part] + others[::-1]

    parts = row_exchange(row_part)
    column_part, first_row, kept, peaks = pl.pallas_call(
        functools.partial(first_column_kernel, table),
        out_shape=(column_shape, row_shape, pltpu.VMEM(panel, jnp.bfloat16), column_shape),
        in_specs=[SMEM] + [VMEM] * (1 + len(parts)),
        out_specs=(VMEM,) * 4,
        scratch_shapes=[wide, tall],
        compiler_params=params(4),
        name="first_column_pass",
    )(lists, similar, *parts)
    for sweep in range(1, ITERS):
        parts = column_exchange(column_part)
        row_part = pl.pallas_call(
            functools.partial(row_kernel, table, log_column),
            out_shape=row_shape,
            in_specs=[SMEM] + [VMEM] * (4 + len(parts)),
            out_specs=VMEM,
            scratch_shapes=[factors, factors, wide],
            compiler_params=params(4),
            name="row_pass",
        )(lists, similar, kept, peaks, first_row, *parts)
        parts = row_exchange(row_part)
        column_part, row_potential, row_out = pl.pallas_call(
            functools.partial(column_kernel, table),
            out_shape=(column_shape, row_shape, row_shape),
            in_specs=[SMEM] + [VMEM] * (4 + len(parts)),
            out_specs=(VMEM,) * 3,
            scratch_shapes=[wide, tall],
            compiler_params=params(4),
            name="column_pass",
        )(lists, similar, kept, peaks, first_row, *parts)
    parts = column_exchange(column_part)
    block = jax.ShapeDtypeStruct((rows, width), jnp.bfloat16)

    def sums(blocks):
        taken = blocks if width % TILE == 0 else lines
        return pltpu.VMEM((row_tiles, TILE, taken * width), jnp.float32)

    last, plan, column_potential = pl.pallas_call(
        functools.partial(plan_kernel, table, log_column, lines),
        out_shape=[
            block,
            pltpu.VMEM((table.items + 1, 4 * TILE, 2 * TILE), jnp.bfloat16),
            jax.ShapeDtypeStruct((half, TILE), jnp.float32),
        ],
        in_specs=[SMEM] + [VMEM] * (3 + len(parts)),
        out_specs=[VMEM] * 3,
        scratch_shapes=[pltpu.VMEM((columns, TILE), jnp.float32), wide, sums(1)],
        compiler_params=params(12),
        name="plan",
    )(lists, similar, row_potential, whole, *parts)
    visits = table.dummy * TILE * TILE
    blocks = pl.pallas_call(
        functools.partial(rest_kernel, table, lines),
        out_shape=[block] * (lines - 1),
        in_specs=[SMEM] + [VMEM] * 2,
        out_specs=[VMEM] * (lines - 1),
        scratch_shapes=[sums(lines - 1)],
        compiler_params=params(12),
        cost_estimate=pl.CostEstimate(
            flops=2 * visits * (lines - 1) * width, bytes_accessed=4 * visits, transcendentals=0
        ),
        name="rest_of_plan",
    )(lists, plan, whole)
    blocks = list(blocks) + [last]
    targets = scatter_partials(blocks)
    return (targets, row_out.reshape(rows), column_potential.reshape(protos // 2))


def solution(mesh):
    return jax.shard_map(
        shards,
        mesh=mesh,
        in_specs=(P("row", None), P("proto", "row"), P("row", "proto")),
        out_specs=(P("row", "proto"), P("row"), P("proto")),
        check_vma=False,
    )
```

```python
import functools
import math

import jax
import jax.numpy as jnp
from jax import lax
from jax.experimental import pallas as pl
from jax.experimental.pallas import tpu as pltpu
from jax.sharding import PartitionSpec as P

ITERS = 3
TILE = 128
NEGATIVE = -1e30

VMEM = pl.BlockSpec(memory_space=pltpu.VMEM)
ANY = pl.BlockSpec(memory_space=pl.ANY)


def swap(x, axis, offset):
    size = lax.axis_size(axis)
    return lax.ppermute(x, axis, [(i, i ^ offset) for i in range(size)])


def pair_sum(terms):
    while len(terms) > 1:
        terms = [terms[i] + terms[i + 1] for i in range(0, len(terms), 2)]
    return terms[0]


def combine(parts):
    peak = functools.reduce(jnp.maximum, parts)
    return peak + jnp.log(pair_sum([jnp.exp(part - peak) for part in parts]))


class Table:
    def __init__(self, row_tiles, columns):
        self.row_tiles, self.columns = row_tiles, columns
        self.line = max(row_tiles, columns) + 8
        self.column_base = row_tiles
        self.pair_base = row_tiles + columns
        self.mask_at = (self.pair_base + columns // 2) * self.line
        self.item_at = self.mask_at + row_tiles * columns
        self.items = (columns // 2) * -(-row_tiles // 4)
        self.total_at = self.item_at + 2 * (self.items + 1)
        self.dummy = row_tiles * columns

    def build(self, mask):
        across = mask.T
        pairs = jnp.max(across.reshape(self.columns // 2, 2, self.row_tiles), axis=1)
        lines = [self.lines(mask), self.lines(across), self.lines(pairs)]
        flat = [part.reshape(-1) for part in lines] + [mask.reshape(-1)]
        steps = (jnp.sum(pairs, axis=1) + 3) // 4
        at = jnp.arange(self.columns // 2, dtype=jnp.int32)
        first = jnp.sum(jnp.where(at[None, :] < at[:, None], steps[None, :], 0), axis=1)
        total = jnp.sum(steps)
        item = jnp.minimum(jnp.arange(self.items + 1, dtype=jnp.int32), total - 1)
        pair = jnp.sum(jnp.where(item[:, None] >= (first + steps)[None, :], 1, 0), axis=1)
        step = item - jnp.sum(jnp.where(pair[:, None] == at[None, :], first[None, :], 0), axis=1)
        flat += [(self.pair_base + pair) * self.line + 4 * step, pair]
        return jnp.concatenate(flat + [jnp.stack([total, (total + 1) // 2])])

    def each_item(self, ref, visit):
        def two(k, carry):
            for i in range(2):
                number = 2 * k + i
                at = ref[self.item_at + number]
                visit(
                    number,
                    number < ref[self.total_at],
                    ref[self.item_at + self.items + 1 + number],
                    [ref[at + n] for n in range(4)],
                )
            return carry

        lax.fori_loop(0, ref[self.total_at + 1], two, 0)

    def empty_bits(self, ref, base, count):
        bits = jnp.int32(0)
        for i in range(count):
            bits = bits + jnp.where(self.steps(ref, base + i, 4) == 0, 1 << i, 0)
        return bits

    def lines(self, mask):
        size = mask.shape[1]
        at = jnp.arange(size, dtype=jnp.int32)
        slot = jnp.arange(self.line, dtype=jnp.int32)
        before = jnp.sum(jnp.where(at[None, :] < at[:, None], mask[:, None, :], 0), axis=2)
        hit = (mask[:, None, :] == 1) & (before[:, None, :] == slot[None, :, None])
        places = jnp.sum(jnp.where(hit, at[None, None, :] - size, 0), axis=2) + size
        count = jnp.sum(mask, axis=1, keepdims=True)
        places = jnp.where(slot[None, :] == self.line - 2, (count + 1) // 2, places)
        return jnp.where(slot[None, :] == self.line - 1, (count + 3) // 4, places)

    def steps(self, ref, line, unroll):
        return ref[line * self.line + self.line - (2 if unroll == 2 else 1)]

    def entry(self, ref, line, k):
        return ref[line * self.line + k]

    def allowed(self, ref, t, u):
        return ref[self.mask_at + t * self.columns + u]

    def loop(self, ref, line, unroll, step, start):
        def several(k, a):
            for i in range(unroll):
                a = step(self.entry(ref, line, unroll * k + i), a)
            return a

        return lax.fori_loop(0, self.steps(ref, line, unroll), several, start)

    def place(self, t, u):
        padding = (t == self.row_tiles) | (u == self.columns)
        return jnp.where(padding, self.dummy, t * self.columns + u)


def with_table(kernel, table, *settings):
    def body(hbm_ref, *refs):
        *refs, smem_ref, sem = refs
        copy = pltpu.make_async_copy(hbm_ref, smem_ref, sem)
        copy.start()

        def arrived():
            copy.wait()
            return smem_ref

        kernel(table, *settings, arrived, *refs)

    return body


def table_scratch(lists):
    return [pltpu.SMEM(lists.shape, jnp.int32), pltpu.SemaphoreType.DMA]


def blank():
    return jnp.zeros((TILE, TILE), jnp.float32)


def lowest():
    return jnp.full((TILE, TILE), NEGATIVE, jnp.float32)


def bad_bits(good):
    bad = jnp.max(jnp.where(good, 0.0, 1.0), axis=1, keepdims=True)
    bit = jnp.left_shift(1, lax.broadcasted_iota(jnp.int32, bad.shape, 0))
    return jnp.sum(bad * bit.astype(jnp.float32)).astype(jnp.int32)


def has_bit(bits, i):
    return jnp.bitwise_and(bits, 1 << i) != 0


def spread_rows(row, wide_ref):
    row_tiles = row.shape[0]
    standing = jnp.concatenate(
        [row, jnp.zeros((TILE - row_tiles, TILE), jnp.float32)], axis=0
    ).T
    for t in range(row_tiles):
        wide_ref[t] = jnp.broadcast_to(standing[:, t : t + 1], (TILE, TILE))


def lying(tiles):
    lane = lax.broadcasted_iota(jnp.int32, (TILE, TILE), 1)
    found = blank()
    for t, tile in enumerate(tiles):
        found = jnp.where(lane == t, jnp.sum(tile, axis=1, keepdims=True), found)
    return found.T[: len(tiles)]


class Piece:
    def __init__(self, own, first, owner):
        self.own, self.first, self.owner = own, first, owner

    def copy_to(self, p_ref, piece):
        core, me = lax.rem(lax.axis_index("proto"), 2), lax.axis_index("row")
        rows, width = piece.shape
        first = (core if self.own else 1 - core) * (p_ref.shape[0] // 2) + self.first
        start = 0
        if self.owner is not None:
            start = pl.multiple_of(jnp.bitwise_xor(me, self.owner) * width, TILE)
        p_ref[pl.ds(pl.multiple_of(first, TILE), rows), pl.ds(start, width)] = piece[...]


def score_pairs(table, table_ref, e_ref, p_ref, s_ref, features, add, done):
    row_tiles, columns = table.row_tiles, table.columns
    scale = 4.0 / math.sqrt(e_ref.shape[1])

    def visit(number, real, pair, tiles):
        at = [jnp.minimum(t, row_tiles - 1) for t in tiles]
        product = None
        for span in features(pair):
            rows = jnp.concatenate(
                [e_ref[pl.ds(pl.multiple_of(t * TILE, TILE), TILE), span] for t in at], axis=0
            )
            block = p_ref[pl.ds(pl.multiple_of(pair * 2 * TILE, TILE), 2 * TILE), span]
            part = lax.dot_general(
                rows, block, (((1,), (1,)), ((), ())), preferred_element_type=jnp.float32
            )
            product = part if product is None else product + part
        product = (jnp.where(real, scale, 0.0) if add else scale) * product
        found = {}
        for i, t in enumerate(at):
            for side in range(2):
                where = t * columns + 2 * pair + side
                tile = product[i * TILE : (i + 1) * TILE, side * TILE : (side + 1) * TILE]
                found[i, side] = (where, s_ref[where] + tile if add else tile)
        for where, tile in found.values():
            s_ref[where] = tile
        if done is not None:
            for i, t in enumerate(at):
                done(t, 2 * pair, found[i, 0][1], found[i, 1][1])

    table.each_item(table_ref, visit)


def quarters(owners, p_ref, columns):
    me = lax.axis_index("row")
    width = p_ref.shape[1] // 4
    pairs = columns // 4

    def features(pair):
        top = lax.rem(pair, pairs) < pairs // 2
        spans = []
        for first, second in owners:
            owner = jnp.bitwise_xor(me, jnp.where(top, first, second))
            spans.append(pl.ds(pl.multiple_of(owner * width, TILE), width))
        return spans

    return features


def early_panel_kernel(table, places, arrived, e_hbm_ref, *refs):
    pieces, (s_ref, p_ref, e_ref, sem) = refs[:-4], refs[-4:]
    load = pltpu.make_async_copy(e_hbm_ref, e_ref, sem)
    load.start()
    for place, piece in zip(places, pieces):
        place.copy_to(p_ref, piece)
    s_ref[table.dummy] = lowest()
    table_ref = arrived()
    load.wait()
    features = quarters([(0, 0), (2, 1)], p_ref, table.columns)
    score_pairs(table, table_ref, e_ref, p_ref, s_ref, features, False, None)


def panel_kernel(table, places, add, arrived, e_ref, *refs):
    pieces, (s_ref, p_ref, out_ref, acc_ref) = refs[:-4], refs[-4:]
    if add:
        pieces = pieces[:-2]
    row_tiles = table.row_tiles
    for place, piece in zip(places, pieces):
        place.copy_to(p_ref, piece)
    for t in range(row_tiles):
        acc_ref[t] = lowest()
    table_ref = arrived()

    def done(t, u, left, right):
        peak = acc_ref[t]
        for side, tile in enumerate((left, right)):
            off = jnp.where(table.allowed(table_ref, t, u + side) == 1, 0.0, NEGATIVE)
            peak = jnp.maximum(peak, tile + off)
        acc_ref[t] = peak

    if add:
        features = quarters([(1, 2), (3, 3)], p_ref, table.columns)
    else:
        s_ref[table.dummy] = lowest()
        features = lambda pair: [slice(None)]
    score_pairs(table, table_ref, e_ref, p_ref, s_ref, features, add, done)

    lane = lax.broadcasted_iota(jnp.int32, (TILE, TILE), 1)
    peaks = blank()
    for t in range(row_tiles):
        peak = jnp.max(acc_ref[t], axis=1, keepdims=True)
        peaks = jnp.where(lane == t, peak, peaks)
        acc_ref[t] = jnp.broadcast_to(peak, (TILE, TILE))
    for t in range(row_tiles):
        acc_ref[t] = table.loop(
            table_ref,
            t,
            4,
            lambda u, a, t=t: a + jnp.exp(s_ref[table.place(t, u)] - acc_ref[t]),
            blank(),
        )
    out_ref[...] = peaks.T[:row_tiles] + jnp.log(lying([acc_ref[t] for t in range(row_tiles)]))


def row_kernel(table, log_column, arrived, s_ref, w_ref, m_ref, r_ref, *refs):
    parts, (out_ref, c_ref, v_ref, acc_ref) = refs[:-4], refs[-4:]
    row_tiles, columns = table.row_tiles, table.columns
    column = log_column - combine([part[...] for part in parts])
    c_ref[:columns] = column
    v_ref[:columns] = jnp.exp(column + m_ref[...])
    rest = jnp.zeros((c_ref.shape[0] - columns, TILE), jnp.float32)
    c_ref[columns:] = rest
    v_ref[columns:] = rest
    table_ref = arrived()

    for t in range(row_tiles):

        def one_tile(u, a, t=t):
            return a + w_ref[table.place(t, u)].astype(jnp.float32) * v_ref[pl.ds(u, 1), :]

        acc_ref[t] = table.loop(table_ref, t, 4, one_tile, blank())
    totals = lying([acc_ref[t] for t in range(row_tiles)])
    out_ref[...] = jnp.log(totals) - r_ref[...]
    bits = bad_bits(totals > 1e-15) - table.empty_bits(table_ref, 0, row_tiles)

    @pl.when(bits != 0)
    def _():
        for t in range(row_tiles):

            @pl.when(has_bit(bits, t))
            def _():
                def score(u):
                    return s_ref[table.place(t, u)] + c_ref[pl.ds(u, 1), :]

                peak = table.loop(table_ref, t, 2, lambda u, a: jnp.maximum(a, score(u)), lowest())
                peak = jnp.max(peak, axis=1, keepdims=True)
                total = table.loop(table_ref, t, 2, lambda u, a: a + jnp.exp(score(u) - peak), blank())
                found = peak + jnp.log(jnp.sum(total, axis=1, keepdims=True))
                out_ref[t : t + 1, :] = jnp.broadcast_to(found, (TILE, TILE)).T[:1]


def slow_column(table, table_ref, u, s_ref, wide_ref, keep):
    line = table.column_base + u

    def score(t):
        at = table.place(t, u)
        return at, s_ref[at] + wide_ref[jnp.minimum(t, table.row_tiles - 1)]

    peak = table.loop(table_ref, line, 2, lambda t, a: jnp.maximum(a, score(t)[1]), lowest())
    peak = jnp.max(peak, axis=0, keepdims=True)

    def one_tile(t, a):
        at, value = score(t)
        value = jnp.exp(value - peak)
        keep(at, value)
        return a + value

    total = table.loop(table_ref, line, 2, one_tile, blank())
    return peak, jnp.sum(total, axis=0, keepdims=True)


def first_column_kernel(table, arrived, s_ref, *refs):
    parts, (out_ref, r_ref, w_ref, m_ref, wide_ref, acc_ref) = refs[:-6], refs[-6:]
    row = -combine([part[...] for part in parts])
    r_ref[...] = row
    spread_rows(row, wide_ref)
    w_ref[table.dummy] = blank().astype(jnp.bfloat16)
    table_ref = arrived()

    def keep(at, value):
        w_ref[at] = value.astype(jnp.bfloat16)

    for u in range(table.columns):

        def one_tile(t, a, u=u):
            at = table.place(t, u)
            value = jnp.exp(s_ref[at] + wide_ref[jnp.minimum(t, table.row_tiles - 1)])
            keep(at, value)
            return a + value

        acc_ref[u] = table.loop(table_ref, table.column_base + u, 4, one_tile, blank())
    totals = jnp.concatenate(
        [jnp.sum(acc_ref[u], axis=0, keepdims=True) for u in range(table.columns)], axis=0
    )
    m_ref[...] = jnp.zeros(m_ref.shape, jnp.float32)
    out_ref[...] = jnp.log(totals)
    bits = bad_bits(totals > 1e-15) - table.empty_bits(table_ref, table.column_base, table.columns)

    @pl.when(bits != 0)
    def _():
        for u in range(table.columns):

            @pl.when(has_bit(bits, u))
            def _():
                peak, total = slow_column(table, table_ref, u, s_ref, wide_ref, keep)
                m_ref[u : u + 1, :] = peak
                out_ref[u : u + 1, :] = peak + jnp.log(total)


def column_kernel(table, arrived, s_ref, w_ref, m_ref, first_ref, *refs):
    parts, (out_ref, r_ref, r_out_ref, wide_ref, acc_ref) = refs[:-5], refs[-5:]
    row = -combine([part[...] for part in parts])
    r_ref[...] = row
    r_out_ref[...] = row
    factor = jnp.exp(row - first_ref[...])
    spread_rows(factor, wide_ref)
    table_ref = arrived()

    for u in range(table.columns):

        def one_tile(t, a, u=u):
            kept = w_ref[table.place(t, u)].astype(jnp.float32)
            return a + kept * wide_ref[jnp.minimum(t, table.row_tiles - 1)]

        acc_ref[u] = table.loop(table_ref, table.column_base + u, 4, one_tile, blank())
    totals = jnp.concatenate(
        [jnp.sum(acc_ref[u], axis=0, keepdims=True) for u in range(table.columns)], axis=0
    )
    out_ref[...] = m_ref[...] + jnp.log(totals)
    largest = jnp.max(jnp.max(factor, axis=1, keepdims=True), axis=0, keepdims=True)
    bits = bad_bits((totals > 1e-15) & (totals < 1e30) & (largest < 1e15))
    bits = bits - table.empty_bits(table_ref, table.column_base, table.columns)

    @pl.when(bits != 0)
    def _():
        spread_rows(row, wide_ref)
        for u in range(table.columns):

            @pl.when(has_bit(bits, u))
            def _():
                peak, total = slow_column(table, table_ref, u, s_ref, wide_ref, lambda at, value: None)
                out_ref[u : u + 1, :] = peak + jnp.log(total)


def plan_blocks(table, table_ref, p_ref, lines, wanted, width, strip, outs, total_ref):
    row_tiles = table.row_tiles
    index = lax.axis_index("proto")
    core, z = lax.rem(index, 2), lax.div(index, 2)
    fits = width % TILE == 0
    total_ref[...] = jnp.zeros(total_ref.shape, jnp.float32)

    def visit(number, real, pair, tiles):
        first = pl.multiple_of(pair * 2 * TILE, TILE)
        blocks = []
        for j in wanted if fits else range(lines):
            if fits:
                start = (2 * jnp.bitwise_xor(z, j) + core) * width
                blocks.append(p_ref[pl.ds(first, 2 * TILE), pl.ds(pl.multiple_of(start, TILE), width)])
            else:
                both = p_ref[pl.ds(first, 2 * TILE), 2 * j * width : 2 * (j + 1) * width]
                blocks.append(jnp.where(core == 0, both[:, :width], both[:, width:]))
        product = jnp.dot(
            strip(number, real, pair, tiles),
            jnp.concatenate(blocks, axis=1),
            preferred_element_type=jnp.float32,
        )
        for i, t in enumerate(tiles):
            total_ref[jnp.minimum(t, row_tiles - 1)] += product[i * TILE : (i + 1) * TILE]

    table.each_item(table_ref, visit)
    for t in range(row_tiles):
        total = total_ref[t].astype(jnp.bfloat16)
        rows = slice(t * TILE, (t + 1) * TILE)
        for n, j in enumerate(wanted):
            if fits:
                outs[n][rows, :] = total[:, n * width : (n + 1) * width]
                continue
            for k in range(lines):

                @pl.when(jnp.bitwise_xor(z, j) == k)
                def _():
                    outs[n][rows, :] = total[:, k * width : (k + 1) * width]


def plan_kernel(table, log_column, lines, arrived, s_ref, r_ref, p_ref, *refs):
    parts, (out_ref, kept_ref, own_ref, c_ref, wide_ref, total_ref) = refs[:-6], refs[-6:]
    row_tiles, columns = table.row_tiles, table.columns
    core = lax.rem(lax.axis_index("proto"), 2)
    c_ref[...] = log_column - combine([part[...] for part in parts])
    half = columns // 2
    own_ref[...] = c_ref[pl.ds(pl.multiple_of(core * half, half), half), :]
    spread_rows(r_ref[...], wide_ref)
    table_ref = arrived()

    def strip(number, real, pair, tiles):
        strips = []
        for t in tiles:
            inside = jnp.minimum(t, row_tiles - 1)
            sides = []
            for side in range(2):
                u = 2 * pair + side
                good = real & (t < row_tiles) & (table.allowed(table_ref, inside, u) == 1)
                tile = s_ref[jnp.where(good, t * columns + u, table.dummy)]
                sides.append(jnp.exp(tile + wide_ref[inside] + c_ref[pl.ds(u, 1), :]).astype(jnp.bfloat16))
            strips.append(jnp.concatenate(sides, axis=1))
        strips = jnp.concatenate(strips, axis=0)
        kept_ref[number] = strips
        return strips

    width = out_ref.shape[1]
    plan_blocks(table, table_ref, p_ref, lines, [lines - 1], width, strip, [out_ref], total_ref)


def rest_kernel(table, lines, arrived, kept_ref, p_ref, *refs):
    outs, total_ref = refs[:-1], refs[-1]
    width = outs[0].shape[1]
    strip = lambda number, real, pair, tiles: kept_ref[number]
    plan_blocks(table, arrived(), p_ref, lines, list(range(lines - 1)), width, strip, outs, total_ref)


def params(mebibytes):
    return pltpu.CompilerParams(vmem_limit_bytes=mebibytes * 2**20)


def sibling(block):
    return swap(block, "proto", 1)


def tied(*arrays):
    return lax.optimization_barrier(arrays)


def make_panel(table, lists, embeddings, shard, rows, features):
    width = shard.shape[1]
    protos = 2 * shard.shape[0]
    panel = pltpu.VMEM((table.dummy + 1, TILE, TILE), jnp.float32)
    whole = pltpu.VMEM((protos, features), jnp.bfloat16)
    row_shape = jax.ShapeDtypeStruct((table.row_tiles, TILE), jnp.float32)
    peaks = pltpu.VMEM((table.row_tiles, TILE, TILE), jnp.float32)

    def late(places, add, e, pieces, before):
        at = 2 + len(pieces)
        return pl.pallas_call(
            with_table(panel_kernel, table, places, add),
            out_shape=(panel, whole, row_shape),
            in_specs=[ANY] + [VMEM] * (1 + len(pieces) + len(before)),
            out_specs=(VMEM, VMEM, VMEM),
            scratch_shapes=[peaks] + table_scratch(lists),
            input_output_aliases={at: 0, at + 1: 1} if add else {},
            compiler_params=params(8),
            name="panel",
        )(lists, e, *pieces, *before)

    if lax.axis_size("row") != 4 or width % TILE:
        every = lax.all_gather(shard, "row", axis=1, tiled=True)
        places = [Piece(True, 0, None), Piece(False, 0, None)]
        return late(places, False, embeddings, [every, sibling(every)], [])
    half = shard.shape[0] // 2
    top, bottom = shard[:half], shard[half:]
    near_bottom = swap(bottom, "row", 1)
    far_top = swap(top, "row", 2)
    near_bottom, far_top, top, bottom, lists = tied(near_bottom, far_top, top, bottom, lists)
    cross_top = swap(far_top, "row", 1)
    cross_bottom = swap(near_bottom, "row", 2)
    near_top = swap(top, "row", 1)
    far_bottom = swap(bottom, "row", 2)
    pieces = [shard, near_bottom, far_top]
    pieces += [sibling(piece) for piece in pieces]
    places = [Piece(own, *at) for own in (True, False) for at in ((0, 0), (half, 1), (0, 2))]
    visits = table.dummy * TILE * TILE
    similar, known, e = pl.pallas_call(
        with_table(early_panel_kernel, table, places),
        out_shape=(panel, whole, pltpu.VMEM(embeddings.shape, jnp.bfloat16)),
        in_specs=[ANY, ANY] + [VMEM] * len(pieces),
        out_specs=(VMEM, VMEM, VMEM),
        scratch_shapes=[pltpu.SemaphoreType.DMA] + table_scratch(lists),
        compiler_params=params(6),
        cost_estimate=pl.CostEstimate(
            flops=visits * features, bytes_accessed=8 * visits, transcendentals=0
        ),
        name="early_panel",
    )(lists, embeddings, *pieces)
    cross_top, cross_bottom, near_top, far_bottom, similar, known, e = tied(
        cross_top, cross_bottom, near_top, far_bottom, similar, known, e
    )
    pieces = [near_top, far_bottom, cross_top, cross_bottom]
    pieces += [sibling(piece) for piece in pieces]
    places = [Piece(own, *at) for own in (True, False) for at in ((0, 1), (half, 2), (0, 3), (half, 3))]
    return late(places, True, e, pieces, [similar, known])


def scatter_partials(blocks):
    blocks = list(blocks)
    distance = 1
    while distance < len(blocks):
        for j in range(len(blocks) - distance, 0, -2 * distance):
            got = swap(blocks[j].astype(jnp.bfloat16), "proto", 2 * distance).astype(jnp.float32)
            blocks[j ^ distance] = blocks[j ^ distance].astype(jnp.float32) + got
        distance *= 2
    return blocks[0].astype(jnp.bfloat16)


def shards(embeddings, prototypes, block_mask):
    n_row, n_proto = lax.axis_size("row"), lax.axis_size("proto")
    lines = n_proto // 2
    rows, features = embeddings.shape
    protos = 2 * prototypes.shape[0]
    width = features // n_proto
    row_tiles, columns = block_mask.shape[0], 2 * block_mask.shape[1]
    log_column = math.log(rows * n_row / (protos * lines))
    table = Table(row_tiles, columns)

    other_mask = swap(block_mask, "proto", 1)
    mask, other_mask = jnp.where(block_mask == 1, 1, 0), jnp.where(other_mask == 1, 1, 0)
    lists = table.build(
        jnp.where(
            lax.axis_index("proto") % 2 == 0,
            jnp.concatenate([mask, other_mask], axis=1),
            jnp.concatenate([other_mask, mask], axis=1),
        )
    )

    row_shape = jax.ShapeDtypeStruct((row_tiles, TILE), jnp.float32)
    column_shape = jax.ShapeDtypeStruct((columns, TILE), jnp.float32)
    half = columns // 2
    panel = (table.dummy + 1, TILE, TILE)
    wide = pltpu.VMEM((row_tiles, TILE, TILE), jnp.float32)
    tall = pltpu.VMEM((columns, TILE, TILE), jnp.float32)
    factors = pltpu.VMEM((columns + 8, TILE), jnp.float32)
    similar, whole, row_part = make_panel(table, lists, embeddings, prototypes, rows, features)

    def row_exchange(part):
        others = [swap(part, "proto", 2 * j) for j in range(lines - 1, 0, -1)]
        return [part] + others[::-1]

    def column_exchange(part):
        others = [swap(part, "row", j) for j in range(n_row - 1, 0, -1)]
        return [part] + others[::-1]

    parts = row_exchange(row_part)
    column_part, first_row, kept, peaks = pl.pallas_call(
        with_table(first_column_kernel, table),
        out_shape=(column_shape, row_shape, pltpu.VMEM(panel, jnp.bfloat16), column_shape),
        in_specs=[ANY] + [VMEM] * (1 + len(parts)),
        out_specs=(VMEM,) * 4,
        scratch_shapes=[wide, tall] + table_scratch(lists),
        compiler_params=params(4),
        name="first_column_pass",
    )(lists, similar, *parts)
    for sweep in range(1, ITERS):
        parts = column_exchange(column_part)
        row_part = pl.pallas_call(
            with_table(row_kernel, table, log_column),
            out_shape=row_shape,
            in_specs=[ANY] + [VMEM] * (4 + len(parts)),
            out_specs=VMEM,
            scratch_shapes=[factors, factors, wide] + table_scratch(lists),
            compiler_params=params(4),
            name="row_pass",
        )(lists, similar, kept, peaks, first_row, *parts)
        parts = row_exchange(row_part)
        column_part, row_potential, row_out = pl.pallas_call(
            with_table(column_kernel, table),
            out_shape=(column_shape, row_shape, row_shape),
            in_specs=[ANY] + [VMEM] * (4 + len(parts)),
            out_specs=(VMEM,) * 3,
            scratch_shapes=[wide, tall] + table_scratch(lists),
            compiler_params=params(4),
            name="column_pass",
        )(lists, similar, kept, peaks, first_row, *parts)
    parts = column_exchange(column_part)
    block = jax.ShapeDtypeStruct((rows, width), jnp.bfloat16)

    def sums(blocks):
        taken = blocks if width % TILE == 0 else lines
        return pltpu.VMEM((row_tiles, TILE, taken * width), jnp.float32)

    last, plan, column_potential = pl.pallas_call(
        with_table(plan_kernel, table, log_column, lines),
        out_shape=[
            block,
            pltpu.VMEM((table.items + 1, 4 * TILE, 2 * TILE), jnp.bfloat16),
            jax.ShapeDtypeStruct((half, TILE), jnp.float32),
        ],
        in_specs=[ANY] + [VMEM] * (3 + len(parts)),
        out_specs=[VMEM] * 3,
        scratch_shapes=[pltpu.VMEM((columns, TILE), jnp.float32), wide, sums(1)] + table_scratch(lists),
        compiler_params=params(12),
        name="plan",
    )(lists, similar, row_potential, whole, *parts)
    visits = table.dummy * TILE * TILE
    blocks = pl.pallas_call(
        with_table(rest_kernel, table, lines),
        out_shape=[block] * (lines - 1),
        in_specs=[ANY] + [VMEM] * 2,
        out_specs=[VMEM] * (lines - 1),
        scratch_shapes=[sums(lines - 1)] + table_scratch(lists),
        compiler_params=params(12),
        cost_estimate=pl.CostEstimate(
            flops=2 * visits * (lines - 1) * width, bytes_accessed=4 * visits, transcendentals=0
        ),
        name="rest_of_plan",
    )(lists, plan, whole)
    blocks = list(blocks) + [last]
    targets = scatter_partials(blocks)
    return (targets, row_out.reshape(rows), column_potential.reshape(protos // 2))


def solution(mesh):
    return jax.shard_map(
        shards,
        mesh=mesh,
        in_specs=(P("row", None), P("proto", "row"), P("row", "proto")),
        out_specs=(P("row", "proto"), P("row"), P("proto")),
        check_vma=False,
    )
```

```python
import functools
import math

import jax
import jax.numpy as jnp
from jax import lax
from jax.experimental import pallas as pl
from jax.experimental.pallas import tpu as pltpu
from jax.sharding import PartitionSpec as P

ITERS = 3
TILE = 128
NEGATIVE = -1e30

VMEM = pl.BlockSpec(memory_space=pltpu.VMEM)
ANY = pl.BlockSpec(memory_space=pl.ANY)


def swap(x, axis, offset):
    size = lax.axis_size(axis)
    return lax.ppermute(x, axis, [(i, i ^ offset) for i in range(size)])


def pair_sum(terms):
    while len(terms) > 1:
        terms = [terms[i] + terms[i + 1] for i in range(0, len(terms), 2)]
    return terms[0]


def butterfly(part, axis, unit, size):
    distance = 1
    while distance < size:
        other = swap(part, axis, unit * distance)
        if 2 * distance >= size:
            return [part, other]
        part = combine([part, other])
        distance *= 2
    return [part]


def combine(parts):
    peak = jnp.maximum(functools.reduce(jnp.maximum, parts), NEGATIVE)
    return peak + jnp.log(pair_sum([jnp.exp(part - peak) for part in parts]))


class Table:
    def __init__(self, row_tiles, columns):
        self.row_tiles, self.columns = row_tiles, columns
        self.line = max(row_tiles, columns) + 8
        self.column_base = row_tiles
        self.pair_base = row_tiles + columns
        self.mask_at = (self.pair_base + columns // 2) * self.line
        self.item_at = self.mask_at + row_tiles * columns
        self.items = (columns // 2) * -(-row_tiles // 4)
        self.total_at = self.item_at + 2 * (self.items + 1)
        self.dummy = row_tiles * columns

    def build(self, mask):
        across = mask.T
        pairs = jnp.max(across.reshape(self.columns // 2, 2, self.row_tiles), axis=1)
        lines = [self.lines(mask), self.lines(across), self.lines(pairs)]
        flat = [part.reshape(-1) for part in lines] + [mask.reshape(-1)]
        steps = (jnp.sum(pairs, axis=1) + 3) // 4
        at = jnp.arange(self.columns // 2, dtype=jnp.int32)
        first = jnp.sum(jnp.where(at[None, :] < at[:, None], steps[None, :], 0), axis=1)
        total = jnp.sum(steps)
        item = jnp.minimum(jnp.arange(self.items + 1, dtype=jnp.int32), total - 1)
        pair = jnp.sum(jnp.where(item[:, None] >= (first + steps)[None, :], 1, 0), axis=1)
        step = item - jnp.sum(jnp.where(pair[:, None] == at[None, :], first[None, :], 0), axis=1)
        flat += [(self.pair_base + pair) * self.line + 4 * step, pair]
        return jnp.concatenate(flat + [jnp.stack([total, (total + 1) // 2])])

    def each_item(self, ref, visit):
        def two(k, carry):
            for i in range(2):
                number = 2 * k + i
                at = ref[self.item_at + number]
                visit(
                    number,
                    number < ref[self.total_at],
                    ref[self.item_at + self.items + 1 + number],
                    [ref[at + n] for n in range(4)],
                )
            return carry

        lax.fori_loop(0, ref[self.total_at + 1], two, 0)

    def empty_bits(self, ref, base, count):
        bits = jnp.int32(0)
        for i in range(count):
            bits = bits + jnp.where(self.steps(ref, base + i, 4) == 0, 1 << i, 0)
        return bits

    def lines(self, mask):
        size = mask.shape[1]
        at = jnp.arange(size, dtype=jnp.int32)
        slot = jnp.arange(self.line, dtype=jnp.int32)
        before = jnp.sum(jnp.where(at[None, :] < at[:, None], mask[:, None, :], 0), axis=2)
        hit = (mask[:, None, :] == 1) & (before[:, None, :] == slot[None, :, None])
        places = jnp.sum(jnp.where(hit, at[None, None, :] - size, 0), axis=2) + size
        count = jnp.sum(mask, axis=1, keepdims=True)
        places = jnp.where(slot[None, :] == self.line - 2, (count + 1) // 2, places)
        return jnp.where(slot[None, :] == self.line - 1, (count + 3) // 4, places)

    def steps(self, ref, line, unroll):
        return ref[line * self.line + self.line - (2 if unroll == 2 else 1)]

    def entry(self, ref, line, k):
        return ref[line * self.line + k]

    def allowed(self, ref, t, u):
        return ref[self.mask_at + t * self.columns + u]

    def loop(self, ref, line, unroll, step, start):
        def several(k, a):
            for i in range(unroll):
                a = step(self.entry(ref, line, unroll * k + i), a)
            return a

        return lax.fori_loop(0, self.steps(ref, line, unroll), several, start)

    def place(self, t, u):
        padding = (t == self.row_tiles) | (u == self.columns)
        return jnp.where(padding, self.dummy, t * self.columns + u)


def with_table(kernel, table, *settings):
    def body(hbm_ref, *refs):
        *refs, smem_ref, sem = refs
        copy = pltpu.make_async_copy(hbm_ref, smem_ref, sem)
        copy.start()

        def arrived():
            copy.wait()
            return smem_ref

        kernel(table, *settings, arrived, *refs)

    return body


def table_scratch(lists):
    return [pltpu.SMEM(lists.shape, jnp.int32), pltpu.SemaphoreType.DMA]


def blank():
    return jnp.zeros((TILE, TILE), jnp.float32)


def lowest():
    return jnp.full((TILE, TILE), NEGATIVE, jnp.float32)


def bad_bits(good):
    bad = jnp.max(jnp.where(good, 0.0, 1.0), axis=1, keepdims=True)
    bit = jnp.left_shift(1, lax.broadcasted_iota(jnp.int32, bad.shape, 0))
    return jnp.sum(bad * bit.astype(jnp.float32)).astype(jnp.int32)


def has_bit(bits, i):
    return jnp.bitwise_and(bits, 1 << i) != 0


def spread_rows(row, wide_ref):
    row_tiles = row.shape[0]
    standing = jnp.concatenate(
        [row, jnp.zeros((TILE - row_tiles, TILE), jnp.float32)], axis=0
    ).T
    for t in range(row_tiles):
        wide_ref[t] = jnp.broadcast_to(standing[:, t : t + 1], (TILE, TILE))


def lying(tiles):
    lane = lax.broadcasted_iota(jnp.int32, (TILE, TILE), 1)
    found = blank()
    for t, tile in enumerate(tiles):
        found = jnp.where(lane == t, jnp.sum(tile, axis=1, keepdims=True), found)
    return found.T[: len(tiles)]


class Piece:
    def __init__(self, own, first, owner):
        self.own, self.first, self.owner = own, first, owner

    def copy_to(self, p_ref, piece):
        core, me = lax.rem(lax.axis_index("proto"), 2), lax.axis_index("row")
        rows, width = piece.shape
        first = (core if self.own else 1 - core) * (p_ref.shape[0] // 2) + self.first
        start = 0
        if self.owner is not None:
            start = pl.multiple_of(jnp.bitwise_xor(me, self.owner) * width, TILE)
        p_ref[pl.ds(pl.multiple_of(first, TILE), rows), pl.ds(start, width)] = piece[...]


def score_pairs(table, table_ref, e_ref, p_ref, s_ref, features, add, done):
    row_tiles, columns = table.row_tiles, table.columns
    scale = 4.0 / math.sqrt(e_ref.shape[1])

    def visit(number, real, pair, tiles):
        at = [jnp.minimum(t, row_tiles - 1) for t in tiles]
        product = None
        for span in features(pair):
            rows = jnp.concatenate(
                [e_ref[pl.ds(pl.multiple_of(t * TILE, TILE), TILE), span] for t in at], axis=0
            )
            block = p_ref[pl.ds(pl.multiple_of(pair * 2 * TILE, TILE), 2 * TILE), span]
            part = lax.dot_general(
                rows, block, (((1,), (1,)), ((), ())), preferred_element_type=jnp.float32
            )
            product = part if product is None else product + part
        product = (jnp.where(real, scale, 0.0) if add else scale) * product
        found = {}
        for i, t in enumerate(at):
            for side in range(2):
                where = t * columns + 2 * pair + side
                tile = product[i * TILE : (i + 1) * TILE, side * TILE : (side + 1) * TILE]
                found[i, side] = (where, s_ref[where] + tile if add else tile)
        for where, tile in found.values():
            s_ref[where] = tile
        if done is not None:
            for i, t in enumerate(at):
                done(t, 2 * pair, found[i, 0][1], found[i, 1][1])

    table.each_item(table_ref, visit)


def quarters(owners, p_ref, columns):
    me = lax.axis_index("row")
    width = p_ref.shape[1] // 4
    pairs = columns // 4

    def features(pair):
        top = lax.rem(pair, pairs) < pairs // 2
        spans = []
        for first, second in owners:
            owner = jnp.bitwise_xor(me, jnp.where(top, first, second))
            spans.append(pl.ds(pl.multiple_of(owner * width, TILE), width))
        return spans

    return features


def early_panel_kernel(table, places, arrived, e_hbm_ref, *refs):
    pieces, (s_ref, p_ref, e_ref, sem) = refs[:-4], refs[-4:]
    load = pltpu.make_async_copy(e_hbm_ref, e_ref, sem)
    load.start()
    for place, piece in zip(places, pieces):
        place.copy_to(p_ref, piece)
    s_ref[table.dummy] = lowest()
    table_ref = arrived()
    load.wait()
    features = quarters([(0, 0), (2, 1)], p_ref, table.columns)
    score_pairs(table, table_ref, e_ref, p_ref, s_ref, features, False, None)


def panel_kernel(table, places, add, arrived, e_ref, *refs):
    pieces, (s_ref, p_ref, out_ref, acc_ref) = refs[:-4], refs[-4:]
    if add:
        pieces = pieces[:-2]
    row_tiles = table.row_tiles
    for place, piece in zip(places, pieces):
        place.copy_to(p_ref, piece)
    for t in range(row_tiles):
        acc_ref[t] = lowest()
    table_ref = arrived()

    def done(t, u, left, right):
        peak = acc_ref[t]
        for side, tile in enumerate((left, right)):
            off = jnp.where(table.allowed(table_ref, t, u + side) == 1, 0.0, NEGATIVE)
            peak = jnp.maximum(peak, tile + off)
        acc_ref[t] = peak

    if add:
        features = quarters([(1, 2), (3, 3)], p_ref, table.columns)
    else:
        s_ref[table.dummy] = lowest()
        features = lambda pair: [slice(None)]
    score_pairs(table, table_ref, e_ref, p_ref, s_ref, features, add, done)

    lane = lax.broadcasted_iota(jnp.int32, (TILE, TILE), 1)
    peaks = blank()
    for t in range(row_tiles):
        peak = jnp.max(acc_ref[t], axis=1, keepdims=True)
        peaks = jnp.where(lane == t, peak, peaks)
        acc_ref[t] = jnp.broadcast_to(peak, (TILE, TILE))
    for t in range(row_tiles):
        acc_ref[t] = table.loop(
            table_ref,
            t,
            4,
            lambda u, a, t=t: a + jnp.exp(s_ref[table.place(t, u)] - acc_ref[t]),
            blank(),
        )
    out_ref[...] = peaks.T[:row_tiles] + jnp.log(lying([acc_ref[t] for t in range(row_tiles)]))


def row_kernel(table, log_column, arrived, s_ref, w_ref, m_ref, r_ref, *refs):
    parts, (out_ref, c_ref, v_ref, acc_ref) = refs[:-4], refs[-4:]
    row_tiles, columns = table.row_tiles, table.columns
    column = log_column - combine([part[...] for part in parts])
    c_ref[:columns] = column
    v_ref[:columns] = jnp.exp(column + m_ref[...])
    rest = jnp.zeros((c_ref.shape[0] - columns, TILE), jnp.float32)
    c_ref[columns:] = rest
    v_ref[columns:] = rest
    table_ref = arrived()

    for t in range(row_tiles):

        def one_tile(u, a, t=t):
            return a + w_ref[table.place(t, u)].astype(jnp.float32) * v_ref[pl.ds(u, 1), :]

        acc_ref[t] = table.loop(table_ref, t, 4, one_tile, blank())
    totals = lying([acc_ref[t] for t in range(row_tiles)])
    out_ref[...] = jnp.log(totals) - r_ref[...]
    bits = bad_bits(totals > 1e-15) - table.empty_bits(table_ref, 0, row_tiles)

    @pl.when(bits != 0)
    def _():
        for t in range(row_tiles):

            @pl.when(has_bit(bits, t))
            def _():
                def score(u):
                    return s_ref[table.place(t, u)] + c_ref[pl.ds(u, 1), :]

                peak = table.loop(table_ref, t, 2, lambda u, a: jnp.maximum(a, score(u)), lowest())
                peak = jnp.max(peak, axis=1, keepdims=True)
                total = table.loop(table_ref, t, 2, lambda u, a: a + jnp.exp(score(u) - peak), blank())
                found = peak + jnp.log(jnp.sum(total, axis=1, keepdims=True))
                out_ref[t : t + 1, :] = jnp.broadcast_to(found, (TILE, TILE)).T[:1]


def slow_column(table, table_ref, u, s_ref, wide_ref, keep):
    line = table.column_base + u

    def score(t):
        at = table.place(t, u)
        return at, s_ref[at] + wide_ref[jnp.minimum(t, table.row_tiles - 1)]

    peak = table.loop(table_ref, line, 2, lambda t, a: jnp.maximum(a, score(t)[1]), lowest())
    peak = jnp.max(peak, axis=0, keepdims=True)

    def one_tile(t, a):
        at, value = score(t)
        value = jnp.exp(value - peak)
        keep(at, value)
        return a + value

    total = table.loop(table_ref, line, 2, one_tile, blank())
    return peak, jnp.sum(total, axis=0, keepdims=True)


def first_column_kernel(table, arrived, s_ref, *refs):
    parts, (out_ref, r_ref, w_ref, m_ref, wide_ref, acc_ref) = refs[:-6], refs[-6:]
    row = -combine([part[...] for part in parts])
    r_ref[...] = row
    spread_rows(row, wide_ref)
    w_ref[table.dummy] = blank().astype(jnp.bfloat16)
    table_ref = arrived()

    def keep(at, value):
        w_ref[at] = value.astype(jnp.bfloat16)

    for u in range(table.columns):

        def one_tile(t, a, u=u):
            at = table.place(t, u)
            value = jnp.exp(s_ref[at] + wide_ref[jnp.minimum(t, table.row_tiles - 1)])
            keep(at, value)
            return a + value

        acc_ref[u] = table.loop(table_ref, table.column_base + u, 4, one_tile, blank())
    totals = jnp.concatenate(
        [jnp.sum(acc_ref[u], axis=0, keepdims=True) for u in range(table.columns)], axis=0
    )
    m_ref[...] = jnp.zeros(m_ref.shape, jnp.float32)
    out_ref[...] = jnp.log(totals)
    bits = bad_bits(totals > 1e-15) - table.empty_bits(table_ref, table.column_base, table.columns)

    @pl.when(bits != 0)
    def _():
        for u in range(table.columns):

            @pl.when(has_bit(bits, u))
            def _():
                peak, total = slow_column(table, table_ref, u, s_ref, wide_ref, keep)
                m_ref[u : u + 1, :] = peak
                out_ref[u : u + 1, :] = peak + jnp.log(total)


def column_kernel(table, arrived, s_ref, w_ref, m_ref, first_ref, *refs):
    parts, (out_ref, r_ref, r_out_ref, wide_ref, acc_ref) = refs[:-5], refs[-5:]
    row = -combine([part[...] for part in parts])
    r_ref[...] = row
    r_out_ref[...] = row
    factor = jnp.exp(row - first_ref[...])
    spread_rows(factor, wide_ref)
    table_ref = arrived()

    for u in range(table.columns):

        def one_tile(t, a, u=u):
            kept = w_ref[table.place(t, u)].astype(jnp.float32)
            return a + kept * wide_ref[jnp.minimum(t, table.row_tiles - 1)]

        acc_ref[u] = table.loop(table_ref, table.column_base + u, 4, one_tile, blank())
    totals = jnp.concatenate(
        [jnp.sum(acc_ref[u], axis=0, keepdims=True) for u in range(table.columns)], axis=0
    )
    out_ref[...] = m_ref[...] + jnp.log(totals)
    largest = jnp.max(jnp.max(factor, axis=1, keepdims=True), axis=0, keepdims=True)
    bits = bad_bits((totals > 1e-15) & (totals < 1e30) & (largest < 1e15))
    bits = bits - table.empty_bits(table_ref, table.column_base, table.columns)

    @pl.when(bits != 0)
    def _():
        spread_rows(row, wide_ref)
        for u in range(table.columns):

            @pl.when(has_bit(bits, u))
            def _():
                peak, total = slow_column(table, table_ref, u, s_ref, wide_ref, lambda at, value: None)
                out_ref[u : u + 1, :] = peak + jnp.log(total)


def plan_blocks(table, table_ref, p_ref, lines, wanted, width, strip, outs, total_ref):
    row_tiles = table.row_tiles
    index = lax.axis_index("proto")
    core, z = lax.rem(index, 2), lax.div(index, 2)
    fits = width % TILE == 0
    total_ref[...] = jnp.zeros(total_ref.shape, jnp.float32)

    def visit(number, real, pair, tiles):
        first = pl.multiple_of(pair * 2 * TILE, TILE)
        blocks = []
        for j in wanted if fits else range(lines):
            if fits:
                start = (2 * jnp.bitwise_xor(z, j) + core) * width
                blocks.append(p_ref[pl.ds(first, 2 * TILE), pl.ds(pl.multiple_of(start, TILE), width)])
            else:
                both = p_ref[pl.ds(first, 2 * TILE), 2 * j * width : 2 * (j + 1) * width]
                blocks.append(jnp.where(core == 0, both[:, :width], both[:, width:]))
        product = jnp.dot(
            strip(number, real, pair, tiles),
            jnp.concatenate(blocks, axis=1),
            preferred_element_type=jnp.float32,
        )
        for i, t in enumerate(tiles):
            total_ref[jnp.minimum(t, row_tiles - 1)] += product[i * TILE : (i + 1) * TILE]

    table.each_item(table_ref, visit)
    for t in range(row_tiles):
        total = total_ref[t].astype(jnp.bfloat16)
        rows = slice(t * TILE, (t + 1) * TILE)
        for n, j in enumerate(wanted):
            if fits:
                outs[n][rows, :] = total[:, n * width : (n + 1) * width]
                continue
            for k in range(lines):

                @pl.when(jnp.bitwise_xor(z, j) == k)
                def _():
                    outs[n][rows, :] = total[:, k * width : (k + 1) * width]


def plan_kernel(table, log_column, lines, arrived, s_ref, r_ref, p_ref, *refs):
    parts, (out_ref, kept_ref, own_ref, c_ref, wide_ref, total_ref) = refs[:-6], refs[-6:]
    row_tiles, columns = table.row_tiles, table.columns
    core = lax.rem(lax.axis_index("proto"), 2)
    c_ref[...] = log_column - combine([part[...] for part in parts])
    half = columns // 2
    own_ref[...] = c_ref[pl.ds(pl.multiple_of(core * half, half), half), :]
    spread_rows(r_ref[...], wide_ref)
    table_ref = arrived()

    def strip(number, real, pair, tiles):
        strips = []
        for t in tiles:
            inside = jnp.minimum(t, row_tiles - 1)
            sides = []
            for side in range(2):
                u = 2 * pair + side
                good = real & (t < row_tiles) & (table.allowed(table_ref, inside, u) == 1)
                tile = s_ref[jnp.where(good, t * columns + u, table.dummy)]
                sides.append(jnp.exp(tile + wide_ref[inside] + c_ref[pl.ds(u, 1), :]).astype(jnp.bfloat16))
            strips.append(jnp.concatenate(sides, axis=1))
        strips = jnp.concatenate(strips, axis=0)
        kept_ref[number] = strips
        return strips

    width = out_ref.shape[1]
    plan_blocks(table, table_ref, p_ref, lines, [lines - 1], width, strip, [out_ref], total_ref)


def rest_kernel(table, lines, arrived, kept_ref, p_ref, *refs):
    outs, total_ref = refs[:-1], refs[-1]
    width = outs[0].shape[1]
    strip = lambda number, real, pair, tiles: kept_ref[number]
    plan_blocks(table, arrived(), p_ref, lines, list(range(lines - 1)), width, strip, outs, total_ref)


def params(mebibytes):
    return pltpu.CompilerParams(vmem_limit_bytes=mebibytes * 2**20)


def sibling(block):
    return swap(block, "proto", 1)


def tied(*arrays):
    return lax.optimization_barrier(arrays)


def make_panel(table, mask, embeddings, shard, rows, features):
    width = shard.shape[1]
    protos = 2 * shard.shape[0]
    panel = pltpu.VMEM((table.dummy + 1, TILE, TILE), jnp.float32)
    whole = pltpu.VMEM((protos, features), jnp.bfloat16)
    row_shape = jax.ShapeDtypeStruct((table.row_tiles, TILE), jnp.float32)
    peaks = pltpu.VMEM((table.row_tiles, TILE, TILE), jnp.float32)

    def late(lists, places, add, e, pieces, before):
        at = 2 + len(pieces)
        return pl.pallas_call(
            with_table(panel_kernel, table, places, add),
            out_shape=(panel, whole, row_shape),
            in_specs=[ANY] + [VMEM] * (1 + len(pieces) + len(before)),
            out_specs=(VMEM, VMEM, VMEM),
            scratch_shapes=[peaks] + table_scratch(lists),
            input_output_aliases={at: 0, at + 1: 1} if add else {},
            compiler_params=params(8),
            name="panel",
        )(lists, e, *pieces, *before)

    if lax.axis_size("row") != 4 or width % TILE:
        lists = table.build(mask)
        every = lax.all_gather(shard, "row", axis=1, tiled=True)
        places = [Piece(True, 0, None), Piece(False, 0, None)]
        return (lists, *late(lists, places, False, embeddings, [every, sibling(every)], []))
    half = shard.shape[0] // 2
    top, bottom = shard[:half], shard[half:]
    near_bottom = swap(bottom, "row", 1)
    far_top = swap(top, "row", 2)
    top, bottom, mask = tied(top, bottom, mask)
    near_top = swap(top, "row", 1)
    far_bottom = swap(bottom, "row", 2)
    lists = table.build(mask)
    near_bottom, far_top, lists = tied(near_bottom, far_top, lists)
    cross_top = swap(far_top, "row", 1)
    cross_bottom = swap(near_bottom, "row", 2)
    pieces = [shard, near_bottom, far_top]
    pieces += [sibling(piece) for piece in pieces]
    places = [Piece(own, *at) for own in (True, False) for at in ((0, 0), (half, 1), (0, 2))]
    visits = table.dummy * TILE * TILE
    similar, known, e = pl.pallas_call(
        with_table(early_panel_kernel, table, places),
        out_shape=(panel, whole, pltpu.VMEM(embeddings.shape, jnp.bfloat16)),
        in_specs=[ANY, ANY] + [VMEM] * len(pieces),
        out_specs=(VMEM, VMEM, VMEM),
        scratch_shapes=[pltpu.SemaphoreType.DMA] + table_scratch(lists),
        compiler_params=params(6),
        cost_estimate=pl.CostEstimate(
            flops=visits * features, bytes_accessed=8 * visits, transcendentals=0
        ),
        name="early_panel",
    )(lists, embeddings, *pieces)
    cross_top, cross_bottom, near_top, far_bottom, similar, known, e = tied(
        cross_top, cross_bottom, near_top, far_bottom, similar, known, e
    )
    pieces = [near_top, far_bottom, cross_top, cross_bottom]
    pieces += [sibling(piece) for piece in pieces]
    places = [Piece(own, *at) for own in (True, False) for at in ((0, 1), (half, 2), (0, 3), (half, 3))]
    return (lists, *late(lists, places, True, e, pieces, [similar, known]))


def scatter_partials(blocks):
    blocks = list(blocks)
    distance = 1
    while distance < len(blocks):
        for j in range(len(blocks) - distance, 0, -2 * distance):
            got = swap(blocks[j].astype(jnp.bfloat16), "proto", 2 * distance).astype(jnp.float32)
            blocks[j ^ distance] = blocks[j ^ distance].astype(jnp.float32) + got
        distance *= 2
    return blocks[0].astype(jnp.bfloat16)


def shards(embeddings, prototypes, block_mask):
    n_row, n_proto = lax.axis_size("row"), lax.axis_size("proto")
    lines = n_proto // 2
    rows, features = embeddings.shape
    protos = 2 * prototypes.shape[0]
    width = features // n_proto
    row_tiles, columns = block_mask.shape[0], 2 * block_mask.shape[1]
    log_column = math.log(rows * n_row / (protos * lines))
    table = Table(row_tiles, columns)

    other_mask = swap(block_mask, "proto", 1)
    mask, other_mask = jnp.where(block_mask == 1, 1, 0), jnp.where(other_mask == 1, 1, 0)
    mask = jnp.where(
        lax.axis_index("proto") % 2 == 0,
        jnp.concatenate([mask, other_mask], axis=1),
        jnp.concatenate([other_mask, mask], axis=1),
    )

    row_shape = jax.ShapeDtypeStruct((row_tiles, TILE), jnp.float32)
    column_shape = jax.ShapeDtypeStruct((columns, TILE), jnp.float32)
    half = columns // 2
    panel = (table.dummy + 1, TILE, TILE)
    wide = pltpu.VMEM((row_tiles, TILE, TILE), jnp.float32)
    tall = pltpu.VMEM((columns, TILE, TILE), jnp.float32)
    factors = pltpu.VMEM((columns + 8, TILE), jnp.float32)
    lists, similar, whole, row_part = make_panel(table, mask, embeddings, prototypes, rows, features)

    def row_exchange(part):
        return butterfly(part, "proto", 2, lines)

    def column_exchange(part):
        return butterfly(part, "row", 1, n_row)

    parts = row_exchange(row_part)
    column_part, first_row, kept, peaks = pl.pallas_call(
        with_table(first_column_kernel, table),
        out_shape=(column_shape, row_shape, pltpu.VMEM(panel, jnp.bfloat16), column_shape),
        in_specs=[ANY] + [VMEM] * (1 + len(parts)),
        out_specs=(VMEM,) * 4,
        scratch_shapes=[wide, tall] + table_scratch(lists),
        compiler_params=params(4),
        name="first_column_pass",
    )(lists, similar, *parts)
    for sweep in range(1, ITERS):
        parts = column_exchange(column_part)
        row_part = pl.pallas_call(
            with_table(row_kernel, table, log_column),
            out_shape=row_shape,
            in_specs=[ANY] + [VMEM] * (4 + len(parts)),
            out_specs=VMEM,
            scratch_shapes=[factors, factors, wide] + table_scratch(lists),
            compiler_params=params(4),
            name="row_pass",
        )(lists, similar, kept, peaks, first_row, *parts)
        parts = row_exchange(row_part)
        column_part, row_potential, row_out = pl.pallas_call(
            with_table(column_kernel, table),
            out_shape=(column_shape, row_shape, row_shape),
            in_specs=[ANY] + [VMEM] * (4 + len(parts)),
            out_specs=(VMEM,) * 3,
            scratch_shapes=[wide, tall] + table_scratch(lists),
            compiler_params=params(4),
            name="column_pass",
        )(lists, similar, kept, peaks, first_row, *parts)
    parts = column_exchange(column_part)
    block = jax.ShapeDtypeStruct((rows, width), jnp.bfloat16)

    def sums(blocks):
        taken = blocks if width % TILE == 0 else lines
        return pltpu.VMEM((row_tiles, TILE, taken * width), jnp.float32)

    last, plan, column_potential = pl.pallas_call(
        with_table(plan_kernel, table, log_column, lines),
        out_shape=[
            block,
            pltpu.VMEM((table.items + 1, 4 * TILE, 2 * TILE), jnp.bfloat16),
            jax.ShapeDtypeStruct((half, TILE), jnp.float32),
        ],
        in_specs=[ANY] + [VMEM] * (3 + len(parts)),
        out_specs=[VMEM] * 3,
        scratch_shapes=[pltpu.VMEM((columns, TILE), jnp.float32), wide, sums(1)] + table_scratch(lists),
        compiler_params=params(12),
        name="plan",
    )(lists, similar, row_potential, whole, *parts)
    visits = table.dummy * TILE * TILE
    blocks = pl.pallas_call(
        with_table(rest_kernel, table, lines),
        out_shape=[block] * (lines - 1),
        in_specs=[ANY] + [VMEM] * 2,
        out_specs=[VMEM] * (lines - 1),
        scratch_shapes=[sums(lines - 1)] + table_scratch(lists),
        compiler_params=params(12),
        cost_estimate=pl.CostEstimate(
            flops=2 * visits * (lines - 1) * width, bytes_accessed=4 * visits, transcendentals=0
        ),
        name="rest_of_plan",
    )(lists, plan, whole)
    blocks = list(blocks) + [last]
    targets = scatter_partials(blocks)
    return (targets, row_out.reshape(rows), column_potential.reshape(protos // 2))


def solution(mesh):
    return jax.shard_map(
        shards,
        mesh=mesh,
        in_specs=(P("row", None), P("proto", "row"), P("row", "proto")),
        out_specs=(P("row", "proto"), P("row"), P("proto")),
        check_vma=False,
    )
```

```python
import functools
import math

import jax
import jax.numpy as jnp
from jax import lax
from jax.experimental import pallas as pl
from jax.experimental.pallas import tpu as pltpu
from jax.sharding import PartitionSpec as P

ITERS = 3
TILE = 128
NEGATIVE = -1e30

VMEM = pl.BlockSpec(memory_space=pltpu.VMEM)
ANY = pl.BlockSpec(memory_space=pl.ANY)


def swap(x, axis, offset):
    size = lax.axis_size(axis)
    return lax.ppermute(x, axis, [(i, i ^ offset) for i in range(size)])


def pair_sum(terms):
    while len(terms) > 1:
        terms = [terms[i] + terms[i + 1] for i in range(0, len(terms), 2)]
    return terms[0]


def combine(parts):
    peak = functools.reduce(jnp.maximum, parts)
    return peak + jnp.log(pair_sum([jnp.exp(part - peak) for part in parts]))


class Table:
    def __init__(self, row_tiles, columns):
        self.row_tiles, self.columns = row_tiles, columns
        self.line = max(row_tiles, columns) + 8
        self.column_base = row_tiles
        self.pair_base = row_tiles + columns
        self.mask_at = (self.pair_base + columns // 2) * self.line
        self.item_at = self.mask_at + row_tiles * columns
        self.items = (columns // 2) * -(-row_tiles // 4)
        self.total_at = self.item_at + 2 * (self.items + 1)
        self.dummy = row_tiles * columns

    def build(self, mask):
        across = mask.T
        pairs = jnp.max(across.reshape(self.columns // 2, 2, self.row_tiles), axis=1)
        lines = [self.lines(mask), self.lines(across), self.lines(pairs)]
        flat = [part.reshape(-1) for part in lines] + [mask.reshape(-1)]
        steps = (jnp.sum(pairs, axis=1) + 3) // 4
        at = jnp.arange(self.columns // 2, dtype=jnp.int32)
        first = jnp.sum(jnp.where(at[None, :] < at[:, None], steps[None, :], 0), axis=1)
        total = jnp.sum(steps)
        item = jnp.minimum(jnp.arange(self.items + 1, dtype=jnp.int32), total - 1)
        pair = jnp.sum(jnp.where(item[:, None] >= (first + steps)[None, :], 1, 0), axis=1)
        step = item - jnp.sum(jnp.where(pair[:, None] == at[None, :], first[None, :], 0), axis=1)
        flat += [(self.pair_base + pair) * self.line + 4 * step, pair]
        return jnp.concatenate(flat + [jnp.stack([total, (total + 1) // 2])])

    def each_item(self, ref, visit):
        def two(k, carry):
            for i in range(2):
                number = 2 * k + i
                at = ref[self.item_at + number]
                visit(
                    number,
                    number < ref[self.total_at],
                    ref[self.item_at + self.items + 1 + number],
                    [ref[at + n] for n in range(4)],
                )
            return carry

        lax.fori_loop(0, ref[self.total_at + 1], two, 0)

    def empty_bits(self, ref, base, count):
        bits = jnp.int32(0)
        for i in range(count):
            bits = bits + jnp.where(self.steps(ref, base + i, 4) == 0, 1 << i, 0)
        return bits

    def lines(self, mask):
        size = mask.shape[1]
        at = jnp.arange(size, dtype=jnp.int32)
        slot = jnp.arange(self.line, dtype=jnp.int32)
        before = jnp.sum(jnp.where(at[None, :] < at[:, None], mask[:, None, :], 0), axis=2)
        hit = (mask[:, None, :] == 1) & (before[:, None, :] == slot[None, :, None])
        places = jnp.sum(jnp.where(hit, at[None, None, :] - size, 0), axis=2) + size
        count = jnp.sum(mask, axis=1, keepdims=True)
        places = jnp.where(slot[None, :] == self.line - 2, (count + 1) // 2, places)
        return jnp.where(slot[None, :] == self.line - 1, (count + 3) // 4, places)

    def steps(self, ref, line, unroll):
        return ref[line * self.line + self.line - (2 if unroll == 2 else 1)]

    def entry(self, ref, line, k):
        return ref[line * self.line + k]

    def allowed(self, ref, t, u):
        return ref[self.mask_at + t * self.columns + u]

    def loop(self, ref, line, unroll, step, start):
        def several(k, a):
            for i in range(unroll):
                a = step(self.entry(ref, line, unroll * k + i), a)
            return a

        return lax.fori_loop(0, self.steps(ref, line, unroll), several, start)

    def sums(self, ref, base, acc_ref, visit):
        lists = range(acc_ref.shape[0])

        def four(i, k):
            tiles = [visit(i, self.entry(ref, base + i, 4 * k + n)) for n in range(4)]
            return (tiles[0] + tiles[1]) + (tiles[2] + tiles[3])

        for i in lists:
            acc_ref[i] = four(i, 0)
        for i in lists:

            @pl.when(self.steps(ref, base + i, 4) > 1)
            def _(i=i):
                acc_ref[i] = lax.fori_loop(
                    1, self.steps(ref, base + i, 4), lambda k, a: a + four(i, k), acc_ref[i]
                )

    def place(self, t, u):
        padding = (t == self.row_tiles) | (u == self.columns)
        return jnp.where(padding, self.dummy, t * self.columns + u)


def with_table(kernel, table, *settings):
    def body(hbm_ref, *refs):
        *refs, smem_ref, sem = refs
        copy = pltpu.make_async_copy(hbm_ref, smem_ref, sem)
        copy.start()

        def arrived():
            copy.wait()
            return smem_ref

        kernel(table, *settings, arrived, *refs)

    return body


def table_scratch(lists):
    return [pltpu.SMEM(lists.shape, jnp.int32), pltpu.SemaphoreType.DMA]


def blank():
    return jnp.zeros((TILE, TILE), jnp.float32)


def lowest():
    return jnp.full((TILE, TILE), NEGATIVE, jnp.float32)


def bad_bits(good):
    bad = jnp.max(jnp.where(good, 0.0, 1.0), axis=1, keepdims=True)
    bit = jnp.left_shift(1, lax.broadcasted_iota(jnp.int32, bad.shape, 0))
    return jnp.sum(bad * bit.astype(jnp.float32)).astype(jnp.int32)


def in_range(totals, factor):
    largest = jnp.max(jnp.max(factor, axis=1, keepdims=True), axis=0, keepdims=True)
    return (totals > 1e-15) & (totals < 1e30) & (largest < 1e15)


def has_bit(bits, i):
    return jnp.bitwise_and(bits, 1 << i) != 0


def spread_rows(row, wide_ref):
    row_tiles = row.shape[0]
    standing = jnp.concatenate(
        [row, jnp.zeros((TILE - row_tiles, TILE), jnp.float32)], axis=0
    ).T
    for t in range(row_tiles):
        wide_ref[t] = jnp.broadcast_to(standing[:, t : t + 1], (TILE, TILE))


def lying(tiles):
    lane = lax.broadcasted_iota(jnp.int32, (TILE, TILE), 1)
    found = blank()
    for t, tile in enumerate(tiles):
        found = jnp.where(lane == t, jnp.sum(tile, axis=1, keepdims=True), found)
    return found.T[: len(tiles)]


class Piece:
    def __init__(self, own, first, owner):
        self.own, self.first, self.owner = own, first, owner

    def copy_to(self, p_ref, piece):
        core, me = lax.rem(lax.axis_index("proto"), 2), lax.axis_index("row")
        rows, width = piece.shape
        first = (core if self.own else 1 - core) * (p_ref.shape[0] // 2) + self.first
        start = 0
        if self.owner is not None:
            start = pl.multiple_of(jnp.bitwise_xor(me, self.owner) * width, TILE)
        p_ref[pl.ds(pl.multiple_of(first, TILE), rows), pl.ds(start, width)] = piece[...]


def score_pairs(table, table_ref, e_ref, p_ref, s_ref, features, add, done):
    row_tiles, columns = table.row_tiles, table.columns
    scale = 4.0 / math.sqrt(e_ref.shape[1])

    def visit(number, real, pair, tiles):
        at = [jnp.minimum(t, row_tiles - 1) for t in tiles]
        product = None
        for span in features(pair):
            rows = jnp.concatenate(
                [e_ref[pl.ds(pl.multiple_of(t * TILE, TILE), TILE), span] for t in at], axis=0
            )
            block = p_ref[pl.ds(pl.multiple_of(pair * 2 * TILE, TILE), 2 * TILE), span]
            part = lax.dot_general(
                rows, block, (((1,), (1,)), ((), ())), preferred_element_type=jnp.float32
            )
            product = part if product is None else product + part
        product = (jnp.where(real, scale, 0.0) if add else scale) * product
        found = {}
        for i, t in enumerate(at):
            for side in range(2):
                where = t * columns + 2 * pair + side
                tile = product[i * TILE : (i + 1) * TILE, side * TILE : (side + 1) * TILE]
                found[i, side] = (where, s_ref[where] + tile if add else tile)
        for where, tile in found.values():
            s_ref[where] = tile
        if done is not None:
            for i, t in enumerate(at):
                done(t, 2 * pair, found[i, 0][1], found[i, 1][1])

    table.each_item(table_ref, visit)


def quarters(owners, p_ref, columns):
    me = lax.axis_index("row")
    width = p_ref.shape[1] // 4
    pairs = columns // 4

    def features(pair):
        top = lax.rem(pair, pairs) < pairs // 2
        spans = []
        for first, second in owners:
            owner = jnp.bitwise_xor(me, jnp.where(top, first, second))
            spans.append(pl.ds(pl.multiple_of(owner * width, TILE), width))
        return spans

    return features


def early_panel_kernel(table, places, arrived, e_ref, *refs):
    pieces, (s_ref, p_ref) = refs[:-2], refs[-2:]
    for place, piece in zip(places, pieces):
        place.copy_to(p_ref, piece)
    s_ref[table.dummy] = lowest()
    features = quarters([(0, 0), (2, 1)], p_ref, table.columns)
    score_pairs(table, arrived(), e_ref, p_ref, s_ref, features, False, None)


def panel_kernel(table, places, add, arrived, e_ref, *refs):
    pieces, (s_ref, p_ref, w_ref, first_ref, out_ref, acc_ref, wide_ref) = refs[:-7], refs[-7:]
    if add:
        pieces = pieces[:-2]
    row_tiles = table.row_tiles
    for place, piece in zip(places, pieces):
        place.copy_to(p_ref, piece)
    for t in range(row_tiles):
        acc_ref[t] = lowest()
    table_ref = arrived()

    def done(t, u, left, right):
        peak = acc_ref[t]
        for side, tile in enumerate((left, right)):
            off = jnp.where(table.allowed(table_ref, t, u + side) == 1, 0.0, NEGATIVE)
            peak = jnp.maximum(peak, tile + off)
        acc_ref[t] = peak

    if add:
        features = quarters([(1, 2), (3, 3)], p_ref, table.columns)
    else:
        s_ref[table.dummy] = lowest()
        features = lambda pair: [slice(None)]
    score_pairs(table, table_ref, e_ref, p_ref, s_ref, features, add, done)

    lane = lax.broadcasted_iota(jnp.int32, (TILE, TILE), 1)
    peaks = blank()
    for t in range(row_tiles):
        peak = jnp.max(acc_ref[t], axis=1, keepdims=True)
        peaks = jnp.where(lane == t, peak, peaks)
        wide_ref[t] = jnp.broadcast_to(peak, (TILE, TILE))
    w_ref[table.dummy] = blank().astype(jnp.bfloat16)

    def visit(t, u):
        at = table.place(t, u)
        value = jnp.exp(s_ref[at] - wide_ref[t])
        w_ref[at] = value.astype(jnp.bfloat16)
        return value

    table.sums(table_ref, 0, acc_ref, visit)
    peaks = peaks.T[:row_tiles]
    first_ref[...] = -peaks
    out_ref[...] = peaks + jnp.log(lying([acc_ref[t] for t in range(row_tiles)]))


def row_kernel(table, log_column, arrived, s_ref, w_ref, first_ref, *refs):
    parts, (out_ref, c_ref, v_ref, acc_ref) = refs[:-4], refs[-4:]
    row_tiles, columns = table.row_tiles, table.columns
    column = log_column - combine([part[...] for part in parts])
    factor = jnp.exp(column)
    c_ref[:columns] = column
    v_ref[:columns] = factor
    rest = jnp.zeros((c_ref.shape[0] - columns, TILE), jnp.float32)
    c_ref[columns:] = rest
    v_ref[columns:] = rest
    table_ref = arrived()

    def visit(t, u):
        return w_ref[table.place(t, u)].astype(jnp.float32) * v_ref[pl.ds(u, 1), :]

    table.sums(table_ref, 0, acc_ref, visit)
    totals = lying([acc_ref[t] for t in range(row_tiles)])
    out_ref[...] = jnp.log(totals) - first_ref[...]
    bits = bad_bits(in_range(totals, factor)) - table.empty_bits(table_ref, 0, row_tiles)

    @pl.when(bits != 0)
    def _():
        for t in range(row_tiles):

            @pl.when(has_bit(bits, t))
            def _():
                def score(u):
                    return s_ref[table.place(t, u)] + c_ref[pl.ds(u, 1), :]

                peak = table.loop(table_ref, t, 2, lambda u, a: jnp.maximum(a, score(u)), lowest())
                peak = jnp.max(peak, axis=1, keepdims=True)
                total = table.loop(table_ref, t, 2, lambda u, a: a + jnp.exp(score(u) - peak), blank())
                found = peak + jnp.log(jnp.sum(total, axis=1, keepdims=True))
                out_ref[t : t + 1, :] = jnp.broadcast_to(found, (TILE, TILE)).T[:1]


def column_kernel(table, arrived, s_ref, w_ref, first_ref, *refs):
    parts, (out_ref, r_ref, r_out_ref, wide_ref, acc_ref) = refs[:-5], refs[-5:]
    row = -combine([part[...] for part in parts])
    r_ref[...] = row
    r_out_ref[...] = row
    factor = jnp.exp(row - first_ref[...])
    spread_rows(factor, wide_ref)
    table_ref = arrived()

    def visit(u, t):
        kept = w_ref[table.place(t, u)].astype(jnp.float32)
        return kept * wide_ref[jnp.minimum(t, table.row_tiles - 1)]

    table.sums(table_ref, table.column_base, acc_ref, visit)
    totals = jnp.concatenate(
        [jnp.sum(acc_ref[u], axis=0, keepdims=True) for u in range(table.columns)], axis=0
    )
    out_ref[...] = jnp.log(totals)
    bits = bad_bits(in_range(totals, factor)) - table.empty_bits(table_ref, table.column_base, table.columns)

    @pl.when(bits != 0)
    def _():
        spread_rows(row, wide_ref)
        for u in range(table.columns):

            @pl.when(has_bit(bits, u))
            def _():
                line = table.column_base + u

                def score(t):
                    return s_ref[table.place(t, u)] + wide_ref[jnp.minimum(t, table.row_tiles - 1)]

                peak = table.loop(table_ref, line, 2, lambda t, a: jnp.maximum(a, score(t)), lowest())
                peak = jnp.max(peak, axis=0, keepdims=True)
                total = table.loop(table_ref, line, 2, lambda t, a: a + jnp.exp(score(t) - peak), blank())
                out_ref[u : u + 1, :] = peak + jnp.log(jnp.sum(total, axis=0, keepdims=True))


def plan_blocks(table, table_ref, p_ref, lines, wanted, width, strip, outs, total_ref):
    row_tiles = table.row_tiles
    index = lax.axis_index("proto")
    core, z = lax.rem(index, 2), lax.div(index, 2)
    fits = width % TILE == 0
    total_ref[...] = jnp.zeros(total_ref.shape, jnp.float32)

    def visit(number, real, pair, tiles):
        first = pl.multiple_of(pair * 2 * TILE, TILE)
        blocks = []
        for j in wanted if fits else range(lines):
            if fits:
                start = (2 * jnp.bitwise_xor(z, j) + core) * width
                blocks.append(p_ref[pl.ds(first, 2 * TILE), pl.ds(pl.multiple_of(start, TILE), width)])
            else:
                both = p_ref[pl.ds(first, 2 * TILE), 2 * j * width : 2 * (j + 1) * width]
                blocks.append(jnp.where(core == 0, both[:, :width], both[:, width:]))
        product = jnp.dot(
            strip(number, real, pair, tiles),
            jnp.concatenate(blocks, axis=1),
            preferred_element_type=jnp.float32,
        )
        for i, t in enumerate(tiles):
            total_ref[jnp.minimum(t, row_tiles - 1)] += product[i * TILE : (i + 1) * TILE]

    table.each_item(table_ref, visit)
    for t in range(row_tiles):
        total = total_ref[t].astype(jnp.bfloat16)
        rows = slice(t * TILE, (t + 1) * TILE)
        for n, j in enumerate(wanted):
            if fits:
                outs[n][rows, :] = total[:, n * width : (n + 1) * width]
                continue
            for k in range(lines):

                @pl.when(jnp.bitwise_xor(z, j) == k)
                def _():
                    outs[n][rows, :] = total[:, k * width : (k + 1) * width]


def plan_kernel(table, log_column, lines, arrived, s_ref, r_ref, p_ref, *refs):
    parts, (out_ref, kept_ref, own_ref, c_ref, wide_ref, total_ref) = refs[:-6], refs[-6:]
    row_tiles, columns = table.row_tiles, table.columns
    core = lax.rem(lax.axis_index("proto"), 2)
    c_ref[...] = log_column - combine([part[...] for part in parts])
    half = columns // 2
    own_ref[...] = c_ref[pl.ds(pl.multiple_of(core * half, half), half), :]
    spread_rows(r_ref[...], wide_ref)
    table_ref = arrived()

    def strip(number, real, pair, tiles):
        strips = []
        for t in tiles:
            inside = jnp.minimum(t, row_tiles - 1)
            sides = []
            for side in range(2):
                u = 2 * pair + side
                good = real & (t < row_tiles) & (table.allowed(table_ref, inside, u) == 1)
                tile = s_ref[jnp.where(good, t * columns + u, table.dummy)]
                sides.append(jnp.exp(tile + wide_ref[inside] + c_ref[pl.ds(u, 1), :]).astype(jnp.bfloat16))
            strips.append(jnp.concatenate(sides, axis=1))
        strips = jnp.concatenate(strips, axis=0)
        kept_ref[number] = strips
        return strips

    width = out_ref.shape[1]
    plan_blocks(table, table_ref, p_ref, lines, [lines - 1], width, strip, [out_ref], total_ref)


def rest_kernel(table, lines, arrived, kept_ref, p_ref, *refs):
    outs, total_ref = refs[:-1], refs[-1]
    width = outs[0].shape[1]
    strip = lambda number, real, pair, tiles: kept_ref[number]
    plan_blocks(table, arrived(), p_ref, lines, list(range(lines - 1)), width, strip, outs, total_ref)


def params(mebibytes):
    return pltpu.CompilerParams(vmem_limit_bytes=mebibytes * 2**20)


def sibling(block):
    return swap(block, "proto", 1)


def tied(*arrays):
    return lax.optimization_barrier(arrays)


def make_panel(table, lists, embeddings, shard, rows, features):
    width = shard.shape[1]
    protos = 2 * shard.shape[0]
    panel = pltpu.VMEM((table.dummy + 1, TILE, TILE), jnp.float32)
    whole = pltpu.VMEM((protos, features), jnp.bfloat16)
    row_shape = jax.ShapeDtypeStruct((table.row_tiles, TILE), jnp.float32)
    kept = pltpu.VMEM((table.dummy + 1, TILE, TILE), jnp.bfloat16)
    tiles = pltpu.VMEM((table.row_tiles, TILE, TILE), jnp.float32)

    def late(places, add, e, pieces, before):
        at = 2 + len(pieces)
        return pl.pallas_call(
            with_table(panel_kernel, table, places, add),
            out_shape=(panel, whole, kept, row_shape, row_shape),
            in_specs=[ANY] + [VMEM] * (1 + len(pieces) + len(before)),
            out_specs=(VMEM,) * 5,
            scratch_shapes=[tiles, tiles] + table_scratch(lists),
            input_output_aliases={at: 0, at + 1: 1} if add else {},
            compiler_params=params(8),
            name="panel",
        )(lists, e, *pieces, *before)

    if lax.axis_size("row") != 4 or width % TILE:
        every = lax.all_gather(shard, "row", axis=1, tiled=True)
        places = [Piece(True, 0, None), Piece(False, 0, None)]
        return late(places, False, embeddings, [every, sibling(every)], [])
    half = shard.shape[0] // 2
    top, bottom = shard[:half], shard[half:]
    near_bottom = swap(bottom, "row", 1)
    far_top = swap(top, "row", 2)
    near_bottom, far_top, top, bottom, lists = tied(near_bottom, far_top, top, bottom, lists)
    cross_top = swap(far_top, "row", 1)
    cross_bottom = swap(near_bottom, "row", 2)
    near_top = swap(top, "row", 1)
    far_bottom = swap(bottom, "row", 2)
    pieces = [top, bottom, near_bottom, far_top, sibling(shard), sibling(near_bottom), sibling(far_top)]
    places = [Piece(True, 0, 0), Piece(True, half, 0), Piece(True, half, 1), Piece(True, 0, 2)]
    places += [Piece(False, 0, 0), Piece(False, half, 1), Piece(False, 0, 2)]
    visits = table.dummy * TILE * TILE
    similar, known = pl.pallas_call(
        with_table(early_panel_kernel, table, places),
        out_shape=(panel, whole),
        in_specs=[ANY] + [VMEM] * (1 + len(pieces)),
        out_specs=(VMEM, VMEM),
        scratch_shapes=table_scratch(lists),
        compiler_params=params(6),
        cost_estimate=pl.CostEstimate(
            flops=visits * features, bytes_accessed=8 * visits, transcendentals=0
        ),
        name="early_panel",
    )(lists, embeddings, *pieces)
    cross_top, cross_bottom, near_top, far_bottom, similar, known = tied(
        cross_top, cross_bottom, near_top, far_bottom, similar, known
    )
    pieces = [near_top, far_bottom, cross_top, cross_bottom]
    pieces += [sibling(piece) for piece in pieces]
    places = [Piece(own, *at) for own in (True, False) for at in ((0, 1), (half, 2), (0, 3), (half, 3))]
    return late(places, True, embeddings, pieces, [similar, known])


def scatter_partials(blocks):
    blocks = list(blocks)
    distance = 1
    while distance < len(blocks):
        for j in range(len(blocks) - distance, 0, -2 * distance):
            got = swap(blocks[j].astype(jnp.bfloat16), "proto", 2 * distance).astype(jnp.float32)
            blocks[j ^ distance] = blocks[j ^ distance].astype(jnp.float32) + got
        distance *= 2
    return blocks[0].astype(jnp.bfloat16)


def shards(embeddings, prototypes, block_mask):
    n_row, n_proto = lax.axis_size("row"), lax.axis_size("proto")
    lines = n_proto // 2
    rows, features = embeddings.shape
    protos = 2 * prototypes.shape[0]
    width = features // n_proto
    row_tiles, columns = block_mask.shape[0], 2 * block_mask.shape[1]
    log_column = math.log(rows * n_row / (protos * lines))
    table = Table(row_tiles, columns)

    other_mask = swap(block_mask, "proto", 1)
    mask, other_mask = jnp.where(block_mask == 1, 1, 0), jnp.where(other_mask == 1, 1, 0)
    lists = table.build(
        jnp.where(
            lax.axis_index("proto") % 2 == 0,
            jnp.concatenate([mask, other_mask], axis=1),
            jnp.concatenate([other_mask, mask], axis=1),
        )
    )

    row_shape = jax.ShapeDtypeStruct((row_tiles, TILE), jnp.float32)
    column_shape = jax.ShapeDtypeStruct((columns, TILE), jnp.float32)
    half = columns // 2
    wide = pltpu.VMEM((row_tiles, TILE, TILE), jnp.float32)
    tall = pltpu.VMEM((columns, TILE, TILE), jnp.float32)
    factors = pltpu.VMEM((columns + 8, TILE), jnp.float32)
    similar, whole, kept, first, row_part = make_panel(table, lists, embeddings, prototypes, rows, features)

    def row_exchange(part):
        others = [swap(part, "proto", 2 * j) for j in range(lines - 1, 0, -1)]
        return [part] + others[::-1]

    def column_exchange(part):
        others = [swap(part, "row", j) for j in range(n_row - 1, 0, -1)]
        return [part] + others[::-1]

    for sweep in range(ITERS):
        if sweep:
            parts = column_exchange(column_part)
            row_part = pl.pallas_call(
                with_table(row_kernel, table, log_column),
                out_shape=row_shape,
                in_specs=[ANY] + [VMEM] * (3 + len(parts)),
                out_specs=VMEM,
                scratch_shapes=[factors, factors, wide] + table_scratch(lists),
                compiler_params=params(4),
                name="row_pass",
            )(lists, similar, kept, first, *parts)
        parts = row_exchange(row_part)
        column_part, row_potential, row_out = pl.pallas_call(
            with_table(column_kernel, table),
            out_shape=(column_shape, row_shape, row_shape),
            in_specs=[ANY] + [VMEM] * (3 + len(parts)),
            out_specs=(VMEM,) * 3,
            scratch_shapes=[wide, tall] + table_scratch(lists),
            compiler_params=params(4),
            name="column_pass",
        )(lists, similar, kept, first, *parts)
    parts = column_exchange(column_part)
    block = jax.ShapeDtypeStruct((rows, width), jnp.bfloat16)

    def sums(blocks):
        taken = blocks if width % TILE == 0 else lines
        return pltpu.VMEM((row_tiles, TILE, taken * width), jnp.float32)

    last, plan, column_potential = pl.pallas_call(
        with_table(plan_kernel, table, log_column, lines),
        out_shape=[
            block,
            pltpu.VMEM((table.items + 1, 4 * TILE, 2 * TILE), jnp.bfloat16),
            jax.ShapeDtypeStruct((half, TILE), jnp.float32),
        ],
        in_specs=[ANY] + [VMEM] * (3 + len(parts)),
        out_specs=[VMEM] * 3,
        scratch_shapes=[pltpu.VMEM((columns, TILE), jnp.float32), wide, sums(1)] + table_scratch(lists),
        compiler_params=params(12),
        name="plan",
    )(lists, similar, row_potential, whole, *parts)
    visits = table.dummy * TILE * TILE
    blocks = pl.pallas_call(
        with_table(rest_kernel, table, lines),
        out_shape=[block] * (lines - 1),
        in_specs=[ANY] + [VMEM] * 2,
        out_specs=[VMEM] * (lines - 1),
        scratch_shapes=[sums(lines - 1)] + table_scratch(lists),
        compiler_params=params(12),
        cost_estimate=pl.CostEstimate(
            flops=2 * visits * (lines - 1) * width, bytes_accessed=4 * visits, transcendentals=0
        ),
        name="rest_of_plan",
    )(lists, plan, whole)
    blocks = list(blocks) + [last]
    targets = scatter_partials(blocks)
    return (targets, row_out.reshape(rows), column_potential.reshape(protos // 2))


def solution(mesh):
    return jax.shard_map(
        shards,
        mesh=mesh,
        in_specs=(P("row", None), P("proto", "row"), P("row", "proto")),
        out_specs=(P("row", "proto"), P("row"), P("proto")),
        check_vma=False,
    )
```

```python
import functools
import math

import jax
import jax.numpy as jnp
from jax import lax
from jax.experimental import pallas as pl
from jax.experimental.pallas import tpu as pltpu
from jax.sharding import PartitionSpec as P

ITERS = 3
TILE = 128
NEGATIVE = -1e30

VMEM = pl.BlockSpec(memory_space=pltpu.VMEM)
ANY = pl.BlockSpec(memory_space=pl.ANY)


def swap(x, axis, offset):
    size = lax.axis_size(axis)
    return lax.ppermute(x, axis, [(i, i ^ offset) for i in range(size)])


def pair_sum(terms):
    while len(terms) > 1:
        terms = [terms[i] + terms[i + 1] for i in range(0, len(terms), 2)]
    return terms[0]


def combine(parts):
    peak = functools.reduce(jnp.maximum, parts)
    return peak + jnp.log(pair_sum([jnp.exp(part - peak) for part in parts]))


class Table:
    def __init__(self, row_tiles, columns):
        self.row_tiles, self.columns = row_tiles, columns
        self.line = max(row_tiles, columns) + 8
        self.column_base = row_tiles
        self.pair_base = row_tiles + columns
        self.mask_at = (self.pair_base + columns // 2) * self.line
        self.item_at = self.mask_at + row_tiles * columns
        self.items = (columns // 2) * -(-row_tiles // 4)
        self.total_at = self.item_at + 2 * (self.items + 1)
        self.dummy = row_tiles * columns

    def build(self, mask):
        across = mask.T
        pairs = jnp.max(across.reshape(self.columns // 2, 2, self.row_tiles), axis=1)
        lines = [self.lines(mask), self.lines(across), self.lines(pairs)]
        flat = [part.reshape(-1) for part in lines] + [mask.reshape(-1)]
        steps = (jnp.sum(pairs, axis=1) + 3) // 4
        at = jnp.arange(self.columns // 2, dtype=jnp.int32)
        first = jnp.sum(jnp.where(at[None, :] < at[:, None], steps[None, :], 0), axis=1)
        total = jnp.sum(steps)
        item = jnp.minimum(jnp.arange(self.items + 1, dtype=jnp.int32), total - 1)
        pair = jnp.sum(jnp.where(item[:, None] >= (first + steps)[None, :], 1, 0), axis=1)
        step = item - jnp.sum(jnp.where(pair[:, None] == at[None, :], first[None, :], 0), axis=1)
        flat += [(self.pair_base + pair) * self.line + 4 * step, pair]
        return jnp.concatenate(flat + [jnp.stack([total, (total + 1) // 2])])

    def each_item(self, ref, visit):
        def two(k, carry):
            for i in range(2):
                number = 2 * k + i
                at = ref[self.item_at + number]
                visit(
                    number,
                    number < ref[self.total_at],
                    ref[self.item_at + self.items + 1 + number],
                    [ref[at + n] for n in range(4)],
                )
            return carry

        lax.fori_loop(0, ref[self.total_at + 1], two, 0)

    def empty_bits(self, ref, base, count):
        bits = jnp.int32(0)
        for i in range(count):
            bits = bits + jnp.where(self.steps(ref, base + i, 4) == 0, 1 << i, 0)
        return bits

    def lines(self, mask):
        size = mask.shape[1]
        at = jnp.arange(size, dtype=jnp.int32)
        slot = jnp.arange(self.line, dtype=jnp.int32)
        before = jnp.sum(jnp.where(at[None, :] < at[:, None], mask[:, None, :], 0), axis=2)
        hit = (mask[:, None, :] == 1) & (before[:, None, :] == slot[None, :, None])
        places = jnp.sum(jnp.where(hit, at[None, None, :] - size, 0), axis=2) + size
        count = jnp.sum(mask, axis=1, keepdims=True)
        places = jnp.where(slot[None, :] == self.line - 2, (count + 1) // 2, places)
        return jnp.where(slot[None, :] == self.line - 1, (count + 3) // 4, places)

    def steps(self, ref, line, unroll):
        return ref[line * self.line + self.line - (2 if unroll == 2 else 1)]

    def entry(self, ref, line, k):
        return ref[line * self.line + k]

    def allowed(self, ref, t, u):
        return ref[self.mask_at + t * self.columns + u]

    def loop(self, ref, line, unroll, step, start):
        def several(k, a):
            for i in range(unroll):
                a = step(self.entry(ref, line, unroll * k + i), a)
            return a

        return lax.fori_loop(0, self.steps(ref, line, unroll), several, start)

    def sums(self, ref, base, acc_ref, visit):
        lists = range(acc_ref.shape[0])

        def four(i, k):
            tiles = [visit(i, self.entry(ref, base + i, 4 * k + n)) for n in range(4)]
            return (tiles[0] + tiles[1]) + (tiles[2] + tiles[3])

        for i in lists:
            acc_ref[i] = four(i, 0)
        for i in lists:

            @pl.when(self.steps(ref, base + i, 4) > 1)
            def _(i=i):
                acc_ref[i] = lax.fori_loop(
                    1, self.steps(ref, base + i, 4), lambda k, a: a + four(i, k), acc_ref[i]
                )

    def place(self, t, u):
        padding = (t == self.row_tiles) | (u == self.columns)
        return jnp.where(padding, self.dummy, t * self.columns + u)


def with_table(kernel, table, *settings):
    def body(hbm_ref, *refs):
        *refs, smem_ref, sem = refs
        copy = pltpu.make_async_copy(hbm_ref, smem_ref, sem)
        copy.start()

        def arrived():
            copy.wait()
            return smem_ref

        kernel(table, *settings, arrived, *refs)

    return body


def table_scratch(lists):
    return [pltpu.SMEM(lists.shape, jnp.int32), pltpu.SemaphoreType.DMA]


def blank():
    return jnp.zeros((TILE, TILE), jnp.float32)


def lowest():
    return jnp.full((TILE, TILE), NEGATIVE, jnp.float32)


def bad_bits(good):
    bad = jnp.max(jnp.where(good, 0.0, 1.0), axis=1, keepdims=True)
    bit = jnp.left_shift(1, lax.broadcasted_iota(jnp.int32, bad.shape, 0))
    return jnp.sum(bad * bit.astype(jnp.float32)).astype(jnp.int32)


def in_range(totals, factor):
    largest = jnp.max(jnp.max(factor, axis=1, keepdims=True), axis=0, keepdims=True)
    return (totals > 1e-15) & (totals < 1e30) & (largest < 1e15)


def has_bit(bits, i):
    return jnp.bitwise_and(bits, 1 << i) != 0


def spread_rows(row, wide_ref):
    row_tiles = row.shape[0]
    standing = jnp.concatenate(
        [row, jnp.zeros((TILE - row_tiles, TILE), jnp.float32)], axis=0
    ).T
    for t in range(row_tiles):
        wide_ref[t] = jnp.broadcast_to(standing[:, t : t + 1], (TILE, TILE))


def lying(tiles):
    lane = lax.broadcasted_iota(jnp.int32, (TILE, TILE), 1)
    found = blank()
    for t, tile in enumerate(tiles):
        found = jnp.where(lane == t, jnp.sum(tile, axis=1, keepdims=True), found)
    return found.T[: len(tiles)]


class Piece:
    def __init__(self, own, first, owner):
        self.own, self.first, self.owner = own, first, owner

    def copy_to(self, p_ref, piece):
        core, me = lax.rem(lax.axis_index("proto"), 2), lax.axis_index("row")
        rows, width = piece.shape
        first = (core if self.own else 1 - core) * (p_ref.shape[0] // 2) + self.first
        start = 0
        if self.owner is not None:
            start = pl.multiple_of(jnp.bitwise_xor(me, self.owner) * width, TILE)
        p_ref[pl.ds(pl.multiple_of(first, TILE), rows), pl.ds(start, width)] = piece[...]


def score_pairs(table, table_ref, e_ref, p_ref, s_ref, features, add, done):
    row_tiles, columns = table.row_tiles, table.columns
    scale = 4.0 / math.sqrt(e_ref.shape[1])

    def visit(number, real, pair, tiles):
        at = [jnp.minimum(t, row_tiles - 1) for t in tiles]
        product = None
        for span in features(pair):
            rows = jnp.concatenate(
                [e_ref[pl.ds(pl.multiple_of(t * TILE, TILE), TILE), span] for t in at], axis=0
            )
            block = p_ref[pl.ds(pl.multiple_of(pair * 2 * TILE, TILE), 2 * TILE), span]
            part = lax.dot_general(
                rows, block, (((1,), (1,)), ((), ())), preferred_element_type=jnp.float32
            )
            product = part if product is None else product + part
        product = (jnp.where(real, scale, 0.0) if add else scale) * product
        found = {}
        for i, t in enumerate(at):
            for side in range(2):
                where = t * columns + 2 * pair + side
                tile = product[i * TILE : (i + 1) * TILE, side * TILE : (side + 1) * TILE]
                found[i, side] = (where, s_ref[where] + tile if add else tile)
        for where, tile in found.values():
            s_ref[where] = tile
        if done is not None:
            for i, t in enumerate(at):
                done(t, 2 * pair, found[i, 0][1], found[i, 1][1])

    table.each_item(table_ref, visit)


def quarters(owners, p_ref):
    me = lax.axis_index("row")
    width = p_ref.shape[1] // 4

    def features(pair):
        return [pl.ds(pl.multiple_of(jnp.bitwise_xor(me, owner) * width, TILE), width) for owner in owners]

    return features


def early_panel_kernel(table, places, owners, add, arrived, e_ref, *refs):
    pieces, (s_ref, p_ref) = refs[:-2], refs[-2:]
    for place, piece in zip(places, pieces):
        place.copy_to(p_ref, piece)
    if not add:
        s_ref[table.dummy] = lowest()
    features = quarters(owners, p_ref)
    score_pairs(table, arrived(), e_ref, p_ref, s_ref, features, add, None)


def panel_kernel(table, places, add, arrived, e_ref, *refs):
    pieces, (s_ref, p_ref, w_ref, first_ref, out_ref, acc_ref, wide_ref) = refs[:-7], refs[-7:]
    if add:
        pieces = pieces[:-2]
    row_tiles = table.row_tiles
    for place, piece in zip(places, pieces):
        place.copy_to(p_ref, piece)
    for t in range(row_tiles):
        acc_ref[t] = lowest()
    table_ref = arrived()

    def done(t, u, left, right):
        peak = acc_ref[t]
        for side, tile in enumerate((left, right)):
            off = jnp.where(table.allowed(table_ref, t, u + side) == 1, 0.0, NEGATIVE)
            peak = jnp.maximum(peak, tile + off)
        acc_ref[t] = peak

    if add:
        features = quarters([3], p_ref)
    else:
        s_ref[table.dummy] = lowest()
        features = lambda pair: [slice(None)]
    score_pairs(table, table_ref, e_ref, p_ref, s_ref, features, add, done)

    lane = lax.broadcasted_iota(jnp.int32, (TILE, TILE), 1)
    peaks = blank()
    for t in range(row_tiles):
        peak = jnp.max(acc_ref[t], axis=1, keepdims=True)
        peaks = jnp.where(lane == t, peak, peaks)
        wide_ref[t] = jnp.broadcast_to(peak, (TILE, TILE))
    w_ref[table.dummy] = blank().astype(jnp.bfloat16)

    def visit(t, u):
        at = table.place(t, u)
        value = jnp.exp(s_ref[at] - wide_ref[t])
        w_ref[at] = value.astype(jnp.bfloat16)
        return value

    table.sums(table_ref, 0, acc_ref, visit)
    peaks = peaks.T[:row_tiles]
    first_ref[...] = -peaks
    out_ref[...] = peaks + jnp.log(lying([acc_ref[t] for t in range(row_tiles)]))


def row_kernel(table, log_column, arrived, s_ref, w_ref, first_ref, *refs):
    parts, (out_ref, c_ref, v_ref, acc_ref) = refs[:-4], refs[-4:]
    row_tiles, columns = table.row_tiles, table.columns
    column = log_column - combine([part[...] for part in parts])
    factor = jnp.exp(column)
    c_ref[:columns] = column
    v_ref[:columns] = factor
    rest = jnp.zeros((c_ref.shape[0] - columns, TILE), jnp.float32)
    c_ref[columns:] = rest
    v_ref[columns:] = rest
    table_ref = arrived()

    def visit(t, u):
        return w_ref[table.place(t, u)].astype(jnp.float32) * v_ref[pl.ds(u, 1), :]

    table.sums(table_ref, 0, acc_ref, visit)
    totals = lying([acc_ref[t] for t in range(row_tiles)])
    out_ref[...] = jnp.log(totals) - first_ref[...]
    bits = bad_bits(in_range(totals, factor)) - table.empty_bits(table_ref, 0, row_tiles)

    @pl.when(bits != 0)
    def _():
        for t in range(row_tiles):

            @pl.when(has_bit(bits, t))
            def _():
                def score(u):
                    return s_ref[table.place(t, u)] + c_ref[pl.ds(u, 1), :]

                peak = table.loop(table_ref, t, 2, lambda u, a: jnp.maximum(a, score(u)), lowest())
                peak = jnp.max(peak, axis=1, keepdims=True)
                total = table.loop(table_ref, t, 2, lambda u, a: a + jnp.exp(score(u) - peak), blank())
                found = peak + jnp.log(jnp.sum(total, axis=1, keepdims=True))
                out_ref[t : t + 1, :] = jnp.broadcast_to(found, (TILE, TILE)).T[:1]


def column_kernel(table, arrived, s_ref, w_ref, first_ref, *refs):
    parts, (out_ref, r_ref, r_out_ref, wide_ref, acc_ref) = refs[:-5], refs[-5:]
    row = -combine([part[...] for part in parts])
    r_ref[...] = row
    r_out_ref[...] = row
    factor = jnp.exp(row - first_ref[...])
    spread_rows(factor, wide_ref)
    table_ref = arrived()

    def visit(u, t):
        kept = w_ref[table.place(t, u)].astype(jnp.float32)
        return kept * wide_ref[jnp.minimum(t, table.row_tiles - 1)]

    table.sums(table_ref, table.column_base, acc_ref, visit)
    totals = jnp.concatenate(
        [jnp.sum(acc_ref[u], axis=0, keepdims=True) for u in range(table.columns)], axis=0
    )
    out_ref[...] = jnp.log(totals)
    bits = bad_bits(in_range(totals, factor)) - table.empty_bits(table_ref, table.column_base, table.columns)

    @pl.when(bits != 0)
    def _():
        spread_rows(row, wide_ref)
        for u in range(table.columns):

            @pl.when(has_bit(bits, u))
            def _():
                line = table.column_base + u

                def score(t):
                    return s_ref[table.place(t, u)] + wide_ref[jnp.minimum(t, table.row_tiles - 1)]

                peak = table.loop(table_ref, line, 2, lambda t, a: jnp.maximum(a, score(t)), lowest())
                peak = jnp.max(peak, axis=0, keepdims=True)
                total = table.loop(table_ref, line, 2, lambda t, a: a + jnp.exp(score(t) - peak), blank())
                out_ref[u : u + 1, :] = peak + jnp.log(jnp.sum(total, axis=0, keepdims=True))


def plan_blocks(table, table_ref, p_ref, lines, wanted, width, strip, outs, total_ref):
    row_tiles = table.row_tiles
    index = lax.axis_index("proto")
    core, z = lax.rem(index, 2), lax.div(index, 2)
    fits = width % TILE == 0
    total_ref[...] = jnp.zeros(total_ref.shape, jnp.float32)

    def visit(number, real, pair, tiles):
        first = pl.multiple_of(pair * 2 * TILE, TILE)
        blocks = []
        for j in wanted if fits else range(lines):
            if fits:
                start = (2 * jnp.bitwise_xor(z, j) + core) * width
                blocks.append(p_ref[pl.ds(first, 2 * TILE), pl.ds(pl.multiple_of(start, TILE), width)])
            else:
                both = p_ref[pl.ds(first, 2 * TILE), 2 * j * width : 2 * (j + 1) * width]
                blocks.append(jnp.where(core == 0, both[:, :width], both[:, width:]))
        product = jnp.dot(
            strip(number, real, pair, tiles),
            jnp.concatenate(blocks, axis=1),
            preferred_element_type=jnp.float32,
        )
        for i, t in enumerate(tiles):
            total_ref[jnp.minimum(t, row_tiles - 1)] += product[i * TILE : (i + 1) * TILE]

    table.each_item(table_ref, visit)
    for t in range(row_tiles):
        total = total_ref[t].astype(jnp.bfloat16)
        rows = slice(t * TILE, (t + 1) * TILE)
        for n, j in enumerate(wanted):
            if fits:
                outs[n][rows, :] = total[:, n * width : (n + 1) * width]
                continue
            for k in range(lines):

                @pl.when(jnp.bitwise_xor(z, j) == k)
                def _():
                    outs[n][rows, :] = total[:, k * width : (k + 1) * width]


def plan_kernel(table, log_column, lines, arrived, s_ref, r_ref, p_ref, *refs):
    parts, (out_ref, kept_ref, own_ref, c_ref, wide_ref, total_ref) = refs[:-6], refs[-6:]
    row_tiles, columns = table.row_tiles, table.columns
    core = lax.rem(lax.axis_index("proto"), 2)
    c_ref[...] = log_column - combine([part[...] for part in parts])
    half = columns // 2
    own_ref[...] = c_ref[pl.ds(pl.multiple_of(core * half, half), half), :]
    spread_rows(r_ref[...], wide_ref)
    table_ref = arrived()

    def strip(number, real, pair, tiles):
        strips = []
        for t in tiles:
            inside = jnp.minimum(t, row_tiles - 1)
            sides = []
            for side in range(2):
                u = 2 * pair + side
                good = real & (t < row_tiles) & (table.allowed(table_ref, inside, u) == 1)
                tile = s_ref[jnp.where(good, t * columns + u, table.dummy)]
                sides.append(jnp.exp(tile + wide_ref[inside] + c_ref[pl.ds(u, 1), :]).astype(jnp.bfloat16))
            strips.append(jnp.concatenate(sides, axis=1))
        strips = jnp.concatenate(strips, axis=0)
        kept_ref[number] = strips
        return strips

    width = out_ref.shape[1]
    plan_blocks(table, table_ref, p_ref, lines, [lines - 1], width, strip, [out_ref], total_ref)


def rest_kernel(table, lines, arrived, kept_ref, p_ref, *refs):
    outs, total_ref = refs[:-1], refs[-1]
    width = outs[0].shape[1]
    strip = lambda number, real, pair, tiles: kept_ref[number]
    plan_blocks(table, arrived(), p_ref, lines, list(range(lines - 1)), width, strip, outs, total_ref)


def params(mebibytes):
    return pltpu.CompilerParams(vmem_limit_bytes=mebibytes * 2**20)


def sibling(block):
    return swap(block, "proto", 1)


def tied(*arrays):
    return lax.optimization_barrier(arrays)


def make_panel(table, mask, embeddings, shard, rows, features):
    width = shard.shape[1]
    protos = 2 * shard.shape[0]
    panel = pltpu.VMEM((table.dummy + 1, TILE, TILE), jnp.float32)
    whole = pltpu.VMEM((protos, features), jnp.bfloat16)
    row_shape = jax.ShapeDtypeStruct((table.row_tiles, TILE), jnp.float32)
    kept = pltpu.VMEM((table.dummy + 1, TILE, TILE), jnp.bfloat16)
    tiles = pltpu.VMEM((table.row_tiles, TILE, TILE), jnp.float32)

    def late(lists, places, add, e, pieces, before):
        at = 2 + len(pieces)
        return pl.pallas_call(
            with_table(panel_kernel, table, places, add),
            out_shape=(panel, whole, kept, row_shape, row_shape),
            in_specs=[ANY] + [VMEM] * (1 + len(pieces) + len(before)),
            out_specs=(VMEM,) * 5,
            scratch_shapes=[tiles, tiles] + table_scratch(lists),
            input_output_aliases={at: 0, at + 1: 1} if add else {},
            compiler_params=params(8),
            name="panel",
        )(lists, e, *pieces, *before)

    if lax.axis_size("row") != 4 or width % TILE:
        lists = table.build(mask)
        every = lax.all_gather(shard, "row", axis=1, tiled=True)
        places = [Piece(True, 0, None), Piece(False, 0, None)]
        return (lists, *late(lists, places, False, embeddings, [every, sibling(every)], []))
    half = shard.shape[0] // 2
    visits = table.dummy * TILE * TILE

    def early(lists, places, owners, pieces, before):
        at = 2 + len(pieces)
        return pl.pallas_call(
            with_table(early_panel_kernel, table, places, owners, bool(before)),
            out_shape=(panel, whole),
            in_specs=[ANY] + [VMEM] * (1 + len(pieces) + len(before)),
            out_specs=(VMEM, VMEM),
            scratch_shapes=table_scratch(lists),
            input_output_aliases={at: 0, at + 1: 1} if before else {},
            compiler_params=params(6),
            cost_estimate=pl.CostEstimate(
                flops=visits * width * len(owners), bytes_accessed=8 * visits, transcendentals=0
            ),
            name="early_panel",
        )(lists, embeddings, *pieces, *before)

    near = swap(shard, "row", 1)
    far = swap(shard, "row", 2)
    lists = table.build(mask)
    places = [Piece(True, 0, 0), Piece(False, 0, 0)]
    similar, known = early(lists, places, [0], [shard, sibling(shard)], [])
    near, far, similar, known = tied(near, far, similar, known)
    cross_top = swap(far[:half], "row", 1)
    cross_bottom = swap(near[half:], "row", 2)
    places = [Piece(own, 0, owner) for own in (True, False) for owner in (1, 2)]
    pieces = [near, far, sibling(near), sibling(far)]
    similar, known = early(lists, places, [1, 2], pieces, [similar, known])
    cross_top, cross_bottom, similar, known = tied(cross_top, cross_bottom, similar, known)
    places = [Piece(own, first, 3) for own in (True, False) for first in (0, half)]
    pieces = [cross_top, cross_bottom, sibling(cross_top), sibling(cross_bottom)]
    return (lists, *late(lists, places, True, embeddings, pieces, [similar, known]))


def scatter_partials(blocks):
    blocks = list(blocks)
    distance = 1
    while distance < len(blocks):
        for j in range(len(blocks) - distance, 0, -2 * distance):
            got = swap(blocks[j].astype(jnp.bfloat16), "proto", 2 * distance).astype(jnp.float32)
            blocks[j ^ distance] = blocks[j ^ distance].astype(jnp.float32) + got
        distance *= 2
    return blocks[0].astype(jnp.bfloat16)


def shards(embeddings, prototypes, block_mask):
    n_row, n_proto = lax.axis_size("row"), lax.axis_size("proto")
    lines = n_proto // 2
    rows, features = embeddings.shape
    protos = 2 * prototypes.shape[0]
    width = features // n_proto
    row_tiles, columns = block_mask.shape[0], 2 * block_mask.shape[1]
    log_column = math.log(rows * n_row / (protos * lines))
    table = Table(row_tiles, columns)

    other_mask = swap(block_mask, "proto", 1)
    mask, other_mask = jnp.where(block_mask == 1, 1, 0), jnp.where(other_mask == 1, 1, 0)
    mask = jnp.where(
        lax.axis_index("proto") % 2 == 0,
        jnp.concatenate([mask, other_mask], axis=1),
        jnp.concatenate([other_mask, mask], axis=1),
    )

    row_shape = jax.ShapeDtypeStruct((row_tiles, TILE), jnp.float32)
    column_shape = jax.ShapeDtypeStruct((columns, TILE), jnp.float32)
    half = columns // 2
    wide = pltpu.VMEM((row_tiles, TILE, TILE), jnp.float32)
    tall = pltpu.VMEM((columns, TILE, TILE), jnp.float32)
    factors = pltpu.VMEM((columns + 8, TILE), jnp.float32)
    lists, similar, whole, kept, first, row_part = make_panel(table, mask, embeddings, prototypes, rows, features)

    def row_exchange(part):
        others = [swap(part, "proto", 2 * j) for j in range(lines - 1, 0, -1)]
        return [part] + others[::-1]

    def column_exchange(part):
        others = [swap(part, "row", j) for j in range(n_row - 1, 0, -1)]
        return [part] + others[::-1]

    for sweep in range(ITERS):
        if sweep:
            parts = column_exchange(column_part)
            row_part = pl.pallas_call(
                with_table(row_kernel, table, log_column),
                out_shape=row_shape,
                in_specs=[ANY] + [VMEM] * (3 + len(parts)),
                out_specs=VMEM,
                scratch_shapes=[factors, factors, wide] + table_scratch(lists),
                compiler_params=params(4),
                name="row_pass",
            )(lists, similar, kept, first, *parts)
        parts = row_exchange(row_part)
        column_part, row_potential, row_out = pl.pallas_call(
            with_table(column_kernel, table),
            out_shape=(column_shape, row_shape, row_shape),
            in_specs=[ANY] + [VMEM] * (3 + len(parts)),
            out_specs=(VMEM,) * 3,
            scratch_shapes=[wide, tall] + table_scratch(lists),
            compiler_params=params(4),
            name="column_pass",
        )(lists, similar, kept, first, *parts)
    parts = column_exchange(column_part)
    block = jax.ShapeDtypeStruct((rows, width), jnp.bfloat16)

    def sums(blocks):
        taken = blocks if width % TILE == 0 else lines
        return pltpu.VMEM((row_tiles, TILE, taken * width), jnp.float32)

    last, plan, column_potential = pl.pallas_call(
        with_table(plan_kernel, table, log_column, lines),
        out_shape=[
            block,
            pltpu.VMEM((table.items + 1, 4 * TILE, 2 * TILE), jnp.bfloat16),
            jax.ShapeDtypeStruct((half, TILE), jnp.float32),
        ],
        in_specs=[ANY] + [VMEM] * (3 + len(parts)),
        out_specs=[VMEM] * 3,
        scratch_shapes=[pltpu.VMEM((columns, TILE), jnp.float32), wide, sums(1)] + table_scratch(lists),
        compiler_params=params(12),
        name="plan",
    )(lists, similar, row_potential, whole, *parts)
    visits = table.dummy * TILE * TILE
    blocks = pl.pallas_call(
        with_table(rest_kernel, table, lines),
        out_shape=[block] * (lines - 1),
        in_specs=[ANY] + [VMEM] * 2,
        out_specs=[VMEM] * (lines - 1),
        scratch_shapes=[sums(lines - 1)] + table_scratch(lists),
        compiler_params=params(12),
        cost_estimate=pl.CostEstimate(
            flops=2 * visits * (lines - 1) * width, bytes_accessed=4 * visits, transcendentals=0
        ),
        name="rest_of_plan",
    )(lists, plan, whole)
    blocks = list(blocks) + [last]
    targets = scatter_partials(blocks)
    return (targets, row_out.reshape(rows), column_potential.reshape(protos // 2))


def solution(mesh):
    return jax.shard_map(
        shards,
        mesh=mesh,
        in_specs=(P("row", None), P("proto", "row"), P("row", "proto")),
        out_specs=(P("row", "proto"), P("row"), P("proto")),
        check_vma=False,
    )
```

```python
import functools
import math

import jax
import jax.numpy as jnp
from jax import lax
from jax.experimental import pallas as pl
from jax.experimental.pallas import tpu as pltpu
from jax.sharding import PartitionSpec as P

ITERS = 3
TILE = 128
NEGATIVE = -1e30

VMEM = pl.BlockSpec(memory_space=pltpu.VMEM)
ANY = pl.BlockSpec(memory_space=pl.ANY)


def swap(x, axis, offset):
    size = lax.axis_size(axis)
    return lax.ppermute(x, axis, [(i, i ^ offset) for i in range(size)])


def pair_sum(terms):
    while len(terms) > 1:
        terms = [terms[i] + terms[i + 1] for i in range(0, len(terms), 2)]
    return terms[0]


def combine(parts):
    peak = functools.reduce(jnp.maximum, parts)
    return peak + jnp.log(pair_sum([jnp.exp(part - peak) for part in parts]))


class Table:
    together = 4

    def __init__(self, row_tiles, columns):
        self.row_tiles, self.columns = row_tiles, columns
        self.line = max(row_tiles, columns) + 8
        self.column_base = row_tiles
        self.pair_base = row_tiles + columns
        self.mask_at = (self.pair_base + columns // 2) * self.line
        self.item_at = self.mask_at + row_tiles * columns
        self.items = (columns // 2) * -(-row_tiles // 4)
        self.slots = self.items + self.together - 1
        self.total_at = self.item_at + 2 * self.slots
        self.dummy = row_tiles * columns

    def build(self, mask):
        across = mask.T
        pairs = jnp.max(across.reshape(self.columns // 2, 2, self.row_tiles), axis=1)
        lines = [self.lines(mask), self.lines(across), self.lines(pairs)]
        flat = [part.reshape(-1) for part in lines] + [mask.reshape(-1)]
        steps = (jnp.sum(pairs, axis=1) + 3) // 4
        at = jnp.arange(self.columns // 2, dtype=jnp.int32)
        first = jnp.sum(jnp.where(at[None, :] < at[:, None], steps[None, :], 0), axis=1)
        total = jnp.sum(steps)
        item = jnp.minimum(jnp.arange(self.slots, dtype=jnp.int32), total - 1)
        pair = jnp.sum(jnp.where(item[:, None] >= (first + steps)[None, :], 1, 0), axis=1)
        step = item - jnp.sum(jnp.where(pair[:, None] == at[None, :], first[None, :], 0), axis=1)
        flat += [(self.pair_base + pair) * self.line + 4 * step, pair]
        rounds = (total + self.together - 1) // self.together
        return jnp.concatenate(flat + [jnp.stack([total, rounds])])

    def each_item(self, ref, visit):
        def several(k, carry):
            for i in range(self.together):
                number = self.together * k + i
                at = ref[self.item_at + number]
                visit(
                    number,
                    number < ref[self.total_at],
                    ref[self.item_at + self.slots + number],
                    [ref[at + n] for n in range(4)],
                )
            return carry

        lax.fori_loop(0, ref[self.total_at + 1], several, 0)

    def empty_bits(self, ref, base, count):
        bits = jnp.int32(0)
        for i in range(count):
            bits = bits + jnp.where(self.steps(ref, base + i, 4) == 0, 1 << i, 0)
        return bits

    def lines(self, mask):
        size = mask.shape[1]
        at = jnp.arange(size, dtype=jnp.int32)
        slot = jnp.arange(self.line, dtype=jnp.int32)
        before = jnp.sum(jnp.where(at[None, :] < at[:, None], mask[:, None, :], 0), axis=2)
        hit = (mask[:, None, :] == 1) & (before[:, None, :] == slot[None, :, None])
        places = jnp.sum(jnp.where(hit, at[None, None, :] - size, 0), axis=2) + size
        count = jnp.sum(mask, axis=1, keepdims=True)
        places = jnp.where(slot[None, :] == self.line - 2, (count + 1) // 2, places)
        return jnp.where(slot[None, :] == self.line - 1, (count + 3) // 4, places)

    def steps(self, ref, line, unroll):
        return ref[line * self.line + self.line - (2 if unroll == 2 else 1)]

    def entry(self, ref, line, k):
        return ref[line * self.line + k]

    def allowed(self, ref, t, u):
        return ref[self.mask_at + t * self.columns + u]

    def loop(self, ref, line, unroll, step, start):
        def several(k, a):
            for i in range(unroll):
                a = step(self.entry(ref, line, unroll * k + i), a)
            return a

        return lax.fori_loop(0, self.steps(ref, line, unroll), several, start)

    def sums(self, ref, base, acc_ref, visit):
        lists = range(acc_ref.shape[0])

        def four(i, k):
            tiles = [visit(i, self.entry(ref, base + i, 4 * k + n)) for n in range(4)]
            return (tiles[0] + tiles[1]) + (tiles[2] + tiles[3])

        for i in lists:
            acc_ref[i] = four(i, 0)
        for i in lists:

            @pl.when(self.steps(ref, base + i, 4) > 1)
            def _(i=i):
                acc_ref[i] = lax.fori_loop(
                    1, self.steps(ref, base + i, 4), lambda k, a: a + four(i, k), acc_ref[i]
                )

    def place(self, t, u):
        padding = (t == self.row_tiles) | (u == self.columns)
        return jnp.where(padding, self.dummy, t * self.columns + u)


def with_table(kernel, table, *settings):
    def body(hbm_ref, *refs):
        *refs, smem_ref, sem = refs
        copy = pltpu.make_async_copy(hbm_ref, smem_ref, sem)
        copy.start()

        def arrived():
            copy.wait()
            return smem_ref

        kernel(table, *settings, arrived, *refs)

    return body


def table_scratch(lists):
    return [pltpu.SMEM(lists.shape, jnp.int32), pltpu.SemaphoreType.DMA]


def blank():
    return jnp.zeros((TILE, TILE), jnp.float32)


def lowest():
    return jnp.full((TILE, TILE), NEGATIVE, jnp.float32)


def bad_bits(good):
    bad = jnp.max(jnp.where(good, 0.0, 1.0), axis=1, keepdims=True)
    bit = jnp.left_shift(1, lax.broadcasted_iota(jnp.int32, bad.shape, 0))
    return jnp.sum(bad * bit.astype(jnp.float32)).astype(jnp.int32)


def in_range(totals, factor):
    largest = jnp.max(jnp.max(factor, axis=1, keepdims=True), axis=0, keepdims=True)
    return (totals > 1e-15) & (totals < 1e30) & (largest < 1e15)


def has_bit(bits, i):
    return jnp.bitwise_and(bits, 1 << i) != 0


def spread_rows(row, wide_ref):
    row_tiles = row.shape[0]
    standing = jnp.concatenate(
        [row, jnp.zeros((TILE - row_tiles, TILE), jnp.float32)], axis=0
    ).T
    for t in range(row_tiles):
        wide_ref[t] = jnp.broadcast_to(standing[:, t : t + 1], (TILE, TILE))


def lying(tiles):
    lane = lax.broadcasted_iota(jnp.int32, (TILE, TILE), 1)
    found = blank()
    for t, tile in enumerate(tiles):
        found = jnp.where(lane == t, jnp.sum(tile, axis=1, keepdims=True), found)
    return found.T[: len(tiles)]


class Piece:
    def __init__(self, own, first, owner):
        self.own, self.first, self.owner = own, first, owner

    def copy_to(self, p_ref, piece):
        core, me = lax.rem(lax.axis_index("proto"), 2), lax.axis_index("row")
        rows, width = piece.shape
        first = (core if self.own else 1 - core) * (p_ref.shape[0] // 2) + self.first
        start = 0
        if self.owner is not None:
            start = pl.multiple_of(jnp.bitwise_xor(me, self.owner) * width, TILE)
        p_ref[pl.ds(pl.multiple_of(first, TILE), rows), pl.ds(start, width)] = piece[...]


def score_pairs(table, table_ref, e_ref, p_ref, s_ref, features, add, done):
    row_tiles, columns = table.row_tiles, table.columns
    scale = 4.0 / math.sqrt(e_ref.shape[1])

    def visit(number, real, pair, tiles):
        at = [jnp.minimum(t, row_tiles - 1) for t in tiles]
        product = None
        for span in features(pair):
            rows = jnp.concatenate(
                [e_ref[pl.ds(pl.multiple_of(t * TILE, TILE), TILE), span] for t in at], axis=0
            )
            block = p_ref[pl.ds(pl.multiple_of(pair * 2 * TILE, TILE), 2 * TILE), span]
            part = lax.dot_general(
                rows, block, (((1,), (1,)), ((), ())), preferred_element_type=jnp.float32
            )
            product = part if product is None else product + part
        product = (jnp.where(real, scale, 0.0) if add else scale) * product
        found = {}
        for i, t in enumerate(at):
            for side in range(2):
                where = t * columns + 2 * pair + side
                tile = product[i * TILE : (i + 1) * TILE, side * TILE : (side + 1) * TILE]
                found[i, side] = (where, s_ref[where] + tile if add else tile)
        for where, tile in found.values():
            s_ref[where] = tile
        if done is not None:
            for i, t in enumerate(at):
                done(t, 2 * pair, found[i, 0][1], found[i, 1][1])

    table.each_item(table_ref, visit)


def quarters(owners, p_ref):
    me = lax.axis_index("row")
    width = p_ref.shape[1] // 4

    def features(pair):
        return [pl.ds(pl.multiple_of(jnp.bitwise_xor(me, owner) * width, TILE), width) for owner in owners]

    return features


def early_panel_kernel(table, places, owners, add, arrived, e_ref, *refs):
    pieces, (s_ref, p_ref) = refs[:-2], refs[-2:]
    for place, piece in zip(places, pieces):
        place.copy_to(p_ref, piece)
    if not add:
        s_ref[table.dummy] = lowest()
    features = quarters(owners, p_ref)
    score_pairs(table, arrived(), e_ref, p_ref, s_ref, features, add, None)


def panel_kernel(table, places, add, arrived, e_ref, *refs):
    pieces, (s_ref, p_ref, w_ref, first_ref, out_ref, acc_ref, wide_ref) = refs[:-7], refs[-7:]
    if add:
        pieces = pieces[:-2]
    row_tiles = table.row_tiles
    for place, piece in zip(places, pieces):
        place.copy_to(p_ref, piece)
    for t in range(row_tiles):
        acc_ref[t] = lowest()
    table_ref = arrived()

    def done(t, u, left, right):
        peak = acc_ref[t]
        for side, tile in enumerate((left, right)):
            off = jnp.where(table.allowed(table_ref, t, u + side) == 1, 0.0, NEGATIVE)
            peak = jnp.maximum(peak, tile + off)
        acc_ref[t] = peak

    if add:
        features = quarters([3], p_ref)
    else:
        s_ref[table.dummy] = lowest()
        features = lambda pair: [slice(None)]
    score_pairs(table, table_ref, e_ref, p_ref, s_ref, features, add, done)

    lane = lax.broadcasted_iota(jnp.int32, (TILE, TILE), 1)
    peaks = blank()
    for t in range(row_tiles):
        peak = jnp.max(acc_ref[t], axis=1, keepdims=True)
        peaks = jnp.where(lane == t, peak, peaks)
        wide_ref[t] = jnp.broadcast_to(peak, (TILE, TILE))
    w_ref[table.dummy] = blank().astype(jnp.bfloat16)

    def visit(t, u):
        at = table.place(t, u)
        value = jnp.exp(s_ref[at] - wide_ref[t])
        w_ref[at] = value.astype(jnp.bfloat16)
        return value

    table.sums(table_ref, 0, acc_ref, visit)
    peaks = peaks.T[:row_tiles]
    first_ref[...] = -peaks
    out_ref[...] = peaks + jnp.log(lying([acc_ref[t] for t in range(row_tiles)]))


def row_kernel(table, log_column, arrived, s_ref, w_ref, first_ref, *refs):
    parts, (out_ref, c_ref, v_ref, acc_ref) = refs[:-4], refs[-4:]
    row_tiles, columns = table.row_tiles, table.columns
    column = log_column - combine([part[...] for part in parts])
    factor = jnp.exp(column)
    c_ref[:columns] = column
    v_ref[:columns] = factor
    rest = jnp.zeros((c_ref.shape[0] - columns, TILE), jnp.float32)
    c_ref[columns:] = rest
    v_ref[columns:] = rest
    table_ref = arrived()

    def visit(t, u):
        return w_ref[table.place(t, u)].astype(jnp.float32) * v_ref[pl.ds(u, 1), :]

    table.sums(table_ref, 0, acc_ref, visit)
    totals = lying([acc_ref[t] for t in range(row_tiles)])
    out_ref[...] = jnp.log(totals) - first_ref[...]
    bits = bad_bits(in_range(totals, factor)) - table.empty_bits(table_ref, 0, row_tiles)

    @pl.when(bits != 0)
    def _():
        for t in range(row_tiles):

            @pl.when(has_bit(bits, t))
            def _():
                def score(u):
                    return s_ref[table.place(t, u)] + c_ref[pl.ds(u, 1), :]

                peak = table.loop(table_ref, t, 2, lambda u, a: jnp.maximum(a, score(u)), lowest())
                peak = jnp.max(peak, axis=1, keepdims=True)
                total = table.loop(table_ref, t, 2, lambda u, a: a + jnp.exp(score(u) - peak), blank())
                found = peak + jnp.log(jnp.sum(total, axis=1, keepdims=True))
                out_ref[t : t + 1, :] = jnp.broadcast_to(found, (TILE, TILE)).T[:1]


def column_kernel(table, arrived, s_ref, w_ref, first_ref, *refs):
    parts, (out_ref, r_ref, r_out_ref, wide_ref, acc_ref) = refs[:-5], refs[-5:]
    row = -combine([part[...] for part in parts])
    r_ref[...] = row
    r_out_ref[...] = row
    factor = jnp.exp(row - first_ref[...])
    spread_rows(factor, wide_ref)
    table_ref = arrived()

    def visit(u, t):
        kept = w_ref[table.place(t, u)].astype(jnp.float32)
        return kept * wide_ref[jnp.minimum(t, table.row_tiles - 1)]

    table.sums(table_ref, table.column_base, acc_ref, visit)
    totals = jnp.concatenate(
        [jnp.sum(acc_ref[u], axis=0, keepdims=True) for u in range(table.columns)], axis=0
    )
    out_ref[...] = jnp.log(totals)
    bits = bad_bits(in_range(totals, factor)) - table.empty_bits(table_ref, table.column_base, table.columns)

    @pl.when(bits != 0)
    def _():
        spread_rows(row, wide_ref)
        for u in range(table.columns):

            @pl.when(has_bit(bits, u))
            def _():
                line = table.column_base + u

                def score(t):
                    return s_ref[table.place(t, u)] + wide_ref[jnp.minimum(t, table.row_tiles - 1)]

                peak = table.loop(table_ref, line, 2, lambda t, a: jnp.maximum(a, score(t)), lowest())
                peak = jnp.max(peak, axis=0, keepdims=True)
                total = table.loop(table_ref, line, 2, lambda t, a: a + jnp.exp(score(t) - peak), blank())
                out_ref[u : u + 1, :] = peak + jnp.log(jnp.sum(total, axis=0, keepdims=True))


def plan_blocks(table, table_ref, p_ref, lines, wanted, width, strip, outs, total_ref):
    row_tiles = table.row_tiles
    index = lax.axis_index("proto")
    core, z = lax.rem(index, 2), lax.div(index, 2)
    fits = width % TILE == 0
    total_ref[...] = jnp.zeros(total_ref.shape, jnp.float32)

    def visit(number, real, pair, tiles):
        first = pl.multiple_of(pair * 2 * TILE, TILE)
        blocks = []
        for j in wanted if fits else range(lines):
            if fits:
                start = (2 * jnp.bitwise_xor(z, j) + core) * width
                blocks.append(p_ref[pl.ds(first, 2 * TILE), pl.ds(pl.multiple_of(start, TILE), width)])
            else:
                both = p_ref[pl.ds(first, 2 * TILE), 2 * j * width : 2 * (j + 1) * width]
                blocks.append(jnp.where(core == 0, both[:, :width], both[:, width:]))
        product = jnp.dot(
            strip(number, real, pair, tiles),
            jnp.concatenate(blocks, axis=1),
            preferred_element_type=jnp.float32,
        )
        for i, t in enumerate(tiles):
            total_ref[jnp.minimum(t, row_tiles - 1)] += product[i * TILE : (i + 1) * TILE]

    table.each_item(table_ref, visit)
    for t in range(row_tiles):
        total = total_ref[t].astype(jnp.bfloat16)
        rows = slice(t * TILE, (t + 1) * TILE)
        for n, j in enumerate(wanted):
            if fits:
                outs[n][rows, :] = total[:, n * width : (n + 1) * width]
                continue
            for k in range(lines):

                @pl.when(jnp.bitwise_xor(z, j) == k)
                def _():
                    outs[n][rows, :] = total[:, k * width : (k + 1) * width]


def plan_kernel(table, log_column, lines, arrived, s_ref, r_ref, p_ref, *refs):
    parts, (out_ref, kept_ref, own_ref, c_ref, wide_ref, total_ref) = refs[:-6], refs[-6:]
    row_tiles, columns = table.row_tiles, table.columns
    core = lax.rem(lax.axis_index("proto"), 2)
    c_ref[...] = log_column - combine([part[...] for part in parts])
    half = columns // 2
    own_ref[...] = c_ref[pl.ds(pl.multiple_of(core * half, half), half), :]
    spread_rows(r_ref[...], wide_ref)
    table_ref = arrived()

    def strip(number, real, pair, tiles):
        strips = []
        for t in tiles:
            inside = jnp.minimum(t, row_tiles - 1)
            sides = []
            for side in range(2):
                u = 2 * pair + side
                good = real & (t < row_tiles) & (table.allowed(table_ref, inside, u) == 1)
                tile = s_ref[jnp.where(good, t * columns + u, table.dummy)]
                sides.append(jnp.exp(tile + wide_ref[inside] + c_ref[pl.ds(u, 1), :]).astype(jnp.bfloat16))
            strips.append(jnp.concatenate(sides, axis=1))
        strips = jnp.concatenate(strips, axis=0)
        kept_ref[number] = strips
        return strips

    width = out_ref.shape[1]
    plan_blocks(table, table_ref, p_ref, lines, [lines - 1], width, strip, [out_ref], total_ref)


def rest_kernel(table, lines, arrived, kept_ref, p_ref, *refs):
    outs, total_ref = refs[:-1], refs[-1]
    width = outs[0].shape[1]
    strip = lambda number, real, pair, tiles: kept_ref[number]
    plan_blocks(table, arrived(), p_ref, lines, list(range(lines - 1)), width, strip, outs, total_ref)


def params(mebibytes):
    return pltpu.CompilerParams(vmem_limit_bytes=mebibytes * 2**20)


def sibling(block):
    return swap(block, "proto", 1)


def tied(*arrays):
    return lax.optimization_barrier(arrays)


def make_panel(table, mask, embeddings, shard, rows, features):
    width = shard.shape[1]
    protos = 2 * shard.shape[0]
    panel = pltpu.VMEM((table.dummy + 1, TILE, TILE), jnp.float32)
    whole = pltpu.VMEM((protos, features), jnp.bfloat16)
    row_shape = jax.ShapeDtypeStruct((table.row_tiles, TILE), jnp.float32)
    kept = pltpu.VMEM((table.dummy + 1, TILE, TILE), jnp.bfloat16)
    tiles = pltpu.VMEM((table.row_tiles, TILE, TILE), jnp.float32)

    def late(lists, places, add, e, pieces, before):
        at = 2 + len(pieces)
        return pl.pallas_call(
            with_table(panel_kernel, table, places, add),
            out_shape=(panel, whole, kept, row_shape, row_shape),
            in_specs=[ANY] + [VMEM] * (1 + len(pieces) + len(before)),
            out_specs=(VMEM,) * 5,
            scratch_shapes=[tiles, tiles] + table_scratch(lists),
            input_output_aliases={at: 0, at + 1: 1} if add else {},
            compiler_params=params(8),
            name="panel",
        )(lists, e, *pieces, *before)

    if lax.axis_size("row") != 4 or width % TILE:
        lists = table.build(mask)
        every = lax.all_gather(shard, "row", axis=1, tiled=True)
        places = [Piece(True, 0, None), Piece(False, 0, None)]
        return (lists, *late(lists, places, False, embeddings, [every, sibling(every)], []))
    half = shard.shape[0] // 2
    visits = table.dummy * TILE * TILE

    def early(lists, places, owners, pieces, before):
        at = 2 + len(pieces)
        return pl.pallas_call(
            with_table(early_panel_kernel, table, places, owners, bool(before)),
            out_shape=(panel, whole),
            in_specs=[ANY] + [VMEM] * (1 + len(pieces) + len(before)),
            out_specs=(VMEM, VMEM),
            scratch_shapes=table_scratch(lists),
            input_output_aliases={at: 0, at + 1: 1} if before else {},
            compiler_params=params(6),
            cost_estimate=pl.CostEstimate(
                flops=visits * width * len(owners), bytes_accessed=8 * visits, transcendentals=0
            ),
            name="early_panel",
        )(lists, embeddings, *pieces, *before)

    near = swap(shard, "row", 1)
    far = swap(shard, "row", 2)
    lists = table.build(mask)
    places = [Piece(True, 0, 0), Piece(False, 0, 0)]
    similar, known = early(lists, places, [0], [shard, sibling(shard)], [])
    near, far, similar, known = tied(near, far, similar, known)
    cross_top = swap(far[:half], "row", 1)
    cross_bottom = swap(near[half:], "row", 2)
    places = [Piece(own, 0, owner) for own in (True, False) for owner in (1, 2)]
    pieces = [near, far, sibling(near), sibling(far)]
    similar, known = early(lists, places, [1, 2], pieces, [similar, known])
    cross_top, cross_bottom, similar, known = tied(cross_top, cross_bottom, similar, known)
    places = [Piece(own, first, 3) for own in (True, False) for first in (0, half)]
    pieces = [cross_top, cross_bottom, sibling(cross_top), sibling(cross_bottom)]
    return (lists, *late(lists, places, True, embeddings, pieces, [similar, known]))


def scatter_partials(blocks):
    blocks = list(blocks)
    distance = 1
    while distance < len(blocks):
        for j in range(len(blocks) - distance, 0, -2 * distance):
            got = swap(blocks[j].astype(jnp.bfloat16), "proto", 2 * distance).astype(jnp.float32)
            blocks[j ^ distance] = blocks[j ^ distance].astype(jnp.float32) + got
        distance *= 2
    return blocks[0].astype(jnp.bfloat16)


def shards(embeddings, prototypes, block_mask):
    n_row, n_proto = lax.axis_size("row"), lax.axis_size("proto")
    lines = n_proto // 2
    rows, features = embeddings.shape
    protos = 2 * prototypes.shape[0]
    width = features // n_proto
    row_tiles, columns = block_mask.shape[0], 2 * block_mask.shape[1]
    log_column = math.log(rows * n_row / (protos * lines))
    table = Table(row_tiles, columns)

    other_mask = swap(block_mask, "proto", 1)
    mask, other_mask = jnp.where(block_mask == 1, 1, 0), jnp.where(other_mask == 1, 1, 0)
    mask = jnp.where(
        lax.axis_index("proto") % 2 == 0,
        jnp.concatenate([mask, other_mask], axis=1),
        jnp.concatenate([other_mask, mask], axis=1),
    )

    row_shape = jax.ShapeDtypeStruct((row_tiles, TILE), jnp.float32)
    column_shape = jax.ShapeDtypeStruct((columns, TILE), jnp.float32)
    half = columns // 2
    wide = pltpu.VMEM((row_tiles, TILE, TILE), jnp.float32)
    tall = pltpu.VMEM((columns, TILE, TILE), jnp.float32)
    factors = pltpu.VMEM((columns + 8, TILE), jnp.float32)
    lists, similar, whole, kept, first, row_part = make_panel(table, mask, embeddings, prototypes, rows, features)

    def row_exchange(part):
        others = [swap(part, "proto", 2 * j) for j in range(lines - 1, 0, -1)]
        return [part] + others[::-1]

    def column_exchange(part):
        others = [swap(part, "row", j) for j in range(n_row - 1, 0, -1)]
        return [part] + others[::-1]

    for sweep in range(ITERS):
        if sweep:
            parts = column_exchange(column_part)
            row_part = pl.pallas_call(
                with_table(row_kernel, table, log_column),
                out_shape=row_shape,
                in_specs=[ANY] + [VMEM] * (3 + len(parts)),
                out_specs=VMEM,
                scratch_shapes=[factors, factors, wide] + table_scratch(lists),
                compiler_params=params(4),
                name="row_pass",
            )(lists, similar, kept, first, *parts)
        parts = row_exchange(row_part)
        column_part, row_potential, row_out = pl.pallas_call(
            with_table(column_kernel, table),
            out_shape=(column_shape, row_shape, row_shape),
            in_specs=[ANY] + [VMEM] * (3 + len(parts)),
            out_specs=(VMEM,) * 3,
            scratch_shapes=[wide, tall] + table_scratch(lists),
            compiler_params=params(4),
            name="column_pass",
        )(lists, similar, kept, first, *parts)
    parts = column_exchange(column_part)
    block = jax.ShapeDtypeStruct((rows, width), jnp.bfloat16)

    def sums(blocks):
        taken = blocks if width % TILE == 0 else lines
        return pltpu.VMEM((row_tiles, TILE, taken * width), jnp.float32)

    last, plan, column_potential = pl.pallas_call(
        with_table(plan_kernel, table, log_column, lines),
        out_shape=[
            block,
            pltpu.VMEM((table.slots, 4 * TILE, 2 * TILE), jnp.bfloat16),
            jax.ShapeDtypeStruct((half, TILE), jnp.float32),
        ],
        in_specs=[ANY] + [VMEM] * (3 + len(parts)),
        out_specs=[VMEM] * 3,
        scratch_shapes=[pltpu.VMEM((columns, TILE), jnp.float32), wide, sums(1)] + table_scratch(lists),
        compiler_params=params(12),
        name="plan",
    )(lists, similar, row_potential, whole, *parts)
    visits = table.dummy * TILE * TILE
    blocks = pl.pallas_call(
        with_table(rest_kernel, table, lines),
        out_shape=[block] * (lines - 1),
        in_specs=[ANY] + [VMEM] * 2,
        out_specs=[VMEM] * (lines - 1),
        scratch_shapes=[sums(lines - 1)] + table_scratch(lists),
        compiler_params=params(12),
        cost_estimate=pl.CostEstimate(
            flops=2 * visits * (lines - 1) * width, bytes_accessed=4 * visits, transcendentals=0
        ),
        name="rest_of_plan",
    )(lists, plan, whole)
    blocks = list(blocks) + [last]
    targets = scatter_partials(blocks)
    return (targets, row_out.reshape(rows), column_potential.reshape(protos // 2))


def solution(mesh):
    return jax.shard_map(
        shards,
        mesh=mesh,
        in_specs=(P("row", None), P("proto", "row"), P("row", "proto")),
        out_specs=(P("row", "proto"), P("row"), P("proto")),
        check_vma=False,
    )
```

```python
import functools
import math

import jax
import jax.numpy as jnp
from jax import lax
from jax.experimental import pallas as pl
from jax.experimental.pallas import tpu as pltpu
from jax.sharding import PartitionSpec as P

ITERS = 3
TILE = 128
NEGATIVE = -1e30

VMEM = pl.BlockSpec(memory_space=pltpu.VMEM)
ANY = pl.BlockSpec(memory_space=pl.ANY)


def swap(x, axis, offset):
    size = lax.axis_size(axis)
    return lax.ppermute(x, axis, [(i, i ^ offset) for i in range(size)])


def pair_sum(terms):
    while len(terms) > 1:
        terms = [terms[i] + terms[i + 1] for i in range(0, len(terms), 2)]
    return terms[0]


def combine(parts):
    peak = functools.reduce(jnp.maximum, parts)
    return peak + jnp.log(pair_sum([jnp.exp(part - peak) for part in parts]))


class Table:
    together = 4

    def __init__(self, row_tiles, columns):
        self.row_tiles, self.columns = row_tiles, columns
        self.line = max(row_tiles, columns) + 8
        self.column_base = row_tiles
        self.pair_base = row_tiles + columns
        self.mask_at = (self.pair_base + columns // 2) * self.line
        self.item_at = self.mask_at + row_tiles * columns
        self.items = (columns // 2) * -(-row_tiles // 4)
        self.slots = self.items + self.together - 1
        self.total_at = self.item_at + 2 * self.slots
        self.dummy = row_tiles * columns

    def build(self, mask):
        across = mask.T
        pairs = jnp.max(across.reshape(self.columns // 2, 2, self.row_tiles), axis=1)
        lines = [self.lines(mask), self.lines(across), self.lines(pairs)]
        flat = [part.reshape(-1) for part in lines] + [mask.reshape(-1)]
        steps = (jnp.sum(pairs, axis=1) + 3) // 4
        at = jnp.arange(self.columns // 2, dtype=jnp.int32)
        first = jnp.sum(jnp.where(at[None, :] < at[:, None], steps[None, :], 0), axis=1)
        total = jnp.sum(steps)
        item = jnp.minimum(jnp.arange(self.slots, dtype=jnp.int32), total - 1)
        pair = jnp.sum(jnp.where(item[:, None] >= (first + steps)[None, :], 1, 0), axis=1)
        step = item - jnp.sum(jnp.where(pair[:, None] == at[None, :], first[None, :], 0), axis=1)
        flat += [(self.pair_base + pair) * self.line + 4 * step, pair]
        rounds = (total + self.together - 1) // self.together
        return jnp.concatenate(flat + [jnp.stack([total, rounds])])

    def each_item(self, ref, visit):
        def several(k, carry):
            for i in range(self.together):
                number = self.together * k + i
                at = ref[self.item_at + number]
                visit(
                    number,
                    number < ref[self.total_at],
                    ref[self.item_at + self.slots + number],
                    [ref[at + n] for n in range(4)],
                )
            return carry

        lax.fori_loop(0, ref[self.total_at + 1], several, 0)

    def empty_bits(self, ref, base, count):
        bits = jnp.int32(0)
        for i in range(count):
            bits = bits + jnp.where(self.steps(ref, base + i, 4) == 0, 1 << i, 0)
        return bits

    def lines(self, mask):
        size = mask.shape[1]
        at = jnp.arange(size, dtype=jnp.int32)
        slot = jnp.arange(self.line, dtype=jnp.int32)
        before = jnp.sum(jnp.where(at[None, :] < at[:, None], mask[:, None, :], 0), axis=2)
        hit = (mask[:, None, :] == 1) & (before[:, None, :] == slot[None, :, None])
        places = jnp.sum(jnp.where(hit, at[None, None, :] - size, 0), axis=2) + size
        count = jnp.sum(mask, axis=1, keepdims=True)
        places = jnp.where(slot[None, :] == self.line - 2, (count + 1) // 2, places)
        return jnp.where(slot[None, :] == self.line - 1, (count + 3) // 4, places)

    def steps(self, ref, line, unroll):
        return ref[line * self.line + self.line - (2 if unroll == 2 else 1)]

    def entry(self, ref, line, k):
        return ref[line * self.line + k]

    def allowed(self, ref, t, u):
        return ref[self.mask_at + t * self.columns + u]

    def loop(self, ref, line, unroll, step, start):
        def several(k, a):
            for i in range(unroll):
                a = step(self.entry(ref, line, unroll * k + i), a)
            return a

        return lax.fori_loop(0, self.steps(ref, line, unroll), several, start)

    def sums(self, ref, base, acc_ref, visit):
        lists = range(acc_ref.shape[0])

        def four(i, k):
            tiles = [visit(i, self.entry(ref, base + i, 4 * k + n)) for n in range(4)]
            return (tiles[0] + tiles[1]) + (tiles[2] + tiles[3])

        for i in lists:
            acc_ref[i] = four(i, 0)
        for i in lists:

            @pl.when(self.steps(ref, base + i, 4) > 1)
            def _(i=i):
                acc_ref[i] = lax.fori_loop(
                    1, self.steps(ref, base + i, 4), lambda k, a: a + four(i, k), acc_ref[i]
                )

    def place(self, t, u):
        padding = (t == self.row_tiles) | (u == self.columns)
        return jnp.where(padding, self.dummy, t * self.columns + u)


def with_table(kernel, table, *settings):
    def body(hbm_ref, *refs):
        *refs, smem_ref, sem = refs
        copy = pltpu.make_async_copy(hbm_ref, smem_ref, sem)
        copy.start()

        def arrived():
            copy.wait()
            return smem_ref

        kernel(table, *settings, arrived, *refs)

    return body


def table_scratch(lists):
    return [pltpu.SMEM(lists.shape, jnp.int32), pltpu.SemaphoreType.DMA]


def blank():
    return jnp.zeros((TILE, TILE), jnp.float32)


def lowest():
    return jnp.full((TILE, TILE), NEGATIVE, jnp.float32)


def bad_bits(good):
    bad = jnp.max(jnp.where(good, 0.0, 1.0), axis=1, keepdims=True)
    bit = jnp.left_shift(1, lax.broadcasted_iota(jnp.int32, bad.shape, 0))
    return jnp.sum(bad * bit.astype(jnp.float32)).astype(jnp.int32)


def in_range(totals, factor):
    largest = jnp.max(jnp.max(factor, axis=1, keepdims=True), axis=0, keepdims=True)
    return (totals > 1e-15) & (totals < 1e30) & (largest < 1e15)


def has_bit(bits, i):
    return jnp.bitwise_and(bits, 1 << i) != 0


def spread_rows(row, wide_ref):
    row_tiles = row.shape[0]
    standing = jnp.concatenate(
        [row, jnp.zeros((TILE - row_tiles, TILE), jnp.float32)], axis=0
    ).T
    for t in range(row_tiles):
        wide_ref[t] = jnp.broadcast_to(standing[:, t : t + 1], (TILE, TILE))


def lying(tiles):
    lane = lax.broadcasted_iota(jnp.int32, (TILE, TILE), 1)
    found = blank()
    for t, tile in enumerate(tiles):
        found = jnp.where(lane == t, jnp.sum(tile, axis=1, keepdims=True), found)
    return found.T[: len(tiles)]


class Piece:
    def __init__(self, own, first, owner):
        self.own, self.first, self.owner = own, first, owner

    def copy_to(self, p_ref, piece):
        core, me = lax.rem(lax.axis_index("proto"), 2), lax.axis_index("row")
        rows, width = piece.shape
        first = (core if self.own else 1 - core) * (p_ref.shape[0] // 2) + self.first
        start = 0
        if self.owner is not None:
            start = pl.multiple_of(jnp.bitwise_xor(me, self.owner) * width, TILE)
        p_ref[pl.ds(pl.multiple_of(first, TILE), rows), pl.ds(start, width)] = piece[...]


def score_pairs(table, table_ref, e_ref, p_ref, s_ref, features, add, done):
    row_tiles, columns = table.row_tiles, table.columns
    scale = 4.0 / math.sqrt(e_ref.shape[1])

    def visit(number, real, pair, tiles):
        at = [jnp.minimum(t, row_tiles - 1) for t in tiles]
        product = None
        for span in features(pair):
            rows = jnp.concatenate(
                [e_ref[pl.ds(pl.multiple_of(t * TILE, TILE), TILE), span] for t in at], axis=0
            )
            block = p_ref[pl.ds(pl.multiple_of(pair * 2 * TILE, TILE), 2 * TILE), span]
            part = lax.dot_general(
                rows, block, (((1,), (1,)), ((), ())), preferred_element_type=jnp.float32
            )
            product = part if product is None else product + part
        product = (jnp.where(real, scale, 0.0) if add else scale) * product
        found = {}
        for i, t in enumerate(at):
            for side in range(2):
                where = t * columns + 2 * pair + side
                tile = product[i * TILE : (i + 1) * TILE, side * TILE : (side + 1) * TILE]
                found[i, side] = (where, s_ref[where] + tile if add else tile)
        for where, tile in found.values():
            s_ref[where] = tile
        if done is not None:
            for i, t in enumerate(at):
                done(t, 2 * pair, found[i, 0][1], found[i, 1][1])

    table.each_item(table_ref, visit)


def quarters(owners, p_ref):
    me = lax.axis_index("row")
    width = p_ref.shape[1] // 4

    def features(pair):
        return [pl.ds(pl.multiple_of(jnp.bitwise_xor(me, owner) * width, TILE), width) for owner in owners]

    return features


def early_panel_kernel(table, places, owners, add, arrived, e_ref, *refs):
    pieces, (s_ref, p_ref) = refs[:-2], refs[-2:]
    for place, piece in zip(places, pieces):
        place.copy_to(p_ref, piece)
    if not add:
        s_ref[table.dummy] = lowest()
    features = quarters(owners, p_ref)
    score_pairs(table, arrived(), e_ref, p_ref, s_ref, features, add, None)


def panel_kernel(table, places, add, arrived, e_ref, *refs):
    pieces, (s_ref, p_ref, w_ref, first_ref, out_ref, acc_ref, wide_ref) = refs[:-7], refs[-7:]
    if add:
        pieces = pieces[:-2]
    row_tiles = table.row_tiles
    for place, piece in zip(places, pieces):
        place.copy_to(p_ref, piece)
    for t in range(row_tiles):
        acc_ref[t] = lowest()
    table_ref = arrived()

    def done(t, u, left, right):
        peak = acc_ref[t]
        for side, tile in enumerate((left, right)):
            off = jnp.where(table.allowed(table_ref, t, u + side) == 1, 0.0, NEGATIVE)
            peak = jnp.maximum(peak, tile + off)
        acc_ref[t] = peak

    if add:
        features = quarters([3], p_ref)
    else:
        s_ref[table.dummy] = lowest()
        features = lambda pair: [slice(None)]
    score_pairs(table, table_ref, e_ref, p_ref, s_ref, features, add, done)

    lane = lax.broadcasted_iota(jnp.int32, (TILE, TILE), 1)
    peaks = blank()
    for t in range(row_tiles):
        peak = jnp.max(acc_ref[t], axis=1, keepdims=True)
        peaks = jnp.where(lane == t, peak, peaks)
        wide_ref[t] = jnp.broadcast_to(peak, (TILE, TILE))
    w_ref[table.dummy] = blank().astype(jnp.bfloat16)

    def visit(t, u):
        at = table.place(t, u)
        value = jnp.exp(s_ref[at] - wide_ref[t])
        w_ref[at] = value.astype(jnp.bfloat16)
        return value

    table.sums(table_ref, 0, acc_ref, visit)
    peaks = peaks.T[:row_tiles]
    first_ref[...] = -peaks
    out_ref[...] = peaks + jnp.log(lying([acc_ref[t] for t in range(row_tiles)]))


def row_kernel(table, log_column, arrived, s_ref, w_ref, first_ref, *refs):
    parts, (out_ref, c_ref, v_ref, acc_ref) = refs[:-4], refs[-4:]
    row_tiles, columns = table.row_tiles, table.columns
    column = log_column - combine([part[...] for part in parts])
    factor = jnp.exp(column)
    c_ref[:columns] = column
    v_ref[:columns] = factor
    rest = jnp.zeros((c_ref.shape[0] - columns, TILE), jnp.float32)
    c_ref[columns:] = rest
    v_ref[columns:] = rest
    table_ref = arrived()

    def visit(t, u):
        return w_ref[table.place(t, u)].astype(jnp.float32) * v_ref[pl.ds(u, 1), :]

    table.sums(table_ref, 0, acc_ref, visit)
    totals = lying([acc_ref[t] for t in range(row_tiles)])
    out_ref[...] = jnp.log(totals) - first_ref[...]
    bits = bad_bits(in_range(totals, factor)) - table.empty_bits(table_ref, 0, row_tiles)

    @pl.when(bits != 0)
    def _():
        for t in range(row_tiles):

            @pl.when(has_bit(bits, t))
            def _():
                def score(u):
                    return s_ref[table.place(t, u)] + c_ref[pl.ds(u, 1), :]

                peak = table.loop(table_ref, t, 2, lambda u, a: jnp.maximum(a, score(u)), lowest())
                peak = jnp.max(peak, axis=1, keepdims=True)
                total = table.loop(table_ref, t, 2, lambda u, a: a + jnp.exp(score(u) - peak), blank())
                found = peak + jnp.log(jnp.sum(total, axis=1, keepdims=True))
                out_ref[t : t + 1, :] = jnp.broadcast_to(found, (TILE, TILE)).T[:1]


def column_kernel(table, arrived, s_ref, w_ref, first_ref, *refs):
    parts, (out_ref, r_ref, r_out_ref, wide_ref, acc_ref) = refs[:-5], refs[-5:]
    row = -combine([part[...] for part in parts])
    r_ref[...] = row
    r_out_ref[...] = row
    factor = jnp.exp(row - first_ref[...])
    spread_rows(factor, wide_ref)
    table_ref = arrived()

    def visit(u, t):
        kept = w_ref[table.place(t, u)].astype(jnp.float32)
        return kept * wide_ref[jnp.minimum(t, table.row_tiles - 1)]

    table.sums(table_ref, table.column_base, acc_ref, visit)
    totals = jnp.concatenate(
        [jnp.sum(acc_ref[u], axis=0, keepdims=True) for u in range(table.columns)], axis=0
    )
    out_ref[...] = jnp.log(totals)
    bits = bad_bits(in_range(totals, factor)) - table.empty_bits(table_ref, table.column_base, table.columns)

    @pl.when(bits != 0)
    def _():
        spread_rows(row, wide_ref)
        for u in range(table.columns):

            @pl.when(has_bit(bits, u))
            def _():
                line = table.column_base + u

                def score(t):
                    return s_ref[table.place(t, u)] + wide_ref[jnp.minimum(t, table.row_tiles - 1)]

                peak = table.loop(table_ref, line, 2, lambda t, a: jnp.maximum(a, score(t)), lowest())
                peak = jnp.max(peak, axis=0, keepdims=True)
                total = table.loop(table_ref, line, 2, lambda t, a: a + jnp.exp(score(t) - peak), blank())
                out_ref[u : u + 1, :] = peak + jnp.log(jnp.sum(total, axis=0, keepdims=True))


def plan_blocks(table, table_ref, p_ref, lines, wanted, width, strip, outs, total_ref):
    row_tiles = table.row_tiles
    index = lax.axis_index("proto")
    core, z = lax.rem(index, 2), lax.div(index, 2)
    fits = width % TILE == 0
    total_ref[...] = jnp.zeros(total_ref.shape, jnp.float32)

    def visit(number, real, pair, tiles):
        first = pl.multiple_of(pair * 2 * TILE, TILE)
        blocks = []
        for j in wanted if fits else range(lines):
            if fits:
                start = (2 * jnp.bitwise_xor(z, j) + core) * width
                blocks.append(p_ref[pl.ds(first, 2 * TILE), pl.ds(pl.multiple_of(start, TILE), width)])
            else:
                both = p_ref[pl.ds(first, 2 * TILE), 2 * j * width : 2 * (j + 1) * width]
                blocks.append(jnp.where(core == 0, both[:, :width], both[:, width:]))
        product = jnp.dot(
            strip(number, real, pair, tiles),
            jnp.concatenate(blocks, axis=1),
            preferred_element_type=jnp.float32,
        )
        for i, t in enumerate(tiles):
            total_ref[jnp.minimum(t, row_tiles - 1)] += product[i * TILE : (i + 1) * TILE]

    table.each_item(table_ref, visit)
    for t in range(row_tiles):
        total = total_ref[t].astype(jnp.bfloat16)
        rows = slice(t * TILE, (t + 1) * TILE)
        for n, j in enumerate(wanted):
            if fits:
                outs[n][rows, :] = total[:, n * width : (n + 1) * width]
                continue
            for k in range(lines):

                @pl.when(jnp.bitwise_xor(z, j) == k)
                def _():
                    outs[n][rows, :] = total[:, k * width : (k + 1) * width]


def plan_kernel(table, log_column, lines, arrived, s_ref, r_ref, p_ref, *refs):
    parts, (out_ref, kept_ref, own_ref, c_ref, wide_ref, total_ref) = refs[:-6], refs[-6:]
    row_tiles, columns = table.row_tiles, table.columns
    core = lax.rem(lax.axis_index("proto"), 2)
    c_ref[...] = log_column - combine([part[...] for part in parts])
    half = columns // 2
    own_ref[...] = c_ref[pl.ds(pl.multiple_of(core * half, half), half), :]
    spread_rows(r_ref[...], wide_ref)
    table_ref = arrived()

    def strip(number, real, pair, tiles):
        strips = []
        for t in tiles:
            inside = jnp.minimum(t, row_tiles - 1)
            sides = []
            for side in range(2):
                u = 2 * pair + side
                good = real & (t < row_tiles) & (table.allowed(table_ref, inside, u) == 1)
                tile = s_ref[jnp.where(good, t * columns + u, table.dummy)]
                sides.append(jnp.exp(tile + wide_ref[inside] + c_ref[pl.ds(u, 1), :]).astype(jnp.bfloat16))
            strips.append(jnp.concatenate(sides, axis=1))
        strips = jnp.concatenate(strips, axis=0)
        kept_ref[number] = strips
        return strips

    width = out_ref.shape[1]
    plan_blocks(table, table_ref, p_ref, lines, [lines - 1], width, strip, [out_ref], total_ref)


def rest_kernel(table, lines, arrived, kept_ref, p_ref, *refs):
    outs, total_ref = refs[:-1], refs[-1]
    width = outs[0].shape[1]
    strip = lambda number, real, pair, tiles: kept_ref[number]
    plan_blocks(table, arrived(), p_ref, lines, list(range(lines - 1)), width, strip, outs, total_ref)


def params(mebibytes):
    return pltpu.CompilerParams(vmem_limit_bytes=mebibytes * 2**20)


def sibling(block):
    return swap(block, "proto", 1)


def tied(*arrays):
    return lax.optimization_barrier(arrays)


def make_panel(table, mask, embeddings, shard, rows, features):
    width = shard.shape[1]
    protos = 2 * shard.shape[0]
    panel = pltpu.VMEM((table.dummy + 1, TILE, TILE), jnp.float32)
    whole = pltpu.VMEM((protos, features), jnp.bfloat16)
    row_shape = jax.ShapeDtypeStruct((table.row_tiles, TILE), jnp.float32)
    kept = pltpu.VMEM((table.dummy + 1, TILE, TILE), jnp.bfloat16)
    tiles = pltpu.VMEM((table.row_tiles, TILE, TILE), jnp.float32)

    def late(lists, places, add, e, pieces, before):
        at = 2 + len(pieces)
        return pl.pallas_call(
            with_table(panel_kernel, table, places, add),
            out_shape=(panel, whole, kept, row_shape, row_shape),
            in_specs=[ANY] + [VMEM] * (1 + len(pieces) + len(before)),
            out_specs=(VMEM,) * 5,
            scratch_shapes=[tiles, tiles] + table_scratch(lists),
            input_output_aliases={at: 0, at + 1: 1} if add else {},
            compiler_params=params(8),
            name="panel",
        )(lists, e, *pieces, *before)

    if lax.axis_size("row") != 4 or width % TILE:
        lists = table.build(mask)
        every = lax.all_gather(shard, "row", axis=1, tiled=True)
        places = [Piece(True, 0, None), Piece(False, 0, None)]
        return (lists, *late(lists, places, False, embeddings, [every, sibling(every)], []))
    half = shard.shape[0] // 2
    visits = table.dummy * TILE * TILE

    def early(lists, places, owners, pieces, before):
        at = 2 + len(pieces)
        return pl.pallas_call(
            with_table(early_panel_kernel, table, places, owners, bool(before)),
            out_shape=(panel, whole),
            in_specs=[ANY] + [VMEM] * (1 + len(pieces) + len(before)),
            out_specs=(VMEM, VMEM),
            scratch_shapes=table_scratch(lists),
            input_output_aliases={at: 0, at + 1: 1} if before else {},
            compiler_params=params(6),
            cost_estimate=pl.CostEstimate(
                flops=visits * width * len(owners), bytes_accessed=8 * visits, transcendentals=0
            ),
            name="early_panel",
        )(lists, embeddings, *pieces, *before)

    near = swap(shard, "row", 1)
    far = swap(shard, "row", 2)
    lists = table.build(mask)
    places = [Piece(True, 0, 0), Piece(False, 0, 0)]
    similar, known = early(lists, places, [0], [shard, sibling(shard)], [])
    near, far, similar, known = tied(near, far, similar, known)
    cross_top = swap(far[:half], "row", 1)
    cross_bottom = swap(near[half:], "row", 2)
    places = [Piece(own, 0, owner) for own in (True, False) for owner in (1, 2)]
    pieces = [near, far, sibling(near), sibling(far)]
    similar, known = early(lists, places, [1, 2], pieces, [similar, known])
    cross_top, cross_bottom, similar, known = tied(cross_top, cross_bottom, similar, known)
    places = [Piece(own, first, 3) for own in (True, False) for first in (0, half)]
    pieces = [cross_top, cross_bottom, sibling(cross_top), sibling(cross_bottom)]
    return (lists, *late(lists, places, True, embeddings, pieces, [similar, known]))


def scatter_partials(blocks):
    blocks = list(blocks)
    distance = 1
    while distance < len(blocks):
        got = None
        for j in range(len(blocks) - distance, 0, -2 * distance):
            if j == distance and got is not None:
                blocks[j], got = tied(blocks[j], got)
            got = swap(blocks[j].astype(jnp.bfloat16), "proto", 2 * distance).astype(jnp.float32)
            blocks[j ^ distance] = blocks[j ^ distance].astype(jnp.float32) + got
        distance *= 2
    return blocks[0].astype(jnp.bfloat16)


def shards(embeddings, prototypes, block_mask):
    n_row, n_proto = lax.axis_size("row"), lax.axis_size("proto")
    lines = n_proto // 2
    rows, features = embeddings.shape
    protos = 2 * prototypes.shape[0]
    width = features // n_proto
    row_tiles, columns = block_mask.shape[0], 2 * block_mask.shape[1]
    log_column = math.log(rows * n_row / (protos * lines))
    table = Table(row_tiles, columns)

    other_mask = swap(block_mask, "proto", 1)
    mask, other_mask = jnp.where(block_mask == 1, 1, 0), jnp.where(other_mask == 1, 1, 0)
    mask = jnp.where(
        lax.axis_index("proto") % 2 == 0,
        jnp.concatenate([mask, other_mask], axis=1),
        jnp.concatenate([other_mask, mask], axis=1),
    )

    row_shape = jax.ShapeDtypeStruct((row_tiles, TILE), jnp.float32)
    column_shape = jax.ShapeDtypeStruct((columns, TILE), jnp.float32)
    half = columns // 2
    wide = pltpu.VMEM((row_tiles, TILE, TILE), jnp.float32)
    tall = pltpu.VMEM((columns, TILE, TILE), jnp.float32)
    factors = pltpu.VMEM((columns + 8, TILE), jnp.float32)
    lists, similar, whole, kept, first, row_part = make_panel(table, mask, embeddings, prototypes, rows, features)

    def row_exchange(part):
        others = [swap(part, "proto", 2 * j) for j in range(lines - 1, 0, -1)]
        return [part] + others[::-1]

    def column_exchange(part):
        others = [swap(part, "row", j) for j in range(n_row - 1, 0, -1)]
        return [part] + others[::-1]

    for sweep in range(ITERS):
        if sweep:
            parts = column_exchange(column_part)
            row_part = pl.pallas_call(
                with_table(row_kernel, table, log_column),
                out_shape=row_shape,
                in_specs=[ANY] + [VMEM] * (3 + len(parts)),
                out_specs=VMEM,
                scratch_shapes=[factors, factors, wide] + table_scratch(lists),
                compiler_params=params(4),
                name="row_pass",
            )(lists, similar, kept, first, *parts)
        parts = row_exchange(row_part)
        column_part, row_potential, row_out = pl.pallas_call(
            with_table(column_kernel, table),
            out_shape=(column_shape, row_shape, row_shape),
            in_specs=[ANY] + [VMEM] * (3 + len(parts)),
            out_specs=(VMEM,) * 3,
            scratch_shapes=[wide, tall] + table_scratch(lists),
            compiler_params=params(4),
            name="column_pass",
        )(lists, similar, kept, first, *parts)
    parts = column_exchange(column_part)
    block = jax.ShapeDtypeStruct((rows, width), jnp.bfloat16)

    def sums(blocks):
        taken = blocks if width % TILE == 0 else lines
        return pltpu.VMEM((row_tiles, TILE, taken * width), jnp.float32)

    last, plan, column_potential = pl.pallas_call(
        with_table(plan_kernel, table, log_column, lines),
        out_shape=[
            block,
            pltpu.VMEM((table.slots, 4 * TILE, 2 * TILE), jnp.bfloat16),
            jax.ShapeDtypeStruct((half, TILE), jnp.float32),
        ],
        in_specs=[ANY] + [VMEM] * (3 + len(parts)),
        out_specs=[VMEM] * 3,
        scratch_shapes=[pltpu.VMEM((columns, TILE), jnp.float32), wide, sums(1)] + table_scratch(lists),
        compiler_params=params(12),
        name="plan",
    )(lists, similar, row_potential, whole, *parts)
    visits = table.dummy * TILE * TILE
    blocks = pl.pallas_call(
        with_table(rest_kernel, table, lines),
        out_shape=[block] * (lines - 1),
        in_specs=[ANY] + [VMEM] * 2,
        out_specs=[VMEM] * (lines - 1),
        scratch_shapes=[sums(lines - 1)] + table_scratch(lists),
        compiler_params=params(12),
        cost_estimate=pl.CostEstimate(
            flops=2 * visits * (lines - 1) * width, bytes_accessed=4 * visits, transcendentals=0
        ),
        name="rest_of_plan",
    )(lists, plan, whole)
    blocks = list(blocks) + [last]
    targets = scatter_partials(blocks)
    return (targets, row_out.reshape(rows), column_potential.reshape(protos // 2))


def solution(mesh):
    return jax.shard_map(
        shards,
        mesh=mesh,
        in_specs=(P("row", None), P("proto", "row"), P("row", "proto")),
        out_specs=(P("row", "proto"), P("row"), P("proto")),
        check_vma=False,
    )
```

```python
import functools
import math

import jax
import jax.numpy as jnp
from jax import lax
from jax.experimental import pallas as pl
from jax.experimental.pallas import tpu as pltpu
from jax.sharding import PartitionSpec as P

ITERS = 3
TILE = 128
NEGATIVE = -1e30

VMEM = pl.BlockSpec(memory_space=pltpu.VMEM)
ANY = pl.BlockSpec(memory_space=pl.ANY)


def swap(x, axis, offset):
    size = lax.axis_size(axis)
    return lax.ppermute(x, axis, [(i, i ^ offset) for i in range(size)])


def pair_sum(terms):
    while len(terms) > 1:
        terms = [terms[i] + terms[i + 1] for i in range(0, len(terms), 2)]
    return terms[0]


def combine(parts):
    peak = functools.reduce(jnp.maximum, parts)
    return peak + jnp.log(pair_sum([jnp.exp(part - peak) for part in parts]))


class Table:
    together = 4

    def __init__(self, row_tiles, columns):
        self.row_tiles, self.columns = row_tiles, columns
        self.line = max(row_tiles, columns) + 8
        self.column_base = row_tiles
        self.pair_base = row_tiles + columns
        self.mask_at = (self.pair_base + columns // 2) * self.line
        self.item_at = self.mask_at + row_tiles * columns
        self.items = (columns // 2) * -(-row_tiles // 4)
        self.slots = self.items + self.together - 1
        self.total_at = self.item_at + 2 * self.slots
        self.dummy = row_tiles * columns

    def build(self, mask):
        across = mask.T
        pairs = jnp.max(across.reshape(self.columns // 2, 2, self.row_tiles), axis=1)
        lines = [self.lines(mask), self.lines(across), self.lines(pairs)]
        flat = [part.reshape(-1) for part in lines] + [mask.reshape(-1)]
        steps = (jnp.sum(pairs, axis=1) + 3) // 4
        at = jnp.arange(self.columns // 2, dtype=jnp.int32)
        first = jnp.sum(jnp.where(at[None, :] < at[:, None], steps[None, :], 0), axis=1)
        total = jnp.sum(steps)
        item = jnp.minimum(jnp.arange(self.slots, dtype=jnp.int32), total - 1)
        pair = jnp.sum(jnp.where(item[:, None] >= (first + steps)[None, :], 1, 0), axis=1)
        step = item - jnp.sum(jnp.where(pair[:, None] == at[None, :], first[None, :], 0), axis=1)
        flat += [(self.pair_base + pair) * self.line + 4 * step, pair]
        rounds = (total + self.together - 1) // self.together
        return jnp.concatenate(flat + [jnp.stack([total, rounds])])

    def each_item(self, ref, visit):
        def several(k, carry):
            for i in range(self.together):
                number = self.together * k + i
                at = ref[self.item_at + number]
                visit(
                    number,
                    number < ref[self.total_at],
                    ref[self.item_at + self.slots + number],
                    [ref[at + n] for n in range(4)],
                )
            return carry

        lax.fori_loop(0, ref[self.total_at + 1], several, 0)

    def empty_bits(self, ref, base, count):
        bits = jnp.int32(0)
        for i in range(count):
            bits = bits + jnp.where(self.steps(ref, base + i, 4) == 0, 1 << i, 0)
        return bits

    def lines(self, mask):
        size = mask.shape[1]
        at = jnp.arange(size, dtype=jnp.int32)
        slot = jnp.arange(self.line, dtype=jnp.int32)
        before = jnp.sum(jnp.where(at[None, :] < at[:, None], mask[:, None, :], 0), axis=2)
        hit = (mask[:, None, :] == 1) & (before[:, None, :] == slot[None, :, None])
        places = jnp.sum(jnp.where(hit, at[None, None, :] - size, 0), axis=2) + size
        count = jnp.sum(mask, axis=1, keepdims=True)
        places = jnp.where(slot[None, :] == self.line - 2, (count + 1) // 2, places)
        return jnp.where(slot[None, :] == self.line - 1, (count + 3) // 4, places)

    def steps(self, ref, line, unroll):
        return ref[line * self.line + self.line - (2 if unroll == 2 else 1)]

    def entry(self, ref, line, k):
        return ref[line * self.line + k]

    def allowed(self, ref, t, u):
        return ref[self.mask_at + t * self.columns + u]

    def loop(self, ref, line, unroll, step, start):
        def several(k, a):
            for i in range(unroll):
                a = step(self.entry(ref, line, unroll * k + i), a)
            return a

        return lax.fori_loop(0, self.steps(ref, line, unroll), several, start)

    def sums(self, ref, base, acc_ref, visit):
        lists = range(acc_ref.shape[0])

        def four(i, k):
            tiles = [visit(i, self.entry(ref, base + i, 4 * k + n)) for n in range(4)]
            return (tiles[0] + tiles[1]) + (tiles[2] + tiles[3])

        for i in lists:
            acc_ref[i] = four(i, 0)
        for i in lists:

            @pl.when(self.steps(ref, base + i, 4) > 1)
            def _(i=i):
                acc_ref[i] = lax.fori_loop(
                    1, self.steps(ref, base + i, 4), lambda k, a: a + four(i, k), acc_ref[i]
                )

    def place(self, t, u):
        padding = (t == self.row_tiles) | (u == self.columns)
        return jnp.where(padding, self.dummy, t * self.columns + u)


def with_table(kernel, table, *settings):
    def body(hbm_ref, *refs):
        *refs, smem_ref, sem = refs
        copy = pltpu.make_async_copy(hbm_ref, smem_ref, sem)
        copy.start()

        def arrived():
            copy.wait()
            return smem_ref

        kernel(table, *settings, arrived, *refs)

    return body


def table_scratch(lists):
    return [pltpu.SMEM(lists.shape, jnp.int32), pltpu.SemaphoreType.DMA]


def blank():
    return jnp.zeros((TILE, TILE), jnp.float32)


def lowest():
    return jnp.full((TILE, TILE), NEGATIVE, jnp.float32)


def bad_bits(good):
    bad = jnp.max(jnp.where(good, 0.0, 1.0), axis=1, keepdims=True)
    bit = jnp.left_shift(1, lax.broadcasted_iota(jnp.int32, bad.shape, 0))
    return jnp.sum(bad * bit.astype(jnp.float32)).astype(jnp.int32)


def in_range(totals, factor):
    largest = jnp.max(jnp.max(factor, axis=1, keepdims=True), axis=0, keepdims=True)
    return (totals > 1e-15) & (totals < 1e30) & (largest < 1e15)


def has_bit(bits, i):
    return jnp.bitwise_and(bits, 1 << i) != 0


def spread_rows(row, wide_ref):
    row_tiles = row.shape[0]
    standing = jnp.concatenate(
        [row, jnp.zeros((TILE - row_tiles, TILE), jnp.float32)], axis=0
    ).T
    for t in range(row_tiles):
        wide_ref[t] = jnp.broadcast_to(standing[:, t : t + 1], (TILE, TILE))


def lying(tiles):
    lane = lax.broadcasted_iota(jnp.int32, (TILE, TILE), 1)
    found = blank()
    for t, tile in enumerate(tiles):
        found = jnp.where(lane == t, jnp.sum(tile, axis=1, keepdims=True), found)
    return found.T[: len(tiles)]


class Piece:
    def __init__(self, own, first, owner):
        self.own, self.first, self.owner = own, first, owner

    def copy_to(self, p_ref, piece):
        core, me = lax.rem(lax.axis_index("proto"), 2), lax.axis_index("row")
        rows, width = piece.shape
        first = (core if self.own else 1 - core) * (p_ref.shape[0] // 2) + self.first
        start = 0
        if self.owner is not None:
            start = pl.multiple_of(jnp.bitwise_xor(me, self.owner) * width, TILE)
        p_ref[pl.ds(pl.multiple_of(first, TILE), rows), pl.ds(start, width)] = piece[...]


def score_pairs(table, table_ref, e_ref, p_ref, s_ref, features, add, done):
    row_tiles, columns = table.row_tiles, table.columns
    scale = 4.0 / math.sqrt(e_ref.shape[1])

    def visit(number, real, pair, tiles):
        at = [jnp.minimum(t, row_tiles - 1) for t in tiles]
        product = None
        for span in features(pair):
            rows = jnp.concatenate(
                [e_ref[pl.ds(pl.multiple_of(t * TILE, TILE), TILE), span] for t in at], axis=0
            )
            block = p_ref[pl.ds(pl.multiple_of(pair * 2 * TILE, TILE), 2 * TILE), span]
            part = lax.dot_general(
                rows, block, (((1,), (1,)), ((), ())), preferred_element_type=jnp.float32
            )
            product = part if product is None else product + part
        product = (jnp.where(real, scale, 0.0) if add else scale) * product
        found = {}
        for i, t in enumerate(at):
            for side in range(2):
                where = t * columns + 2 * pair + side
                tile = product[i * TILE : (i + 1) * TILE, side * TILE : (side + 1) * TILE]
                found[i, side] = (where, s_ref[where] + tile if add else tile)
        for where, tile in found.values():
            s_ref[where] = tile
        if done is not None:
            for i, t in enumerate(at):
                done(t, 2 * pair, found[i, 0][1], found[i, 1][1])

    table.each_item(table_ref, visit)


def quarters(owners, p_ref):
    me = lax.axis_index("row")
    width = p_ref.shape[1] // 4

    def features(pair):
        return [pl.ds(pl.multiple_of(jnp.bitwise_xor(me, owner) * width, TILE), width) for owner in owners]

    return features


def early_panel_kernel(table, places, owners, add, arrived, e_ref, *refs):
    pieces, (s_ref, p_ref) = refs[:-2], refs[-2:]
    for place, piece in zip(places, pieces):
        place.copy_to(p_ref, piece)
    if not add:
        s_ref[table.dummy] = lowest()
    features = quarters(owners, p_ref)
    score_pairs(table, arrived(), e_ref, p_ref, s_ref, features, add, None)


def panel_kernel(table, places, add, arrived, e_ref, *refs):
    pieces, (s_ref, p_ref, w_ref, first_ref, out_ref, acc_ref, wide_ref) = refs[:-7], refs[-7:]
    if add:
        pieces = pieces[:-2]
    row_tiles = table.row_tiles
    for place, piece in zip(places, pieces):
        place.copy_to(p_ref, piece)
    for t in range(row_tiles):
        acc_ref[t] = lowest()
    table_ref = arrived()

    def done(t, u, left, right):
        peak = acc_ref[t]
        for side, tile in enumerate((left, right)):
            off = jnp.where(table.allowed(table_ref, t, u + side) == 1, 0.0, NEGATIVE)
            peak = jnp.maximum(peak, tile + off)
        acc_ref[t] = peak

    if add:
        features = quarters([3], p_ref)
    else:
        s_ref[table.dummy] = lowest()
        features = lambda pair: [slice(None)]
    score_pairs(table, table_ref, e_ref, p_ref, s_ref, features, add, done)

    lane = lax.broadcasted_iota(jnp.int32, (TILE, TILE), 1)
    peaks = blank()
    for t in range(row_tiles):
        peak = jnp.max(acc_ref[t], axis=1, keepdims=True)
        peaks = jnp.where(lane == t, peak, peaks)
        wide_ref[t] = jnp.broadcast_to(peak, (TILE, TILE))
    w_ref[table.dummy] = blank().astype(jnp.bfloat16)

    def visit(t, u):
        at = table.place(t, u)
        value = jnp.exp(s_ref[at] - wide_ref[t])
        w_ref[at] = value.astype(jnp.bfloat16)
        return value

    table.sums(table_ref, 0, acc_ref, visit)
    peaks = peaks.T[:row_tiles]
    first_ref[...] = -peaks
    out_ref[...] = peaks + jnp.log(lying([acc_ref[t] for t in range(row_tiles)]))


def row_kernel(table, log_column, arrived, s_ref, w_ref, first_ref, *refs):
    parts, (out_ref, c_ref, v_ref, acc_ref) = refs[:-4], refs[-4:]
    row_tiles, columns = table.row_tiles, table.columns
    column = log_column - combine([part[...] for part in parts])
    factor = jnp.exp(column)
    c_ref[:columns] = column
    v_ref[:columns] = factor
    rest = jnp.zeros((c_ref.shape[0] - columns, TILE), jnp.float32)
    c_ref[columns:] = rest
    v_ref[columns:] = rest
    table_ref = arrived()

    def visit(t, u):
        return w_ref[table.place(t, u)].astype(jnp.float32) * v_ref[pl.ds(u, 1), :]

    table.sums(table_ref, 0, acc_ref, visit)
    totals = lying([acc_ref[t] for t in range(row_tiles)])
    out_ref[...] = jnp.log(totals) - first_ref[...]
    bits = bad_bits(in_range(totals, factor)) - table.empty_bits(table_ref, 0, row_tiles)

    @pl.when(bits != 0)
    def _():
        for t in range(row_tiles):

            @pl.when(has_bit(bits, t))
            def _():
                def score(u):
                    return s_ref[table.place(t, u)] + c_ref[pl.ds(u, 1), :]

                peak = table.loop(table_ref, t, 2, lambda u, a: jnp.maximum(a, score(u)), lowest())
                peak = jnp.max(peak, axis=1, keepdims=True)
                total = table.loop(table_ref, t, 2, lambda u, a: a + jnp.exp(score(u) - peak), blank())
                found = peak + jnp.log(jnp.sum(total, axis=1, keepdims=True))
                out_ref[t : t + 1, :] = jnp.broadcast_to(found, (TILE, TILE)).T[:1]


def column_kernel(table, arrived, s_ref, w_ref, first_ref, *refs):
    parts, (out_ref, r_ref, r_out_ref, wide_ref, acc_ref) = refs[:-5], refs[-5:]
    row = -combine([part[...] for part in parts])
    r_ref[...] = row
    r_out_ref[...] = row
    factor = jnp.exp(row - first_ref[...])
    spread_rows(factor, wide_ref)
    table_ref = arrived()

    def visit(u, t):
        kept = w_ref[table.place(t, u)].astype(jnp.float32)
        return kept * wide_ref[jnp.minimum(t, table.row_tiles - 1)]

    table.sums(table_ref, table.column_base, acc_ref, visit)
    totals = jnp.concatenate(
        [jnp.sum(acc_ref[u], axis=0, keepdims=True) for u in range(table.columns)], axis=0
    )
    out_ref[...] = jnp.log(totals)
    bits = bad_bits(in_range(totals, factor)) - table.empty_bits(table_ref, table.column_base, table.columns)

    @pl.when(bits != 0)
    def _():
        spread_rows(row, wide_ref)
        for u in range(table.columns):

            @pl.when(has_bit(bits, u))
            def _():
                line = table.column_base + u

                def score(t):
                    return s_ref[table.place(t, u)] + wide_ref[jnp.minimum(t, table.row_tiles - 1)]

                peak = table.loop(table_ref, line, 2, lambda t, a: jnp.maximum(a, score(t)), lowest())
                peak = jnp.max(peak, axis=0, keepdims=True)
                total = table.loop(table_ref, line, 2, lambda t, a: a + jnp.exp(score(t) - peak), blank())
                out_ref[u : u + 1, :] = peak + jnp.log(jnp.sum(total, axis=0, keepdims=True))


def plan_blocks(table, table_ref, p_ref, lines, wanted, width, strip, outs, total_ref):
    row_tiles = table.row_tiles
    index = lax.axis_index("proto")
    core, z = lax.rem(index, 2), lax.div(index, 2)
    fits = width % TILE == 0
    total_ref[...] = jnp.zeros(total_ref.shape, jnp.float32)

    def visit(number, real, pair, tiles):
        first = pl.multiple_of(pair * 2 * TILE, TILE)
        blocks = []
        for j in wanted if fits else range(lines):
            if fits:
                start = (2 * jnp.bitwise_xor(z, j) + core) * width
                blocks.append(p_ref[pl.ds(first, 2 * TILE), pl.ds(pl.multiple_of(start, TILE), width)])
            else:
                both = p_ref[pl.ds(first, 2 * TILE), 2 * j * width : 2 * (j + 1) * width]
                blocks.append(jnp.where(core == 0, both[:, :width], both[:, width:]))
        product = jnp.dot(
            strip(number, real, pair, tiles),
            jnp.concatenate(blocks, axis=1),
            preferred_element_type=jnp.float32,
        )
        for i, t in enumerate(tiles):
            total_ref[jnp.minimum(t, row_tiles - 1)] += product[i * TILE : (i + 1) * TILE]

    table.each_item(table_ref, visit)
    for t in range(row_tiles):
        total = total_ref[t].astype(jnp.bfloat16)
        rows = slice(t * TILE, (t + 1) * TILE)
        for n, j in enumerate(wanted):
            if fits:
                outs[n][rows, :] = total[:, n * width : (n + 1) * width]
                continue
            for k in range(lines):

                @pl.when(jnp.bitwise_xor(z, j) == k)
                def _():
                    outs[n][rows, :] = total[:, k * width : (k + 1) * width]


def plan_kernel(table, log_column, lines, arrived, s_ref, r_ref, p_ref, *refs):
    parts, (out_ref, kept_ref, own_ref, c_ref, wide_ref, total_ref) = refs[:-6], refs[-6:]
    row_tiles, columns = table.row_tiles, table.columns
    core = lax.rem(lax.axis_index("proto"), 2)
    c_ref[...] = log_column - combine([part[...] for part in parts])
    half = columns // 2
    own_ref[...] = c_ref[pl.ds(pl.multiple_of(core * half, half), half), :]
    spread_rows(r_ref[...], wide_ref)
    table_ref = arrived()

    def strip(number, real, pair, tiles):
        strips = []
        for t in tiles:
            inside = jnp.minimum(t, row_tiles - 1)
            sides = []
            for side in range(2):
                u = 2 * pair + side
                good = real & (t < row_tiles) & (table.allowed(table_ref, inside, u) == 1)
                tile = s_ref[jnp.where(good, t * columns + u, table.dummy)]
                sides.append(jnp.exp(tile + wide_ref[inside] + c_ref[pl.ds(u, 1), :]).astype(jnp.bfloat16))
            strips.append(jnp.concatenate(sides, axis=1))
        strips = jnp.concatenate(strips, axis=0)
        kept_ref[number] = strips
        return strips

    width = out_ref.shape[1]
    plan_blocks(table, table_ref, p_ref, lines, [lines - 1], width, strip, [out_ref], total_ref)


def rest_kernel(table, lines, arrived, kept_ref, p_ref, *refs):
    outs, total_ref = refs[:-1], refs[-1]
    width = outs[0].shape[1]
    strip = lambda number, real, pair, tiles: kept_ref[number]
    plan_blocks(table, arrived(), p_ref, lines, list(range(lines - 1)), width, strip, outs, total_ref)


def params(mebibytes):
    return pltpu.CompilerParams(vmem_limit_bytes=mebibytes * 2**20)


def sibling(block):
    return swap(block, "proto", 1)


def tied(*arrays):
    return lax.optimization_barrier(arrays)


def make_panel(table, mask, embeddings, shard, rows, features):
    width = shard.shape[1]
    protos = 2 * shard.shape[0]
    panel = pltpu.VMEM((table.dummy + 1, TILE, TILE), jnp.float32)
    whole = pltpu.VMEM((protos, features), jnp.bfloat16)
    row_shape = jax.ShapeDtypeStruct((table.row_tiles, TILE), jnp.float32)
    kept = pltpu.VMEM((table.dummy + 1, TILE, TILE), jnp.bfloat16)
    tiles = pltpu.VMEM((table.row_tiles, TILE, TILE), jnp.float32)

    def late(lists, places, add, e, pieces, before):
        at = 2 + len(pieces)
        return pl.pallas_call(
            with_table(panel_kernel, table, places, add),
            out_shape=(panel, whole, kept, row_shape, row_shape),
            in_specs=[ANY] + [VMEM] * (1 + len(pieces) + len(before)),
            out_specs=(VMEM,) * 5,
            scratch_shapes=[tiles, tiles] + table_scratch(lists),
            input_output_aliases={at: 0, at + 1: 1} if add else {},
            compiler_params=params(8),
            name="panel",
        )(lists, e, *pieces, *before)

    if lax.axis_size("row") != 4 or width % TILE:
        lists = table.build(mask)
        every = lax.all_gather(shard, "row", axis=1, tiled=True)
        places = [Piece(True, 0, None), Piece(False, 0, None)]
        return (lists, *late(lists, places, False, embeddings, [every, sibling(every)], []))
    half = shard.shape[0] // 2
    visits = table.dummy * TILE * TILE

    def early(lists, places, owners, pieces, before):
        at = 2 + len(pieces)
        return pl.pallas_call(
            with_table(early_panel_kernel, table, places, owners, bool(before)),
            out_shape=(panel, whole),
            in_specs=[ANY] + [VMEM] * (1 + len(pieces) + len(before)),
            out_specs=(VMEM, VMEM),
            scratch_shapes=table_scratch(lists),
            input_output_aliases={at: 0, at + 1: 1} if before else {},
            compiler_params=params(6),
            cost_estimate=pl.CostEstimate(
                flops=visits * width * len(owners), bytes_accessed=8 * visits, transcendentals=0
            ),
            name="early_panel",
        )(lists, embeddings, *pieces, *before)

    near = swap(shard, "row", 1)
    far = swap(shard, "row", 2)
    lists = table.build(mask)
    places = [Piece(True, 0, 0), Piece(False, 0, 0)]
    similar, known = early(lists, places, [0], [shard, sibling(shard)], [])
    near, far, similar, known = tied(near, far, similar, known)
    cross_top = swap(far[:half], "row", 1)
    cross_bottom = swap(near[half:], "row", 2)
    places = [Piece(own, 0, owner) for own in (True, False) for owner in (1, 2)]
    pieces = [near, far, sibling(near), sibling(far)]
    similar, known = early(lists, places, [1, 2], pieces, [similar, known])
    cross_top, cross_bottom, similar, known = tied(cross_top, cross_bottom, similar, known)
    places = [Piece(own, first, 3) for own in (True, False) for first in (0, half)]
    pieces = [cross_top, cross_bottom, sibling(cross_top), sibling(cross_bottom)]
    return (lists, *late(lists, places, True, embeddings, pieces, [similar, known]))


def scatter_partials(blocks):
    blocks = list(blocks)
    distance = 1
    while distance < len(blocks):
        for j in range(len(blocks) - distance, 0, -2 * distance):
            got = swap(blocks[j].astype(jnp.bfloat16), "proto", 2 * distance)
            if j == 3 * distance:
                got, blocks[distance] = tied(got, blocks[distance])
            blocks[j ^ distance] = blocks[j ^ distance].astype(jnp.float32) + got.astype(jnp.float32)
        distance *= 2
    return blocks[0].astype(jnp.bfloat16)


def shards(embeddings, prototypes, block_mask):
    n_row, n_proto = lax.axis_size("row"), lax.axis_size("proto")
    lines = n_proto // 2
    rows, features = embeddings.shape
    protos = 2 * prototypes.shape[0]
    width = features // n_proto
    row_tiles, columns = block_mask.shape[0], 2 * block_mask.shape[1]
    log_column = math.log(rows * n_row / (protos * lines))
    table = Table(row_tiles, columns)

    other_mask = swap(block_mask, "proto", 1)
    mask, other_mask = jnp.where(block_mask == 1, 1, 0), jnp.where(other_mask == 1, 1, 0)
    mask = jnp.where(
        lax.axis_index("proto") % 2 == 0,
        jnp.concatenate([mask, other_mask], axis=1),
        jnp.concatenate([other_mask, mask], axis=1),
    )

    row_shape = jax.ShapeDtypeStruct((row_tiles, TILE), jnp.float32)
    column_shape = jax.ShapeDtypeStruct((columns, TILE), jnp.float32)
    half = columns // 2
    wide = pltpu.VMEM((row_tiles, TILE, TILE), jnp.float32)
    tall = pltpu.VMEM((columns, TILE, TILE), jnp.float32)
    factors = pltpu.VMEM((columns + 8, TILE), jnp.float32)
    lists, similar, whole, kept, first, row_part = make_panel(table, mask, embeddings, prototypes, rows, features)

    def row_exchange(part):
        others = [swap(part, "proto", 2 * j) for j in range(lines - 1, 0, -1)]
        return [part] + others[::-1]

    def column_exchange(part):
        others = [swap(part, "row", j) for j in range(n_row - 1, 0, -1)]
        return [part] + others[::-1]

    for sweep in range(ITERS):
        if sweep:
            parts = column_exchange(column_part)
            row_part = pl.pallas_call(
                with_table(row_kernel, table, log_column),
                out_shape=row_shape,
                in_specs=[ANY] + [VMEM] * (3 + len(parts)),
                out_specs=VMEM,
                scratch_shapes=[factors, factors, wide] + table_scratch(lists),
                compiler_params=params(4),
                name="row_pass",
            )(lists, similar, kept, first, *parts)
        parts = row_exchange(row_part)
        column_part, row_potential, row_out = pl.pallas_call(
            with_table(column_kernel, table),
            out_shape=(column_shape, row_shape, row_shape),
            in_specs=[ANY] + [VMEM] * (3 + len(parts)),
            out_specs=(VMEM,) * 3,
            scratch_shapes=[wide, tall] + table_scratch(lists),
            compiler_params=params(4),
            name="column_pass",
        )(lists, similar, kept, first, *parts)
    parts = column_exchange(column_part)
    block = jax.ShapeDtypeStruct((rows, width), jnp.bfloat16)

    def sums(blocks):
        taken = blocks if width % TILE == 0 else lines
        return pltpu.VMEM((row_tiles, TILE, taken * width), jnp.float32)

    last, plan, column_potential = pl.pallas_call(
        with_table(plan_kernel, table, log_column, lines),
        out_shape=[
            block,
            pltpu.VMEM((table.slots, 4 * TILE, 2 * TILE), jnp.bfloat16),
            jax.ShapeDtypeStruct((half, TILE), jnp.float32),
        ],
        in_specs=[ANY] + [VMEM] * (3 + len(parts)),
        out_specs=[VMEM] * 3,
        scratch_shapes=[pltpu.VMEM((columns, TILE), jnp.float32), wide, sums(1)] + table_scratch(lists),
        compiler_params=params(12),
        name="plan",
    )(lists, similar, row_potential, whole, *parts)
    visits = table.dummy * TILE * TILE
    blocks = pl.pallas_call(
        with_table(rest_kernel, table, lines),
        out_shape=[block] * (lines - 1),
        in_specs=[ANY] + [VMEM] * 2,
        out_specs=[VMEM] * (lines - 1),
        scratch_shapes=[sums(lines - 1)] + table_scratch(lists),
        compiler_params=params(12),
        cost_estimate=pl.CostEstimate(
            flops=2 * visits * (lines - 1) * width, bytes_accessed=4 * visits, transcendentals=0
        ),
        name="rest_of_plan",
    )(lists, plan, whole)
    blocks = list(blocks) + [last]
    targets = scatter_partials(blocks)
    return (targets, row_out.reshape(rows), column_potential.reshape(protos // 2))


def solution(mesh):
    return jax.shard_map(
        shards,
        mesh=mesh,
        in_specs=(P("row", None), P("proto", "row"), P("row", "proto")),
        out_specs=(P("row", "proto"), P("row"), P("proto")),
        check_vma=False,
    )
```

```python
import functools
import math

import jax
import jax.numpy as jnp
from jax import lax
from jax.experimental import pallas as pl
from jax.experimental.pallas import tpu as pltpu
from jax.sharding import PartitionSpec as P

ITERS = 3
TILE = 128
PARTS = 2
NEGATIVE = -1e30

VMEM = pl.BlockSpec(memory_space=pltpu.VMEM)
ANY = pl.BlockSpec(memory_space=pl.ANY)


def swap(x, axis, offset):
    size = lax.axis_size(axis)
    return lax.ppermute(x, axis, [(i, i ^ offset) for i in range(size)])


def pair_sum(terms):
    while len(terms) > 1:
        terms = [terms[i] + terms[i + 1] for i in range(0, len(terms), 2)]
    return terms[0]


def combine(parts):
    peak = functools.reduce(jnp.maximum, parts)
    return peak + jnp.log(pair_sum([jnp.exp(part - peak) for part in parts]))


class Table:
    together = 4

    def __init__(self, row_tiles, columns):
        self.row_tiles, self.columns = row_tiles, columns
        self.line = max(row_tiles, columns) + 8
        self.column_base = row_tiles
        self.pair_base = row_tiles + columns
        self.mask_at = (self.pair_base + columns // 2) * self.line
        self.item_at = self.mask_at + row_tiles * columns
        self.items = (columns // 2) * -(-row_tiles // 4)
        self.slots = self.items + self.together - 1
        self.total_at = self.item_at + 2 * self.slots
        self.dummy = row_tiles * columns

    def build(self, mask):
        across = mask.T
        pairs = jnp.max(across.reshape(self.columns // 2, 2, self.row_tiles), axis=1)
        lines = [self.lines(mask), self.lines(across), self.lines(pairs)]
        flat = [part.reshape(-1) for part in lines] + [mask.reshape(-1)]
        steps = (jnp.sum(pairs, axis=1) + 3) // 4
        at = jnp.arange(self.columns // 2, dtype=jnp.int32)
        first = jnp.sum(jnp.where(at[None, :] < at[:, None], steps[None, :], 0), axis=1)
        total = jnp.sum(steps)
        item = jnp.minimum(jnp.arange(self.slots, dtype=jnp.int32), total - 1)
        pair = jnp.sum(jnp.where(item[:, None] >= (first + steps)[None, :], 1, 0), axis=1)
        step = item - jnp.sum(jnp.where(pair[:, None] == at[None, :], first[None, :], 0), axis=1)
        flat += [(self.pair_base + pair) * self.line + 4 * step, pair]
        rounds = (total + self.together - 1) // self.together
        return jnp.concatenate(flat + [jnp.stack([total, rounds])])

    def each_item(self, ref, visit):
        def several(k, carry):
            for i in range(self.together):
                number = self.together * k + i
                at = ref[self.item_at + number]
                visit(
                    number,
                    number < ref[self.total_at],
                    ref[self.item_at + self.slots + number],
                    [ref[at + n] for n in range(4)],
                )
            return carry

        lax.fori_loop(0, ref[self.total_at + 1], several, 0)

    def empty_bits(self, ref, base, count):
        bits = jnp.int32(0)
        for i in range(count):
            bits = bits + jnp.where(self.steps(ref, base + i, 4) == 0, 1 << i, 0)
        return bits

    def lines(self, mask):
        size = mask.shape[1]
        at = jnp.arange(size, dtype=jnp.int32)
        slot = jnp.arange(self.line, dtype=jnp.int32)
        before = jnp.sum(jnp.where(at[None, :] < at[:, None], mask[:, None, :], 0), axis=2)
        hit = (mask[:, None, :] == 1) & (before[:, None, :] == slot[None, :, None])
        places = jnp.sum(jnp.where(hit, at[None, None, :] - size, 0), axis=2) + size
        count = jnp.sum(mask, axis=1, keepdims=True)
        places = jnp.where(slot[None, :] == self.line - 2, (count + 1) // 2, places)
        return jnp.where(slot[None, :] == self.line - 1, (count + 3) // 4, places)

    def steps(self, ref, line, unroll):
        return ref[line * self.line + self.line - (2 if unroll == 2 else 1)]

    def entry(self, ref, line, k):
        return ref[line * self.line + k]

    def allowed(self, ref, t, u):
        return ref[self.mask_at + t * self.columns + u]

    def loop(self, ref, line, unroll, step, start):
        def several(k, a):
            for i in range(unroll):
                a = step(self.entry(ref, line, unroll * k + i), a)
            return a

        return lax.fori_loop(0, self.steps(ref, line, unroll), several, start)

    def sums(self, ref, base, acc_ref, visit):
        lists = range(acc_ref.shape[0])

        def four(i, k):
            tiles = [visit(i, self.entry(ref, base + i, 4 * k + n)) for n in range(4)]
            return (tiles[0] + tiles[1]) + (tiles[2] + tiles[3])

        for i in lists:
            acc_ref[i] = four(i, 0)
        for i in lists:

            @pl.when(self.steps(ref, base + i, 4) > 1)
            def _(i=i):
                acc_ref[i] = lax.fori_loop(
                    1, self.steps(ref, base + i, 4), lambda k, a: a + four(i, k), acc_ref[i]
                )

    def place(self, t, u):
        padding = (t == self.row_tiles) | (u == self.columns)
        return jnp.where(padding, self.dummy, t * self.columns + u)


def with_table(kernel, table, *settings):
    def body(hbm_ref, *refs):
        *refs, smem_ref, sem = refs
        copy = pltpu.make_async_copy(hbm_ref, smem_ref, sem)
        copy.start()

        def arrived():
            copy.wait()
            return smem_ref

        kernel(table, *settings, arrived, *refs)

    return body


def table_scratch(lists):
    return [pltpu.SMEM(lists.shape, jnp.int32), pltpu.SemaphoreType.DMA]


def blank():
    return jnp.zeros((TILE, TILE), jnp.float32)


def lowest():
    return jnp.full((TILE, TILE), NEGATIVE, jnp.float32)


def bad_bits(good):
    bad = jnp.max(jnp.where(good, 0.0, 1.0), axis=1, keepdims=True)
    bit = jnp.left_shift(1, lax.broadcasted_iota(jnp.int32, bad.shape, 0))
    return jnp.sum(bad * bit.astype(jnp.float32)).astype(jnp.int32)


def in_range(totals, factor):
    largest = jnp.max(jnp.max(factor, axis=1, keepdims=True), axis=0, keepdims=True)
    return (totals > 1e-15) & (totals < 1e30) & (largest < 1e15)


def has_bit(bits, i):
    return jnp.bitwise_and(bits, 1 << i) != 0


def spread_rows(row, wide_ref):
    row_tiles = row.shape[0]
    standing = jnp.concatenate(
        [row, jnp.zeros((TILE - row_tiles, TILE), jnp.float32)], axis=0
    ).T
    for t in range(row_tiles):
        wide_ref[t] = jnp.broadcast_to(standing[:, t : t + 1], (TILE, TILE))


def lying(tiles):
    lane = lax.broadcasted_iota(jnp.int32, (TILE, TILE), 1)
    found = blank()
    for t, tile in enumerate(tiles):
        found = jnp.where(lane == t, jnp.sum(tile, axis=1, keepdims=True), found)
    return found.T[: len(tiles)]


class Piece:
    def __init__(self, own, first, owner):
        self.own, self.first, self.owner = own, first, owner

    def copy_to(self, p_ref, piece):
        core, me = lax.rem(lax.axis_index("proto"), 2), lax.axis_index("row")
        rows, width = piece.shape
        first = (core if self.own else 1 - core) * (p_ref.shape[0] // 2) + self.first
        start = 0
        if self.owner is not None:
            start = pl.multiple_of(jnp.bitwise_xor(me, self.owner) * width, TILE)
        p_ref[pl.ds(pl.multiple_of(first, TILE), rows), pl.ds(start, width)] = piece[...]


def score_pairs(table, table_ref, e_ref, p_ref, s_ref, features, add, done):
    row_tiles, columns = table.row_tiles, table.columns
    scale = 4.0 / math.sqrt(e_ref.shape[1])

    def visit(number, real, pair, tiles):
        at = [jnp.minimum(t, row_tiles - 1) for t in tiles]
        product = None
        for span in features(pair):
            rows = jnp.concatenate(
                [e_ref[pl.ds(pl.multiple_of(t * TILE, TILE), TILE), span] for t in at], axis=0
            )
            block = p_ref[pl.ds(pl.multiple_of(pair * 2 * TILE, TILE), 2 * TILE), span]
            part = lax.dot_general(
                rows, block, (((1,), (1,)), ((), ())), preferred_element_type=jnp.float32
            )
            product = part if product is None else product + part
        product = (jnp.where(real, scale, 0.0) if add else scale) * product
        found = {}
        for i, t in enumerate(at):
            for side in range(2):
                where = t * columns + 2 * pair + side
                tile = product[i * TILE : (i + 1) * TILE, side * TILE : (side + 1) * TILE]
                found[i, side] = (where, s_ref[where] + tile if add else tile)
        for where, tile in found.values():
            s_ref[where] = tile
        if done is not None:
            for i, t in enumerate(at):
                done(t, 2 * pair, found[i, 0][1], found[i, 1][1])

    table.each_item(table_ref, visit)


def quarters(owners, p_ref):
    me = lax.axis_index("row")
    width = p_ref.shape[1] // 4

    def features(pair):
        return [pl.ds(pl.multiple_of(jnp.bitwise_xor(me, owner) * width, TILE), width) for owner in owners]

    return features


def early_panel_kernel(table, places, owners, add, arrived, e_ref, *refs):
    pieces, (s_ref, p_ref) = refs[:-2], refs[-2:]
    for place, piece in zip(places, pieces):
        place.copy_to(p_ref, piece)
    if not add:
        s_ref[table.dummy] = lowest()
    features = quarters(owners, p_ref)
    score_pairs(table, arrived(), e_ref, p_ref, s_ref, features, add, None)


def panel_kernel(table, places, add, arrived, e_ref, *refs):
    pieces, (s_ref, p_ref, w_ref, first_ref, out_ref, acc_ref, wide_ref) = refs[:-7], refs[-7:]
    if add:
        pieces = pieces[:-2]
    row_tiles = table.row_tiles
    for place, piece in zip(places, pieces):
        place.copy_to(p_ref, piece)
    for t in range(row_tiles):
        acc_ref[t] = lowest()
    table_ref = arrived()

    def done(t, u, left, right):
        peak = acc_ref[t]
        for side, tile in enumerate((left, right)):
            off = jnp.where(table.allowed(table_ref, t, u + side) == 1, 0.0, NEGATIVE)
            peak = jnp.maximum(peak, tile + off)
        acc_ref[t] = peak

    if add:
        features = quarters([3], p_ref)
    else:
        s_ref[table.dummy] = lowest()
        features = lambda pair: [slice(None)]
    score_pairs(table, table_ref, e_ref, p_ref, s_ref, features, add, done)

    lane = lax.broadcasted_iota(jnp.int32, (TILE, TILE), 1)
    peaks = blank()
    for t in range(row_tiles):
        peak = jnp.max(acc_ref[t], axis=1, keepdims=True)
        peaks = jnp.where(lane == t, peak, peaks)
        wide_ref[t] = jnp.broadcast_to(peak, (TILE, TILE))
    w_ref[table.dummy] = blank().astype(jnp.bfloat16)

    def visit(t, u):
        at = table.place(t, u)
        value = jnp.exp(s_ref[at] - wide_ref[t])
        w_ref[at] = value.astype(jnp.bfloat16)
        return value

    table.sums(table_ref, 0, acc_ref, visit)
    peaks = peaks.T[:row_tiles]
    first_ref[...] = -peaks
    out_ref[...] = peaks + jnp.log(lying([acc_ref[t] for t in range(row_tiles)]))


def row_kernel(table, log_column, arrived, s_ref, w_ref, first_ref, *refs):
    parts, (out_ref, c_ref, v_ref, acc_ref) = refs[:-4], refs[-4:]
    row_tiles, columns = table.row_tiles, table.columns
    column = log_column - combine([part[...] for part in parts])
    factor = jnp.exp(column)
    c_ref[:columns] = column
    v_ref[:columns] = factor
    rest = jnp.zeros((c_ref.shape[0] - columns, TILE), jnp.float32)
    c_ref[columns:] = rest
    v_ref[columns:] = rest
    table_ref = arrived()

    def visit(t, u):
        return w_ref[table.place(t, u)].astype(jnp.float32) * v_ref[pl.ds(u, 1), :]

    table.sums(table_ref, 0, acc_ref, visit)
    totals = lying([acc_ref[t] for t in range(row_tiles)])
    out_ref[...] = jnp.log(totals) - first_ref[...]
    bits = bad_bits(in_range(totals, factor)) - table.empty_bits(table_ref, 0, row_tiles)

    @pl.when(bits != 0)
    def _():
        for t in range(row_tiles):

            @pl.when(has_bit(bits, t))
            def _():
                def score(u):
                    return s_ref[table.place(t, u)] + c_ref[pl.ds(u, 1), :]

                peak = table.loop(table_ref, t, 2, lambda u, a: jnp.maximum(a, score(u)), lowest())
                peak = jnp.max(peak, axis=1, keepdims=True)
                total = table.loop(table_ref, t, 2, lambda u, a: a + jnp.exp(score(u) - peak), blank())
                found = peak + jnp.log(jnp.sum(total, axis=1, keepdims=True))
                out_ref[t : t + 1, :] = jnp.broadcast_to(found, (TILE, TILE)).T[:1]


def column_kernel(table, arrived, s_ref, w_ref, first_ref, *refs):
    parts, (out_ref, r_ref, r_out_ref, wide_ref, acc_ref) = refs[:-5], refs[-5:]
    row = -combine([part[...] for part in parts])
    r_ref[...] = row
    r_out_ref[...] = row
    factor = jnp.exp(row - first_ref[...])
    spread_rows(factor, wide_ref)
    table_ref = arrived()

    def visit(u, t):
        kept = w_ref[table.place(t, u)].astype(jnp.float32)
        return kept * wide_ref[jnp.minimum(t, table.row_tiles - 1)]

    table.sums(table_ref, table.column_base, acc_ref, visit)
    totals = jnp.concatenate(
        [jnp.sum(acc_ref[u], axis=0, keepdims=True) for u in range(table.columns)], axis=0
    )
    out_ref[...] = jnp.log(totals)
    bits = bad_bits(in_range(totals, factor)) - table.empty_bits(table_ref, table.column_base, table.columns)

    @pl.when(bits != 0)
    def _():
        spread_rows(row, wide_ref)
        for u in range(table.columns):

            @pl.when(has_bit(bits, u))
            def _():
                line = table.column_base + u

                def score(t):
                    return s_ref[table.place(t, u)] + wide_ref[jnp.minimum(t, table.row_tiles - 1)]

                peak = table.loop(table_ref, line, 2, lambda t, a: jnp.maximum(a, score(t)), lowest())
                peak = jnp.max(peak, axis=0, keepdims=True)
                total = table.loop(table_ref, line, 2, lambda t, a: a + jnp.exp(score(t) - peak), blank())
                out_ref[u : u + 1, :] = peak + jnp.log(jnp.sum(total, axis=0, keepdims=True))


def plan_blocks(table, table_ref, p_ref, lines, wanted, width, strip, outs, total_ref):
    row_tiles = table.row_tiles
    index = lax.axis_index("proto")
    core, z = lax.rem(index, 2), lax.div(index, 2)
    fits = width % TILE == 0
    total_ref[...] = jnp.zeros(total_ref.shape, jnp.float32)

    def visit(number, real, pair, tiles):
        first = pl.multiple_of(pair * 2 * TILE, TILE)
        blocks = []
        for j in wanted if fits else range(lines):
            if fits:
                start = (2 * jnp.bitwise_xor(z, j) + core) * width
                blocks.append(p_ref[pl.ds(first, 2 * TILE), pl.ds(pl.multiple_of(start, TILE), width)])
            else:
                both = p_ref[pl.ds(first, 2 * TILE), 2 * j * width : 2 * (j + 1) * width]
                blocks.append(jnp.where(core == 0, both[:, :width], both[:, width:]))
        product = jnp.dot(
            strip(number, real, pair, tiles),
            jnp.concatenate(blocks, axis=1),
            preferred_element_type=jnp.float32,
        )
        for i, t in enumerate(tiles):
            total_ref[jnp.minimum(t, row_tiles - 1)] += product[i * TILE : (i + 1) * TILE]

    table.each_item(table_ref, visit)
    for t in range(row_tiles):
        total = total_ref[t].astype(jnp.bfloat16)
        part, at = divmod(t * TILE, outs[0].shape[0])
        rows = slice(at, at + TILE)
        for n, j in enumerate(wanted):
            out_ref = outs[PARTS * n + part]
            if fits:
                out_ref[rows, :] = total[:, n * width : (n + 1) * width]
                continue
            for k in range(lines):

                @pl.when(jnp.bitwise_xor(z, j) == k)
                def _():
                    out_ref[rows, :] = total[:, k * width : (k + 1) * width]


def plan_kernel(table, log_column, lines, arrived, s_ref, r_ref, p_ref, *refs):
    *refs, kept_ref, own_ref, c_ref, wide_ref, total_ref = refs
    parts, outs = refs[:-PARTS], refs[-PARTS:]
    row_tiles, columns = table.row_tiles, table.columns
    core = lax.rem(lax.axis_index("proto"), 2)
    c_ref[...] = log_column - combine([part[...] for part in parts])
    half = columns // 2
    own_ref[...] = c_ref[pl.ds(pl.multiple_of(core * half, half), half), :]
    spread_rows(r_ref[...], wide_ref)
    table_ref = arrived()

    def strip(number, real, pair, tiles):
        strips = []
        for t in tiles:
            inside = jnp.minimum(t, row_tiles - 1)
            sides = []
            for side in range(2):
                u = 2 * pair + side
                good = real & (t < row_tiles) & (table.allowed(table_ref, inside, u) == 1)
                tile = s_ref[jnp.where(good, t * columns + u, table.dummy)]
                sides.append(jnp.exp(tile + wide_ref[inside] + c_ref[pl.ds(u, 1), :]).astype(jnp.bfloat16))
            strips.append(jnp.concatenate(sides, axis=1))
        strips = jnp.concatenate(strips, axis=0)
        kept_ref[number] = strips
        return strips

    width = outs[0].shape[1]
    plan_blocks(table, table_ref, p_ref, lines, [lines - 1], width, strip, outs, total_ref)


def rest_kernel(table, lines, arrived, kept_ref, p_ref, *refs):
    outs, total_ref = refs[:-1], refs[-1]
    width = outs[0].shape[1]
    strip = lambda number, real, pair, tiles: kept_ref[number]
    plan_blocks(table, arrived(), p_ref, lines, list(range(lines - 1)), width, strip, outs, total_ref)


def params(mebibytes):
    return pltpu.CompilerParams(vmem_limit_bytes=mebibytes * 2**20)


def sibling(block):
    return swap(block, "proto", 1)


def tied(*arrays):
    return lax.optimization_barrier(arrays)


def make_panel(table, mask, embeddings, shard, rows, features):
    width = shard.shape[1]
    protos = 2 * shard.shape[0]
    panel = pltpu.VMEM((table.dummy + 1, TILE, TILE), jnp.float32)
    whole = pltpu.VMEM((protos, features), jnp.bfloat16)
    row_shape = jax.ShapeDtypeStruct((table.row_tiles, TILE), jnp.float32)
    kept = pltpu.VMEM((table.dummy + 1, TILE, TILE), jnp.bfloat16)
    tiles = pltpu.VMEM((table.row_tiles, TILE, TILE), jnp.float32)

    def late(lists, places, add, e, pieces, before):
        at = 2 + len(pieces)
        return pl.pallas_call(
            with_table(panel_kernel, table, places, add),
            out_shape=(panel, whole, kept, row_shape, row_shape),
            in_specs=[ANY] + [VMEM] * (1 + len(pieces) + len(before)),
            out_specs=(VMEM,) * 5,
            scratch_shapes=[tiles, tiles] + table_scratch(lists),
            input_output_aliases={at: 0, at + 1: 1} if add else {},
            compiler_params=params(8),
            name="panel",
        )(lists, e, *pieces, *before)

    if lax.axis_size("row") != 4 or width % TILE:
        lists = table.build(mask)
        every = lax.all_gather(shard, "row", axis=1, tiled=True)
        places = [Piece(True, 0, None), Piece(False, 0, None)]
        return (lists, *late(lists, places, False, embeddings, [every, sibling(every)], []))
    half = shard.shape[0] // 2
    visits = table.dummy * TILE * TILE

    def early(lists, places, owners, pieces, before):
        at = 2 + len(pieces)
        return pl.pallas_call(
            with_table(early_panel_kernel, table, places, owners, bool(before)),
            out_shape=(panel, whole),
            in_specs=[ANY] + [VMEM] * (1 + len(pieces) + len(before)),
            out_specs=(VMEM, VMEM),
            scratch_shapes=table_scratch(lists),
            input_output_aliases={at: 0, at + 1: 1} if before else {},
            compiler_params=params(6),
            cost_estimate=pl.CostEstimate(
                flops=visits * width * len(owners), bytes_accessed=8 * visits, transcendentals=0
            ),
            name="early_panel",
        )(lists, embeddings, *pieces, *before)

    near = swap(shard, "row", 1)
    far = swap(shard, "row", 2)
    lists = table.build(mask)
    places = [Piece(True, 0, 0), Piece(False, 0, 0)]
    similar, known = early(lists, places, [0], [shard, sibling(shard)], [])
    near, far, similar, known = tied(near, far, similar, known)
    cross_top = swap(far[:half], "row", 1)
    cross_bottom = swap(near[half:], "row", 2)
    places = [Piece(own, 0, owner) for own in (True, False) for owner in (1, 2)]
    pieces = [near, far, sibling(near), sibling(far)]
    similar, known = early(lists, places, [1, 2], pieces, [similar, known])
    cross_top, cross_bottom, similar, known = tied(cross_top, cross_bottom, similar, known)
    places = [Piece(own, first, 3) for own in (True, False) for first in (0, half)]
    pieces = [cross_top, cross_bottom, sibling(cross_top), sibling(cross_bottom)]
    return (lists, *late(lists, places, True, embeddings, pieces, [similar, known]))


def scatter_partials(blocks):
    blocks = [blocks[at : at + PARTS] for at in range(0, len(blocks), PARTS)]
    distance = 1
    while distance < len(blocks):
        for j in range(len(blocks) - distance, 0, -2 * distance):
            got = [swap(part.astype(jnp.bfloat16), "proto", 2 * distance) for part in blocks[j]]
            if j == 3 * distance:
                tie = tied(*got, *blocks[distance])
                got, blocks[distance] = tie[:PARTS], tie[PARTS:]
            blocks[j ^ distance] = [
                part.astype(jnp.float32) + other.astype(jnp.float32)
                for part, other in zip(blocks[j ^ distance], got)
            ]
        distance *= 2
    return jnp.concatenate([part.astype(jnp.bfloat16) for part in blocks[0]], axis=0)


def shards(embeddings, prototypes, block_mask):
    n_row, n_proto = lax.axis_size("row"), lax.axis_size("proto")
    lines = n_proto // 2
    rows, features = embeddings.shape
    protos = 2 * prototypes.shape[0]
    width = features // n_proto
    row_tiles, columns = block_mask.shape[0], 2 * block_mask.shape[1]
    log_column = math.log(rows * n_row / (protos * lines))
    table = Table(row_tiles, columns)

    other_mask = swap(block_mask, "proto", 1)
    mask, other_mask = jnp.where(block_mask == 1, 1, 0), jnp.where(other_mask == 1, 1, 0)
    mask = jnp.where(
        lax.axis_index("proto") % 2 == 0,
        jnp.concatenate([mask, other_mask], axis=1),
        jnp.concatenate([other_mask, mask], axis=1),
    )

    row_shape = jax.ShapeDtypeStruct((row_tiles, TILE), jnp.float32)
    column_shape = jax.ShapeDtypeStruct((columns, TILE), jnp.float32)
    half = columns // 2
    wide = pltpu.VMEM((row_tiles, TILE, TILE), jnp.float32)
    tall = pltpu.VMEM((columns, TILE, TILE), jnp.float32)
    factors = pltpu.VMEM((columns + 8, TILE), jnp.float32)
    lists, similar, whole, kept, first, row_part = make_panel(table, mask, embeddings, prototypes, rows, features)

    def row_exchange(part):
        others = [swap(part, "proto", 2 * j) for j in range(lines - 1, 0, -1)]
        return [part] + others[::-1]

    def column_exchange(part):
        others = [swap(part, "row", j) for j in range(n_row - 1, 0, -1)]
        return [part] + others[::-1]

    for sweep in range(ITERS):
        if sweep:
            parts = column_exchange(column_part)
            row_part = pl.pallas_call(
                with_table(row_kernel, table, log_column),
                out_shape=row_shape,
                in_specs=[ANY] + [VMEM] * (3 + len(parts)),
                out_specs=VMEM,
                scratch_shapes=[factors, factors, wide] + table_scratch(lists),
                compiler_params=params(4),
                name="row_pass",
            )(lists, similar, kept, first, *parts)
        parts = row_exchange(row_part)
        column_part, row_potential, row_out = pl.pallas_call(
            with_table(column_kernel, table),
            out_shape=(column_shape, row_shape, row_shape),
            in_specs=[ANY] + [VMEM] * (3 + len(parts)),
            out_specs=(VMEM,) * 3,
            scratch_shapes=[wide, tall] + table_scratch(lists),
            compiler_params=params(4),
            name="column_pass",
        )(lists, similar, kept, first, *parts)
    parts = column_exchange(column_part)
    block = jax.ShapeDtypeStruct((rows // PARTS, width), jnp.bfloat16)

    def sums(blocks):
        taken = blocks if width % TILE == 0 else lines
        return pltpu.VMEM((row_tiles, TILE, taken * width), jnp.float32)

    *last, plan, column_potential = pl.pallas_call(
        with_table(plan_kernel, table, log_column, lines),
        out_shape=[block] * PARTS
        + [
            pltpu.VMEM((table.slots, 4 * TILE, 2 * TILE), jnp.bfloat16),
            jax.ShapeDtypeStruct((half, TILE), jnp.float32),
        ],
        in_specs=[ANY] + [VMEM] * (3 + len(parts)),
        out_specs=[VMEM] * (PARTS + 2),
        scratch_shapes=[pltpu.VMEM((columns, TILE), jnp.float32), wide, sums(1)] + table_scratch(lists),
        compiler_params=params(12),
        name="plan",
    )(lists, similar, row_potential, whole, *parts)
    visits = table.dummy * TILE * TILE
    blocks = pl.pallas_call(
        with_table(rest_kernel, table, lines),
        out_shape=[block] * (PARTS * (lines - 1)),
        in_specs=[ANY] + [VMEM] * 2,
        out_specs=[VMEM] * (PARTS * (lines - 1)),
        scratch_shapes=[sums(lines - 1)] + table_scratch(lists),
        compiler_params=params(12),
        cost_estimate=pl.CostEstimate(
            flops=2 * visits * (lines - 1) * width, bytes_accessed=4 * visits, transcendentals=0
        ),
        name="rest_of_plan",
    )(lists, plan, whole)
    blocks = list(blocks) + last
    targets = scatter_partials(blocks)
    return (targets, row_out.reshape(rows), column_potential.reshape(protos // 2))


def solution(mesh):
    return jax.shard_map(
        shards,
        mesh=mesh,
        in_specs=(P("row", None), P("proto", "row"), P("row", "proto")),
        out_specs=(P("row", "proto"), P("row"), P("proto")),
        check_vma=False,
    )
```

```python
import functools
import math

import jax
import jax.numpy as jnp
from jax import lax
from jax.experimental import pallas as pl
from jax.experimental.pallas import tpu as pltpu
from jax.sharding import PartitionSpec as P

ITERS = 3
TILE = 128
NEGATIVE = -1e30

VMEM = pl.BlockSpec(memory_space=pltpu.VMEM)
ANY = pl.BlockSpec(memory_space=pl.ANY)


def swap(x, axis, offset):
    size = lax.axis_size(axis)
    return lax.ppermute(x, axis, [(i, i ^ offset) for i in range(size)])


def pair_sum(terms):
    while len(terms) > 1:
        terms = [terms[i] + terms[i + 1] for i in range(0, len(terms), 2)]
    return terms[0]


def combine(parts):
    peak = functools.reduce(jnp.maximum, parts)
    return peak + jnp.log(pair_sum([jnp.exp(part - peak) for part in parts]))


class Table:
    together = 4

    def __init__(self, row_tiles, columns):
        self.row_tiles, self.columns = row_tiles, columns
        self.line = max(row_tiles, columns) + 8
        self.column_base = row_tiles
        self.pair_base = row_tiles + columns
        self.mask_at = (self.pair_base + columns // 2) * self.line
        self.item_at = self.mask_at + row_tiles * columns
        self.items = (columns // 2) * -(-row_tiles // 4)
        self.slots = self.items + self.together - 1
        self.total_at = self.item_at + 2 * self.slots
        self.dummy = row_tiles * columns

    def build(self, mask):
        across = mask.T
        pairs = jnp.max(across.reshape(self.columns // 2, 2, self.row_tiles), axis=1)
        lines = [self.lines(mask), self.lines(across), self.lines(pairs)]
        flat = [part.reshape(-1) for part in lines] + [mask.reshape(-1)]
        steps = (jnp.sum(pairs, axis=1) + 3) // 4
        at = jnp.arange(self.columns // 2, dtype=jnp.int32)
        first = jnp.sum(jnp.where(at[None, :] < at[:, None], steps[None, :], 0), axis=1)
        total = jnp.sum(steps)
        item = jnp.minimum(jnp.arange(self.slots, dtype=jnp.int32), total - 1)
        pair = jnp.sum(jnp.where(item[:, None] >= (first + steps)[None, :], 1, 0), axis=1)
        step = item - jnp.sum(jnp.where(pair[:, None] == at[None, :], first[None, :], 0), axis=1)
        flat += [(self.pair_base + pair) * self.line + 4 * step, pair]
        rounds = (total + self.together - 1) // self.together
        return jnp.concatenate(flat + [jnp.stack([total, rounds])])

    def each_item(self, ref, visit):
        def several(k, carry):
            for i in range(self.together):
                number = self.together * k + i
                at = ref[self.item_at + number]
                visit(
                    number,
                    number < ref[self.total_at],
                    ref[self.item_at + self.slots + number],
                    [ref[at + n] for n in range(4)],
                )
            return carry

        lax.fori_loop(0, ref[self.total_at + 1], several, 0)

    def empty_bits(self, ref, base, count):
        bits = jnp.int32(0)
        for i in range(count):
            bits = bits + jnp.where(self.steps(ref, base + i, 4) == 0, 1 << i, 0)
        return bits

    def lines(self, mask):
        size = mask.shape[1]
        at = jnp.arange(size, dtype=jnp.int32)
        slot = jnp.arange(self.line, dtype=jnp.int32)
        before = jnp.sum(jnp.where(at[None, :] < at[:, None], mask[:, None, :], 0), axis=2)
        hit = (mask[:, None, :] == 1) & (before[:, None, :] == slot[None, :, None])
        places = jnp.sum(jnp.where(hit, at[None, None, :] - size, 0), axis=2) + size
        count = jnp.sum(mask, axis=1, keepdims=True)
        places = jnp.where(slot[None, :] == self.line - 2, (count + 1) // 2, places)
        return jnp.where(slot[None, :] == self.line - 1, (count + 3) // 4, places)

    def steps(self, ref, line, unroll):
        return ref[line * self.line + self.line - (2 if unroll == 2 else 1)]

    def entry(self, ref, line, k):
        return ref[line * self.line + k]

    def allowed(self, ref, t, u):
        return ref[self.mask_at + t * self.columns + u]

    def loop(self, ref, line, unroll, step, start):
        def several(k, a):
            for i in range(unroll):
                a = step(self.entry(ref, line, unroll * k + i), a)
            return a

        return lax.fori_loop(0, self.steps(ref, line, unroll), several, start)

    def sums(self, ref, base, acc_ref, visit):
        lists = range(acc_ref.shape[0])

        def four(i, k):
            tiles = [visit(i, self.entry(ref, base + i, 4 * k + n)) for n in range(4)]
            return (tiles[0] + tiles[1]) + (tiles[2] + tiles[3])

        for i in lists:
            acc_ref[i] = four(i, 0)
        for i in lists:

            @pl.when(self.steps(ref, base + i, 4) > 1)
            def _(i=i):
                acc_ref[i] = lax.fori_loop(
                    1, self.steps(ref, base + i, 4), lambda k, a: a + four(i, k), acc_ref[i]
                )

    def place(self, t, u):
        padding = (t == self.row_tiles) | (u == self.columns)
        return jnp.where(padding, self.dummy, t * self.columns + u)


def with_table(kernel, table, *settings):
    def body(hbm_ref, *refs):
        *refs, smem_ref, sem = refs
        copy = pltpu.make_async_copy(hbm_ref, smem_ref, sem)
        copy.start()

        def arrived():
            copy.wait()
            return smem_ref

        kernel(table, *settings, arrived, *refs)

    return body


def table_scratch(lists):
    return [pltpu.SMEM(lists.shape, jnp.int32), pltpu.SemaphoreType.DMA]


def blank():
    return jnp.zeros((TILE, TILE), jnp.float32)


def lowest():
    return jnp.full((TILE, TILE), NEGATIVE, jnp.float32)


def bad_bits(good):
    bad = jnp.max(jnp.where(good, 0.0, 1.0), axis=1, keepdims=True)
    bit = jnp.left_shift(1, lax.broadcasted_iota(jnp.int32, bad.shape, 0))
    return jnp.sum(bad * bit.astype(jnp.float32)).astype(jnp.int32)


def in_range(totals, factor):
    largest = jnp.max(jnp.max(factor, axis=1, keepdims=True), axis=0, keepdims=True)
    return (totals > 1e-15) & (totals < 1e30) & (largest < 1e15)


def has_bit(bits, i):
    return jnp.bitwise_and(bits, 1 << i) != 0


def spread_rows(row, wide_ref):
    row_tiles = row.shape[0]
    standing = jnp.concatenate(
        [row, jnp.zeros((TILE - row_tiles, TILE), jnp.float32)], axis=0
    ).T
    for t in range(row_tiles):
        wide_ref[t] = jnp.broadcast_to(standing[:, t : t + 1], (TILE, TILE))


def lying(tiles):
    lane = lax.broadcasted_iota(jnp.int32, (TILE, TILE), 1)
    found = blank()
    for t, tile in enumerate(tiles):
        found = jnp.where(lane == t, jnp.sum(tile, axis=1, keepdims=True), found)
    return found.T[: len(tiles)]


class Piece:
    def __init__(self, own, first, owner):
        self.own, self.first, self.owner = own, first, owner

    def copy_to(self, p_ref, piece):
        core, me = lax.rem(lax.axis_index("proto"), 2), lax.axis_index("row")
        rows, width = piece.shape
        first = (core if self.own else 1 - core) * (p_ref.shape[0] // 2) + self.first
        start = 0
        if self.owner is not None:
            start = pl.multiple_of(jnp.bitwise_xor(me, self.owner) * width, TILE)
        p_ref[pl.ds(pl.multiple_of(first, TILE), rows), pl.ds(start, width)] = piece[...]


def score_pairs(table, table_ref, e_ref, p_ref, s_ref, features, add, done):
    row_tiles, columns = table.row_tiles, table.columns
    scale = 4.0 / math.sqrt(e_ref.shape[1])

    def visit(number, real, pair, tiles):
        at = [jnp.minimum(t, row_tiles - 1) for t in tiles]
        product = None
        for span in features(pair):
            rows = jnp.concatenate(
                [e_ref[pl.ds(pl.multiple_of(t * TILE, TILE), TILE), span] for t in at], axis=0
            )
            block = p_ref[pl.ds(pl.multiple_of(pair * 2 * TILE, TILE), 2 * TILE), span]
            part = lax.dot_general(
                rows, block, (((1,), (1,)), ((), ())), preferred_element_type=jnp.float32
            )
            product = part if product is None else product + part
        product = (jnp.where(real, scale, 0.0) if add else scale) * product
        found = {}
        for i, t in enumerate(at):
            for side in range(2):
                where = t * columns + 2 * pair + side
                tile = product[i * TILE : (i + 1) * TILE, side * TILE : (side + 1) * TILE]
                found[i, side] = (where, s_ref[where] + tile if add else tile)
        for where, tile in found.values():
            s_ref[where] = tile
        if done is not None:
            for i, t in enumerate(at):
                done(t, 2 * pair, found[i, 0][1], found[i, 1][1])

    table.each_item(table_ref, visit)


def quarters(owners, p_ref):
    me = lax.axis_index("row")
    width = p_ref.shape[1] // 4

    def features(pair):
        return [pl.ds(pl.multiple_of(jnp.bitwise_xor(me, owner) * width, TILE), width) for owner in owners]

    return features


def early_panel_kernel(table, places, owners, add, arrived, e_ref, *refs):
    pieces, (s_ref, p_ref) = refs[:-2], refs[-2:]
    for place, piece in zip(places, pieces):
        place.copy_to(p_ref, piece)
    if not add:
        s_ref[table.dummy] = lowest()
    features = quarters(owners, p_ref)
    score_pairs(table, arrived(), e_ref, p_ref, s_ref, features, add, None)


def panel_kernel(table, places, add, arrived, e_ref, *refs):
    pieces, (s_ref, p_ref, w_ref, first_ref, out_ref, acc_ref, wide_ref) = refs[:-7], refs[-7:]
    if add:
        pieces = pieces[:-2]
    row_tiles = table.row_tiles
    for place, piece in zip(places, pieces):
        place.copy_to(p_ref, piece)
    for t in range(row_tiles):
        acc_ref[t] = lowest()
    table_ref = arrived()

    def done(t, u, left, right):
        peak = acc_ref[t]
        for side, tile in enumerate((left, right)):
            off = jnp.where(table.allowed(table_ref, t, u + side) == 1, 0.0, NEGATIVE)
            peak = jnp.maximum(peak, tile + off)
        acc_ref[t] = peak

    if add:
        features = quarters([3], p_ref)
    else:
        s_ref[table.dummy] = lowest()
        features = lambda pair: [slice(None)]
    score_pairs(table, table_ref, e_ref, p_ref, s_ref, features, add, done)

    lane = lax.broadcasted_iota(jnp.int32, (TILE, TILE), 1)
    peaks = blank()
    for t in range(row_tiles):
        peak = jnp.max(acc_ref[t], axis=1, keepdims=True)
        peaks = jnp.where(lane == t, peak, peaks)
        wide_ref[t] = jnp.broadcast_to(peak, (TILE, TILE))
    w_ref[table.dummy] = blank().astype(jnp.bfloat16)

    def visit(t, u):
        at = table.place(t, u)
        value = jnp.exp(s_ref[at] - wide_ref[t])
        w_ref[at] = value.astype(jnp.bfloat16)
        return value

    table.sums(table_ref, 0, acc_ref, visit)
    peaks = peaks.T[:row_tiles]
    first_ref[...] = -peaks
    out_ref[...] = peaks + jnp.log(lying([acc_ref[t] for t in range(row_tiles)]))


def row_kernel(table, log_column, arrived, s_ref, w_ref, first_ref, *refs):
    parts, (out_ref, c_ref, v_ref, acc_ref) = refs[:-4], refs[-4:]
    row_tiles, columns = table.row_tiles, table.columns
    column = log_column - combine([part[...] for part in parts])
    factor = jnp.exp(column)
    c_ref[:columns] = column
    v_ref[:columns] = factor
    rest = jnp.zeros((c_ref.shape[0] - columns, TILE), jnp.float32)
    c_ref[columns:] = rest
    v_ref[columns:] = rest
    table_ref = arrived()

    def visit(t, u):
        return w_ref[table.place(t, u)].astype(jnp.float32) * v_ref[pl.ds(u, 1), :]

    table.sums(table_ref, 0, acc_ref, visit)
    totals = lying([acc_ref[t] for t in range(row_tiles)])
    out_ref[...] = jnp.log(totals) - first_ref[...]
    bits = bad_bits(in_range(totals, factor)) - table.empty_bits(table_ref, 0, row_tiles)

    @pl.when(bits != 0)
    def _():
        for t in range(row_tiles):

            @pl.when(has_bit(bits, t))
            def _():
                def score(u):
                    return s_ref[table.place(t, u)] + c_ref[pl.ds(u, 1), :]

                peak = table.loop(table_ref, t, 2, lambda u, a: jnp.maximum(a, score(u)), lowest())
                peak = jnp.max(peak, axis=1, keepdims=True)
                total = table.loop(table_ref, t, 2, lambda u, a: a + jnp.exp(score(u) - peak), blank())
                found = peak + jnp.log(jnp.sum(total, axis=1, keepdims=True))
                out_ref[t : t + 1, :] = jnp.broadcast_to(found, (TILE, TILE)).T[:1]


def column_kernel(table, arrived, s_ref, w_ref, first_ref, *refs):
    parts, (out_ref, r_ref, r_out_ref, wide_ref, acc_ref) = refs[:-5], refs[-5:]
    row = -combine([part[...] for part in parts])
    r_ref[...] = row
    r_out_ref[...] = row
    factor = jnp.exp(row - first_ref[...])
    spread_rows(factor, wide_ref)
    table_ref = arrived()

    def visit(u, t):
        kept = w_ref[table.place(t, u)].astype(jnp.float32)
        return kept * wide_ref[jnp.minimum(t, table.row_tiles - 1)]

    table.sums(table_ref, table.column_base, acc_ref, visit)
    totals = jnp.concatenate(
        [jnp.sum(acc_ref[u], axis=0, keepdims=True) for u in range(table.columns)], axis=0
    )
    out_ref[...] = jnp.log(totals)
    bits = bad_bits(in_range(totals, factor)) - table.empty_bits(table_ref, table.column_base, table.columns)

    @pl.when(bits != 0)
    def _():
        spread_rows(row, wide_ref)
        for u in range(table.columns):

            @pl.when(has_bit(bits, u))
            def _():
                line = table.column_base + u

                def score(t):
                    return s_ref[table.place(t, u)] + wide_ref[jnp.minimum(t, table.row_tiles - 1)]

                peak = table.loop(table_ref, line, 2, lambda t, a: jnp.maximum(a, score(t)), lowest())
                peak = jnp.max(peak, axis=0, keepdims=True)
                total = table.loop(table_ref, line, 2, lambda t, a: a + jnp.exp(score(t) - peak), blank())
                out_ref[u : u + 1, :] = peak + jnp.log(jnp.sum(total, axis=0, keepdims=True))


def plan_blocks(table, table_ref, p_ref, lines, wanted, width, strip, outs, total_ref):
    row_tiles = table.row_tiles
    index = lax.axis_index("proto")
    core, z = lax.rem(index, 2), lax.div(index, 2)
    fits = width % TILE == 0
    total_ref[...] = jnp.zeros(total_ref.shape, jnp.float32)

    def visit(number, real, pair, tiles):
        first = pl.multiple_of(pair * 2 * TILE, TILE)
        blocks = []
        for j in wanted if fits else range(lines):
            if fits:
                start = (2 * jnp.bitwise_xor(z, j) + core) * width
                blocks.append(p_ref[pl.ds(first, 2 * TILE), pl.ds(pl.multiple_of(start, TILE), width)])
            else:
                both = p_ref[pl.ds(first, 2 * TILE), 2 * j * width : 2 * (j + 1) * width]
                blocks.append(jnp.where(core == 0, both[:, :width], both[:, width:]))
        product = jnp.dot(
            strip(number, real, pair, tiles),
            jnp.concatenate(blocks, axis=1),
            preferred_element_type=jnp.float32,
        )
        for i, t in enumerate(tiles):
            total_ref[jnp.minimum(t, row_tiles - 1)] += product[i * TILE : (i + 1) * TILE]

    table.each_item(table_ref, visit)
    for t in range(row_tiles):
        total = total_ref[t].astype(jnp.bfloat16)
        rows = slice(t * TILE, (t + 1) * TILE)
        for n, j in enumerate(wanted):
            if fits:
                outs[n][rows, :] = total[:, n * width : (n + 1) * width]
                continue
            for k in range(lines):

                @pl.when(jnp.bitwise_xor(z, j) == k)
                def _():
                    outs[n][rows, :] = total[:, k * width : (k + 1) * width]


def plan_kernel(table, log_column, lines, arrived, s_ref, r_ref, p_ref, *refs):
    parts, (out_ref, kept_ref, own_ref, c_ref, wide_ref, total_ref) = refs[:-6], refs[-6:]
    row_tiles, columns = table.row_tiles, table.columns
    core = lax.rem(lax.axis_index("proto"), 2)
    c_ref[...] = log_column - combine([part[...] for part in parts])
    half = columns // 2
    own_ref[...] = c_ref[pl.ds(pl.multiple_of(core * half, half), half), :]
    spread_rows(r_ref[...], wide_ref)
    table_ref = arrived()

    def strip(number, real, pair, tiles):
        strips = []
        for t in tiles:
            inside = jnp.minimum(t, row_tiles - 1)
            sides = []
            for side in range(2):
                u = 2 * pair + side
                good = real & (t < row_tiles) & (table.allowed(table_ref, inside, u) == 1)
                tile = s_ref[jnp.where(good, t * columns + u, table.dummy)]
                sides.append(jnp.exp(tile + wide_ref[inside] + c_ref[pl.ds(u, 1), :]).astype(jnp.bfloat16))
            strips.append(jnp.concatenate(sides, axis=1))
        strips = jnp.concatenate(strips, axis=0)
        kept_ref[number] = strips
        return strips

    width = out_ref.shape[1]
    plan_blocks(table, table_ref, p_ref, lines, [lines - 1], width, strip, [out_ref], total_ref)


def rest_kernel(table, lines, arrived, kept_ref, p_ref, *refs):
    outs, total_ref = refs[:-1], refs[-1]
    width = outs[0].shape[1]
    strip = lambda number, real, pair, tiles: kept_ref[number]
    plan_blocks(table, arrived(), p_ref, lines, list(range(lines - 1)), width, strip, outs, total_ref)


def params(mebibytes):
    return pltpu.CompilerParams(vmem_limit_bytes=mebibytes * 2**20)


def sibling(block):
    return swap(block, "proto", 1)


def tied(*arrays):
    return lax.optimization_barrier(arrays)


def make_panel(table, mask, embeddings, shard, rows, features):
    width = shard.shape[1]
    protos = 2 * shard.shape[0]
    panel = pltpu.VMEM((table.dummy + 1, TILE, TILE), jnp.float32)
    whole = pltpu.VMEM((protos, features), jnp.bfloat16)
    row_shape = jax.ShapeDtypeStruct((table.row_tiles, TILE), jnp.float32)
    kept = pltpu.VMEM((table.dummy + 1, TILE, TILE), jnp.bfloat16)
    tiles = pltpu.VMEM((table.row_tiles, TILE, TILE), jnp.float32)

    def late(lists, places, add, e, pieces, before):
        at = 2 + len(pieces)
        return pl.pallas_call(
            with_table(panel_kernel, table, places, add),
            out_shape=(panel, whole, kept, row_shape, row_shape),
            in_specs=[ANY] + [VMEM] * (1 + len(pieces) + len(before)),
            out_specs=(VMEM,) * 5,
            scratch_shapes=[tiles, tiles] + table_scratch(lists),
            input_output_aliases={at: 0, at + 1: 1} if add else {},
            compiler_params=params(8),
            name="panel",
        )(lists, e, *pieces, *before)

    if lax.axis_size("row") != 4 or width % TILE:
        lists = table.build(mask)
        every = lax.all_gather(shard, "row", axis=1, tiled=True)
        places = [Piece(True, 0, None), Piece(False, 0, None)]
        return (lists, *late(lists, places, False, embeddings, [every, sibling(every)], []))
    half = shard.shape[0] // 2
    visits = table.dummy * TILE * TILE

    def early(lists, places, owners, pieces, before):
        at = 2 + len(pieces)
        return pl.pallas_call(
            with_table(early_panel_kernel, table, places, owners, bool(before)),
            out_shape=(panel, whole),
            in_specs=[ANY] + [VMEM] * (1 + len(pieces) + len(before)),
            out_specs=(VMEM, VMEM),
            scratch_shapes=table_scratch(lists),
            input_output_aliases={at: 0, at + 1: 1} if before else {},
            compiler_params=params(6),
            cost_estimate=pl.CostEstimate(
                flops=visits * width * len(owners), bytes_accessed=8 * visits, transcendentals=0
            ),
            name="early_panel",
        )(lists, embeddings, *pieces, *before)

    near = swap(shard, "row", 1)
    far = swap(shard, "row", 2)
    lists = table.build(mask)
    places = [Piece(True, 0, 0), Piece(False, 0, 0)]
    similar, known = early(lists, places, [0], [shard, sibling(shard)], [])
    near, far, similar, known = tied(near, far, similar, known)
    cross_top = swap(far[:half], "row", 1)
    cross_bottom = swap(near[half:], "row", 2)
    places = [Piece(own, 0, owner) for own in (True, False) for owner in (1, 2)]
    pieces = [near, far, sibling(near), sibling(far)]
    similar, known = early(lists, places, [1, 2], pieces, [similar, known])
    cross_top, cross_bottom, similar, known = tied(cross_top, cross_bottom, similar, known)
    places = [Piece(own, first, 3) for own in (True, False) for first in (0, half)]
    pieces = [cross_top, cross_bottom, sibling(cross_top), sibling(cross_bottom)]
    return (lists, *late(lists, places, True, embeddings, pieces, [similar, known]))


def scatter_partials(blocks):
    total = blocks[0].astype(jnp.float32)
    for j in range(len(blocks) - 1, 0, -1):
        total = total + swap(blocks[j].astype(jnp.bfloat16), "proto", 2 * j).astype(jnp.float32)
    return total.astype(jnp.bfloat16)


def shards(embeddings, prototypes, block_mask):
    n_row, n_proto = lax.axis_size("row"), lax.axis_size("proto")
    lines = n_proto // 2
    rows, features = embeddings.shape
    protos = 2 * prototypes.shape[0]
    width = features // n_proto
    row_tiles, columns = block_mask.shape[0], 2 * block_mask.shape[1]
    log_column = math.log(rows * n_row / (protos * lines))
    table = Table(row_tiles, columns)

    other_mask = swap(block_mask, "proto", 1)
    mask, other_mask = jnp.where(block_mask == 1, 1, 0), jnp.where(other_mask == 1, 1, 0)
    mask = jnp.where(
        lax.axis_index("proto") % 2 == 0,
        jnp.concatenate([mask, other_mask], axis=1),
        jnp.concatenate([other_mask, mask], axis=1),
    )

    row_shape = jax.ShapeDtypeStruct((row_tiles, TILE), jnp.float32)
    column_shape = jax.ShapeDtypeStruct((columns, TILE), jnp.float32)
    half = columns // 2
    wide = pltpu.VMEM((row_tiles, TILE, TILE), jnp.float32)
    tall = pltpu.VMEM((columns, TILE, TILE), jnp.float32)
    factors = pltpu.VMEM((columns + 8, TILE), jnp.float32)
    lists, similar, whole, kept, first, row_part = make_panel(table, mask, embeddings, prototypes, rows, features)

    def row_exchange(part):
        others = [swap(part, "proto", 2 * j) for j in range(lines - 1, 0, -1)]
        return [part] + others[::-1]

    def column_exchange(part):
        others = [swap(part, "row", j) for j in range(n_row - 1, 0, -1)]
        return [part] + others[::-1]

    for sweep in range(ITERS):
        if sweep:
            parts = column_exchange(column_part)
            row_part = pl.pallas_call(
                with_table(row_kernel, table, log_column),
                out_shape=row_shape,
                in_specs=[ANY] + [VMEM] * (3 + len(parts)),
                out_specs=VMEM,
                scratch_shapes=[factors, factors, wide] + table_scratch(lists),
                compiler_params=params(4),
                name="row_pass",
            )(lists, similar, kept, first, *parts)
        parts = row_exchange(row_part)
        column_part, row_potential, row_out = pl.pallas_call(
            with_table(column_kernel, table),
            out_shape=(column_shape, row_shape, row_shape),
            in_specs=[ANY] + [VMEM] * (3 + len(parts)),
            out_specs=(VMEM,) * 3,
            scratch_shapes=[wide, tall] + table_scratch(lists),
            compiler_params=params(4),
            name="column_pass",
        )(lists, similar, kept, first, *parts)
    parts = column_exchange(column_part)
    block = jax.ShapeDtypeStruct((rows, width), jnp.bfloat16)

    def sums(blocks):
        taken = blocks if width % TILE == 0 else lines
        return pltpu.VMEM((row_tiles, TILE, taken * width), jnp.float32)

    last, plan, column_potential = pl.pallas_call(
        with_table(plan_kernel, table, log_column, lines),
        out_shape=[
            block,
            pltpu.VMEM((table.slots, 4 * TILE, 2 * TILE), jnp.bfloat16),
            jax.ShapeDtypeStruct((half, TILE), jnp.float32),
        ],
        in_specs=[ANY] + [VMEM] * (3 + len(parts)),
        out_specs=[VMEM] * 3,
        scratch_shapes=[pltpu.VMEM((columns, TILE), jnp.float32), wide, sums(1)] + table_scratch(lists),
        compiler_params=params(12),
        name="plan",
    )(lists, similar, row_potential, whole, *parts)
    visits = table.dummy * TILE * TILE
    blocks = pl.pallas_call(
        with_table(rest_kernel, table, lines),
        out_shape=[block] * (lines - 1),
        in_specs=[ANY] + [VMEM] * 2,
        out_specs=[VMEM] * (lines - 1),
        scratch_shapes=[sums(lines - 1)] + table_scratch(lists),
        compiler_params=params(12),
        cost_estimate=pl.CostEstimate(
            flops=2 * visits * (lines - 1) * width, bytes_accessed=4 * visits, transcendentals=0
        ),
        name="rest_of_plan",
    )(lists, plan, whole)
    blocks = list(blocks) + [last]
    targets = scatter_partials(blocks)
    return (targets, row_out.reshape(rows), column_potential.reshape(protos // 2))


def solution(mesh):
    return jax.shard_map(
        shards,
        mesh=mesh,
        in_specs=(P("row", None), P("proto", "row"), P("row", "proto")),
        out_specs=(P("row", "proto"), P("row"), P("proto")),
        check_vma=False,
    )
```

```python
import functools
import math

import jax
import jax.numpy as jnp
from jax import lax
from jax.experimental import pallas as pl
from jax.experimental.pallas import tpu as pltpu
from jax.sharding import PartitionSpec as P

ITERS = 3
TILE = 128
NEGATIVE = -1e30

VMEM = pl.BlockSpec(memory_space=pltpu.VMEM)
ANY = pl.BlockSpec(memory_space=pl.ANY)


def swap(x, axis, offset):
    size = lax.axis_size(axis)
    return lax.ppermute(x, axis, [(i, i ^ offset) for i in range(size)])


def pair_sum(terms):
    while len(terms) > 1:
        terms = [terms[i] + terms[i + 1] for i in range(0, len(terms), 2)]
    return terms[0]


def combine(parts):
    peak = functools.reduce(jnp.maximum, parts)
    return peak + jnp.log(pair_sum([jnp.exp(part - peak) for part in parts]))


class Table:
    together = 6

    def __init__(self, row_tiles, columns):
        self.row_tiles, self.columns = row_tiles, columns
        self.line = max(row_tiles, columns) + 8
        self.column_base = row_tiles
        self.pair_base = row_tiles + columns
        self.mask_at = (self.pair_base + columns // 2) * self.line
        self.item_at = self.mask_at + row_tiles * columns
        self.items = (columns // 2) * -(-row_tiles // 4)
        self.slots = self.items + self.together - 1
        self.total_at = self.item_at + 2 * self.slots
        self.dummy = row_tiles * columns

    def build(self, mask):
        across = mask.T
        pairs = jnp.max(across.reshape(self.columns // 2, 2, self.row_tiles), axis=1)
        lines = [self.lines(mask), self.lines(across), self.lines(pairs)]
        flat = [part.reshape(-1) for part in lines] + [mask.reshape(-1)]
        steps = (jnp.sum(pairs, axis=1) + 3) // 4
        at = jnp.arange(self.columns // 2, dtype=jnp.int32)
        first = jnp.sum(jnp.where(at[None, :] < at[:, None], steps[None, :], 0), axis=1)
        total = jnp.sum(steps)
        item = jnp.minimum(jnp.arange(self.slots, dtype=jnp.int32), total - 1)
        pair = jnp.sum(jnp.where(item[:, None] >= (first + steps)[None, :], 1, 0), axis=1)
        step = item - jnp.sum(jnp.where(pair[:, None] == at[None, :], first[None, :], 0), axis=1)
        flat += [(self.pair_base + pair) * self.line + 4 * step, pair]
        rounds = (total + self.together - 1) // self.together
        return jnp.concatenate(flat + [jnp.stack([total, rounds])])

    def each_item(self, ref, visit):
        def several(k, carry):
            for i in range(self.together):
                number = self.together * k + i
                at = ref[self.item_at + number]
                visit(
                    number,
                    number < ref[self.total_at],
                    ref[self.item_at + self.slots + number],
                    [ref[at + n] for n in range(4)],
                )
            return carry

        lax.fori_loop(0, ref[self.total_at + 1], several, 0)

    def empty_bits(self, ref, base, count):
        bits = jnp.int32(0)
        for i in range(count):
            bits = bits + jnp.where(self.steps(ref, base + i, 4) == 0, 1 << i, 0)
        return bits

    def lines(self, mask):
        size = mask.shape[1]
        at = jnp.arange(size, dtype=jnp.int32)
        slot = jnp.arange(self.line, dtype=jnp.int32)
        before = jnp.sum(jnp.where(at[None, :] < at[:, None], mask[:, None, :], 0), axis=2)
        hit = (mask[:, None, :] == 1) & (before[:, None, :] == slot[None, :, None])
        places = jnp.sum(jnp.where(hit, at[None, None, :] - size, 0), axis=2) + size
        count = jnp.sum(mask, axis=1, keepdims=True)
        places = jnp.where(slot[None, :] == self.line - 2, (count + 1) // 2, places)
        return jnp.where(slot[None, :] == self.line - 1, (count + 3) // 4, places)

    def steps(self, ref, line, unroll):
        return ref[line * self.line + self.line - (2 if unroll == 2 else 1)]

    def entry(self, ref, line, k):
        return ref[line * self.line + k]

    def allowed(self, ref, t, u):
        return ref[self.mask_at + t * self.columns + u]

    def loop(self, ref, line, unroll, step, start):
        def several(k, a):
            for i in range(unroll):
                a = step(self.entry(ref, line, unroll * k + i), a)
            return a

        return lax.fori_loop(0, self.steps(ref, line, unroll), several, start)

    def sums(self, ref, base, acc_ref, visit):
        lists = range(acc_ref.shape[0])

        def four(i, k):
            tiles = [visit(i, self.entry(ref, base + i, 4 * k + n)) for n in range(4)]
            return (tiles[0] + tiles[1]) + (tiles[2] + tiles[3])

        for i in lists:
            acc_ref[i] = four(i, 0)
        for i in lists:

            @pl.when(self.steps(ref, base + i, 4) > 1)
            def _(i=i):
                acc_ref[i] = lax.fori_loop(
                    1, self.steps(ref, base + i, 4), lambda k, a: a + four(i, k), acc_ref[i]
                )

    def place(self, t, u):
        padding = (t == self.row_tiles) | (u == self.columns)
        return jnp.where(padding, self.dummy, t * self.columns + u)


def with_table(kernel, table, *settings):
    def body(hbm_ref, *refs):
        *refs, smem_ref, sem = refs
        copy = pltpu.make_async_copy(hbm_ref, smem_ref, sem)
        copy.start()

        def arrived():
            copy.wait()
            return smem_ref

        kernel(table, *settings, arrived, *refs)

    return body


def table_scratch(lists):
    return [pltpu.SMEM(lists.shape, jnp.int32), pltpu.SemaphoreType.DMA]


def blank():
    return jnp.zeros((TILE, TILE), jnp.float32)


def lowest():
    return jnp.full((TILE, TILE), NEGATIVE, jnp.float32)


def bad_bits(good):
    bad = jnp.max(jnp.where(good, 0.0, 1.0), axis=1, keepdims=True)
    bit = jnp.left_shift(1, lax.broadcasted_iota(jnp.int32, bad.shape, 0))
    return jnp.sum(bad * bit.astype(jnp.float32)).astype(jnp.int32)


def in_range(totals, factor):
    largest = jnp.max(jnp.max(factor, axis=1, keepdims=True), axis=0, keepdims=True)
    return (totals > 1e-15) & (totals < 1e30) & (largest < 1e15)


def has_bit(bits, i):
    return jnp.bitwise_and(bits, 1 << i) != 0


def spread_rows(row, wide_ref):
    row_tiles = row.shape[0]
    standing = jnp.concatenate(
        [row, jnp.zeros((TILE - row_tiles, TILE), jnp.float32)], axis=0
    ).T
    for t in range(row_tiles):
        wide_ref[t] = jnp.broadcast_to(standing[:, t : t + 1], (TILE, TILE))


def lying(tiles):
    lane = lax.broadcasted_iota(jnp.int32, (TILE, TILE), 1)
    found = blank()
    for t, tile in enumerate(tiles):
        found = jnp.where(lane == t, jnp.sum(tile, axis=1, keepdims=True), found)
    return found.T[: len(tiles)]


class Piece:
    def __init__(self, own, first, owner):
        self.own, self.first, self.owner = own, first, owner

    def copy_to(self, p_ref, piece):
        core, me = lax.rem(lax.axis_index("proto"), 2), lax.axis_index("row")
        rows, width = piece.shape
        first = (core if self.own else 1 - core) * (p_ref.shape[0] // 2) + self.first
        start = 0
        if self.owner is not None:
            start = pl.multiple_of(jnp.bitwise_xor(me, self.owner) * width, TILE)
        p_ref[pl.ds(pl.multiple_of(first, TILE), rows), pl.ds(start, width)] = piece[...]


def score_pairs(table, table_ref, e_ref, p_ref, s_ref, features, add, done):
    row_tiles, columns = table.row_tiles, table.columns
    scale = 4.0 / math.sqrt(e_ref.shape[1])

    def visit(number, real, pair, tiles):
        at = [jnp.minimum(t, row_tiles - 1) for t in tiles]
        product = None
        for span in features(pair):
            rows = jnp.concatenate(
                [e_ref[pl.ds(pl.multiple_of(t * TILE, TILE), TILE), span] for t in at], axis=0
            )
            block = p_ref[pl.ds(pl.multiple_of(pair * 2 * TILE, TILE), 2 * TILE), span]
            part = lax.dot_general(
                rows, block, (((1,), (1,)), ((), ())), preferred_element_type=jnp.float32
            )
            product = part if product is None else product + part
        product = (jnp.where(real, scale, 0.0) if add else scale) * product
        found = {}
        for i, t in enumerate(at):
            for side in range(2):
                where = t * columns + 2 * pair + side
                tile = product[i * TILE : (i + 1) * TILE, side * TILE : (side + 1) * TILE]
                found[i, side] = (where, s_ref[where] + tile if add else tile)
        for where, tile in found.values():
            s_ref[where] = tile
        if done is not None:
            for i, t in enumerate(at):
                done(t, 2 * pair, found[i, 0][1], found[i, 1][1])

    table.each_item(table_ref, visit)


def quarters(owners, p_ref):
    me = lax.axis_index("row")
    width = p_ref.shape[1] // 4

    def features(pair):
        return [pl.ds(pl.multiple_of(jnp.bitwise_xor(me, owner) * width, TILE), width) for owner in owners]

    return features


def early_panel_kernel(table, places, owners, add, arrived, e_ref, *refs):
    pieces, (s_ref, p_ref) = refs[:-2], refs[-2:]
    for place, piece in zip(places, pieces):
        place.copy_to(p_ref, piece)
    if not add:
        s_ref[table.dummy] = lowest()
    features = quarters(owners, p_ref)
    score_pairs(table, arrived(), e_ref, p_ref, s_ref, features, add, None)


def panel_kernel(table, places, add, arrived, e_ref, *refs):
    pieces, (s_ref, p_ref, w_ref, first_ref, out_ref, acc_ref, wide_ref) = refs[:-7], refs[-7:]
    if add:
        pieces = pieces[:-2]
    row_tiles = table.row_tiles
    for place, piece in zip(places, pieces):
        place.copy_to(p_ref, piece)
    for t in range(row_tiles):
        acc_ref[t] = lowest()
    table_ref = arrived()

    def done(t, u, left, right):
        peak = acc_ref[t]
        for side, tile in enumerate((left, right)):
            off = jnp.where(table.allowed(table_ref, t, u + side) == 1, 0.0, NEGATIVE)
            peak = jnp.maximum(peak, tile + off)
        acc_ref[t] = peak

    if add:
        features = quarters([3], p_ref)
    else:
        s_ref[table.dummy] = lowest()
        features = lambda pair: [slice(None)]
    score_pairs(table, table_ref, e_ref, p_ref, s_ref, features, add, done)

    lane = lax.broadcasted_iota(jnp.int32, (TILE, TILE), 1)
    peaks = blank()
    for t in range(row_tiles):
        peak = jnp.max(acc_ref[t], axis=1, keepdims=True)
        peaks = jnp.where(lane == t, peak, peaks)
        wide_ref[t] = jnp.broadcast_to(peak, (TILE, TILE))
    w_ref[table.dummy] = blank().astype(jnp.bfloat16)

    def visit(t, u):
        at = table.place(t, u)
        value = jnp.exp(s_ref[at] - wide_ref[t])
        w_ref[at] = value.astype(jnp.bfloat16)
        return value

    table.sums(table_ref, 0, acc_ref, visit)
    peaks = peaks.T[:row_tiles]
    first_ref[...] = -peaks
    out_ref[...] = peaks + jnp.log(lying([acc_ref[t] for t in range(row_tiles)]))


def row_kernel(table, log_column, arrived, s_ref, w_ref, first_ref, *refs):
    parts, (out_ref, c_ref, v_ref, acc_ref) = refs[:-4], refs[-4:]
    row_tiles, columns = table.row_tiles, table.columns
    column = log_column - combine([part[...] for part in parts])
    factor = jnp.exp(column)
    c_ref[:columns] = column
    v_ref[:columns] = factor
    rest = jnp.zeros((c_ref.shape[0] - columns, TILE), jnp.float32)
    c_ref[columns:] = rest
    v_ref[columns:] = rest
    table_ref = arrived()

    def visit(t, u):
        return w_ref[table.place(t, u)].astype(jnp.float32) * v_ref[pl.ds(u, 1), :]

    table.sums(table_ref, 0, acc_ref, visit)
    totals = lying([acc_ref[t] for t in range(row_tiles)])
    out_ref[...] = jnp.log(totals) - first_ref[...]
    bits = bad_bits(in_range(totals, factor)) - table.empty_bits(table_ref, 0, row_tiles)

    @pl.when(bits != 0)
    def _():
        for t in range(row_tiles):

            @pl.when(has_bit(bits, t))
            def _():
                def score(u):
                    return s_ref[table.place(t, u)] + c_ref[pl.ds(u, 1), :]

                peak = table.loop(table_ref, t, 2, lambda u, a: jnp.maximum(a, score(u)), lowest())
                peak = jnp.max(peak, axis=1, keepdims=True)
                total = table.loop(table_ref, t, 2, lambda u, a: a + jnp.exp(score(u) - peak), blank())
                found = peak + jnp.log(jnp.sum(total, axis=1, keepdims=True))
                out_ref[t : t + 1, :] = jnp.broadcast_to(found, (TILE, TILE)).T[:1]


def column_kernel(table, arrived, s_ref, w_ref, first_ref, *refs):
    parts, (out_ref, r_ref, r_out_ref, wide_ref, acc_ref) = refs[:-5], refs[-5:]
    row = -combine([part[...] for part in parts])
    r_ref[...] = row
    r_out_ref[...] = row
    factor = jnp.exp(row - first_ref[...])
    spread_rows(factor, wide_ref)
    table_ref = arrived()

    def visit(u, t):
        kept = w_ref[table.place(t, u)].astype(jnp.float32)
        return kept * wide_ref[jnp.minimum(t, table.row_tiles - 1)]

    table.sums(table_ref, table.column_base, acc_ref, visit)
    totals = jnp.concatenate(
        [jnp.sum(acc_ref[u], axis=0, keepdims=True) for u in range(table.columns)], axis=0
    )
    out_ref[...] = jnp.log(totals)
    bits = bad_bits(in_range(totals, factor)) - table.empty_bits(table_ref, table.column_base, table.columns)

    @pl.when(bits != 0)
    def _():
        spread_rows(row, wide_ref)
        for u in range(table.columns):

            @pl.when(has_bit(bits, u))
            def _():
                line = table.column_base + u

                def score(t):
                    return s_ref[table.place(t, u)] + wide_ref[jnp.minimum(t, table.row_tiles - 1)]

                peak = table.loop(table_ref, line, 2, lambda t, a: jnp.maximum(a, score(t)), lowest())
                peak = jnp.max(peak, axis=0, keepdims=True)
                total = table.loop(table_ref, line, 2, lambda t, a: a + jnp.exp(score(t) - peak), blank())
                out_ref[u : u + 1, :] = peak + jnp.log(jnp.sum(total, axis=0, keepdims=True))


def plan_blocks(table, table_ref, p_ref, lines, wanted, width, strip, outs, total_ref):
    row_tiles = table.row_tiles
    index = lax.axis_index("proto")
    core, z = lax.rem(index, 2), lax.div(index, 2)
    fits = width % TILE == 0
    total_ref[...] = jnp.zeros(total_ref.shape, jnp.float32)

    def visit(number, real, pair, tiles):
        first = pl.multiple_of(pair * 2 * TILE, TILE)
        blocks = []
        for j in wanted if fits else range(lines):
            if fits:
                start = (2 * jnp.bitwise_xor(z, j) + core) * width
                blocks.append(p_ref[pl.ds(first, 2 * TILE), pl.ds(pl.multiple_of(start, TILE), width)])
            else:
                both = p_ref[pl.ds(first, 2 * TILE), 2 * j * width : 2 * (j + 1) * width]
                blocks.append(jnp.where(core == 0, both[:, :width], both[:, width:]))
        product = jnp.dot(
            strip(number, real, pair, tiles),
            jnp.concatenate(blocks, axis=1),
            preferred_element_type=jnp.float32,
        )
        for i, t in enumerate(tiles):
            total_ref[jnp.minimum(t, row_tiles - 1)] += product[i * TILE : (i + 1) * TILE]

    table.each_item(table_ref, visit)
    for t in range(row_tiles):
        total = total_ref[t].astype(jnp.bfloat16)
        rows = slice(t * TILE, (t + 1) * TILE)
        for n, j in enumerate(wanted):
            if fits:
                outs[n][rows, :] = total[:, n * width : (n + 1) * width]
                continue
            for k in range(lines):

                @pl.when(jnp.bitwise_xor(z, j) == k)
                def _():
                    outs[n][rows, :] = total[:, k * width : (k + 1) * width]


def plan_kernel(table, log_column, lines, arrived, s_ref, r_ref, p_ref, *refs):
    parts, (out_ref, kept_ref, own_ref, c_ref, wide_ref, total_ref) = refs[:-6], refs[-6:]
    row_tiles, columns = table.row_tiles, table.columns
    core = lax.rem(lax.axis_index("proto"), 2)
    c_ref[...] = log_column - combine([part[...] for part in parts])
    half = columns // 2
    own_ref[...] = c_ref[pl.ds(pl.multiple_of(core * half, half), half), :]
    spread_rows(r_ref[...], wide_ref)
    table_ref = arrived()

    def strip(number, real, pair, tiles):
        strips = []
        for t in tiles:
            inside = jnp.minimum(t, row_tiles - 1)
            sides = []
            for side in range(2):
                u = 2 * pair + side
                good = real & (t < row_tiles) & (table.allowed(table_ref, inside, u) == 1)
                tile = s_ref[jnp.where(good, t * columns + u, table.dummy)]
                sides.append(jnp.exp(tile + wide_ref[inside] + c_ref[pl.ds(u, 1), :]).astype(jnp.bfloat16))
            strips.append(jnp.concatenate(sides, axis=1))
        strips = jnp.concatenate(strips, axis=0)
        kept_ref[number] = strips
        return strips

    width = out_ref.shape[1]
    plan_blocks(table, table_ref, p_ref, lines, [lines - 1], width, strip, [out_ref], total_ref)


def rest_kernel(table, lines, arrived, kept_ref, p_ref, *refs):
    outs, total_ref = refs[:-1], refs[-1]
    width = outs[0].shape[1]
    strip = lambda number, real, pair, tiles: kept_ref[number]
    plan_blocks(table, arrived(), p_ref, lines, list(range(lines - 1)), width, strip, outs, total_ref)


def params(mebibytes):
    return pltpu.CompilerParams(vmem_limit_bytes=mebibytes * 2**20)


def sibling(block):
    return swap(block, "proto", 1)


def tied(*arrays):
    return lax.optimization_barrier(arrays)


def make_panel(table, mask, embeddings, shard, rows, features):
    width = shard.shape[1]
    protos = 2 * shard.shape[0]
    panel = pltpu.VMEM((table.dummy + 1, TILE, TILE), jnp.float32)
    whole = pltpu.VMEM((protos, features), jnp.bfloat16)
    row_shape = jax.ShapeDtypeStruct((table.row_tiles, TILE), jnp.float32)
    kept = pltpu.VMEM((table.dummy + 1, TILE, TILE), jnp.bfloat16)
    tiles = pltpu.VMEM((table.row_tiles, TILE, TILE), jnp.float32)

    def late(lists, places, add, e, pieces, before):
        at = 2 + len(pieces)
        return pl.pallas_call(
            with_table(panel_kernel, table, places, add),
            out_shape=(panel, whole, kept, row_shape, row_shape),
            in_specs=[ANY] + [VMEM] * (1 + len(pieces) + len(before)),
            out_specs=(VMEM,) * 5,
            scratch_shapes=[tiles, tiles] + table_scratch(lists),
            input_output_aliases={at: 0, at + 1: 1} if add else {},
            compiler_params=params(8),
            name="panel",
        )(lists, e, *pieces, *before)

    if lax.axis_size("row") != 4 or width % TILE:
        lists = table.build(mask)
        every = lax.all_gather(shard, "row", axis=1, tiled=True)
        places = [Piece(True, 0, None), Piece(False, 0, None)]
        return (lists, *late(lists, places, False, embeddings, [every, sibling(every)], []))
    half = shard.shape[0] // 2
    visits = table.dummy * TILE * TILE

    def early(lists, places, owners, pieces, before):
        at = 2 + len(pieces)
        return pl.pallas_call(
            with_table(early_panel_kernel, table, places, owners, bool(before)),
            out_shape=(panel, whole),
            in_specs=[ANY] + [VMEM] * (1 + len(pieces) + len(before)),
            out_specs=(VMEM, VMEM),
            scratch_shapes=table_scratch(lists),
            input_output_aliases={at: 0, at + 1: 1} if before else {},
            compiler_params=params(6),
            cost_estimate=pl.CostEstimate(
                flops=visits * width * len(owners), bytes_accessed=8 * visits, transcendentals=0
            ),
            name="early_panel",
        )(lists, embeddings, *pieces, *before)

    near = swap(shard, "row", 1)
    far = swap(shard, "row", 2)
    lists = table.build(mask)
    places = [Piece(True, 0, 0), Piece(False, 0, 0)]
    similar, known = early(lists, places, [0], [shard, sibling(shard)], [])
    near, far, similar, known = tied(near, far, similar, known)
    cross_top = swap(far[:half], "row", 1)
    cross_bottom = swap(near[half:], "row", 2)
    places = [Piece(own, 0, owner) for own in (True, False) for owner in (1, 2)]
    pieces = [near, far, sibling(near), sibling(far)]
    similar, known = early(lists, places, [1, 2], pieces, [similar, known])
    cross_top, cross_bottom, similar, known = tied(cross_top, cross_bottom, similar, known)
    places = [Piece(own, first, 3) for own in (True, False) for first in (0, half)]
    pieces = [cross_top, cross_bottom, sibling(cross_top), sibling(cross_bottom)]
    return (lists, *late(lists, places, True, embeddings, pieces, [similar, known]))


def scatter_partials(blocks):
    blocks = list(blocks)
    distance = 1
    while distance < len(blocks):
        for j in range(len(blocks) - distance, 0, -2 * distance):
            got = swap(blocks[j].astype(jnp.bfloat16), "proto", 2 * distance).astype(jnp.float32)
            blocks[j ^ distance] = blocks[j ^ distance].astype(jnp.float32) + got
        distance *= 2
    return blocks[0].astype(jnp.bfloat16)


def shards(embeddings, prototypes, block_mask):
    n_row, n_proto = lax.axis_size("row"), lax.axis_size("proto")
    lines = n_proto // 2
    rows, features = embeddings.shape
    protos = 2 * prototypes.shape[0]
    width = features // n_proto
    row_tiles, columns = block_mask.shape[0], 2 * block_mask.shape[1]
    log_column = math.log(rows * n_row / (protos * lines))
    table = Table(row_tiles, columns)

    other_mask = swap(block_mask, "proto", 1)
    mask, other_mask = jnp.where(block_mask == 1, 1, 0), jnp.where(other_mask == 1, 1, 0)
    mask = jnp.where(
        lax.axis_index("proto") % 2 == 0,
        jnp.concatenate([mask, other_mask], axis=1),
        jnp.concatenate([other_mask, mask], axis=1),
    )

    row_shape = jax.ShapeDtypeStruct((row_tiles, TILE), jnp.float32)
    column_shape = jax.ShapeDtypeStruct((columns, TILE), jnp.float32)
    half = columns // 2
    wide = pltpu.VMEM((row_tiles, TILE, TILE), jnp.float32)
    tall = pltpu.VMEM((columns, TILE, TILE), jnp.float32)
    factors = pltpu.VMEM((columns + 8, TILE), jnp.float32)
    lists, similar, whole, kept, first, row_part = make_panel(table, mask, embeddings, prototypes, rows, features)

    def row_exchange(part):
        others = [swap(part, "proto", 2 * j) for j in range(lines - 1, 0, -1)]
        return [part] + others[::-1]

    def column_exchange(part):
        others = [swap(part, "row", j) for j in range(n_row - 1, 0, -1)]
        return [part] + others[::-1]

    for sweep in range(ITERS):
        if sweep:
            parts = column_exchange(column_part)
            row_part = pl.pallas_call(
                with_table(row_kernel, table, log_column),
                out_shape=row_shape,
                in_specs=[ANY] + [VMEM] * (3 + len(parts)),
                out_specs=VMEM,
                scratch_shapes=[factors, factors, wide] + table_scratch(lists),
                compiler_params=params(4),
                name="row_pass",
            )(lists, similar, kept, first, *parts)
        parts = row_exchange(row_part)
        column_part, row_potential, row_out = pl.pallas_call(
            with_table(column_kernel, table),
            out_shape=(column_shape, row_shape, row_shape),
            in_specs=[ANY] + [VMEM] * (3 + len(parts)),
            out_specs=(VMEM,) * 3,
            scratch_shapes=[wide, tall] + table_scratch(lists),
            compiler_params=params(4),
            name="column_pass",
        )(lists, similar, kept, first, *parts)
    parts = column_exchange(column_part)
    block = jax.ShapeDtypeStruct((rows, width), jnp.bfloat16)

    def sums(blocks):
        taken = blocks if width % TILE == 0 else lines
        return pltpu.VMEM((row_tiles, TILE, taken * width), jnp.float32)

    last, plan, column_potential = pl.pallas_call(
        with_table(plan_kernel, table, log_column, lines),
        out_shape=[
            block,
            pltpu.VMEM((table.slots, 4 * TILE, 2 * TILE), jnp.bfloat16),
            jax.ShapeDtypeStruct((half, TILE), jnp.float32),
        ],
        in_specs=[ANY] + [VMEM] * (3 + len(parts)),
        out_specs=[VMEM] * 3,
        scratch_shapes=[pltpu.VMEM((columns, TILE), jnp.float32), wide, sums(1)] + table_scratch(lists),
        compiler_params=params(12),
        name="plan",
    )(lists, similar, row_potential, whole, *parts)
    visits = table.dummy * TILE * TILE
    blocks = pl.pallas_call(
        with_table(rest_kernel, table, lines),
        out_shape=[block] * (lines - 1),
        in_specs=[ANY] + [VMEM] * 2,
        out_specs=[VMEM] * (lines - 1),
        scratch_shapes=[sums(lines - 1)] + table_scratch(lists),
        compiler_params=params(12),
        cost_estimate=pl.CostEstimate(
            flops=2 * visits * (lines - 1) * width, bytes_accessed=4 * visits, transcendentals=0
        ),
        name="rest_of_plan",
    )(lists, plan, whole)
    blocks = list(blocks) + [last]
    targets = scatter_partials(blocks)
    return (targets, row_out.reshape(rows), column_potential.reshape(protos // 2))


def solution(mesh):
    return jax.shard_map(
        shards,
        mesh=mesh,
        in_specs=(P("row", None), P("proto", "row"), P("row", "proto")),
        out_specs=(P("row", "proto"), P("row"), P("proto")),
        check_vma=False,
    )
```
